32 devices in a mesh: dp: 8 (over y, x, core), section: 4 (over z).
Axes of the slice: x: 2, y: 2, z: 4, core: 2. Of those that a mesh axis runs over, the one named last changes fastest.
Arguments:
- tokens: bfloat16 [8192, 768], P(('dp', 'section')), may hold values from -6 to 6
- cotangent: bfloat16 [8192, 768], P(('dp', 'section')), may hold values from -6 to 6
- seg_doc: int32 [32, 2], P('dp'), may hold values from 0 to 1, as said below
- wide_in: bfloat16 [4, 768, 3072], P('section')
- half_out: bfloat16 [4, 1536, 768], P('section'), may hold values from -0.109375 to 0.109375
- norm_gain: float32 [4, 768], P('section'), may hold values from 0.5 to 1.5
- norm_bias: float32 [4, 768], P('section'), may hold values from -1.8 to 1.8
Outputs:
- layer_out: bfloat16 [8192, 768], P(('dp', 'section'))
- tokens_grad: bfloat16 [8192, 768], P(('dp', 'section'))
- wide_in_grad: float32 [4, 768, 3072], P('section')
- half_out_grad: float32 [4, 1536, 768], P('section')
- gain_grad: float32 [4, 768], P('section')
- bias_grad: float32 [4, 768], P('section')
The draws below stay inside these ranges and needn't reach their ends.
Inputs may be any that keep to these rules, and one draw needn't show every extreme that they name: `seg_doc`: in each row the numbers start at 0 and rise by 0 or 1 from segment to segment. Every group (the 4 rows i with the same i // 4) has a row holding one document of all 2 segments.
All inputs are finite; a program needn't handle non-finite values.
Results may differ from the reference program's by a relative error of at most 0.012.
Values may be sent and summed in bfloat16 or wider, within the bound.
A program may use at most 512 MiB of HBM per device.

```python
import jax
import jax.numpy as jnp
from jax import lax

D = 768
HEADS = 12
FF = 3072
SEG = 128
SEGS_MB = 2
MICRO = 4
SECTIONS = 4
MB_ALL = 32
TOKENS = 8192


def draw_seg_doc(key, part):
    key = jax.random.fold_in(key, 9)
    start_key, long_key, split_key = jax.random.split(key, 3)
    starts = jax.random.randint(start_key, (MB_ALL, SEGS_MB), 0, 2)
    group_count = MB_ALL // MICRO
    long_pick = jax.random.randint(long_key, (group_count,), 0, MICRO)
    row_ids = jnp.arange(MB_ALL)
    is_long = row_ids % MICRO == jnp.repeat(long_pick, MICRO)
    split_group = jax.random.randint(split_key, (), 0, group_count)
    split_row = split_group * MICRO + (long_pick[split_group] + 1) % MICRO
    starts = jnp.where(row_ids[:, None] == split_row, 1, starts)
    starts = jnp.where(is_long[:, None], 0, starts)
    starts = starts.at[:, 0].set(0)
    return jnp.cumsum(starts, axis=1).astype(jnp.int32)


def draw_wide_in(key, part):
    key = jax.random.fold_in(key, 5)
    full_shape = (SECTIONS, D, FF)
    entries = jax.random.normal(key, full_shape, jnp.float32)
    section_ids = lax.broadcasted_iota(jnp.int32, full_shape, 0)
    column_ids = lax.broadcasted_iota(jnp.int32, full_shape, 2)
    column_scale = jnp.where((section_ids % 2 == 0) & (column_ids >= 3 * D), 3.0, 1.0)
    return (entries * column_scale * D ** (-0.5)).astype(jnp.bfloat16)


def steps_of(stream_key, shape, cuts, smallest, top_value):
    def one(position, parts):
        draws = jax.random.uniform(jax.random.fold_in(jax.random.fold_in(stream_key, 6), position), (parts,), jnp.float32, smallest / len(cuts), top_value / len(cuts))
        return jnp.repeat(jnp.exp(draws), shape[position] // parts).reshape((-1,) + (1,) * (len(shape) - position - 1))

    level = one(*cuts[0])
    for cut in cuts[1:]:
        level = level * one(*cut)
    return level


def noise(stream_key, dims, width, bound, cuts=(), dtype=jnp.bfloat16):
    array = jax.random.normal(stream_key, dims, jnp.float32) * width
    if len(cuts) > 0:
        array = steps_of(stream_key, dims, cuts, -0.22, 0.18) * array
    return jnp.clip(array, min=-bound, max=bound).astype(dtype)


def setup_inputs(seed: int = 0) -> dict:
    keys = jax.random.split(jax.random.key(seed), 8)
    return {
        "tokens": noise(keys[0], (TOKENS, D), 1.0, 6.0, ((0, 32),)),
        "cotangent": noise(keys[1], (TOKENS, D), 1.0, 6.0, ((0, 32),)),
        "seg_doc": draw_seg_doc(jax.random.fold_in(keys[7], 71), 0),
        "wide_in": draw_wide_in(jax.random.fold_in(keys[7], 71), 0),
        "half_out": noise(keys[4], (SECTIONS, FF // 2, D), FF ** -0.5, 0.109375, ((0, 4),)),
        "norm_gain": jnp.clip(1.0 + 0.1 * jax.random.normal(keys[5], (SECTIONS, D), jnp.float32), 0.5, 1.5),
        "norm_bias": noise(keys[6], (SECTIONS, D), 0.3, 1.8, ((0, 4),), jnp.float32),
    }


@jax.custom_vjp
def low(v):
    return lax.optimization_barrier(v.astype(jnp.bfloat16)).astype(jnp.float32)

@jax.custom_vjp
def low_back(v):
    return v

def low_keep(v):
    return (low(v), None)

def low_pass(kept, grad):
    return (grad,)

def back_keep(v):
    return (v, None)

def back_low(kept, grad):
    return (low(grad),)
low.defvjp(low_keep, low_pass)
low_back.defvjp(back_keep, back_low)

def normalize(summed, gain_row, bias_row):
    average = lax.optimization_barrier(jnp.mean(summed, axis=-1, keepdims=True))
    centred = summed - average
    spread = lax.optimization_barrier(jnp.mean(centred * centred, axis=-1, keepdims=True))
    return centred * lax.rsqrt(spread + 1e-05) * gain_row + bias_row

def attend(hidden, weights, gain_row, bias_row, allowed, groups):
    highest = lax.Precision.HIGHEST
    row_count = hidden.shape[0]
    length = row_count // groups
    head_dim = D // HEADS
    qkv_all = low_back(low(jnp.dot(hidden, weights[:, :3 * D], precision=highest)))
    split = qkv_all.reshape(groups, length, 3, HEADS, head_dim)
    queries = split[:, :, 0]
    keys_all = split[:, :, 1]
    values = split[:, :, 2]
    scores = low_back(jnp.einsum('glhd,gmhd->ghlm', queries, keys_all, precision=highest) * head_dim ** (-0.5))
    if allowed is not None:
        scores = jnp.where(allowed, scores, -1000000000.0)
    attn_probs = jax.nn.softmax(scores, axis=-1)
    context = jnp.einsum('ghlm,gmhd->glhd', low(attn_probs), values, precision=highest).reshape(row_count, D)
    context = low_back(low(context))
    branch = low_back(jnp.dot(context, weights[:, 3 * D:].T, precision=highest))
    return normalize(hidden + branch, gain_row, bias_row)

def feed_forward(hidden, w_first, w_second, gain_row, bias_row):
    highest = lax.Precision.HIGHEST
    inner = low_back(jnp.dot(hidden, w_first, precision=highest))
    activated = low(jax.nn.gelu(inner, approximate=False))
    branch = low_back(jnp.dot(activated, w_second, precision=highest))
    return normalize(hidden + branch, gain_row, bias_row)

def forward(micro_in, weights_in, halves, gains, biases, doc_row):
    blocks_first = low_back(low(attend(micro_in, weights_in[0], gains[0], biases[0], None, SEGS_MB)))
    second_w = jnp.concatenate([halves[0], halves[1]], axis=0)
    second = low_back(low(feed_forward(blocks_first, weights_in[1], second_w, gains[1], biases[1])))
    blocks = second.reshape(SEGS_MB, SEG, D)
    leaders = blocks[:, 0]
    same_doc = (doc_row[:, None] == doc_row[None, :])[None, None]
    third = low_back(low(attend(leaders, weights_in[2], gains[2], biases[2], same_doc, 1)))
    last_w = jnp.concatenate([halves[2], halves[3]], axis=0)
    fourth = feed_forward(third, weights_in[3], last_w, gains[3], biases[3])
    return blocks.at[:, 0].set(fourth).reshape(SEGS_MB * SEG, D)

def reference(tokens, cotangent, seg_doc, wide_in, half_out, norm_gain, norm_bias):
    weights_in = wide_in.astype(jnp.float32)
    halves = half_out.astype(jnp.float32)
    micro_count = seg_doc.shape[0]
    inputs_mb = tokens.astype(jnp.float32).reshape(micro_count, SEGS_MB * SEG, D)
    cotan_mb = cotangent.astype(jnp.float32).reshape(micro_count, SEGS_MB * SEG, D)

    def one_micro(totals, packed):
        micro_in, micro_cot, doc_row = packed

        def local_fn(micro_x, w_in, w_half, gains, biases):
            return forward(micro_x, w_in, w_half, gains, biases, doc_row)
        result, pullback = jax.vjp(local_fn, micro_in, weights_in, halves, norm_gain, norm_bias)
        grads_all = pullback(micro_cot)
        totals = tuple((total + grad_one for total, grad_one in zip(totals, grads_all[1:])))
        return (totals, (result.astype(jnp.bfloat16), grads_all[0].astype(jnp.bfloat16)))
    zero_grads = (jnp.zeros_like(weights_in), jnp.zeros_like(halves), jnp.zeros_like(norm_gain), jnp.zeros_like(norm_bias))
    totals, (outputs, input_grads) = lax.scan(one_micro, zero_grads, (inputs_mb, cotan_mb, seg_doc))
    return (outputs.reshape(-1, D), input_grads.reshape(-1, D), totals[0], totals[1], totals[2], totals[3])
```

```python
from functools import partial

import jax
import jax.numpy as jnp
from jax import lax
from jax.experimental import pallas as pl
from jax.experimental.pallas import tpu as pltpu
from jax.sharding import PartitionSpec as P

D = 768
HEADS = 12
CUBE = 8
PIECE = D // CUBE
HALF = PIECE // 2
HOLDER = (0, 0, 0, 0, 1, 1, 1, 1, 0, 0, 1, 1, 2, 2)
GATHERED = len(HOLDER)
REDUCED = 12
OWN = {0: (0, 1, 2, 3, 8, 9), 1: (4, 5, 6, 7, 10, 11)}
PACK = 2 * D + 4 * D + 2 * D + D


def position():
    index = lax.axis_index("dp")
    return (lax.rem(index // 4, 2), lax.rem(index // 2, 2), lax.rem(index, 2), index // CUBE)


def cube_peer(y, x, core, group):
    return {"dp": group * CUBE + y * 4 + x * 2 + core}


def greet(partners):
    barrier = pltpu.get_barrier_semaphore()
    for partner in partners:
        pl.semaphore_signal(
            barrier, inc=1, device_id=partner, device_id_type=pl.DeviceIdType.MESH
        )
    return barrier


def remote(source, target, send, receive, device):
    return pltpu.make_async_remote_copy(
        src_ref=source,
        dst_ref=target,
        send_sem=send,
        recv_sem=receive,
        device_id=device,
        device_id_type=pl.DeviceIdType.MESH,
    )


def gather_kernel(
    sections, order, wide, half, vector, full, vectors,
    line_send, line_recv, cube_send, cube_recv, vector_send, vector_recv, local_sem,
):
    me = lax.axis_index("section")
    y, x, core, group = position()
    beside_x = cube_peer(y, 1 - x, core, group)
    beside_y = cube_peer(1 - y, x, core, group)
    beside_core = cube_peer(y, x, 1 - core, group)
    others = [{"section": lax.rem(me + step, sections)} for step in range(1, sections)]
    barrier = greet([beside_x, beside_y, beside_core] + others)
    pl.semaphore_wait(barrier, sections + 2)

    row = ((y * 2 + x) * 2 + core) * PIECE

    def held(block, first, rows):
        if block < 8:
            return wide.at[pl.ds(first, rows), pl.ds((block % 4) * D, D)]
        return half.at[pl.ds((block % 2) * D + first, rows), :]

    def line_copy(block, step, from_holder):
        piece = full.at[block, y, x, core]
        source = held(block, pl.multiple_of(row, PIECE), PIECE) if from_holder else piece
        return remote(
            source,
            piece,
            line_send.at[block, 0 if step > 0 else 1],
            line_recv.at[block],
            {"section": lax.rem(me + step + sections, sections)},
        )

    def local_copy(block, part):
        yy, xx, cc = part // 4, part // 2 % 2, part % 2
        return pltpu.make_async_copy(
            held(block, part * PIECE, PIECE), full.at[block, yy, xx, cc], local_sem.at[block, part]
        )

    vector_copies = [
        remote(
            vector, vectors.at[me], vector_send.at[step], vector_recv.at[step], others[step - 1]
        )
        for step in range(1, sections)
    ]
    for copy in vector_copies:
        copy.start()
    own_vector = pltpu.make_async_copy(vector, vectors.at[me], vector_send.at[0])
    own_vector.start()

    def cube_copies(block):
        upper, lower = pl.ds(0, HALF), pl.ds(HALF, HALF)
        parts = [
            (full.at[block, y, x, core, upper], beside_x),
            (full.at[block, y, x, core, lower], beside_y),
            (full.at[block, y, :, core, upper], beside_y),
            (full.at[block, :, x, core, lower], beside_x),
            (full.at[block, :, :, core], beside_core),
        ]
        return [
            partial(remote, ref, ref, cube_send.at[block, i], cube_recv.at[block, i], peer)
            for i, (ref, peer) in enumerate(parts)
        ]

    def gets(block):
        return me > HOLDER[block] if block >= REDUCED else me != HOLDER[block]

    def stage_line(block):
        holder = HOLDER[block]

        @pl.when(me == holder)
        def _():
            line_copy(block, 1, True).start()
            if holder > 0 and block < REDUCED:
                line_copy(block, -1, True).start()
            if block < REDUCED:
                for part in range(CUBE):
                    local_copy(block, part).start()

        @pl.when(me > holder)
        def _():
            copy = line_copy(block, 1, False)
            copy.wait_recv()

            @pl.when(me < sections - 1)
            def _():
                copy.start()

        if holder > 0 and block < REDUCED:

            @pl.when(me < holder)
            def _():
                copy = line_copy(block, -1, False)
                copy.wait_recv()

                @pl.when(me > 0)
                def _():
                    copy.start()

    def stage_one(block):
        @pl.when(gets(block))
        def _():
            copies = cube_copies(block)
            copies[0]().start()
            copies[1]().start()

    def stage_two(block):
        @pl.when(gets(block))
        def _():
            copies = cube_copies(block)
            copies[0]().wait_recv()
            copies[2]().start()
            copies[1]().wait_recv()
            copies[3]().start()

    def stage_three(block):
        @pl.when(gets(block))
        def _():
            copies = cube_copies(block)
            copies[2]().wait_recv()
            copies[3]().wait_recv()
            copies[4]().start()

    def finish(block):
        holder = HOLDER[block]

        @pl.when(gets(block))
        def _():
            copies = cube_copies(block)
            copies[4]().wait_recv()
            for copy in copies:
                copy().wait_send()

        @pl.when(me == holder)
        def _():
            line_copy(block, 1, True).wait_send()
            if holder > 0 and block < REDUCED:
                line_copy(block, -1, True).wait_send()
            if block < REDUCED:
                for part in range(CUBE):
                    local_copy(block, part).wait()

        @pl.when((me > holder) & (me < sections - 1))
        def _():
            line_copy(block, 1, False).wait_send()

        if holder > 1 and block < REDUCED:

            @pl.when((me < holder) & (me > 0))
            def _():
                line_copy(block, -1, False).wait_send()

    stages = (stage_line, stage_one, stage_two, stage_three)
    for tick in range(len(order) + len(stages) - 1):
        for place, stage in enumerate(stages):
            if 0 <= tick - place < len(order):
                stage(order[tick - place])
    for block in order:
        finish(block)
    own_vector.wait()
    for copy in vector_copies:
        copy.wait()


def gather_weights(sections, wide, half, vector):
    order = (0, 1, 2, 4, 3, 5, 6, 7, 8, 10, 9, 11, 12, 13)
    full, vectors = pl.pallas_call(
        partial(gather_kernel, sections, order),
        out_shape=(
            jax.ShapeDtypeStruct((GATHERED, 2, 2, 2, PIECE, D), jnp.bfloat16),
            jax.ShapeDtypeStruct((sections,) + vector.shape, jnp.float32),
        ),
        in_specs=[pl.BlockSpec(memory_space=pl.ANY)] * 3,
        out_specs=[pl.BlockSpec(memory_space=pl.ANY)] * 2,
        scratch_shapes=[
            pltpu.SemaphoreType.DMA((GATHERED, 2)),
            pltpu.SemaphoreType.DMA((GATHERED,)),
            pltpu.SemaphoreType.DMA((GATHERED, 5)),
            pltpu.SemaphoreType.DMA((GATHERED, 5)),
            pltpu.SemaphoreType.DMA((sections,)),
            pltpu.SemaphoreType.DMA((sections,)),
            pltpu.SemaphoreType.DMA((GATHERED, CUBE)),
        ],
        compiler_params=pltpu.CompilerParams(collective_id=0, has_side_effects=True),
    )(wide, half, vector)
    return full.reshape(GATHERED, D, D), vectors


def reduce_kernel(
    sections, replicas, order, parts, pack, small, total, packs, smalls,
    core_in, running, one_a, one_b, two_a, two_b, line_in, group_in, small_all, small_sum,
    load_sem, rs_send, rs_recv, line_send, line_recv, group_send, group_recv,
    ag_send, ag_recv, own_sem, pack_send, pack_recv, small_send, small_recv, sum_send, sum_recv,
):
    me = lax.axis_index("section")
    index = lax.axis_index("dp")
    y, x, core, group = position()
    groups = replicas // CUBE
    beside_x = cube_peer(y, 1 - x, core, group)
    beside_y = cube_peer(1 - y, x, core, group)
    beside_core = cube_peer(y, x, 1 - core, group)
    others = [{"section": lax.rem(me + step, sections)} for step in range(1, sections)]
    barrier = greet(others)

    def replica(step):
        return {"dp": lax.rem(index + step, replicas)}

    @pl.loop(1, replicas)
    def _(step):
        pl.semaphore_signal(
            barrier, inc=1, device_id=replica(step), device_id_type=pl.DeviceIdType.MESH
        )

    pl.semaphore_wait(barrier, sections - 1 + replicas - 1)

    upper, lower = pl.ds(0, HALF), pl.ds(HALF, HALF)

    def add(target, *sources):
        value = target[...].astype(jnp.float32)
        for source in sources:
            value = value + source[...].astype(jnp.float32)
        target[...] = value.astype(jnp.bfloat16)

    def small_copy(step):
        return remote(
            small, small_all.at[index], small_send.at[step], small_recv.at[step], replica(step)
        )

    def pack_copy(step):
        return remote(
            pack, packs.at[index], pack_send.at[step], pack_recv.at[step], replica(step)
        )

    @pl.loop(1, replicas)
    def _(step):
        small_copy(step).start()

    own_small = pltpu.make_async_copy(small, small_all.at[index], small_send.at[0])
    own_small.start()
    own_pack = pltpu.make_async_copy(pack, packs.at[index], pack_send.at[0])
    own_pack.start()

    def load(block):
        return pltpu.make_async_copy(
            parts.at[block, :, :, core], running.at[block], load_sem.at[block]
        )

    def scatter(block):
        run = running.at[block]
        pairs = [
            (parts.at[block, :, :, 1 - core], core_in.at[block], beside_core),
            (run.at[:, 1 - x, upper], one_a.at[block], beside_x),
            (run.at[1 - y, :, lower], one_b.at[block], beside_y),
            (run.at[1 - y, x, upper], two_a.at[block], beside_y),
            (run.at[y, 1 - x, lower], two_b.at[block], beside_x),
        ]
        return [
            partial(remote, source, target, rs_send.at[block, i], rs_recv.at[block, i], peer)
            for i, (source, target, peer) in enumerate(pairs)
        ]

    def to_line(block, step):
        return remote(
            running.at[block, y, x],
            line_in.at[block, 0 if step < 0 else 1],
            line_send.at[block],
            line_recv.at[block, 0 if step < 0 else 1],
            {"section": lax.rem(me + step + sections, sections)},
        )

    def to_group(block, step):
        return remote(
            running.at[block, y, x],
            group_in.at[block, step - 1],
            group_send.at[block, step - 1],
            group_recv.at[block, step - 1],
            {"dp": lax.rem(index + step * CUBE, replicas)},
        )

    def gather(block):
        place = OWN[HOLDER[block]].index(block)
        out = total.at[place]
        pairs = [
            (running.at[block, y, x, upper], out.at[y, x, core, upper], beside_y),
            (running.at[block, y, x, lower], out.at[y, x, core, lower], beside_x),
            (out.at[:, x, core, upper], out.at[:, x, core, upper], beside_x),
            (out.at[y, :, core, lower], out.at[y, :, core, lower], beside_y),
            (out.at[:, :, core], out.at[:, :, core], beside_core),
        ]
        return [
            partial(remote, source, target, ag_send.at[place, i], ag_recv.at[place, i], peer)
            for i, (source, target, peer) in enumerate(pairs)
        ]

    def own_piece(block):
        place = OWN[HOLDER[block]].index(block)
        return pltpu.make_async_copy(
            running.at[block, y, x], total.at[place, y, x, core], own_sem.at[place]
        )

    def stage_core(block):
        scatter(block)[0]().start()
        load(block).start()

    def stage_one(block):
        copies = scatter(block)
        load(block).wait()
        copies[0]().wait_recv()
        for yy in range(2):
            for xx in range(2):
                add(running.at[block, yy, xx], core_in.at[block, yy, xx])
        copies[1]().start()
        copies[2]().start()

    def stage_two(block):
        copies = scatter(block)
        copies[1]().wait_recv()
        for yy in range(2):
            add(running.at[block, yy, x, upper], one_a.at[block, yy])
        copies[3]().start()
        copies[2]().wait_recv()
        for xx in range(2):
            add(running.at[block, y, xx, lower], one_b.at[block, xx])
        copies[4]().start()

    def stage_three(block):
        copies = scatter(block)
        copies[3]().wait_recv()
        add(running.at[block, y, x, upper], two_a.at[block])
        copies[4]().wait_recv()
        add(running.at[block, y, x, lower], two_b.at[block])
        if groups > 1:
            for step in range(1, groups):
                to_group(block, step).start()
            for step in range(1, groups):
                to_group(block, step).wait()
            for step in range(1, groups):
                add(running.at[block, y, x], group_in.at[block, step - 1])

    def stage_line(hop, block):
        holder = HOLDER[block]
        for section in range(sections):
            distance = abs(section - holder)
            from_above = sections - 1 - section if section >= holder else -1
            from_below = section if section <= holder else -1
            if max(from_above, from_below) != hop:
                continue

            @pl.when(me == section)
            def _():
                if from_above > 0:
                    to_line(block, -1).wait_recv()
                    add(running.at[block, y, x], line_in.at[block, 0])
                if from_below > 0:
                    to_line(block, 1).wait_recv()
                    add(running.at[block, y, x], line_in.at[block, 1])
                if distance > 0:
                    to_line(block, -1 if section > holder else 1).start()

    def stage_spread(block):
        @pl.when(me == HOLDER[block])
        def _():
            copies = gather(block)
            own_piece(block).start()
            copies[0]().start()
            copies[1]().start()

    def stage_spread_two(block):
        @pl.when(me == HOLDER[block])
        def _():
            copies = gather(block)
            own_piece(block).wait()
            copies[0]().wait_recv()
            copies[2]().start()
            copies[1]().wait_recv()
            copies[3]().start()

    def stage_spread_core(block):
        @pl.when(me == HOLDER[block])
        def _():
            copies = gather(block)
            copies[2]().wait_recv()
            copies[3]().wait_recv()
            copies[4]().start()

    def finish(block):
        for copy in scatter(block):
            copy().wait_send()

        @pl.when(me != HOLDER[block])
        def _():
            to_line(block, 1).wait_send()

        @pl.when(me == HOLDER[block])
        def _():
            copies = gather(block)
            copies[4]().wait_recv()
            for copy in copies:
                copy().wait_send()

    stages = (
        [stage_core, stage_one, stage_two, stage_three]
        + [partial(stage_line, hop) for hop in range(sections)]
        + [stage_spread, stage_spread_two, stage_spread_core]
    )
    for tick in range(len(order) + len(stages) - 1):
        for place, stage in enumerate(stages):
            if 0 <= tick - place < len(order):
                stage(order[tick - place])
        if tick == 2:

            @pl.loop(1, replicas)
            def _(step):
                pack_copy(step).start()

        if tick == 4:
            own_small.wait()

            @pl.loop(1, replicas)
            def _(step):
                small_copy(step).wait()

            small_sum[...] = jnp.sum(small_all[...], axis=0)
            for step in range(1, sections):
                remote(
                    small_sum, smalls.at[me], sum_send.at[step], sum_recv.at[step],
                    others[step - 1],
                ).start()
            pltpu.make_async_copy(small_sum, smalls.at[me], sum_send.at[0]).start()
    for block in order:
        finish(block)
    for step in range(1, sections):
        remote(
            small_sum, smalls.at[me], sum_send.at[step], sum_recv.at[step], others[step - 1]
        ).wait()
    pltpu.make_async_copy(small_sum, smalls.at[me], sum_send.at[0]).wait()
    own_pack.wait()

    @pl.loop(1, replicas)
    def _(step):
        pack_copy(step).wait()


def reduce_grads(sections, replicas, parts, pack, small):
    order = (8, 10, 9, 11, 4, 5, 6, 7, 0, 1, 2, 3)
    groups = replicas // CUBE
    owned = len(OWN[0])
    cube = (2, 2, 2, PIECE, D)
    low = jnp.bfloat16
    dma = pltpu.SemaphoreType.DMA
    return pl.pallas_call(
        partial(reduce_kernel, sections, replicas, order),
        out_shape=(
            jax.ShapeDtypeStruct((owned,) + cube, low),
            jax.ShapeDtypeStruct((replicas,) + pack.shape, low),
            jax.ShapeDtypeStruct((sections,) + small.shape, jnp.float32),
        ),
        in_specs=[pl.BlockSpec(memory_space=pl.ANY)] * 3,
        out_specs=[pl.BlockSpec(memory_space=pl.ANY)] * 3,
        scratch_shapes=[
            pltpu.VMEM((REDUCED, 2, 2, PIECE, D), low),
            pltpu.VMEM((REDUCED, 2, 2, PIECE, D), low),
            pltpu.VMEM((REDUCED, 2, HALF, D), low),
            pltpu.VMEM((REDUCED, 2, HALF, D), low),
            pltpu.VMEM((REDUCED, HALF, D), low),
            pltpu.VMEM((REDUCED, HALF, D), low),
            pltpu.VMEM((REDUCED, 2, PIECE, D), low),
            pltpu.VMEM((REDUCED, max(groups - 1, 1), PIECE, D), low),
            pltpu.VMEM((replicas,) + small.shape, jnp.float32),
            pltpu.VMEM(small.shape, jnp.float32),
            dma((REDUCED,)),
            dma((REDUCED, 5)),
            dma((REDUCED, 5)),
            dma((REDUCED,)),
            dma((REDUCED, 2)),
            dma((REDUCED, max(groups - 1, 1))),
            dma((REDUCED, max(groups - 1, 1))),
            dma((owned, 5)),
            dma((owned, 5)),
            dma((owned,)),
            dma((replicas,)),
            dma((replicas,)),
            dma((replicas,)),
            dma((replicas,)),
            dma((sections,)),
            dma((sections,)),
        ],
        compiler_params=pltpu.CompilerParams(
            collective_id=1, has_side_effects=True, vmem_limit_bytes=56 * 1024 * 1024
        ),
    )(parts.reshape((REDUCED,) + cube), pack, small)


def passed_along(value, axis, steps):
    count = lax.axis_size(axis)
    leading, last = (max(0, -steps), min(count, count - steps))
    return lax.ppermute(value, axis, [(source, source + steps) for source in range(leading, last)])


def normalize(summed, gain_row, bias_row):
    average = jnp.mean(summed, axis=-1, keepdims=True)
    centred = summed - average
    inv_dev = lax.rsqrt(jnp.mean(centred * centred, axis=-1, keepdims=True) + 1e-05)
    normed = centred * inv_dev
    return (normed * gain_row + bias_row, normed, inv_dev)


def normalize_backward(grad_out, normed, inv_dev, gain_row):
    grad_full = grad_out.astype(jnp.float32)
    grad_gain = jnp.sum(grad_full * normed, axis=0)
    grad_bias = jnp.sum(grad_full, axis=0)
    grad_normed = grad_full * gain_row
    grad_sum = inv_dev * (
        grad_normed
        - jnp.mean(grad_normed, axis=-1, keepdims=True)
        - normed * jnp.mean(grad_normed * normed, axis=-1, keepdims=True)
    )
    return (grad_sum, grad_gain, grad_bias)


def attention_forward(hidden, w_qkv, w_out, gain_row, bias_row, allowed, groups):
    row_count = hidden.shape[0]
    length = row_count // groups
    head_dim = D // HEADS
    qkv_all = jnp.dot(hidden, w_qkv, preferred_element_type=jnp.float32).astype(jnp.bfloat16)
    split = qkv_all.reshape(groups, length, 3, HEADS, head_dim)
    queries = split[:, :, 0]
    keys_all = split[:, :, 1]
    values = split[:, :, 2]
    scores = jnp.einsum(
        "glhd,gmhd->ghlm", queries, keys_all, preferred_element_type=jnp.float32
    ) * head_dim ** (-0.5)
    if allowed is not None:
        scores = jnp.where(allowed, scores, -1000000000.0)
    attn_probs = jax.nn.softmax(scores, axis=-1)
    probs_low = attn_probs.astype(jnp.bfloat16)
    context = jnp.einsum("ghlm,gmhd->glhd", probs_low, values, preferred_element_type=jnp.float32)
    context = context.reshape(row_count, D).astype(jnp.bfloat16)
    branch = lax.dot_general(
        context, w_out, (((1,), (1,)), ((), ())), preferred_element_type=jnp.float32
    )
    output, normed, inv_dev = normalize(hidden.astype(jnp.float32) + branch, gain_row, bias_row)
    return (output, (queries, keys_all, values, attn_probs, probs_low, context, normed, inv_dev))


def attention_backward(hidden, w_qkv, w_out, gain_row, saved, grad_out, groups):
    queries, keys_all, values, attn_probs, probs_low, context, normed, inv_dev = saved
    row_count = hidden.shape[0]
    length = row_count // groups
    head_dim = D // HEADS
    scale = head_dim ** (-0.5)
    grad_sum, grad_gain, grad_bias = normalize_backward(grad_out, normed, inv_dev, gain_row)
    grad_branch = grad_sum.astype(jnp.bfloat16)
    grad_context = jnp.dot(grad_branch, w_out, preferred_element_type=jnp.float32).astype(
        jnp.bfloat16
    )
    grad_heads = grad_context.reshape(groups, length, HEADS, head_dim)
    grad_probs = jnp.einsum(
        "glhd,gmhd->ghlm", grad_heads, values, preferred_element_type=jnp.float32
    )
    grad_values = jnp.einsum(
        "ghlm,glhd->gmhd", probs_low, grad_heads, preferred_element_type=jnp.float32
    )
    grad_scores = attn_probs * (
        grad_probs - jnp.sum(attn_probs * grad_probs, axis=-1, keepdims=True)
    )
    grad_scores = grad_scores.astype(jnp.bfloat16)
    grad_queries = (
        jnp.einsum("ghlm,gmhd->glhd", grad_scores, keys_all, preferred_element_type=jnp.float32)
        * scale
    )
    grad_keys = (
        jnp.einsum("ghlm,glhd->gmhd", grad_scores, queries, preferred_element_type=jnp.float32)
        * scale
    )
    grad_qkv = (
        jnp.stack([grad_queries, grad_keys, grad_values], axis=2)
        .reshape(row_count, 3 * D)
        .astype(jnp.bfloat16)
    )
    grad_hidden = (
        lax.dot_general(
            grad_qkv, w_qkv, (((1,), (1,)), ((), ())), preferred_element_type=jnp.float32
        )
        + grad_sum
    )
    return (grad_hidden, grad_branch, grad_qkv, grad_gain, grad_bias)


def mlp_forward(hidden, w_first, w_second, gain_row, bias_row):
    inner = jnp.dot(hidden, w_first, preferred_element_type=jnp.float32)
    activated = jax.nn.gelu(inner, approximate=False).astype(jnp.bfloat16)
    branch = jnp.dot(activated, w_second, preferred_element_type=jnp.float32)
    output, normed, inv_dev = normalize(hidden.astype(jnp.float32) + branch, gain_row, bias_row)
    return (output, (inner, activated, normed, inv_dev))


def mlp_backward(hidden, w_first, w_second, gain_row, saved, grad_out):
    inner, activated, normed, inv_dev = saved
    grad_sum, grad_gain, grad_bias = normalize_backward(grad_out, normed, inv_dev, gain_row)
    grad_branch = grad_sum.astype(jnp.bfloat16)
    grad_act = lax.dot_general(
        grad_branch, w_second, (((1,), (1,)), ((), ())), preferred_element_type=jnp.float32
    )
    unused_out, gelu_pull = jax.vjp(partial(jax.nn.gelu, approximate=False), inner)
    grad_inner = gelu_pull(grad_act)[0].astype(jnp.bfloat16)
    grad_hidden = (
        lax.dot_general(
            grad_inner, w_first, (((1,), (1,)), ((), ())), preferred_element_type=jnp.float32
        )
        + grad_sum
    )
    return (grad_hidden, grad_branch, grad_inner, grad_gain, grad_bias)


def outer(left, right):
    return lax.dot_general(
        left, right, (((0,), (0,)), ((), ())), preferred_element_type=jnp.float32
    )


def on_device(tokens, cotangent, seg_doc, wide_in, half_out, norm_gain, norm_bias):
    sections = lax.axis_size("section")
    replicas = lax.axis_size("dp")
    me = lax.axis_index("section")
    seg_count = seg_doc.shape[1]
    low = jnp.bfloat16
    own_wide, own_half = wide_in[0], half_out[0]
    own_gain, own_bias = norm_gain[0], norm_bias[0]
    vector = jnp.concatenate([norm_gain, norm_bias, jnp.zeros((6, D), jnp.float32)], axis=0)
    blocks, vectors = gather_weights(sections, own_wide, own_half, vector)

    def wide_of(first):
        return jnp.concatenate([blocks[first + i] for i in range(4)], axis=1)

    w_qkv = jnp.concatenate([blocks[i] for i in range(3)], axis=1)
    w_out = blocks[3]
    w_first = wide_of(4)
    w_second = blocks[8:12].reshape(4 * D, D)
    last_second = jnp.concatenate([blocks[12:14].reshape(2 * D, D), own_half], axis=0)

    first, saved_first = attention_forward(
        tokens, w_qkv, w_out, vectors[0, 0], vectors[0, 1], None, seg_count
    )
    h1 = first.astype(low)
    second, saved_second = mlp_forward(h1, w_first, w_second, vectors[1, 0], vectors[1, 1])
    h2 = second.astype(low)

    def leaders_of(rows):
        return rows.reshape(seg_count, -1, D)[:, 0]

    both = jnp.stack([leaders_of(h2), leaders_of(cotangent)])
    both = lax.all_gather(both, "section", axis=1, tiled=True)
    leaders, lead_cot = both[0], both[1]
    allowed = (seg_doc[:, :, None] == seg_doc[:, None, :])[:, None]
    third, saved_third = attention_forward(
        leaders, own_wide[:, : 3 * D], own_wide[:, 3 * D :], own_gain, own_bias, allowed,
        seg_doc.shape[0],
    )
    h3 = passed_along(third.astype(low), "section", 1)
    fourth, saved_fourth = mlp_forward(h3, own_wide, last_second, own_gain, own_bias)
    grad_h3, lead_branch, lead_inner, gain_fourth, bias_fourth = mlp_backward(
        h3, own_wide, last_second, own_gain, saved_fourth, lead_cot
    )
    grad_third = passed_along(grad_h3.astype(low), "section", -1)
    grad_lead, lead_out_branch, lead_qkv, gain_third, bias_third = attention_backward(
        leaders, own_wide[:, : 3 * D], own_wide[:, 3 * D :], own_gain, saved_third, grad_third,
        seg_doc.shape[0],
    )
    pair = jnp.where(me == sections - 1, fourth, grad_lead).astype(low)
    pairs = lax.all_gather(pair, "section", axis=0)
    mine = lax.dynamic_slice_in_dim(pairs, me * seg_count, seg_count, axis=1)
    lead_out, lead_grad = mine[sections - 1], mine[sections - 2]

    def with_leaders(rows, lead_rows):
        return rows.reshape(seg_count, -1, D).at[:, 0].set(lead_rows).reshape(rows.shape)

    layer_out = with_leaders(h2, lead_out)
    grad_h2 = with_leaders(cotangent, lead_grad)
    grad_h1, gb_second, grad_inner, gain_second, bias_second = mlp_backward(
        h1, w_first, w_second, vectors[1, 0], saved_second, grad_h2
    )
    grad_tokens, gb_first, grad_qkv, gain_first, bias_first = attention_backward(
        tokens, w_qkv, w_out, vectors[0, 0], saved_first, grad_h1.astype(low), seg_count
    )
    context, activated = saved_first[5], saved_second[1]
    grad_blocks = (
        [outer(tokens, grad_qkv[:, i * D : (i + 1) * D]) for i in range(3)]
        + [outer(gb_first, context)]
        + [outer(h1, grad_inner[:, i * D : (i + 1) * D]) for i in range(4)]
        + [outer(activated[:, i * D : (i + 1) * D], gb_second) for i in range(4)]
    )
    parts = jnp.stack([block.astype(low) for block in grad_blocks])

    is_last = me == sections - 1
    act = saved_fourth[1]
    handed = passed_along(jnp.concatenate([act[:, : 2 * D], lead_branch], axis=1), "section", -1)
    pack = jnp.concatenate(
        [
            jnp.where(is_last, h3, leaders),
            jnp.where(is_last, h3, lead_out_branch),
            jnp.where(is_last, lead_inner, jnp.concatenate([lead_qkv, saved_third[5]], axis=1)),
            jnp.where(is_last, act[:, 2 * D :], handed[:, : 2 * D]),
            jnp.where(is_last, lead_branch, handed[:, 2 * D :]),
        ],
        axis=1,
    )
    pack = jnp.concatenate([pack, jnp.zeros((16 - pack.shape[0], PACK), low)], axis=0)
    small = jnp.stack(
        [
            gain_first,
            bias_first,
            gain_second,
            bias_second,
            jnp.where(is_last, gain_fourth, gain_third),
            jnp.where(is_last, bias_fourth, bias_third),
            jnp.zeros_like(gain_first),
            jnp.zeros_like(gain_first),
        ]
    )
    total, packs, smalls = reduce_grads(sections, replicas, parts, pack, small)
    total = total.reshape(-1, D, D)
    packs = packs.reshape(-1, PACK)
    cross = me >= 2
    lead_wide = jnp.concatenate(
        [
            outer(packs[:, :D], packs[:, 2 * D : 5 * D]),
            outer(packs[:, D : 2 * D], packs[:, 5 * D : 6 * D]),
        ],
        axis=1,
    )
    lead_half = outer(packs[:, 6 * D : 8 * D], packs[:, 8 * D :])
    wide_total = jnp.where(
        cross, lead_wide, jnp.concatenate([total[i] for i in range(4)], axis=1).astype(jnp.float32)
    )
    half_total = jnp.where(cross, lead_half, total[4:].reshape(2 * D, D).astype(jnp.float32))
    small_total = jnp.sum(smalls, axis=0)
    own_small = lax.dynamic_index_in_dim(smalls, me, 0, keepdims=False)

    def vector_total(row):
        near = jnp.where(me == 0, small_total[row], small_total[2 + row])
        return jnp.where(cross, own_small[4 + row], near)

    return (
        layer_out,
        grad_tokens.astype(low),
        wide_total[None],
        half_total[None],
        vector_total(0)[None],
        vector_total(1)[None],
    )


def solution(mesh):
    placed = (
        P(("dp", "section"), None),
        P(("dp", "section"), None),
        P("dp", None),
        P("section", None, None),
        P("section", None, None),
        P("section", None),
        P("section", None),
    )
    return jax.shard_map(
        on_device,
        mesh=mesh,
        in_specs=placed,
        out_specs=(
            P(("dp", "section"), None),
            P(("dp", "section"), None),
            P("section", None, None),
            P("section", None, None),
            P("section", None),
            P("section", None),
        ),
        check_vma=False,
    )
```

```python
from functools import partial

import jax
import jax.numpy as jnp
from jax import lax
from jax.experimental import pallas as pl
from jax.experimental.pallas import tpu as pltpu
from jax.sharding import PartitionSpec as P

D = 768
HEADS = 12
PAIRS = HEADS // 2
CUBE = 8
PIECE = D // CUBE
HALF = PIECE // 2
SLAB = 16
HOLDER = (0, 0, 0, 0, 1, 1, 1, 1, 0, 0, 1, 1, 2, 2)
GATHERED = len(HOLDER)
REDUCED = 12
OWN = {0: (0, 1, 2, 3, 8, 9), 1: (4, 5, 6, 7, 10, 11)}
OWNED = len(OWN[0])
LEFT_OUT, RIGHT, LEFT_HALF, RIGHT_HALF, PACK = D, 2 * D, 6 * D, 8 * D, 9 * D
LOW = jnp.bfloat16
F32 = jnp.float32
DMA = pltpu.SemaphoreType.DMA
MESH = pl.DeviceIdType.MESH


def dot(left, right):
    return jnp.dot(left, right, preferred_element_type=F32)


def dot_right(left, right):
    return lax.dot_general(left, right, (((1,), (1,)), ((), ())), preferred_element_type=F32)


def outer(left, right):
    return lax.dot_general(left, right, (((0,), (0,)), ((), ())), preferred_element_type=F32)


def normalize(summed, gain, bias):
    average = jnp.mean(summed, axis=-1, keepdims=True)
    centred = summed - average
    inv_dev = lax.rsqrt(jnp.mean(centred * centred, axis=-1, keepdims=True) + 1e-05)
    normed = centred * inv_dev
    return normed * gain + bias, normed, inv_dev


def normalize_backward(grad, normed, inv_dev, gain):
    scaled = grad * gain
    mean_scaled = jnp.mean(scaled, axis=-1, keepdims=True)
    mean_normed = jnp.mean(scaled * normed, axis=-1, keepdims=True)
    grad_sum = inv_dev * (scaled - mean_scaled - normed * mean_normed)
    return (
        grad_sum,
        jnp.sum(grad * normed, axis=0, keepdims=True),
        jnp.sum(grad, axis=0, keepdims=True),
    )


def gelu_pair(value):
    bell = jnp.exp(-0.5 * value * value)
    base = 1.0 + (0.3275911 * 0.7071067811865476) * jnp.abs(value)
    guess = pl.reciprocal(base, approx=True)
    t = guess * (2.0 - base * guess)
    poly = t * (
        0.5 * 0.254829592
        + t
        * (
            0.5 * -0.284496736
            + t * (0.5 * 1.421413741 + t * (0.5 * -1.453152027 + t * (0.5 * 1.061405429)))
        )
    )
    tail = poly * bell
    below = jnp.where(value >= 0, 1.0 - tail, tail)
    return value * below, below + value * bell * 0.3989422804014327


def position():
    index = lax.axis_index("dp")
    return (lax.rem(index // 4, 2), lax.rem(index // 2, 2), lax.rem(index, 2), index // CUBE)


def remote(source, target, send, receive, device):
    return pltpu.make_async_remote_copy(
        src_ref=source,
        dst_ref=target,
        send_sem=send,
        recv_sem=receive,
        device_id=device,
        device_id_type=MESH,
    )


def layer_kernel(
    sections, replicas,
    tokens, cotangent, code, vector, wide, half,
    layer_out, grad_tokens, total, packs, smalls, group_in,
    blocks, own, core_in, one_a, one_b, two_a, two_b, line_in, vectors,
    qkv, probs, context, h1, norm0, dev0, summed, act, slope, norm1, dev1, branch, kept,
    cot_slab, h1_slab, h2_slab, cot_leads, h1_leads, h2_leads,
    lead_third, lead_fourth, lead_grad3, lead_grad2, lead_grad1, handed,
    lead_qkv, lead_probs, lead_context, lead_norm, lead_dev, lead_act, lead_slope, pack,
    small, small_all, small_sum, group_piece,
    line_send, line_recv, cube_send, cube_recv, load_sem,
    rs_send, rs_recv, z_send, z_recv, group_send, group_recv, group_load, ag_send, ag_recv,
    out_sem, pack_send, pack_recv, small_send, small_recv, sum_send, sum_recv,
    vector_send, vector_recv, lead_send, lead_recv, spread_send, spread_recv, hop_send, hop_recv,
    credit,
):
    me = lax.axis_index("section")
    index = lax.axis_index("dp")
    y, x, core, group = position()
    groups = replicas // CUBE
    rows_all = tokens.shape[0]
    seg_rows = rows_all // 2

    def cube_peer(yy, xx, cc):
        return {"dp": group * CUBE + yy * 4 + xx * 2 + cc}

    beside_x = cube_peer(y, 1 - x, core)
    beside_y = cube_peer(1 - y, x, core)
    beside_core = cube_peer(y, x, 1 - core)
    others = [{"section": lax.rem(me + step, sections)} for step in range(1, sections)]

    def replica(step):
        return {"dp": lax.rem(index + step, replicas)}

    barrier = pltpu.get_barrier_semaphore()
    for other in others:
        pl.semaphore_signal(barrier, inc=1, device_id=other, device_id_type=MESH)

    @pl.loop(1, replicas)
    def _(step):
        pl.semaphore_signal(barrier, inc=1, device_id=replica(step), device_id_type=MESH)

    def held(block):
        if block < 8:
            return wide.at[:, :, :, :, pl.ds((block % 4) * D, D)]
        return half.at[block % 2]

    def load(block):
        return pltpu.make_async_copy(held(block), blocks.at[block], load_sem.at[block])

    def load_own(place):
        return pltpu.make_async_copy(
            held(place if place < 4 else 4 + place), own.at[place], load_sem.at[place]
        )

    for holder in (0, 1):

        @pl.when(me == holder)
        def _():
            for block in OWN[holder]:
                load(block).start()

    @pl.when(me >= 2)
    def _():
        for place in range(4):
            load_own(place).start()

    @pl.when(me == 3)
    def _():
        for place in (4, 5):
            load_own(place).start()

    pl.semaphore_wait(barrier, sections - 1 + replicas - 1)

    row_of = lax.broadcasted_iota(jnp.int32, (SLAB, D), 0)

    def lead_rows(ref):
        first = ref[0:SLAB].astype(F32)[0:1]
        second = ref[seg_rows : seg_rows + SLAB].astype(F32)[0:1]
        return jnp.where(row_of == 0, first, jnp.where(row_of == 1, second, 0.0)).astype(LOW)

    def lead_copy(kind, slab, target, reader):
        return remote(
            slab, target.at[me], lead_send.at[kind], lead_recv.at[kind, me], {"section": reader}
        )

    def lead_start(kind, slab, target, reader):
        @pl.when(me != reader)
        def _():
            lead_copy(kind, slab, target, reader).start()

        @pl.when(me == reader)
        def _():
            target[reader] = slab[...]

    def lead_wait(kind, slab, target, reader):
        for section in range(sections):
            if section != reader:
                remote(
                    slab, target.at[section], lead_send.at[kind], lead_recv.at[kind, section],
                    {"section": section},
                ).wait_recv()

    def collected(target):
        value = jnp.zeros((SLAB, D), F32)
        for section in range(sections):
            slab = target[section].astype(F32)
            for lead in range(2):
                value = jnp.where(row_of == 2 * section + lead, slab[lead : lead + 1], value)
        return value

    def spread_copy(kind, slab, step):
        return remote(
            slab, slab, spread_send.at[kind, step], spread_recv.at[kind], others[step - 1]
        )

    def hop_copy(kind, slab, step):
        return remote(
            slab, slab, hop_send.at[kind], hop_recv.at[kind],
            {"section": lax.rem(me + step + sections, sections)},
        )

    def my_leads(slab):
        value = slab[...].astype(F32)
        return [
            jnp.sum(jnp.where(row_of == 2 * me + lead, value, 0.0), axis=0, keepdims=True)
            for lead in range(2)
        ]

    COT, H1, H2 = 0, 1, 2
    FOURTH, GRAD1 = 0, 1
    THIRD, GRAD3, GRAD2, HAND = 0, 1, 2, 3

    def vector_copy(step):
        return remote(
            vector, vectors.at[me], vector_send.at[step], vector_recv.at[step], others[step - 1]
        )

    for step in range(1, sections):
        vector_copy(step).start()
    vectors[me] = vector[...]
    cot_slab[...] = lead_rows(cotangent)
    lead_start(COT, cot_slab, cot_leads, 3)

    upper, lower = pl.ds(0, HALF), pl.ds(HALF, HALF)

    def place_of(block):
        return blocks.at[block] if block < REDUCED else own.at[block - REDUCED + 6]

    def line_copy(block, step, from_holder):
        piece = place_of(block).at[y, x, core]
        if not from_holder:
            source = piece
        elif block < 8:
            source = wide.at[y, x, core, :, pl.ds((block % 4) * D, D)]
        else:
            source = half.at[block % 2, y, x, core]
        return remote(
            source,
            piece,
            line_send.at[block, 0 if step > 0 else 1],
            line_recv.at[block],
            {"section": lax.rem(me + step + sections, sections)},
        )

    def cube_copy(block, stage):
        full = place_of(block)
        ref, peer = (
            (full.at[y, x, core, upper], beside_x),
            (full.at[y, x, core, lower], beside_y),
            (full.at[y, :, core, upper], beside_y),
            (full.at[:, x, core, lower], beside_x),
            (full.at[:, :, core], beside_core),
        )[stage]
        return remote(ref, ref, cube_send.at[block, stage], cube_recv.at[block, stage], peer)

    def gets(block):
        return me > HOLDER[block] if block >= REDUCED else me != HOLDER[block]

    def gather_line(block):
        holder = HOLDER[block]

        @pl.when(me == holder)
        def _():
            line_copy(block, 1, True).start()
            if holder > 0 and block < REDUCED:
                line_copy(block, -1, True).start()

        @pl.when(me > holder)
        def _():
            copy = line_copy(block, 1, False)
            copy.wait_recv()

            @pl.when(me < sections - 1)
            def _():
                copy.start()

        if holder > 0 and block < REDUCED:

            @pl.when(me < holder)
            def _():
                copy = line_copy(block, -1, False)
                copy.wait_recv()

                @pl.when(me > 0)
                def _():
                    copy.start()

    def gather_one(block):
        @pl.when(gets(block))
        def _():
            cube_copy(block, 0).start()
            cube_copy(block, 1).start()

    def gather_two(block):
        @pl.when(gets(block))
        def _():
            cube_copy(block, 0).wait_recv()
            cube_copy(block, 2).start()
            cube_copy(block, 1).wait_recv()
            cube_copy(block, 3).start()

    def gather_three(block):
        @pl.when(gets(block))
        def _():
            cube_copy(block, 2).wait_recv()
            cube_copy(block, 3).wait_recv()
            cube_copy(block, 4).start()

    def gather_ready(block):
        @pl.when(gets(block))
        def _():
            cube_copy(block, 4).wait_recv()

        if block < REDUCED:

            @pl.when(me == HOLDER[block])
            def _():
                load(block).wait()

    def gather_finish(block):
        holder = HOLDER[block]

        @pl.when(gets(block))
        def _():
            for stage in range(5):
                cube_copy(block, stage).wait_send()

        @pl.when(me == holder)
        def _():
            line_copy(block, 1, True).wait_send()
            if holder > 0 and block < REDUCED:
                line_copy(block, -1, True).wait_send()

        @pl.when((me > holder) & (me < sections - 1))
        def _():
            line_copy(block, 1, False).wait_send()

    gather_order = tuple(range(GATHERED))
    gather_stages = (gather_line, gather_one, gather_two, gather_three)

    def gather_tick(tick):
        for place, stage in enumerate(gather_stages):
            if 0 <= tick - place < GATHERED:
                stage(gather_order[tick - place])
        if 0 <= tick - 4 < GATHERED:
            gather_ready(gather_order[tick - 4])

    def weight(block):
        return blocks[block].reshape(D, D)

    lane_of = lax.broadcasted_iota(jnp.int32, (1, 128), 1)
    first_half = lane_of < 64
    head_masks = (first_half.astype(LOW), (~first_half).astype(LOW))

    def chunks(count, body):
        size = rows_all // count

        @pl.loop(0, count)
        def _(step):
            body(pl.multiple_of(step * size, size), size)

    def project(block):
        qkv[:, block * D : (block + 1) * D] = dot(tokens[...], weight(block)).astype(LOW)

    def pair_slices(seg, pair):
        rows = pl.ds(seg * seg_rows, seg_rows)
        return rows, [
            pl.ds(pl.multiple_of(part * D + pair * 128, 128), 128) for part in range(3)
        ]

    def heads_forward(seg):
        @pl.loop(0, PAIRS)
        def _(pair):
            rows, (at_q, at_k, at_v) = pair_slices(seg, pair)
            query, key, value = qkv[rows, at_q], qkv[rows, at_k], qkv[rows, at_v]
            parts = []
            for place in range(2):
                scores = dot_right(query * head_masks[place], key) * 0.125
                raised = jnp.exp(scores - jnp.max(scores, axis=-1, keepdims=True))
                prob = raised / jnp.sum(raised, axis=-1, keepdims=True)
                probs[seg, pair, place] = prob
                parts.append(dot(prob.astype(LOW), value))
            context[rows, at_q] = jnp.where(first_half, parts[0], parts[1]).astype(LOW)

    def attention_close():
        summed[...] = dot_right(context[...], weight(3))
        gain, bias = vectors[0, 0:1], vectors[0, 1:2]

        def body(start, size):
            rows = pl.ds(start, size)
            out, normed, inv_dev = normalize(
                tokens[rows].astype(F32) + summed[rows], gain, bias
            )
            norm0[rows] = normed
            dev0[rows] = jnp.broadcast_to(inv_dev, (size, 128))
            h1[rows] = out.astype(LOW)

        chunks(8, body)

    def inner_block(block):
        summed[...] = dot(h1[...], weight(4 + block))
        lanes = slice(block * D, (block + 1) * D)

        def body(start, size):
            rows = pl.ds(start, size)
            value, grade = gelu_pair(summed[rows])
            act[rows, lanes] = value.astype(LOW)
            slope[rows, lanes] = grade

        chunks(8, body)

    def second_block(block):
        product = dot(act[:, block * D : (block + 1) * D], weight(8 + block))
        if block == 0:
            branch[...] = product
        else:
            branch[...] += product

    def mlp_close():
        gain, bias = vectors[1, 0:1], vectors[1, 1:2]

        def body(start, size):
            rows = pl.ds(start, size)
            out, normed, inv_dev = normalize(h1[rows].astype(F32) + branch[rows], gain, bias)
            norm1[rows] = normed
            dev1[rows] = jnp.broadcast_to(inv_dev, (size, 128))
            layer_out[rows] = out.astype(LOW)

        chunks(8, body)

    def add_small(row, value):
        small[row : row + 1] += value

    def mlp_open_backward():
        gain = vectors[1, 0:1]

        def body(start, size):
            rows = pl.ds(start, size)
            place = start + lax.broadcasted_iota(jnp.int32, (size, D), 0)
            grad = jnp.where(
                lax.rem(place, seg_rows) == 0, 0.0, cotangent[rows].astype(F32)
            )
            grad_sum, grad_gain, grad_bias = normalize_backward(
                grad, norm1[rows], dev1[rows][:, 0:1], gain
            )
            branch[rows] = grad_sum
            kept[rows] = grad_sum.astype(LOW)
            add_small(2, grad_gain)
            add_small(3, grad_bias)

        chunks(8, body)

    def part(block):
        return block + 4 if block < 4 else block + 8

    def store_part(block, value):
        blocks[part(block)] = value.astype(LOW).reshape(2, 2, 2, PIECE, D)

    def second_grad(block):
        store_part(8 + block, outer(act[:, block * D : (block + 1) * D], kept[...]))

    def inner_grad(block):
        lanes = slice(block * D, (block + 1) * D)
        grad_act = dot_right(kept[...], weight(8 + block))
        act[:, lanes] = (grad_act * slope[:, lanes]).astype(LOW)
        branch[...] += dot_right(act[:, lanes], weight(4 + block))
        store_part(4 + block, outer(h1[...], act[:, lanes]))

    def attention_open_backward():
        gain = vectors[0, 0:1]
        leads = my_leads(lead_grad1)

        def body(start, size):
            rows = pl.ds(start, size)
            place = start + lax.broadcasted_iota(jnp.int32, (size, D), 0)
            grad = branch[rows]
            grad = jnp.where(place == 0, leads[0], jnp.where(place == seg_rows, leads[1], grad))
            grad = grad.astype(LOW).astype(F32)
            grad_sum, grad_gain, grad_bias = normalize_backward(
                grad, norm0[rows], dev0[rows][:, 0:1], gain
            )
            summed[rows] = grad_sum
            kept[rows] = grad_sum.astype(LOW)
            add_small(0, grad_gain)
            add_small(1, grad_bias)

        chunks(8, body)

    def out_grad():
        store_part(3, outer(kept[...], context[...]))
        context[...] = dot(kept[...], weight(3)).astype(LOW)

    def heads_backward(seg):
        @pl.loop(0, PAIRS)
        def _(pair):
            rows, (at_q, at_k, at_v) = pair_slices(seg, pair)
            query, key, value = qkv[rows, at_q], qkv[rows, at_k], qkv[rows, at_v]
            grad = context[rows, at_q]
            grads = ([], [], [])
            for place in range(2):
                prob = probs[seg, pair, place]
                grad_prob = dot_right(grad * head_masks[place], value)
                inside = prob * grad_prob
                grad_score = inside - prob * jnp.sum(inside, axis=-1, keepdims=True)
                grad_score = grad_score.astype(LOW)
                grads[0].append(dot(grad_score, key))
                grads[1].append(outer(grad_score, query))
                grads[2].append(outer(prob.astype(LOW), grad))
            for at, pair_grads, scale in zip((at_q, at_k, at_v), grads, (0.125, 0.125, 1.0)):
                merged = jnp.where(first_half, pair_grads[0], pair_grads[1]) * scale
                qkv[rows, at] = merged.astype(LOW)

    def project_grad(block):
        store_part(block, outer(tokens[...], qkv[:, block * D : (block + 1) * D]))

    def tokens_back(block):
        summed[...] += dot_right(qkv[:, block * D : (block + 1) * D], weight(block))

    def leads_mlp_forward(value, first, second, gain, bias):
        total_branch = value.astype(F32)
        for block in range(4):
            lanes = slice(block * D, (block + 1) * D)
            out, grade = gelu_pair(dot(value, first(block)))
            lead_act[:, lanes] = out.astype(LOW)
            lead_slope[:, lanes] = grade
            total_branch = total_branch + dot(lead_act[:, lanes], second(block))
        out, normed, inv_dev = normalize(total_branch, gain, bias)
        lead_norm[...] = normed
        lead_dev[...] = jnp.broadcast_to(inv_dev, (SLAB, 128))
        pack[:, 0:D] = value
        pack[:, LEFT_OUT:RIGHT] = value
        return out

    def leads_mlp_backward(grad, first, second, gain):
        grad_sum, grad_gain, grad_bias = normalize_backward(
            grad, lead_norm[...], lead_dev[:, 0:1], gain
        )
        add_small(4, grad_gain)
        add_small(5, grad_bias)
        low_sum = grad_sum.astype(LOW)
        result = grad_sum
        for block in range(4):
            lanes = slice(block * D, (block + 1) * D)
            grad_inner = (dot_right(low_sum, second(block)) * lead_slope[:, lanes]).astype(LOW)
            pack[:, RIGHT + block * D : RIGHT + (block + 1) * D] = grad_inner
            result = result + dot_right(grad_inner, first(block))
        pack[:, LEFT_HALF:RIGHT_HALF] = lead_act[:, 2 * D :]
        pack[:, RIGHT_HALF:] = low_sum
        handed[:, 0 : 2 * D] = lead_act[:, 0 : 2 * D]
        handed[:, 2 * D :] = low_sum
        return result

    def own_weight(place):
        return own[place].reshape(D, D)

    def last_second(block):
        return own_weight(6 + block if block < 2 else 2 + block)

    def leads_first():
        @pl.when(me == 2)
        def _():
            lead_wait(H2, h2_slab, h2_leads, 2)
            for place in range(4):
                load_own(place).wait()
            value = collected(h2_leads).astype(LOW)
            pack[:, 0:D] = value
            for block in range(3):
                lead_qkv[:, block * D : (block + 1) * D] = dot(value, own_weight(block)).astype(LOW)
            sort = code[...]
            for pair in range(PAIRS):
                at = [slice(p * D + pair * 128, p * D + (pair + 1) * 128) for p in range(3)]
                query, key, val = (lead_qkv[:, lanes] for lanes in at)
                parts = []
                for place in range(2):
                    scores = dot_right(query * head_masks[place], key) * 0.125
                    scores = jnp.where(
                        sort > 1.5, scores, jnp.where(sort > 0.5, -1000000000.0, -1e30)
                    )
                    raised = jnp.exp(scores - jnp.max(scores, axis=-1, keepdims=True))
                    prob = raised / jnp.sum(raised, axis=-1, keepdims=True)
                    lead_probs[pair, place] = prob
                    parts.append(dot(prob.astype(LOW), val))
                lead_context[:, pair * 128 : (pair + 1) * 128] = jnp.where(
                    first_half, parts[0], parts[1]
                ).astype(LOW)
            summed_rows = value.astype(F32) + dot_right(lead_context[...], own_weight(3))
            out, normed, inv_dev = normalize(summed_rows, vectors[2, 0:1], vectors[2, 1:2])
            lead_norm[...] = normed
            lead_dev[...] = jnp.broadcast_to(inv_dev, (SLAB, 128))
            lead_third[...] = out.astype(LOW)
            hop_copy(THIRD, lead_third, 1).start()

        @pl.when(me == 1)
        def _():
            lead_wait(H1, h1_slab, h1_leads, 1)
            leads_mlp_forward(
                collected(h1_leads).astype(LOW),
                lambda block: weight(4 + block),
                lambda block: weight(8 + block),
                vectors[1, 0:1],
                vectors[1, 1:2],
            )

    def leads_second():
        @pl.when(me == 3)
        def _():
            hop_copy(THIRD, lead_third, -1).wait_recv()
            for place in range(6):
                load_own(place).wait()
            out = leads_mlp_forward(
                lead_third[...], own_weight, last_second, vectors[3, 0:1], vectors[3, 1:2]
            )
            lead_fourth[...] = out.astype(LOW)
            for step in range(1, sections):
                spread_copy(FOURTH, lead_fourth, step).start()
            lead_wait(COT, cot_slab, cot_leads, 3)
            grad = leads_mlp_backward(
                collected(cot_leads), own_weight, last_second, vectors[3, 0:1]
            )
            lead_grad3[...] = grad.astype(LOW)
            hop_copy(GRAD3, lead_grad3, -1).start()
            hop_copy(HAND, handed, -1).start()

    def leads_third():
        @pl.when(me == 2)
        def _():
            hop_copy(GRAD3, lead_grad3, 1).wait_recv()
            grad_sum, grad_gain, grad_bias = normalize_backward(
                lead_grad3[...].astype(F32), lead_norm[...], lead_dev[:, 0:1], vectors[2, 0:1]
            )
            add_small(4, grad_gain)
            add_small(5, grad_bias)
            low_sum = grad_sum.astype(LOW)
            pack[:, LEFT_OUT:RIGHT] = low_sum
            pack[:, RIGHT + 3 * D : LEFT_HALF] = lead_context[...]
            grad_context = dot(low_sum, own_weight(3)).astype(LOW)
            for pair in range(PAIRS):
                at = [slice(p * D + pair * 128, p * D + (pair + 1) * 128) for p in range(3)]
                query, key, val = (lead_qkv[:, lanes] for lanes in at)
                grad = grad_context[:, pair * 128 : (pair + 1) * 128]
                grads = ([], [], [])
                for place in range(2):
                    prob = lead_probs[pair, place]
                    grad_prob = dot_right(grad * head_masks[place], val)
                    inside = prob * grad_prob
                    grad_score = inside - prob * jnp.sum(inside, axis=-1, keepdims=True)
                    grad_score = grad_score.astype(LOW)
                    grads[0].append(dot(grad_score, key))
                    grads[1].append(outer(grad_score, query))
                    grads[2].append(outer(prob.astype(LOW), grad))
                for lanes, pair_grads, scale in zip(at, grads, (0.125, 0.125, 1.0)):
                    merged = jnp.where(first_half, pair_grads[0], pair_grads[1]) * scale
                    pack[:, RIGHT + lanes.start : RIGHT + lanes.stop] = merged.astype(LOW)
            result = grad_sum
            for block in range(3):
                result = result + dot_right(
                    pack[:, RIGHT + block * D : RIGHT + (block + 1) * D], own_weight(block)
                )
            lead_grad2[...] = result.astype(LOW)
            hop_copy(GRAD2, lead_grad2, -1).start()
            hop_copy(HAND, handed, 1).wait_recv()
            pack[:, LEFT_HALF:] = handed[...]

    def leads_fourth():
        @pl.when(me == 1)
        def _():
            hop_copy(GRAD2, lead_grad2, 1).wait_recv()
            grad = leads_mlp_backward(
                lead_grad2[...].astype(F32),
                lambda block: weight(4 + block),
                lambda block: weight(8 + block),
                vectors[1, 0:1],
            )
            lead_grad1[...] = grad.astype(LOW)
            for step in range(1, sections):
                spread_copy(GRAD1, lead_grad1, step).start()
            hop_copy(HAND, handed, -1).start()

    def pack_copy(step):
        return remote(
            pack, packs.at[index], pack_send.at[step], pack_recv.at[step], replica(step)
        )

    def own_pack():
        return pltpu.make_async_copy(pack, packs.at[index], pack_send.at[0])

    def leads_close():
        @pl.when(me != 3)
        def _():
            spread_copy(FOURTH, lead_fourth, 1).wait_recv()

        leads = my_leads(lead_fourth)
        for lead in range(2):
            rows = pl.ds(lead * seg_rows, SLAB)
            layer_out[rows] = jnp.where(
                row_of == 0, leads[lead], layer_out[rows].astype(F32)
            ).astype(LOW)

        @pl.when(me != 1)
        def _():
            spread_copy(GRAD1, lead_grad1, 1).wait_recv()

        @pl.when(me == 0)
        def _():
            hop_copy(HAND, handed, 1).wait_recv()
            pack[:, 0:LEFT_HALF] = jnp.zeros((SLAB, LEFT_HALF), LOW)
            pack[:, LEFT_HALF:] = handed[...]

        own_pack().start()

        @pl.loop(1, replicas)
        def _(step):
            pack_copy(step).start()

    def add(target, *sources):
        value = target[...].astype(F32)
        for source in sources:
            value = value + source[...].astype(F32)
        target[...] = value.astype(LOW)

    def landing(block):
        return blocks.at[8 + block, 0] if block < 4 else core_in.at[block - 4]

    def scatter(block, stage):
        run = blocks.at[part(block)]
        source, target, peer = (
            (run.at[:, :, 1 - core], landing(block), beside_core),
            (run.at[:, 1 - x, core, upper], one_a.at[block], beside_x),
            (run.at[1 - y, :, core, lower], one_b.at[block], beside_y),
            (run.at[1 - y, x, core, upper], two_a.at[block], beside_y),
            (run.at[y, 1 - x, core, lower], two_b.at[block], beside_x),
        )[stage]
        return remote(source, target, rs_send.at[block, stage], rs_recv.at[block, stage], peer)

    def to_line(block, step):
        side = 0 if step < 0 else 1
        return remote(
            blocks.at[part(block), y, x, core],
            line_in.at[block, side],
            z_send.at[block],
            z_recv.at[block, side],
            {"section": lax.rem(me + step + sections, sections)},
        )

    def to_group(block, step):
        return remote(
            blocks.at[part(block), y, x, core],
            group_in.at[block, step - 1],
            group_send.at[block, step - 1],
            group_recv.at[block, step - 1],
            {"dp": lax.rem(index + step * CUBE, replicas)},
        )

    def gather_back(block, stage):
        place = OWN[HOLDER[block]].index(block)
        run = blocks.at[part(block)]
        ref, peer = (
            (run.at[y, x, core, upper], beside_y),
            (run.at[y, x, core, lower], beside_x),
            (run.at[:, x, core, upper], beside_x),
            (run.at[y, :, core, lower], beside_y),
            (run.at[:, :, core], beside_core),
        )[stage]
        return remote(ref, ref, ag_send.at[place, stage], ag_recv.at[place, stage], peer)

    def write_out(block):
        place = OWN[HOLDER[block]].index(block)
        return pltpu.make_async_copy(
            blocks.at[part(block)], total.at[place], out_sem.at[place]
        )

    def reduce_core(block):
        scatter(block, 0).start()

    def reduce_one(block):
        scatter(block, 0).wait()
        arrived = landing(block)
        for yy in range(2):
            for xx in range(2):
                add(blocks.at[part(block), yy, xx, core], arrived.at[yy, xx])
        scatter(block, 1).start()
        scatter(block, 2).start()

    def reduce_two(block):
        run = blocks.at[part(block)]
        scatter(block, 1).wait()
        for yy in range(2):
            add(run.at[yy, x, core, upper], one_a.at[block, yy])
        scatter(block, 3).start()
        scatter(block, 2).wait()
        for xx in range(2):
            add(run.at[y, xx, core, lower], one_b.at[block, xx])
        scatter(block, 4).start()

    def reduce_three(block):
        run = blocks.at[part(block)]
        scatter(block, 3).wait()
        add(run.at[y, x, core, upper], two_a.at[block])
        scatter(block, 4).wait()
        add(run.at[y, x, core, lower], two_b.at[block])
        if groups > 1:
            for step in range(1, groups):
                to_group(block, step).start()
            for step in range(1, groups):
                to_group(block, step).wait()
            for step in range(1, groups):
                copy = pltpu.make_async_copy(group_in.at[block, step - 1], group_piece, group_load)
                copy.start()
                copy.wait()
                add(run.at[y, x, core], group_piece)
        reduce_line(0, block)

    def reduce_line(hop, block):
        holder = HOLDER[block]
        target = blocks.at[part(block), y, x, core]
        for section in range(sections):
            from_above = sections - 1 - section if section >= holder else -1
            from_below = section if section <= holder else -1
            if max(from_above, from_below) != hop:
                continue

            @pl.when(me == section)
            def _():
                if from_above > 0:
                    to_line(block, -1).wait_recv()
                    add(target, line_in.at[block, 0])
                if from_below > 0:
                    to_line(block, 1).wait_recv()
                    add(target, line_in.at[block, 1])
                if section != holder:
                    to_line(block, -1 if section > holder else 1).start()

    def spread_one(block):
        @pl.when(me == HOLDER[block])
        def _():
            gather_back(block, 0).start()
            gather_back(block, 1).start()

    def spread_two(block):
        @pl.when(me == HOLDER[block])
        def _():
            gather_back(block, 0).wait()
            gather_back(block, 2).start()
            gather_back(block, 1).wait()
            gather_back(block, 3).start()

    def spread_core(block):
        @pl.when(me == HOLDER[block])
        def _():
            gather_back(block, 2).wait()
            gather_back(block, 3).wait()
            gather_back(block, 4).start()

    def spread_done(block):
        @pl.when(me == HOLDER[block])
        def _():
            gather_back(block, 4).wait()
            write_out(block).start()

        @pl.when(me != HOLDER[block])
        def _():
            to_line(block, 1).wait_send()

    reduce_stages = (
        [reduce_one, reduce_two, reduce_three]
        + [partial(reduce_line, hop) for hop in range(1, sections)]
        + [spread_one, spread_two, spread_core, spread_done]
    )

    def reduce_tick(order, tick):
        for place, stage in enumerate(reduce_stages):
            if 0 <= tick - 1 - place < len(order):
                stage(order[tick - 1 - place])

    wave_one, wave_two = (8, 9, 10, 11, 4, 5, 6, 7), (3, 0, 1, 2)
    ticks_one = len(wave_one) + len(reduce_stages)
    ticks_two = len(wave_two) + len(reduce_stages)

    small[...] = jnp.zeros_like(small)
    for tick in range(GATHERED + 4):
        gather_tick(tick)
        if tick == 4:
            for step in range(1, sections):
                vector_copy(step).wait()
        if 4 <= tick < 7:
            project(tick - 4)
        if tick == 6:
            heads_forward(0)
        if tick == 7:
            heads_forward(1)
            attention_close()
            h1_slab[...] = lead_rows(h1)
            lead_start(H1, h1_slab, h1_leads, 1)
        if 8 <= tick < 12:
            inner_block(tick - 8)
        if 12 <= tick < 16:
            second_block(tick - 12)
        if tick == 15:
            mlp_close()
            h2_slab[...] = lead_rows(layer_out)
            lead_start(H2, h2_slab, h2_leads, 2)
            mlp_open_backward()

    for block in gather_order:
        gather_finish(block)

    step = 0
    for block in range(4):
        second_grad(block)
        reduce_core(8 + block)
        reduce_tick(wave_one, step)
        step += 1
    leads_first()
    for block in range(4):
        inner_grad(block)
        reduce_core(4 + block)
        reduce_tick(wave_one, step)
        step += 1
    leads_second()
    for _ in range(2):
        reduce_tick(wave_one, step)
        step += 1
    leads_third()
    reduce_tick(wave_one, step)
    step += 1
    leads_fourth()
    pl.semaphore_signal(credit, inc=1, device_id=beside_core, device_id_type=MESH)
    reduce_tick(wave_one, step)
    step += 1
    leads_close()
    attention_open_backward()
    out_grad()
    pl.semaphore_wait(credit, 1)
    reduce_core(3)
    reduce_tick(wave_one, step)
    step += 1
    heads_backward(0)
    heads_backward(1)
    later = 1
    for block in range(3):
        project_grad(block)
        reduce_core(block)
        reduce_tick(wave_one, step)
        reduce_tick(wave_two, later)
        step += 1
        later += 1

    def small_copy(step):
        return remote(
            small, small_all.at[index], small_send.at[step], small_recv.at[step], replica(step)
        )

    def sum_copy(step):
        return remote(
            small_sum, smalls.at[me], sum_send.at[step], sum_recv.at[step], others[step - 1]
        )

    def own_sum():
        return pltpu.make_async_copy(small_sum, smalls.at[me], sum_send.at[0])

    @pl.loop(1, replicas)
    def _(step):
        small_copy(step).start()

    small_all[index] = small[...]
    for block in range(3):
        tokens_back(block)
        if step < ticks_one:
            reduce_tick(wave_one, step)
            step += 1
        reduce_tick(wave_two, later)
        later += 1
    grad_tokens[...] = summed[...].astype(LOW)

    @pl.loop(1, replicas)
    def _(step):
        small_copy(step).wait()

    small_sum[...] = jnp.sum(small_all[...], axis=0)
    for place in range(1, sections):
        sum_copy(place).start()
    own_sum().start()
    while step < ticks_one or later < ticks_two:
        if step < ticks_one:
            reduce_tick(wave_one, step)
            step += 1
        if later < ticks_two:
            reduce_tick(wave_two, later)
            later += 1

    for place in range(1, sections):
        sum_copy(place).wait()
    own_sum().wait()
    own_pack().wait()

    @pl.loop(1, replicas)
    def _(step):
        pack_copy(step).wait()

    for holder in (0, 1):

        @pl.when(me == holder)
        def _():
            for block in OWN[holder]:
                write_out(block).wait()

    for kind, slab, target, reader in (
        (COT, cot_slab, cot_leads, 3),
        (H1, h1_slab, h1_leads, 1),
        (H2, h2_slab, h2_leads, 2),
    ):

        @pl.when(me != reader)
        def _():
            lead_copy(kind, slab, target, reader).wait_send()

    @pl.when(me == 1)
    def _():
        for place in range(1, sections):
            spread_copy(GRAD1, lead_grad1, place).wait_send()
        hop_copy(HAND, handed, -1).wait_send()

    @pl.when(me == 2)
    def _():
        hop_copy(THIRD, lead_third, 1).wait_send()
        hop_copy(GRAD2, lead_grad2, -1).wait_send()

    @pl.when(me == 3)
    def _():
        for place in range(1, sections):
            spread_copy(FOURTH, lead_fourth, place).wait_send()
        hop_copy(GRAD3, lead_grad3, -1).wait_send()
        hop_copy(HAND, handed, -1).wait_send()


def run_layers(sections, replicas, tokens, cotangent, code, vector, wide, half):
    groups = replicas // CUBE
    rows = tokens.shape[0]
    block = (2, 2, 2, PIECE, D)
    reduced_groups = max(groups - 1, 1)
    in_vmem = pl.BlockSpec(memory_space=pltpu.VMEM)
    anywhere = pl.BlockSpec(memory_space=pl.ANY)
    slab = pltpu.VMEM((SLAB, D), LOW)
    leads = pltpu.VMEM((sections, SLAB, D), LOW)
    return pl.pallas_call(
        partial(layer_kernel, sections, replicas),
        out_shape=(
            jax.ShapeDtypeStruct(tokens.shape, LOW),
            jax.ShapeDtypeStruct(tokens.shape, LOW),
            jax.ShapeDtypeStruct((OWNED,) + block, LOW),
            jax.ShapeDtypeStruct((replicas, SLAB, PACK), LOW),
            jax.ShapeDtypeStruct((sections,) + vector.shape, F32),
            jax.ShapeDtypeStruct(
                (REDUCED if groups > 1 else 1, reduced_groups, PIECE, D), LOW
            ),
        ),
        in_specs=[in_vmem] * 4 + [anywhere] * 2,
        out_specs=[in_vmem] * 2 + [anywhere] * 4,
        scratch_shapes=[
            pltpu.VMEM((REDUCED + 8,) + block, LOW),
            pltpu.VMEM((8,) + block, LOW),
            pltpu.VMEM((8, 2, 2, PIECE, D), LOW),
            pltpu.VMEM((REDUCED, 2, HALF, D), LOW),
            pltpu.VMEM((REDUCED, 2, HALF, D), LOW),
            pltpu.VMEM((REDUCED, HALF, D), LOW),
            pltpu.VMEM((REDUCED, HALF, D), LOW),
            pltpu.VMEM((REDUCED, 2, PIECE, D), LOW),
            pltpu.VMEM((sections,) + vector.shape, F32),
            pltpu.VMEM((rows, 3 * D), LOW),
            pltpu.VMEM((2, PAIRS, 2, rows // 2, rows // 2), F32),
            pltpu.VMEM((rows, D), LOW),
            pltpu.VMEM((rows, D), LOW),
            pltpu.VMEM((rows, D), F32),
            pltpu.VMEM((rows, 128), F32),
            pltpu.VMEM((rows, D), F32),
            pltpu.VMEM((rows, 4 * D), LOW),
            pltpu.VMEM((rows, 4 * D), F32),
            pltpu.VMEM((rows, D), F32),
            pltpu.VMEM((rows, 128), F32),
            pltpu.VMEM((rows, D), F32),
            pltpu.VMEM((rows, D), LOW),
            slab, slab, slab, leads, leads, leads,
            slab, slab, slab, slab, slab,
            pltpu.VMEM((SLAB, 3 * D), LOW),
            pltpu.VMEM((SLAB, 3 * D), LOW),
            pltpu.VMEM((PAIRS, 2, SLAB, SLAB), F32),
            slab,
            pltpu.VMEM((SLAB, D), F32),
            pltpu.VMEM((SLAB, 128), F32),
            pltpu.VMEM((SLAB, 4 * D), LOW),
            pltpu.VMEM((SLAB, 4 * D), F32),
            pltpu.VMEM((SLAB, PACK), LOW),
            pltpu.VMEM(vector.shape, F32),
            pltpu.VMEM((replicas,) + vector.shape, F32),
            pltpu.VMEM(vector.shape, F32),
            pltpu.VMEM((PIECE, D), LOW),
            DMA((GATHERED, 2)),
            DMA((GATHERED,)),
            DMA((GATHERED, 5)),
            DMA((GATHERED, 5)),
            DMA((GATHERED,)),
            DMA((REDUCED, 5)),
            DMA((REDUCED, 5)),
            DMA((REDUCED,)),
            DMA((REDUCED, 2)),
            DMA((REDUCED, reduced_groups)),
            DMA((REDUCED, reduced_groups)),
            DMA,
            DMA((OWNED, 5)),
            DMA((OWNED, 5)),
            DMA((OWNED,)),
            DMA((replicas,)),
            DMA((replicas,)),
            DMA((replicas,)),
            DMA((replicas,)),
            DMA((sections,)),
            DMA((sections,)),
            DMA((sections,)),
            DMA((sections,)),
            DMA((3,)),
            DMA((3, sections)),
            DMA((2, sections)),
            DMA((2,)),
            DMA((4,)),
            DMA((4,)),
            pltpu.SemaphoreType.REGULAR,
        ],
        compiler_params=pltpu.CompilerParams(
            collective_id=0, has_side_effects=True, vmem_limit_bytes=VMEM_BYTES
        ),
    )(tokens, cotangent, code, vector, wide, half)


VMEM_BYTES = 62 * 1024 * 1024


def close_kernel(total, packs, smalls, wide_out, half_out, gain_out, bias_out):
    me = lax.axis_index("section")
    step = pl.program_id(0)
    near = me < 2
    packed = packs[...].reshape(-1, PACK)
    summed = jnp.where(near, total[0].reshape(D, D).astype(F32), 0.0)

    def wide_step(block):
        @pl.when(step == block)
        def _():
            left = packed[:, 0:D] if block < 3 else packed[:, LEFT_OUT:RIGHT]
            right = packed[:, RIGHT + block * D : RIGHT + (block + 1) * D]
            wide_out[0] = summed + outer(left, right)

    def half_step(block):
        @pl.when(step == 4 + block)
        def _():
            left = packed[:, LEFT_HALF + block * D : LEFT_HALF + (block + 1) * D]
            half_out[0] = summed + outer(left, packed[:, RIGHT_HALF:])

    for block in range(4):
        wide_step(block)
    for block in range(2):
        half_step(block)

    @pl.when(step == 0)
    def _():
        every = jnp.sum(smalls[...], axis=0)
        mine = smalls[me]
        for row, out in ((0, gain_out), (1, bias_out)):
            value = jnp.where(me == 0, every[row : row + 1], every[2 + row : 3 + row])
            value = jnp.where(near, value, 0.0) + mine[4 + row : 5 + row]
            out[...] = value


def close(total, packs, smalls):
    whole = lambda array: pl.BlockSpec(array.shape, lambda step: (0,) * array.ndim)
    return pl.pallas_call(
        close_kernel,
        grid=(OWNED,),
        out_shape=(
            jax.ShapeDtypeStruct((1, D, 4 * D), F32),
            jax.ShapeDtypeStruct((1, 2 * D, D), F32),
            jax.ShapeDtypeStruct((1, D), F32),
            jax.ShapeDtypeStruct((1, D), F32),
        ),
        in_specs=[
            pl.BlockSpec((1,) + total.shape[1:], lambda step: (step, 0, 0, 0, 0, 0)),
            whole(packs),
            whole(smalls),
        ],
        out_specs=[
            pl.BlockSpec((1, D, D), lambda step: (0, 0, jnp.minimum(step, 3))),
            pl.BlockSpec((1, D, D), lambda step: (0, jnp.maximum(step - 4, 0), 0)),
            pl.BlockSpec((1, D), lambda step: (0, 0)),
            pl.BlockSpec((1, D), lambda step: (0, 0)),
        ],
        compiler_params=pltpu.CompilerParams(vmem_limit_bytes=VMEM_BYTES),
    )(total, packs, smalls)


def on_device(tokens, cotangent, seg_doc, wide_in, half_out, norm_gain, norm_bias):
    sections = lax.axis_size("section")
    replicas = lax.axis_size("dp")
    vector = jnp.concatenate([norm_gain, norm_bias, jnp.zeros((6, D), F32)], axis=0)
    doc = jnp.concatenate([seg_doc.reshape(-1), jnp.zeros((SLAB - seg_doc.size,), jnp.int32)])
    owner = jnp.arange(SLAB) // seg_doc.shape[1]
    same = owner[:, None] == owner[None, :]
    code = jnp.where(same, jnp.where(doc[:, None] == doc[None, :], 2.0, 1.0), 0.0)
    wide = wide_in.reshape(2, 2, 2, PIECE, 4 * D)
    half = half_out.reshape(2, 2, 2, 2, PIECE, D)
    layer_out, grad_tokens, total, packs, smalls, _ = run_layers(
        sections, replicas, tokens, cotangent, code.astype(F32), vector, wide, half
    )
    return (layer_out, grad_tokens) + tuple(close(total, packs, smalls))


def solution(mesh):
    placed = (
        P(("dp", "section"), None),
        P(("dp", "section"), None),
        P("dp", None),
        P("section", None, None),
        P("section", None, None),
        P("section", None),
        P("section", None),
    )
    return jax.shard_map(
        on_device,
        mesh=mesh,
        in_specs=placed,
        out_specs=(
            P(("dp", "section"), None),
            P(("dp", "section"), None),
            P("section", None, None),
            P("section", None, None),
            P("section", None),
            P("section", None),
        ),
        check_vma=False,
    )
```

```python
from functools import partial

import jax
import jax.numpy as jnp
from jax import lax
from jax.experimental import pallas as pl
from jax.experimental.pallas import tpu as pltpu
from jax.sharding import PartitionSpec as P

D = 768
HEADS = 12
PAIRS = HEADS // 2
CUBE = 8
PIECE = D // CUBE
HALF = PIECE // 2
WIDTH = D // 2
SLAB = 16
HOLDER = (0, 0, 0, 0, 1, 1, 1, 1, 0, 0, 1, 1, 2, 2)
GATHERED = len(HOLDER)
ROUNDS = 2 * GATHERED
REDUCED = 12
OWN = {0: (0, 1, 2, 3, 8, 9), 1: (4, 5, 6, 7, 10, 11)}
OWNED = len(OWN[0])
LEFT_OUT, RIGHT, LEFT_HALF, RIGHT_HALF, PACK = D, 2 * D, 6 * D, 8 * D, 9 * D
HALF_PACK = PACK // 2
LOW = jnp.bfloat16
F32 = jnp.float32
DMA = pltpu.SemaphoreType.DMA
MESH = pl.DeviceIdType.MESH


def dot(left, right):
    return jnp.dot(left, right, preferred_element_type=F32)


def dot_right(left, right):
    return lax.dot_general(left, right, (((1,), (1,)), ((), ())), preferred_element_type=F32)


def outer(left, right):
    return lax.dot_general(left, right, (((0,), (0,)), ((), ())), preferred_element_type=F32)


def normalize(summed, gain, bias):
    average = jnp.mean(summed, axis=-1, keepdims=True)
    centred = summed - average
    inv_dev = lax.rsqrt(jnp.mean(centred * centred, axis=-1, keepdims=True) + 1e-05)
    normed = centred * inv_dev
    return normed * gain + bias, normed, inv_dev


def normalize_backward(grad, normed, inv_dev, gain):
    scaled = grad * gain
    mean_scaled = jnp.mean(scaled, axis=-1, keepdims=True)
    mean_normed = jnp.mean(scaled * normed, axis=-1, keepdims=True)
    grad_sum = inv_dev * (scaled - mean_scaled - normed * mean_normed)
    return (
        grad_sum,
        jnp.sum(grad * normed, axis=0, keepdims=True),
        jnp.sum(grad, axis=0, keepdims=True),
    )


def gelu_pair(value):
    bell = jnp.exp(-0.5 * value * value)
    base = 1.0 + (0.3275911 * 0.7071067811865476) * jnp.abs(value)
    guess = pl.reciprocal(base, approx=True)
    t = guess * (2.0 - base * guess)
    poly = t * (
        0.5 * 0.254829592
        + t
        * (
            0.5 * -0.284496736
            + t * (0.5 * 1.421413741 + t * (0.5 * -1.453152027 + t * (0.5 * 1.061405429)))
        )
    )
    tail = poly * bell
    below = jnp.where(value >= 0, 1.0 - tail, tail)
    return value * below, below + value * bell * 0.3989422804014327


def position():
    index = lax.axis_index("dp")
    return (lax.rem(index // 4, 2), lax.rem(index // 2, 2), lax.rem(index, 2), index // CUBE)


def remote(source, target, send, receive, device):
    return pltpu.make_async_remote_copy(
        src_ref=source,
        dst_ref=target,
        send_sem=send,
        recv_sem=receive,
        device_id=device,
        device_id_type=MESH,
    )


def layer_kernel(
    sections, replicas,
    tokens, cotangent, seg_doc, norm_gain, norm_bias, wide, half,
    layer_out, grad_tokens, total, packs, smalls, group_in,
    blocks, own, core_in, one_a, one_b, two_a, two_b, line_in, vectors,
    qkv, probs, context, h1, norm0, dev0, summed, act, slope, norm1, dev1, branch, kept,
    cot_slab, h1_slab, h2_slab, cot_leads, h1_leads, h2_leads,
    lead_third, lead_fourth, lead_grad3, lead_grad2, lead_grad1, handed,
    lead_qkv, lead_probs, lead_context, lead_norm, lead_dev, lead_act, lead_slope, pack, pack_in, factors,
    small, small_all, small_sum, group_piece,
    line_send, line_recv, cube_send, cube_recv, load_sem,
    rs_send, rs_recv, z_send, z_recv, group_send, group_recv, group_load, ag_send, ag_recv,
    out_sem, pack_send, pack_recv, group_pack_send, group_pack_recv, small_send, small_recv, sum_send, sum_recv,
    vector_send, vector_recv, lead_send, lead_recv, spread_send, spread_recv, hop_send, hop_recv,
    credit,
):
    me = lax.axis_index("section")
    index = lax.axis_index("dp")
    y, x, core, group = position()
    groups = replicas // CUBE
    rows_all = tokens.shape[0]
    seg_rows = rows_all // 2

    def cube_peer(yy, xx, cc):
        return {"dp": group * CUBE + yy * 4 + xx * 2 + cc}

    beside_x = cube_peer(y, 1 - x, core)
    beside_y = cube_peer(1 - y, x, core)
    beside_core = cube_peer(y, x, 1 - core)
    others = [{"section": lax.rem(me + step, sections)} for step in range(1, sections)]

    def replica(step):
        return {"dp": lax.rem(index + step, replicas)}

    barrier = pltpu.get_barrier_semaphore()
    for other in others:
        pl.semaphore_signal(barrier, inc=1, device_id=other, device_id_type=MESH)

    @pl.loop(1, replicas)
    def _(step):
        pl.semaphore_signal(barrier, inc=1, device_id=replica(step), device_id_type=MESH)

    def held(block):
        if block < 8:
            return wide.at[:, :, :, :, pl.ds((block % 4) * D, D)]
        return half.at[block % 2]

    def load(block):
        return pltpu.make_async_copy(held(block), blocks.at[block], load_sem.at[block])

    def load_own(place):
        return pltpu.make_async_copy(
            held(place if place < 4 else 4 + place), own.at[place], load_sem.at[place]
        )

    for holder in (0, 1):

        @pl.when(me == holder)
        def _():
            for block in OWN[holder]:
                load(block).start()

    @pl.when(me >= 2)
    def _():
        for place in range(4):
            load_own(place).start()

    @pl.when(me == 3)
    def _():
        for place in (4, 5):
            load_own(place).start()

    pl.semaphore_wait(barrier, sections - 1 + replicas - 1)

    row_of = lax.broadcasted_iota(jnp.int32, (SLAB, D), 0)

    def lead_rows(ref):
        first = ref[0:SLAB].astype(F32)[0:1]
        second = ref[seg_rows : seg_rows + SLAB].astype(F32)[0:1]
        return jnp.where(row_of == 0, first, jnp.where(row_of == 1, second, 0.0)).astype(LOW)

    def lead_copy(kind, slab, target, reader):
        return remote(
            slab, target.at[me], lead_send.at[kind], lead_recv.at[kind, me], {"section": reader}
        )

    def lead_start(kind, slab, target, reader):
        @pl.when(me != reader)
        def _():
            lead_copy(kind, slab, target, reader).start()

        @pl.when(me == reader)
        def _():
            target[reader] = slab[...]

    def lead_wait(kind, slab, target, reader):
        for section in range(sections):
            if section != reader:
                remote(
                    slab, target.at[section], lead_send.at[kind], lead_recv.at[kind, section],
                    {"section": section},
                ).wait_recv()

    def collected(target):
        value = jnp.zeros((SLAB, D), F32)
        for section in range(sections):
            slab = target[section].astype(F32)
            for lead in range(2):
                value = jnp.where(row_of == 2 * section + lead, slab[lead : lead + 1], value)
        return value

    def spread_copy(kind, slab, step):
        return remote(
            slab, slab, spread_send.at[kind, step], spread_recv.at[kind], others[step - 1]
        )

    def hop_copy(kind, slab, step):
        return remote(
            slab, slab, hop_send.at[kind], hop_recv.at[kind],
            {"section": lax.rem(me + step + sections, sections)},
        )

    def my_leads(slab):
        value = slab[...].astype(F32)
        return [
            jnp.sum(jnp.where(row_of == 2 * me + lead, value, 0.0), axis=0, keepdims=True)
            for lead in range(2)
        ]

    COT, H1, H2 = 0, 1, 2
    FOURTH, GRAD1 = 0, 1
    THIRD, GRAD3, GRAD2, HAND = 0, 1, 2, 3

    def vector_copy(step):
        return remote(
            vectors.at[me], vectors.at[me], vector_send.at[step], vector_recv.at[step],
            others[step - 1],
        )

    vectors[me, 0:1] = norm_gain[...]
    vectors[me, 1:2] = norm_bias[...]
    for step in range(1, sections):
        vector_copy(step).start()
    cot_slab[...] = lead_rows(cotangent)
    lead_start(COT, cot_slab, cot_leads, 3)

    upper, lower = pl.ds(0, HALF), pl.ds(HALF, HALF)

    def lanes_of(turn):
        return pl.ds((turn % 2) * WIDTH, WIDTH)

    def place_of(block):
        return blocks.at[block] if block < REDUCED else own.at[block - REDUCED + 6]

    def line_copy(turn, step, from_holder):
        block, lanes = turn // 2, lanes_of(turn)
        piece = place_of(block).at[y, x, core, :, lanes]
        if not from_holder:
            source = piece
        elif block < 8:
            source = wide.at[y, x, core, :, pl.ds((block % 4) * D + turn % 2 * WIDTH, WIDTH)]
        else:
            source = half.at[block % 2, y, x, core, :, lanes]
        return remote(
            source,
            piece,
            line_send.at[turn, 0 if step > 0 else 1],
            line_recv.at[turn],
            {"section": lax.rem(me + step + sections, sections)},
        )

    def cube_copy(turn, stage):
        full, lanes = place_of(turn // 2), lanes_of(turn)
        ref, peer = (
            (full.at[y, x, core, upper, lanes], beside_x),
            (full.at[y, x, core, lower, lanes], beside_y),
            (full.at[y, :, core, upper, lanes], beside_y),
            (full.at[:, x, core, lower, lanes], beside_x),
            (full.at[:, :, core, :, lanes], beside_core),
        )[stage]
        return remote(ref, ref, cube_send.at[turn, stage], cube_recv.at[turn, stage], peer)

    def gets(block):
        return me > HOLDER[block] if block >= REDUCED else me != HOLDER[block]

    def gather_line(turn):
        holder, both_ways = HOLDER[turn // 2], turn // 2 < REDUCED

        @pl.when(me == holder)
        def _():
            line_copy(turn, 1, True).start()
            if holder > 0 and both_ways:
                line_copy(turn, -1, True).start()

        @pl.when(me > holder)
        def _():
            copy = line_copy(turn, 1, False)
            copy.wait_recv()

            @pl.when(me < sections - 1)
            def _():
                copy.start()

            cube_copy(turn, 0).start()
            cube_copy(turn, 1).start()

        if holder > 0 and both_ways:

            @pl.when(me < holder)
            def _():
                copy = line_copy(turn, -1, False)
                copy.wait_recv()

                @pl.when(me > 0)
                def _():
                    copy.start()

                cube_copy(turn, 0).start()
                cube_copy(turn, 1).start()

    def gather_two(turn):
        @pl.when(gets(turn // 2))
        def _():
            cube_copy(turn, 0).wait_recv()
            cube_copy(turn, 2).start()
            cube_copy(turn, 1).wait_recv()
            cube_copy(turn, 3).start()

    def gather_three(turn):
        @pl.when(gets(turn // 2))
        def _():
            cube_copy(turn, 2).wait_recv()
            cube_copy(turn, 3).wait_recv()
            cube_copy(turn, 4).start()

    def gather_ready(turn):
        @pl.when(gets(turn // 2))
        def _():
            cube_copy(turn, 4).wait_recv()

        if turn // 2 < REDUCED and turn % 2 == 1:

            @pl.when(me == HOLDER[turn // 2])
            def _():
                load(turn // 2).wait()

    def gather_finish(turn):
        holder = HOLDER[turn // 2]

        @pl.when(gets(turn // 2))
        def _():
            for stage in range(5):
                cube_copy(turn, stage).wait_send()

        @pl.when(me == holder)
        def _():
            line_copy(turn, 1, True).wait_send()
            if holder > 0 and turn // 2 < REDUCED:
                line_copy(turn, -1, True).wait_send()

        @pl.when((me > holder) & (me < sections - 1))
        def _():
            line_copy(turn, 1, False).wait_send()

    gather_order = tuple(range(2 * REDUCED, ROUNDS)) + tuple(range(2 * REDUCED))
    gather_plan = ((gather_ready, 6), (gather_three, 4), (gather_two, 2), (gather_line, 0))
    gather_ticks = ROUNDS + gather_plan[0][1]

    def gather_tick(tick):
        for stage, offset in gather_plan:
            if 0 <= tick - offset < ROUNDS:
                stage(gather_order[tick - offset])

    def weight(block):
        return blocks[block].reshape(D, D)

    lane_of = lax.broadcasted_iota(jnp.int32, (1, 128), 1)
    first_half = lane_of < 64
    head_masks = (first_half.astype(LOW), (~first_half).astype(LOW))

    def chunks(count, body):
        size = rows_all // count

        @pl.loop(0, count)
        def _(step):
            body(pl.multiple_of(step * size, size), size)

    def project(block):
        qkv[:, block * D : (block + 1) * D] = dot(tokens[...], weight(block)).astype(LOW)

    def pair_slices(seg, pair):
        rows = pl.ds(seg * seg_rows, seg_rows)
        return rows, [
            pl.ds(pl.multiple_of(part * D + pair * 128, 128), 128) for part in range(3)
        ]

    def heads_forward(seg):
        @pl.loop(0, PAIRS)
        def _(pair):
            rows, (at_q, at_k, at_v) = pair_slices(seg, pair)
            query, key, value = qkv[rows, at_q], qkv[rows, at_k], qkv[rows, at_v]
            parts = []
            for place in range(2):
                scores = dot_right(query * head_masks[place], key) * 0.125
                raised = jnp.exp(scores - jnp.max(scores, axis=-1, keepdims=True))
                prob = raised / jnp.sum(raised, axis=-1, keepdims=True)
                probs[seg, pair, place] = prob
                parts.append(dot(prob.astype(LOW), value))
            context[rows, at_q] = jnp.where(first_half, parts[0], parts[1]).astype(LOW)

    def attention_close():
        summed[...] = dot_right(context[...], weight(3))
        gain, bias = vectors[0, 0:1], vectors[0, 1:2]

        def body(start, size):
            rows = pl.ds(start, size)
            out, normed, inv_dev = normalize(
                tokens[rows].astype(F32) + summed[rows], gain, bias
            )
            norm0[rows] = normed
            dev0[rows] = jnp.broadcast_to(inv_dev, (size, 128))
            h1[rows] = out.astype(LOW)

        chunks(8, body)

    def inner_block(block):
        summed[...] = dot(h1[...], weight(4 + block))
        lanes = slice(block * D, (block + 1) * D)

        def body(start, size):
            rows = pl.ds(start, size)
            value, grade = gelu_pair(summed[rows])
            act[rows, lanes] = value.astype(LOW)
            slope[rows, lanes] = grade

        chunks(8, body)

    def second_block(block):
        product = dot(act[:, block * D : (block + 1) * D], weight(8 + block))
        if block == 0:
            branch[...] = product
        else:
            branch[...] += product

    def mlp_close():
        gain, bias = vectors[1, 0:1], vectors[1, 1:2]

        def body(start, size):
            rows = pl.ds(start, size)
            out, normed, inv_dev = normalize(h1[rows].astype(F32) + branch[rows], gain, bias)
            norm1[rows] = normed
            dev1[rows] = jnp.broadcast_to(inv_dev, (size, 128))
            layer_out[rows] = out.astype(LOW)

        chunks(8, body)

    def add_small(row, value):
        small[row : row + 1] += value

    def mlp_open_backward():
        gain = vectors[1, 0:1]

        def body(start, size):
            rows = pl.ds(start, size)
            place = start + lax.broadcasted_iota(jnp.int32, (size, D), 0)
            grad = jnp.where(
                lax.rem(place, seg_rows) == 0, 0.0, cotangent[rows].astype(F32)
            )
            grad_sum, grad_gain, grad_bias = normalize_backward(
                grad, norm1[rows], dev1[rows][:, 0:1], gain
            )
            branch[rows] = grad_sum
            kept[rows] = grad_sum.astype(LOW)
            add_small(2, grad_gain)
            add_small(3, grad_bias)

        chunks(8, body)

    def part(block):
        return block + 4 if block < 4 else block + 8

    def store_part(block, value):
        blocks[part(block)] = value.astype(LOW).reshape(2, 2, 2, PIECE, D)

    def second_grad(block):
        store_part(8 + block, outer(act[:, block * D : (block + 1) * D], kept[...]))

    def inner_grad(block):
        lanes = slice(block * D, (block + 1) * D)
        grad_act = dot_right(kept[...], weight(8 + block))
        act[:, lanes] = (grad_act * slope[:, lanes]).astype(LOW)
        branch[...] += dot_right(act[:, lanes], weight(4 + block))
        store_part(4 + block, outer(h1[...], act[:, lanes]))

    def attention_open_backward():
        gain = vectors[0, 0:1]
        leads = my_leads(lead_grad1)

        def body(start, size):
            rows = pl.ds(start, size)
            place = start + lax.broadcasted_iota(jnp.int32, (size, D), 0)
            grad = branch[rows]
            grad = jnp.where(place == 0, leads[0], jnp.where(place == seg_rows, leads[1], grad))
            grad = grad.astype(LOW).astype(F32)
            grad_sum, grad_gain, grad_bias = normalize_backward(
                grad, norm0[rows], dev0[rows][:, 0:1], gain
            )
            summed[rows] = grad_sum
            kept[rows] = grad_sum.astype(LOW)
            add_small(0, grad_gain)
            add_small(1, grad_bias)

        chunks(8, body)

    def out_grad():
        store_part(3, outer(kept[...], context[...]))
        context[...] = dot(kept[...], weight(3)).astype(LOW)

    def heads_backward(seg):
        @pl.loop(0, PAIRS)
        def _(pair):
            rows, (at_q, at_k, at_v) = pair_slices(seg, pair)
            query, key, value = qkv[rows, at_q], qkv[rows, at_k], qkv[rows, at_v]
            grad = context[rows, at_q]
            grads = ([], [], [])
            for place in range(2):
                prob = probs[seg, pair, place]
                grad_prob = dot_right(grad * head_masks[place], value)
                inside = prob * grad_prob
                grad_score = inside - prob * jnp.sum(inside, axis=-1, keepdims=True)
                grad_score = grad_score.astype(LOW)
                grads[0].append(dot(grad_score, key))
                grads[1].append(outer(grad_score, query))
                grads[2].append(outer(prob.astype(LOW), grad))
            for at, pair_grads, scale in zip((at_q, at_k, at_v), grads, (0.125, 0.125, 1.0)):
                merged = jnp.where(first_half, pair_grads[0], pair_grads[1]) * scale
                qkv[rows, at] = merged.astype(LOW)

    def project_grad(block):
        store_part(block, outer(tokens[...], qkv[:, block * D : (block + 1) * D]))

    def tokens_back(block):
        summed[...] += dot_right(qkv[:, block * D : (block + 1) * D], weight(block))

    def leads_mlp_forward(value, first, second, gain, bias):
        total_branch = value.astype(F32)
        for block in range(4):
            lanes = slice(block * D, (block + 1) * D)
            out, grade = gelu_pair(dot(value, first(block)))
            lead_act[:, lanes] = out.astype(LOW)
            lead_slope[:, lanes] = grade
            total_branch = total_branch + dot(lead_act[:, lanes], second(block))
        out, normed, inv_dev = normalize(total_branch, gain, bias)
        lead_norm[...] = normed
        lead_dev[...] = jnp.broadcast_to(inv_dev, (SLAB, 128))
        pack[:, 0:D] = value
        pack[:, LEFT_OUT:RIGHT] = value
        return out

    def leads_mlp_backward(grad, first, second, gain):
        grad_sum, grad_gain, grad_bias = normalize_backward(
            grad, lead_norm[...], lead_dev[:, 0:1], gain
        )
        add_small(4, grad_gain)
        add_small(5, grad_bias)
        low_sum = grad_sum.astype(LOW)
        result = grad_sum
        for block in range(4):
            lanes = slice(block * D, (block + 1) * D)
            grad_inner = (dot_right(low_sum, second(block)) * lead_slope[:, lanes]).astype(LOW)
            pack[:, RIGHT + block * D : RIGHT + (block + 1) * D] = grad_inner
            result = result + dot_right(grad_inner, first(block))
        pack[:, LEFT_HALF:RIGHT_HALF] = lead_act[:, 2 * D :]
        pack[:, RIGHT_HALF:] = low_sum
        handed[:, 0 : 2 * D] = lead_act[:, 0 : 2 * D]
        handed[:, 2 * D :] = low_sum
        return result

    def own_weight(place):
        return own[place].reshape(D, D)

    def last_second(block):
        return own_weight(6 + block if block < 2 else 2 + block)

    def leads_first():
        @pl.when(me == 2)
        def _():
            lead_wait(H2, h2_slab, h2_leads, 2)
            for place in range(4):
                load_own(place).wait()
            value = collected(h2_leads).astype(LOW)
            pack[:, 0:D] = value
            for block in range(3):
                lead_qkv[:, block * D : (block + 1) * D] = dot(value, own_weight(block)).astype(LOW)
            docs = seg_doc[...]
            row, column = (lax.broadcasted_iota(jnp.int32, (SLAB, SLAB), i) for i in range(2))
            sort = jnp.where(row == column, 2.0, 0.0)
            for micro in range(seg_doc.shape[0]):
                pair_sort = jnp.where(
                    docs[micro : micro + 1, 0:1] == docs[micro : micro + 1, 1:2], 2.0, 1.0
                )
                near = (row // 2 == micro) & (column // 2 == micro) & (row != column)
                sort = jnp.where(near, pair_sort, sort)
            for pair in range(PAIRS):
                at = [slice(p * D + pair * 128, p * D + (pair + 1) * 128) for p in range(3)]
                query, key, val = (lead_qkv[:, lanes] for lanes in at)
                parts = []
                for place in range(2):
                    scores = dot_right(query * head_masks[place], key) * 0.125
                    scores = jnp.where(
                        sort > 1.5, scores, jnp.where(sort > 0.5, -1000000000.0, -1e30)
                    )
                    raised = jnp.exp(scores - jnp.max(scores, axis=-1, keepdims=True))
                    prob = raised / jnp.sum(raised, axis=-1, keepdims=True)
                    lead_probs[pair, place] = prob
                    parts.append(dot(prob.astype(LOW), val))
                lead_context[:, pair * 128 : (pair + 1) * 128] = jnp.where(
                    first_half, parts[0], parts[1]
                ).astype(LOW)
            summed_rows = value.astype(F32) + dot_right(lead_context[...], own_weight(3))
            out, normed, inv_dev = normalize(summed_rows, vectors[2, 0:1], vectors[2, 1:2])
            lead_norm[...] = normed
            lead_dev[...] = jnp.broadcast_to(inv_dev, (SLAB, 128))
            lead_third[...] = out.astype(LOW)
            hop_copy(THIRD, lead_third, 1).start()

        @pl.when(me == 1)
        def _():
            lead_wait(H1, h1_slab, h1_leads, 1)
            leads_mlp_forward(
                collected(h1_leads).astype(LOW),
                lambda block: weight(4 + block),
                lambda block: weight(8 + block),
                vectors[1, 0:1],
                vectors[1, 1:2],
            )

    def leads_second():
        @pl.when(me == 3)
        def _():
            hop_copy(THIRD, lead_third, -1).wait_recv()
            for place in range(6):
                load_own(place).wait()
            out = leads_mlp_forward(
                lead_third[...], own_weight, last_second, vectors[3, 0:1], vectors[3, 1:2]
            )
            lead_fourth[...] = out.astype(LOW)
            for step in range(1, sections):
                spread_copy(FOURTH, lead_fourth, step).start()
            lead_wait(COT, cot_slab, cot_leads, 3)
            grad = leads_mlp_backward(
                collected(cot_leads), own_weight, last_second, vectors[3, 0:1]
            )
            lead_grad3[...] = grad.astype(LOW)
            hop_copy(GRAD3, lead_grad3, -1).start()
            hop_copy(HAND, handed, -1).start()

    def leads_third():
        @pl.when(me == 2)
        def _():
            hop_copy(GRAD3, lead_grad3, 1).wait_recv()
            grad_sum, grad_gain, grad_bias = normalize_backward(
                lead_grad3[...].astype(F32), lead_norm[...], lead_dev[:, 0:1], vectors[2, 0:1]
            )
            add_small(4, grad_gain)
            add_small(5, grad_bias)
            low_sum = grad_sum.astype(LOW)
            pack[:, LEFT_OUT:RIGHT] = low_sum
            pack[:, RIGHT + 3 * D : LEFT_HALF] = lead_context[...]
            grad_context = dot(low_sum, own_weight(3)).astype(LOW)
            for pair in range(PAIRS):
                at = [slice(p * D + pair * 128, p * D + (pair + 1) * 128) for p in range(3)]
                query, key, val = (lead_qkv[:, lanes] for lanes in at)
                grad = grad_context[:, pair * 128 : (pair + 1) * 128]
                grads = ([], [], [])
                for place in range(2):
                    prob = lead_probs[pair, place]
                    grad_prob = dot_right(grad * head_masks[place], val)
                    inside = prob * grad_prob
                    grad_score = inside - prob * jnp.sum(inside, axis=-1, keepdims=True)
                    grad_score = grad_score.astype(LOW)
                    grads[0].append(dot(grad_score, key))
                    grads[1].append(outer(grad_score, query))
                    grads[2].append(outer(prob.astype(LOW), grad))
                for lanes, pair_grads, scale in zip(at, grads, (0.125, 0.125, 1.0)):
                    merged = jnp.where(first_half, pair_grads[0], pair_grads[1]) * scale
                    pack[:, RIGHT + lanes.start : RIGHT + lanes.stop] = merged.astype(LOW)
            result = grad_sum
            for block in range(3):
                result = result + dot_right(
                    pack[:, RIGHT + block * D : RIGHT + (block + 1) * D], own_weight(block)
                )
            lead_grad2[...] = result.astype(LOW)
            hop_copy(GRAD2, lead_grad2, -1).start()
            hop_copy(HAND, handed, 1).wait_recv()
            pack[:, LEFT_HALF:] = handed[...]

    def leads_fourth():
        @pl.when(me == 1)
        def _():
            hop_copy(GRAD2, lead_grad2, 1).wait_recv()
            grad = leads_mlp_backward(
                lead_grad2[...].astype(F32),
                lambda block: weight(4 + block),
                lambda block: weight(8 + block),
                vectors[1, 0:1],
            )
            lead_grad1[...] = grad.astype(LOW)
            for step in range(1, sections):
                spread_copy(GRAD1, lead_grad1, step).start()
            hop_copy(HAND, handed, -1).start()

    half_lanes = pl.ds(pl.multiple_of(core * HALF_PACK, 128), HALF_PACK)
    first_peer = {"dp": group * CUBE + (y + core - 2 * y * core) * 4
                  + (x + (1 - core) * (1 - 2 * x)) * 2 + core}
    second_peer = {"dp": group * CUBE + (y + (1 - core) * (1 - 2 * y)) * 4
                   + (x + core - 2 * x * core) * 2 + core}

    def pack_copy(stage):
        chip = y * 2 + x
        first_chip = (y + core - 2 * y * core) * 2 + x + (1 - core) * (1 - 2 * x)
        if stage == 0:
            source, target, peer = pack, pack_in, beside_core
        elif stage == 1:
            source = target = factors.at[chip, :, half_lanes]
            peer = first_peer
        elif stage == 2:
            source = target = factors.at[chip, :, half_lanes]
            peer = second_peer
        elif stage == 3:
            source = target = factors.at[first_chip, :, half_lanes]
            peer = second_peer
        else:
            source = target = factors.at[:, :, half_lanes]
            peer = beside_core
        return remote(source, target, pack_send.at[stage], pack_recv.at[stage], peer)

    def pack_join():
        pack_copy(0).wait()

        @pl.loop(0, PACK // D)
        def _(step):
            lanes = pl.ds(pl.multiple_of(step * D, D), D)
            mine, theirs = pack[:, lanes].astype(F32)[0:8], pack_in[:, lanes].astype(F32)[0:8]
            low_rows = jnp.where(core == 0, mine, theirs)
            high_rows = jnp.where(core == 0, theirs, mine)
            factors[y * 2 + x, :, lanes] = jnp.concatenate([low_rows, high_rows]).astype(LOW)

        pack_copy(1).start()

    def pack_second():
        pack_copy(1).wait()
        pack_copy(2).start()
        pack_copy(3).start()

    def pack_third():
        pack_copy(2).wait()
        pack_copy(3).wait()
        pack_copy(4).start()

    def to_packs(step):
        return remote(
            factors, packs.at[group], group_pack_send.at[step], group_pack_recv.at[step],
            {"dp": lax.rem(index + step * CUBE, replicas)},
        )

    def own_pack():
        return pltpu.make_async_copy(factors, packs.at[group], group_pack_send.at[0])

    def pack_fourth():
        pack_copy(4).wait()
        own_pack().start()
        for step in range(1, groups):
            to_packs(step).start()

    def pack_last():
        own_pack().wait()
        for step in range(1, groups):
            to_packs(step).wait()

    def leads_close():
        @pl.when(me != 3)
        def _():
            spread_copy(FOURTH, lead_fourth, 1).wait_recv()

        leads = my_leads(lead_fourth)
        for lead in range(2):
            rows = pl.ds(lead * seg_rows, SLAB)
            layer_out[rows] = jnp.where(
                row_of == 0, leads[lead], layer_out[rows].astype(F32)
            ).astype(LOW)

        @pl.when(me != 1)
        def _():
            spread_copy(GRAD1, lead_grad1, 1).wait_recv()

        @pl.when(me == 0)
        def _():
            hop_copy(HAND, handed, 1).wait_recv()
            pack[:, 0:LEFT_HALF] = jnp.zeros((SLAB, LEFT_HALF), LOW)
            pack[:, LEFT_HALF:] = handed[...]

        pack_copy(0).start()

    def add(target, *sources):
        value = target[...].astype(F32)
        for source in sources:
            value = value + source[...].astype(F32)
        target[...] = value.astype(LOW)

    def landing(block):
        return blocks.at[8 + block, 0] if block < 4 else core_in.at[block - 4]

    def scatter(turn, stage):
        block, lanes = turn // 2, lanes_of(turn)
        run = blocks.at[part(block)]
        source, target, peer = (
            (run.at[:, :, 1 - core, :, lanes], landing(block).at[:, :, :, lanes], beside_core),
            (run.at[:, 1 - x, core, upper, lanes], one_a.at[block, :, :, lanes], beside_x),
            (run.at[1 - y, :, core, lower, lanes], one_b.at[block, :, :, lanes], beside_y),
            (run.at[1 - y, x, core, upper, lanes], two_a.at[block, :, lanes], beside_y),
            (run.at[y, 1 - x, core, lower, lanes], two_b.at[block, :, lanes], beside_x),
        )[stage]
        return remote(source, target, rs_send.at[turn, stage], rs_recv.at[turn, stage], peer)

    def to_line(turn, step):
        side = 0 if step < 0 else 1
        return remote(
            blocks.at[part(turn // 2), y, x, core, :, lanes_of(turn)],
            line_in.at[turn // 2, side, :, lanes_of(turn)],
            z_send.at[turn],
            z_recv.at[turn, side],
            {"section": lax.rem(me + step + sections, sections)},
        )

    def to_group(turn, step):
        return remote(
            blocks.at[part(turn // 2), y, x, core, :, lanes_of(turn)],
            group_in.at[turn // 2, step - 1, :, lanes_of(turn)],
            group_send.at[turn, step - 1],
            group_recv.at[turn, step - 1],
            {"dp": lax.rem(index + step * CUBE, replicas)},
        )

    def gather_back(turn, stage):
        place = 2 * OWN[HOLDER[turn // 2]].index(turn // 2) + turn % 2
        run, lanes = blocks.at[part(turn // 2)], lanes_of(turn)
        ref, peer = (
            (run.at[y, x, core, upper, lanes], beside_y),
            (run.at[y, x, core, lower, lanes], beside_x),
            (run.at[:, x, core, upper, lanes], beside_x),
            (run.at[y, :, core, lower, lanes], beside_y),
            (run.at[:, :, core, :, lanes], beside_core),
        )[stage]
        return remote(ref, ref, ag_send.at[place, stage], ag_recv.at[place, stage], peer)

    def write_out(block):
        place = OWN[HOLDER[block]].index(block)
        return pltpu.make_async_copy(
            blocks.at[part(block)], total.at[place], out_sem.at[place]
        )

    def reduce_core(block):
        scatter(2 * block, 0).start()
        scatter(2 * block + 1, 0).start()

    def reduce_one(turn):
        block, lanes = turn // 2, lanes_of(turn)
        scatter(turn, 0).wait()
        arrived = landing(block)
        for yy in range(2):
            for xx in range(2):
                add(
                    blocks.at[part(block), yy, xx, core, :, lanes], arrived.at[yy, xx, :, lanes]
                )
        scatter(turn, 1).start()
        scatter(turn, 2).start()

    def reduce_two(turn):
        block, lanes = turn // 2, lanes_of(turn)
        run = blocks.at[part(block)]
        scatter(turn, 1).wait()
        for yy in range(2):
            add(run.at[yy, x, core, upper, lanes], one_a.at[block, yy, :, lanes])
        scatter(turn, 3).start()
        scatter(turn, 2).wait()
        for xx in range(2):
            add(run.at[y, xx, core, lower, lanes], one_b.at[block, xx, :, lanes])
        scatter(turn, 4).start()

    def reduce_three(turn):
        block, lanes = turn // 2, lanes_of(turn)
        run = blocks.at[part(block)]
        scatter(turn, 3).wait()
        add(run.at[y, x, core, upper, lanes], two_a.at[block, :, lanes])
        scatter(turn, 4).wait()
        add(run.at[y, x, core, lower, lanes], two_b.at[block, :, lanes])
        if groups > 1:
            for step in range(1, groups):
                to_group(turn, step).start()
            for step in range(1, groups):
                to_group(turn, step).wait()
            for step in range(1, groups):
                copy = pltpu.make_async_copy(
                    group_in.at[block, step - 1, :, lanes], group_piece, group_load
                )
                copy.start()
                copy.wait()
                add(run.at[y, x, core, :, lanes], group_piece)
        reduce_line(0, turn)

    def reduce_line(hop, turn):
        block, lanes = turn // 2, lanes_of(turn)
        holder = HOLDER[block]
        target = blocks.at[part(block), y, x, core, :, lanes]
        for section in range(sections):
            from_above = sections - 1 - section if section >= holder else -1
            from_below = section if section <= holder else -1
            if max(from_above, from_below) != hop:
                continue

            @pl.when(me == section)
            def _():
                if from_above > 0:
                    to_line(turn, -1).wait_recv()
                    add(target, line_in.at[block, 0, :, lanes])
                if from_below > 0:
                    to_line(turn, 1).wait_recv()
                    add(target, line_in.at[block, 1, :, lanes])
                if section == holder:
                    gather_back(turn, 0).start()
                    gather_back(turn, 1).start()
                else:
                    to_line(turn, -1 if section > holder else 1).start()

    def spread_two(turn):
        @pl.when(me == HOLDER[turn // 2])
        def _():
            gather_back(turn, 0).wait()
            gather_back(turn, 2).start()
            gather_back(turn, 1).wait()
            gather_back(turn, 3).start()

    def spread_core(turn):
        @pl.when(me == HOLDER[turn // 2])
        def _():
            gather_back(turn, 2).wait()
            gather_back(turn, 3).wait()
            gather_back(turn, 4).start()

    def spread_done(turn):
        @pl.when(me == HOLDER[turn // 2])
        def _():
            gather_back(turn, 4).wait()
            if turn % 2 == 1:
                write_out(turn // 2).start()

        @pl.when(me != HOLDER[turn // 2])
        def _():
            to_line(turn, 1).wait_send()

    LINE = 7
    reduce_plan = (
        (spread_done, LINE + 10),
        (spread_core, LINE + 8),
        (spread_two, LINE + 6),
        (partial(reduce_line, 3), LINE + 4),
        (partial(reduce_line, 2), LINE + 2),
        (partial(reduce_line, 1), LINE),
        (reduce_three, 5),
        (reduce_two, 3),
        (reduce_one, 1),
    )

    def turns(*order):
        return tuple(2 * block + side for block in order for side in range(2))

    class Wave:
        def __init__(self, order):
            self.order, self.at = turns(*order), 0

        def tick(self, count=1):
            for _ in range(count):
                for stage, offset in reduce_plan:
                    if 0 <= self.at - offset < len(self.order):
                        stage(self.order[self.at - offset])
                self.at += 1

        def left(self):
            return self.at < len(self.order) + reduce_plan[0][1]

    one, two = Wave((8, 9, 10, 11, 4, 5, 6, 7)), Wave((3, 0, 1, 2))

    small[...] = jnp.zeros_like(small)
    for tick in range(gather_ticks):
        gather_tick(tick)
        block, side = divmod(tick - gather_plan[0][1] - (ROUNDS - 2 * REDUCED), 2)
        if tick == 8:
            for step in range(1, sections):
                vector_copy(step).wait()
        if block < 0:
            continue
        if side == 0:
            if block == 3:
                heads_forward(0)
            continue
        if block < 3:
            project(block)
        elif block == 3:
            heads_forward(1)
            attention_close()
            h1_slab[...] = lead_rows(h1)
            lead_start(H1, h1_slab, h1_leads, 1)
        elif block < 8:
            inner_block(block - 4)
        else:
            second_block(block - 8)
    mlp_close()
    h2_slab[...] = lead_rows(layer_out)
    lead_start(H2, h2_slab, h2_leads, 2)
    mlp_open_backward()

    for turn in gather_order:
        gather_finish(turn)

    for block in range(4):
        second_grad(block)
        reduce_core(8 + block)
        one.tick(2)
        if block == 1:
            leads_first()
    for block in range(4):
        inner_grad(block)
        reduce_core(4 + block)
        one.tick(2)
        if block == 0:
            leads_second()
        if block == 2:
            leads_third()
    leads_fourth()
    pl.semaphore_signal(credit, inc=1, device_id=beside_core, device_id_type=MESH)
    one.tick(2)
    leads_close()
    attention_open_backward()
    out_grad()
    pack_join()
    pl.semaphore_wait(credit, 1)
    reduce_core(3)
    one.tick()
    heads_backward(0)
    one.tick()
    two.tick()
    heads_backward(1)
    pack_second()
    for block in range(3):
        project_grad(block)
        reduce_core(block)
        one.tick(2)
        two.tick(2)

    def small_copy(step):
        return remote(
            small, small_all.at[index], small_send.at[step], small_recv.at[step], replica(step)
        )

    def sum_copy(step):
        return remote(
            small_sum, smalls.at[me], sum_send.at[step], sum_recv.at[step], others[step - 1]
        )

    def own_sum():
        return pltpu.make_async_copy(small_sum, smalls.at[me], sum_send.at[0])

    @pl.loop(1, replicas)
    def _(step):
        small_copy(step).start()

    small_all[index] = small[...]
    for block in range(3):
        tokens_back(block)
        one.tick()
        two.tick()
    grad_tokens[...] = summed[...].astype(LOW)
    pack_third()

    @pl.loop(1, replicas)
    def _(step):
        small_copy(step).wait()

    small_sum[...] = jnp.sum(small_all[...], axis=0)
    for place in range(1, sections):
        sum_copy(place).start()
    own_sum().start()
    pack_fourth()
    while one.left() or two.left():
        if one.left():
            one.tick()
        if two.left():
            two.tick()

    for place in range(1, sections):
        sum_copy(place).wait()
    own_sum().wait()
    pack_last()

    for holder in (0, 1):

        @pl.when(me == holder)
        def _():
            for block in OWN[holder]:
                write_out(block).wait()

    for kind, slab, target, reader in (
        (COT, cot_slab, cot_leads, 3),
        (H1, h1_slab, h1_leads, 1),
        (H2, h2_slab, h2_leads, 2),
    ):

        @pl.when(me != reader)
        def _():
            lead_copy(kind, slab, target, reader).wait_send()

    @pl.when(me == 1)
    def _():
        for place in range(1, sections):
            spread_copy(GRAD1, lead_grad1, place).wait_send()
        hop_copy(HAND, handed, -1).wait_send()

    @pl.when(me == 2)
    def _():
        hop_copy(THIRD, lead_third, 1).wait_send()
        hop_copy(GRAD2, lead_grad2, -1).wait_send()

    @pl.when(me == 3)
    def _():
        for place in range(1, sections):
            spread_copy(FOURTH, lead_fourth, place).wait_send()
        hop_copy(GRAD3, lead_grad3, -1).wait_send()
        hop_copy(HAND, handed, -1).wait_send()


def run_layers(sections, replicas, tokens, cotangent, seg_doc, gain, bias, wide, half):
    groups = replicas // CUBE
    rows = tokens.shape[0]
    vector = (8, D)
    block = (2, 2, 2, PIECE, D)
    reduced_groups = max(groups - 1, 1)
    in_vmem = pl.BlockSpec(memory_space=pltpu.VMEM)
    anywhere = pl.BlockSpec(memory_space=pl.ANY)
    slab = pltpu.VMEM((SLAB, D), LOW)
    leads = pltpu.VMEM((sections, SLAB, D), LOW)
    return pl.pallas_call(
        partial(layer_kernel, sections, replicas),
        out_shape=(
            jax.ShapeDtypeStruct(tokens.shape, LOW),
            jax.ShapeDtypeStruct(tokens.shape, LOW),
            jax.ShapeDtypeStruct((OWNED,) + block, LOW),
            jax.ShapeDtypeStruct((groups, CUBE // 2, SLAB, PACK), LOW),
            jax.ShapeDtypeStruct((sections,) + vector, F32),
            jax.ShapeDtypeStruct(
                (REDUCED if groups > 1 else 1, reduced_groups, PIECE, D), LOW
            ),
        ),
        in_specs=[in_vmem] * 5 + [anywhere] * 2,
        out_specs=[in_vmem] * 2 + [anywhere] * 4,
        scratch_shapes=[
            pltpu.VMEM((REDUCED + 8,) + block, LOW),
            pltpu.VMEM((8,) + block, LOW),
            pltpu.VMEM((8, 2, 2, PIECE, D), LOW),
            pltpu.VMEM((REDUCED, 2, HALF, D), LOW),
            pltpu.VMEM((REDUCED, 2, HALF, D), LOW),
            pltpu.VMEM((REDUCED, HALF, D), LOW),
            pltpu.VMEM((REDUCED, HALF, D), LOW),
            pltpu.VMEM((REDUCED, 2, PIECE, D), LOW),
            pltpu.VMEM((sections,) + vector, F32),
            pltpu.VMEM((rows, 3 * D), LOW),
            pltpu.VMEM((2, PAIRS, 2, rows // 2, rows // 2), F32),
            pltpu.VMEM((rows, D), LOW),
            pltpu.VMEM((rows, D), LOW),
            pltpu.VMEM((rows, D), F32),
            pltpu.VMEM((rows, 128), F32),
            pltpu.VMEM((rows, D), F32),
            pltpu.VMEM((rows, 4 * D), LOW),
            pltpu.VMEM((rows, 4 * D), F32),
            pltpu.VMEM((rows, D), F32),
            pltpu.VMEM((rows, 128), F32),
            pltpu.VMEM((rows, D), F32),
            pltpu.VMEM((rows, D), LOW),
            slab, slab, slab, leads, leads, leads,
            slab, slab, slab, slab, slab,
            pltpu.VMEM((SLAB, 3 * D), LOW),
            pltpu.VMEM((SLAB, 3 * D), LOW),
            pltpu.VMEM((PAIRS, 2, SLAB, SLAB), F32),
            slab,
            pltpu.VMEM((SLAB, D), F32),
            pltpu.VMEM((SLAB, 128), F32),
            pltpu.VMEM((SLAB, 4 * D), LOW),
            pltpu.VMEM((SLAB, 4 * D), F32),
            pltpu.VMEM((SLAB, PACK), LOW),
            pltpu.VMEM((SLAB, PACK), LOW),
            pltpu.VMEM((CUBE // 2, SLAB, PACK), LOW),
            pltpu.VMEM(vector, F32),
            pltpu.VMEM((replicas,) + vector, F32),
            pltpu.VMEM(vector, F32),
            pltpu.VMEM((PIECE, WIDTH), LOW),
            DMA((ROUNDS, 2)),
            DMA((ROUNDS,)),
            DMA((ROUNDS, 5)),
            DMA((ROUNDS, 5)),
            DMA((GATHERED,)),
            DMA((2 * REDUCED, 5)),
            DMA((2 * REDUCED, 5)),
            DMA((2 * REDUCED,)),
            DMA((2 * REDUCED, 2)),
            DMA((2 * REDUCED, reduced_groups)),
            DMA((2 * REDUCED, reduced_groups)),
            DMA,
            DMA((2 * OWNED, 5)),
            DMA((2 * OWNED, 5)),
            DMA((OWNED,)),
            DMA((5,)),
            DMA((5,)),
            DMA((groups,)),
            DMA((groups,)),
            DMA((replicas,)),
            DMA((replicas,)),
            DMA((sections,)),
            DMA((sections,)),
            DMA((sections,)),
            DMA((sections,)),
            DMA((3,)),
            DMA((3, sections)),
            DMA((2, sections)),
            DMA((2,)),
            DMA((4,)),
            DMA((4,)),
            pltpu.SemaphoreType.REGULAR,
        ],
        compiler_params=pltpu.CompilerParams(
            collective_id=0, has_side_effects=True, vmem_limit_bytes=VMEM_BYTES
        ),
    )(tokens, cotangent, seg_doc, gain, bias, wide, half)


VMEM_BYTES = 62 * 1024 * 1024


def close_kernel(
    total, packs, smalls, rows_in, grads_in,
    wide_out, half_out, gain_out, bias_out, rows_out, grads_out,
):
    me = lax.axis_index("section")
    step = pl.program_id(0)
    near = me < 2
    packed = packs.reshape(-1, PACK)
    summed = jnp.where(near, total[0, 0].reshape(WIDTH, D).astype(F32), 0.0)

    def wide_step(block, side):
        @pl.when(step == 2 * block + side)
        def _():
            first = (0 if block < 3 else LEFT_OUT) + side * WIDTH
            left = packed[:, first : first + WIDTH]
            right = packed[:, RIGHT + block * D : RIGHT + (block + 1) * D]
            wide_out[0] = summed + outer(left, right)

    def half_step(side):
        @pl.when(step == 8 + side)
        def _():
            first = LEFT_HALF + side * WIDTH
            half_out[0] = summed + outer(packed[:, first : first + WIDTH], packed[:, RIGHT_HALF:])

    for block in range(4):
        for side in range(2):
            wide_step(block, side)
    for side in range(4):
        half_step(side)

    @pl.when(step == 0)
    def _():
        every = jnp.sum(smalls[...], axis=0)
        mine = smalls[me]
        for row, out in ((0, gain_out), (1, bias_out)):
            value = jnp.where(me == 0, every[row : row + 1], every[2 + row : 3 + row])
            value = jnp.where(near, value, 0.0) + mine[4 + row : 5 + row]
            out[...] = value
        rows_out[...] = rows_in[...]
        grads_out[...] = grads_in[...]


def close(total, packs, smalls, rows, grads):
    def whole(shape):
        return pl.BlockSpec(shape, lambda step: (0,) * len(shape))

    return pl.pallas_call(
        close_kernel,
        grid=(2 * OWNED,),
        out_shape=(
            jax.ShapeDtypeStruct((1, D, 4 * D), F32),
            jax.ShapeDtypeStruct((1, 2 * D, D), F32),
            jax.ShapeDtypeStruct((1, D), F32),
            jax.ShapeDtypeStruct((1, D), F32),
            jax.ShapeDtypeStruct(rows.shape, LOW),
            jax.ShapeDtypeStruct(rows.shape, LOW),
        ),
        in_specs=[
            pl.BlockSpec(
                (1, 1) + total.shape[2:], lambda step: (step // 2, lax.rem(step, 2), 0, 0, 0, 0)
            ),
            whole(packs.shape),
            whole(smalls.shape),
            whole(rows.shape),
            whole(rows.shape),
        ],
        out_specs=[
            pl.BlockSpec(
                (1, WIDTH, D),
                lambda step: (
                    0,
                    jnp.where(step < 8, lax.rem(step, 2), 1),
                    jnp.minimum(step // 2, 3),
                ),
            ),
            pl.BlockSpec((1, WIDTH, D), lambda step: (0, jnp.maximum(step - 8, 0), 0)),
            whole((1, D)),
            whole((1, D)),
            whole(rows.shape),
            whole(rows.shape),
        ],
        compiler_params=pltpu.CompilerParams(vmem_limit_bytes=VMEM_BYTES),
    )(total, packs, smalls, rows, grads)


def on_device(tokens, cotangent, seg_doc, wide_in, half_out, norm_gain, norm_bias):
    sections = lax.axis_size("section")
    replicas = lax.axis_size("dp")
    wide = wide_in.reshape(2, 2, 2, PIECE, 4 * D)
    half = half_out.reshape(2, 2, 2, 2, PIECE, D)
    rows, grads, total, packs, smalls, _ = run_layers(
        sections, replicas, tokens, cotangent, seg_doc, norm_gain, norm_bias, wide, half
    )
    wide_grad, half_grad, gain_grad, bias_grad, layer_out, tokens_grad = close(
        total, packs, smalls, rows, grads
    )
    return layer_out, tokens_grad, wide_grad, half_grad, gain_grad, bias_grad


def solution(mesh):
    placed = (
        P(("dp", "section"), None),
        P(("dp", "section"), None),
        P("dp", None),
        P("section", None, None),
        P("section", None, None),
        P("section", None),
        P("section", None),
    )
    return jax.shard_map(
        on_device,
        mesh=mesh,
        in_specs=placed,
        out_specs=(
            P(("dp", "section"), None),
            P(("dp", "section"), None),
            P("section", None, None),
            P("section", None, None),
            P("section", None),
            P("section", None),
        ),
        check_vma=False,
    )
```

```python
from functools import partial

import jax
import jax.numpy as jnp
from jax import lax
from jax.experimental import pallas as pl
from jax.experimental.pallas import tpu as pltpu
from jax.sharding import PartitionSpec as P

D = 768
HEADS = 12
PAIRS = HEADS // 2
CUBE = 8
PIECE = D // CUBE
HALF = PIECE // 2
WIDTH = D // 2
SLAB = 16
HOLDER = (0, 0, 0, 0, 1, 1, 1, 1, 0, 0, 1, 1, 2, 2)
GATHERED = len(HOLDER)
ROUNDS = 2 * GATHERED
WANTED = {0: (4, 5, 6, 7, 10, 11), 1: (0, 1, 2, 3, 8, 9), 3: (12, 13)}
EARLY = ()
REDUCED = 12
OWN = {0: (0, 1, 2, 3, 8, 9), 1: (4, 5, 6, 7, 10, 11)}
OWNED = len(OWN[0])
LEFT_OUT, RIGHT, LEFT_HALF, RIGHT_HALF, PACK = D, 2 * D, 6 * D, 8 * D, 9 * D
HALF_PACK = PACK // 2
LOW = jnp.bfloat16
F32 = jnp.float32
DMA = pltpu.SemaphoreType.DMA
MESH = pl.DeviceIdType.MESH


def dot(left, right):
    return jnp.dot(left, right, preferred_element_type=F32)


def dot_right(left, right):
    return lax.dot_general(left, right, (((1,), (1,)), ((), ())), preferred_element_type=F32)


def outer(left, right):
    return lax.dot_general(left, right, (((0,), (0,)), ((), ())), preferred_element_type=F32)


def normalize(summed, gain, bias):
    average = jnp.mean(summed, axis=-1, keepdims=True)
    centred = summed - average
    inv_dev = lax.rsqrt(jnp.mean(centred * centred, axis=-1, keepdims=True) + 1e-05)
    normed = centred * inv_dev
    return normed * gain + bias, normed, inv_dev


def normalize_backward(grad, normed, inv_dev, gain):
    scaled = grad * gain
    mean_scaled = jnp.mean(scaled, axis=-1, keepdims=True)
    mean_normed = jnp.mean(scaled * normed, axis=-1, keepdims=True)
    grad_sum = inv_dev * (scaled - mean_scaled - normed * mean_normed)
    return (
        grad_sum,
        jnp.sum(grad * normed, axis=0, keepdims=True),
        jnp.sum(grad, axis=0, keepdims=True),
    )


def gelu_pair(value):
    bell = jnp.exp(-0.5 * value * value)
    base = 1.0 + (0.3275911 * 0.7071067811865476) * jnp.abs(value)
    guess = pl.reciprocal(base, approx=True)
    t = guess * (2.0 - base * guess)
    poly = t * (
        0.5 * 0.254829592
        + t
        * (
            0.5 * -0.284496736
            + t * (0.5 * 1.421413741 + t * (0.5 * -1.453152027 + t * (0.5 * 1.061405429)))
        )
    )
    tail = poly * bell
    below = jnp.where(value >= 0, 1.0 - tail, tail)
    return value * below, below + value * bell * 0.3989422804014327


def position():
    index = lax.axis_index("dp")
    return (lax.rem(index // 4, 2), lax.rem(index // 2, 2), lax.rem(index, 2), index // CUBE)


def remote(source, target, send, receive, device):
    return pltpu.make_async_remote_copy(
        src_ref=source,
        dst_ref=target,
        send_sem=send,
        recv_sem=receive,
        device_id=device,
        device_id_type=MESH,
    )


def layer_kernel(
    sections, replicas,
    tokens, cotangent, seg_doc, norm_gain, norm_bias, wide, half, wide_flat, half_flat,
    layer_out, grad_tokens, total, packs, smalls, group_in,
    blocks, flat, core_in, one_a, one_b, two_a, two_b, line_in, early_in, vectors,
    token_rows, cot_rows, out_rows,
    qkv, probs, context, h1, norm0, dev0, summed, norm1, dev1, branch, kept,
    cot_slab, h1_slab, h2_slab, cot_leads, h1_leads, h2_leads,
    lead_third, lead_fourth, lead_grad3, lead_grad2, lead_grad1, handed,
    lead_qkv, lead_probs, lead_context, lead_norm, lead_dev, lead_act, lead_slope,
    pack, pack_in, factors, small, small_all, small_sum, group_piece,
    rows_load, guest_send, guest_recv, rows_out,
    line_send, line_recv, cube_send, cube_recv, load_sem,
    rs_send, rs_recv, z_send, z_recv, group_send, group_recv, group_load, ag_send, ag_recv,
    out_sem, pack_send, pack_recv, group_pack_send, group_pack_recv,
    small_send, small_recv, sum_send, sum_recv,
    vector_send, vector_recv, lead_send, lead_recv, spread_send, spread_recv, hop_send, hop_recv,
    credit,
):
    me = lax.axis_index("section")
    index = lax.axis_index("dp")
    y, x, core, group = position()
    groups = replicas // CUBE
    micro_rows = tokens.shape[0]
    seg_rows = micro_rows // 2
    rows_all = 2 * micro_rows
    works = me < 2

    def cube_peer(yy, xx, cc):
        return {"dp": group * CUBE + yy * 4 + xx * 2 + cc}

    beside_x = cube_peer(y, 1 - x, core)
    beside_y = cube_peer(1 - y, x, core)
    beside_core = cube_peer(y, x, 1 - core)
    others = [{"section": lax.rem(me + step, sections)} for step in range(1, sections)]

    def replica(step):
        return {"dp": lax.rem(index + step, replicas)}

    barrier = pltpu.get_barrier_semaphore()
    for other in others:
        pl.semaphore_signal(barrier, inc=1, device_id=other, device_id_type=MESH)

    @pl.loop(1, replicas)
    def _(step):
        pl.semaphore_signal(barrier, inc=1, device_id=replica(step), device_id_type=MESH)

    own_part, guest_part = pl.ds(0, micro_rows), pl.ds(micro_rows, micro_rows)

    def load_rows(place):
        source, target = ((tokens, token_rows), (cotangent, cot_rows))[place]
        return pltpu.make_async_copy(source, target.at[own_part], rows_load.at[place])

    load_rows(0).start()
    load_rows(1).start()

    def load(block):
        if block < 8:
            source = wide.at[:, :, :, :, pl.ds((block % 4) * D, D)]
        else:
            source = half.at[block % 2]
        return pltpu.make_async_copy(source, blocks.at[block], load_sem.at[block])

    def flat_rows(place):
        return pl.ds(place * D, D)

    def load_own(place):
        if place < 4:
            source = wide_flat.at[:, pl.ds(place * D, D)]
        else:
            source = half_flat.at[flat_rows(place - 4)]
        return pltpu.make_async_copy(source, flat.at[flat_rows(place)], load_sem.at[place])

    for holder in (0, 1):

        @pl.when(me == holder)
        def _():
            for block in OWN[holder]:
                load(block).start()

    @pl.when(me >= 2)
    def _():
        for place in range(4):
            load_own(place).start()

    @pl.when(me == 3)
    def _():
        for place in (4, 5):
            load_own(place).start()

    pl.semaphore_wait(barrier, sections - 1 + replicas - 1)

    def guest_copy(kind):
        down = {"section": lax.rem(me + sections - 2, sections)}
        up = {"section": lax.rem(me + 2, sections)}
        source, target, device = (
            (tokens, token_rows.at[guest_part], down),
            (cotangent, cot_rows.at[guest_part], down),
            (out_rows.at[guest_part], out_rows.at[own_part], up),
            (h1.at[guest_part], h1.at[own_part], up),
        )[kind]
        return remote(source, target, guest_send.at[kind], guest_recv.at[kind], device)

    TOKENS, COTANGENT, OUT, GRAD = 0, 1, 2, 3

    @pl.when(me >= 2)
    def _():
        guest_copy(TOKENS).start()
        guest_copy(COTANGENT).start()

    row_of = lax.broadcasted_iota(jnp.int32, (SLAB, D), 0)

    def lead_rows(ref, count):
        value = jnp.zeros((SLAB, D), F32)
        for lead in range(count):
            row = ref[lead * seg_rows : lead * seg_rows + SLAB].astype(F32)[0:1]
            value = jnp.where(row_of == lead, row, value)
        return value.astype(LOW)

    def lead_copy(kind, slab, target, reader):
        return remote(
            slab, target.at[me], lead_send.at[kind], lead_recv.at[kind, me], {"section": reader}
        )

    def lead_start(kind, slab, target, reader):
        @pl.when(me != reader)
        def _():
            lead_copy(kind, slab, target, reader).start()

        @pl.when(me == reader)
        def _():
            target[reader] = slab[...]

    def lead_wait(kind, slab, target, reader, senders):
        for section in range(senders):
            if section != reader:
                remote(
                    slab, target.at[section], lead_send.at[kind], lead_recv.at[kind, section],
                    {"section": section},
                ).wait_recv()

    def collected(target, senders):
        value = jnp.zeros((SLAB, D), F32)
        for section in range(senders):
            slab = target[section].astype(F32)
            for micro in range(section, sections, senders):
                for lead in range(2):
                    place = (micro - section) // senders * 2 + lead
                    value = jnp.where(
                        row_of == 2 * micro + lead, slab[place : place + 1], value
                    )
        return value

    def spread_copy(kind, slab, step):
        return remote(
            slab, slab, spread_send.at[kind, step], spread_recv.at[kind], others[step - 1]
        )

    def hop_copy(kind, slab, step):
        return remote(
            slab, slab, hop_send.at[kind], hop_recv.at[kind],
            {"section": lax.rem(me + step + sections, sections)},
        )

    def leads_of(slab, micro):
        value = slab[...].astype(F32)
        return [
            jnp.sum(jnp.where(row_of == 2 * micro + lead, value, 0.0), axis=0, keepdims=True)
            for lead in range(2)
        ]

    COT, H1, H2 = 0, 1, 2
    FOURTH = 0
    THIRD, GRAD3, GRAD2, HAND, GRAD1 = 0, 1, 2, 3, 4

    def vector_copy(step):
        return remote(
            vectors.at[me], vectors.at[me], vector_send.at[step], vector_recv.at[step],
            others[step - 1],
        )

    vectors[me, 0:1] = norm_gain[...]
    vectors[me, 1:2] = norm_bias[...]
    for step in range(1, sections):
        vector_copy(step).start()
    load_rows(0).wait()
    load_rows(1).wait()
    cot_slab[...] = lead_rows(cot_rows, 2)
    lead_start(COT, cot_slab, cot_leads, 3)

    upper, lower = pl.ds(0, HALF), pl.ds(HALF, HALF)

    def lanes_of(turn):
        return pl.ds((turn % 2) * WIDTH, WIDTH)

    def place_of(block):
        if block < REDUCED:
            return blocks.at[block]
        return core_in.at[pl.ds(2 * (block - REDUCED), 2)]

    def line_copy(turn, reader):
        block, lanes = turn // 2, lanes_of(turn)
        if block < 8:
            source = wide.at[y, x, core, :, pl.ds((block % 4) * D + turn % 2 * WIDTH, WIDTH)]
        else:
            source = half.at[block % 2, y, x, core, :, lanes]
        return remote(
            source,
            place_of(block).at[y, x, core, :, lanes],
            line_send.at[turn],
            line_recv.at[turn],
            {"section": reader},
        )

    def cube_copy(turn, stage):
        full, lanes = place_of(turn // 2), lanes_of(turn)
        ref, peer = (
            (full.at[y, x, core, upper, lanes], beside_x),
            (full.at[y, x, core, lower, lanes], beside_y),
            (full.at[y, :, core, upper, lanes], beside_y),
            (full.at[:, x, core, lower, lanes], beside_x),
            (full.at[:, :, core, :, lanes], beside_core),
        )[stage]
        return remote(ref, ref, cube_send.at[turn, stage], cube_recv.at[turn, stage], peer)

    def gather_line(turn, reader):
        @pl.when(me == HOLDER[turn // 2])
        def _():
            line_copy(turn, reader).start()

        @pl.when(me == reader)
        def _():
            line_copy(turn, reader).wait_recv()
            cube_copy(turn, 0).start()
            cube_copy(turn, 1).start()

    def gather_two(turn, reader):
        @pl.when(me == reader)
        def _():
            cube_copy(turn, 0).wait_recv()
            cube_copy(turn, 2).start()
            cube_copy(turn, 1).wait_recv()
            cube_copy(turn, 3).start()

    def gather_three(turn, reader):
        @pl.when(me == reader)
        def _():
            cube_copy(turn, 2).wait_recv()
            cube_copy(turn, 3).wait_recv()
            cube_copy(turn, 4).start()

    def gather_ready(turn, reader):
        @pl.when(me == reader)
        def _():
            cube_copy(turn, 4).wait_recv()

    def gather_finish(turn, reader):
        @pl.when(me == reader)
        def _():
            for stage in range(5):
                cube_copy(turn, stage).wait_send()

        @pl.when(me == HOLDER[turn // 2])
        def _():
            line_copy(turn, reader).wait_send()

    gather_plan = ((gather_ready, 6), (gather_three, 4), (gather_two, 2), (gather_line, 0))
    gather_ticks = 2 * OWNED + gather_plan[0][1]

    def gather_tick(tick):
        for stage, offset in gather_plan:
            at = tick - offset
            for reader, wanted in WANTED.items():
                if 0 <= at < 2 * len(wanted):
                    stage(2 * wanted[at // 2] + at % 2, reader)

    def gather_wait_own():
        for holder in (0, 1):

            @pl.when(me == holder)
            def _():
                for block in OWN[holder]:
                    load(block).wait()

    def worker(step):
        def run(*given):
            @pl.when(works)
            def _():
                step(*given)

        return run

    def weight(block):
        return blocks[block].reshape(D, D)

    def act_rows(block):
        return pl.ds(pl.multiple_of(block * rows_all, SLAB), rows_all)

    def slope_rows(block):
        return pl.ds(pl.multiple_of((4 + block) * rows_all, SLAB), rows_all)

    lane_of = lax.broadcasted_iota(jnp.int32, (1, 128), 1)
    first_half = lane_of < 64
    head_masks = (first_half.astype(LOW), (~first_half).astype(LOW))
    segs = range(4)

    def chunks(size, body):
        @pl.loop(0, rows_all // size)
        def _(step):
            body(pl.multiple_of(step * size, size), size)

    @worker
    def project(block):
        qkv[:, block * D : (block + 1) * D] = dot(token_rows[...], weight(block)).astype(LOW)

    def seg_slice(seg):
        return pl.ds(seg * seg_rows, seg_rows)

    def pair_lanes(pair):
        return [pl.ds(pl.multiple_of(part * D + pair * 128, 128), 128) for part in range(3)]

    def softmax(scores):
        raised = jnp.exp(scores - jnp.max(scores, axis=-1, keepdims=True))
        return raised / jnp.sum(raised, axis=-1, keepdims=True)

    @worker
    def heads_forward():
        @pl.loop(0, PAIRS)
        def _(pair):
            at_q, at_k, at_v = pair_lanes(pair)
            heads = [(seg, place) for seg in segs for place in range(2)]
            scores = [
                dot_right(qkv[seg_slice(seg), at_q] * head_masks[place], qkv[seg_slice(seg), at_k])
                * 0.125
                for seg, place in heads
            ]
            found = [softmax(score) for score in scores]
            for (seg, place), prob in zip(heads, found):
                probs[seg, pair, place] = prob
            mixed = [
                dot(prob.astype(LOW), qkv[seg_slice(seg), at_v])
                for (seg, place), prob in zip(heads, found)
            ]
            for seg in segs:
                context[seg_slice(seg), at_q] = jnp.where(
                    first_half, mixed[2 * seg], mixed[2 * seg + 1]
                ).astype(LOW)

    @worker
    def attention_close():
        summed[...] = dot_right(context[...], weight(3))
        gain, bias = vectors[0, 0:1], vectors[0, 1:2]

        def body(start, size):
            rows = pl.ds(start, size)
            out, normed, inv_dev = normalize(
                token_rows[rows].astype(F32) + summed[rows], gain, bias
            )
            norm0[rows] = normed
            dev0[rows] = jnp.broadcast_to(inv_dev, (size, 128))
            h1[rows] = out.astype(LOW)

        chunks(32, body)
        h1_slab[...] = lead_rows(h1, 4)
        lead_start(H1, h1_slab, h1_leads, 1)

    @worker
    def inner_block(block):
        summed[...] = dot(h1[...], weight(4 + block))

        def body(start, size):
            value, grade = gelu_pair(summed[pl.ds(start, size)])
            flat[pl.ds(block * rows_all + start, size)] = value.astype(LOW)
            flat[pl.ds((4 + block) * rows_all + start, size)] = grade.astype(LOW)

        chunks(32, body)

    @worker
    def second_block(place):
        block = lax.rem(2 * me + place, 4)
        product = dot(flat[act_rows(block)], weight(8 + block))
        if place == 0:
            branch[...] = product
        else:
            branch[...] += product

    @worker
    def mlp_close():
        gain, bias = vectors[1, 0:1], vectors[1, 1:2]

        def body(start, size):
            rows = pl.ds(start, size)
            out, normed, inv_dev = normalize(h1[rows].astype(F32) + branch[rows], gain, bias)
            norm1[rows] = normed
            dev1[rows] = jnp.broadcast_to(inv_dev, (size, 128))
            out_rows[rows] = out.astype(LOW)

        chunks(32, body)
        h2_slab[...] = lead_rows(out_rows, 4)
        lead_start(H2, h2_slab, h2_leads, 2)
        guest_copy(OUT).start()

    def add_small(row, value):
        small[row : row + 1] += value

    @worker
    def mlp_open_backward():
        gain = vectors[1, 0:1]

        def body(start, size):
            rows = pl.ds(start, size)
            place = start + lax.broadcasted_iota(jnp.int32, (size, D), 0)
            grad = jnp.where(lax.rem(place, seg_rows) == 0, 0.0, cot_rows[rows].astype(F32))
            grad_sum, grad_gain, grad_bias = normalize_backward(
                grad, norm1[rows], dev1[rows][:, 0:1], gain
            )
            branch[rows] = grad_sum
            kept[rows] = grad_sum.astype(LOW)
            add_small(2, grad_gain)
            add_small(3, grad_bias)

        chunks(32, body)

    def part(block):
        return block + 4 if block < 4 else block + 8

    def store_part(block, left, right):
        for strip in range(2):
            lanes = slice(strip * WIDTH, (strip + 1) * WIDTH)
            blocks[part(block), strip] = (
                outer(left[:, lanes], right).astype(LOW).reshape(2, 2, PIECE, D)
            )

    @worker
    def second_grad(block):
        store_part(8 + block, flat[act_rows(block)], kept[...])

    @worker
    def inner_grad(block):
        grad_act = dot_right(kept[...], weight(8 + block))
        grad_inner = (grad_act * flat[slope_rows(block)].astype(F32)).astype(LOW)
        flat[act_rows(block)] = grad_inner
        branch[...] += dot_right(flat[act_rows(block)], weight(4 + block))
        store_part(4 + block, h1[...], flat[act_rows(block)])

    @worker
    def attention_open_backward():
        gain = vectors[0, 0:1]
        leads = leads_of(lead_grad1, me) + leads_of(lead_grad1, me + 2)

        def body(start, size):
            rows = pl.ds(start, size)
            place = start + lax.broadcasted_iota(jnp.int32, (size, D), 0)
            grad = branch[rows]
            for lead in range(4):
                grad = jnp.where(place == lead * seg_rows, leads[lead], grad)
            grad = grad.astype(LOW).astype(F32)
            grad_sum, grad_gain, grad_bias = normalize_backward(
                grad, norm0[rows], dev0[rows][:, 0:1], gain
            )
            summed[rows] = grad_sum
            kept[rows] = grad_sum.astype(LOW)
            add_small(0, grad_gain)
            add_small(1, grad_bias)

        chunks(32, body)

    @worker
    def out_grad():
        store_part(3, kept[...], context[...])
        context[...] = dot(kept[...], weight(3)).astype(LOW)

    @worker
    def heads_backward():
        @pl.loop(0, PAIRS)
        def _(pair):
            at_q, at_k, at_v = pair_lanes(pair)
            heads = [(seg, place) for seg in segs for place in range(2)]
            grad_probs = [
                dot_right(
                    context[seg_slice(seg), at_q] * head_masks[place], qkv[seg_slice(seg), at_v]
                )
                for seg, place in heads
            ]
            grad_scores = []
            for (seg, place), grad_prob in zip(heads, grad_probs):
                prob = probs[seg, pair, place]
                inside = prob * grad_prob
                grad_score = inside - prob * jnp.sum(inside, axis=-1, keepdims=True)
                grad_scores.append(grad_score.astype(LOW))
            for seg in segs:
                rows = seg_slice(seg)
                query, key, grad = qkv[rows, at_q], qkv[rows, at_k], context[rows, at_q]
                mine = grad_scores[2 * seg : 2 * seg + 2]
                found = [probs[seg, pair, place].astype(LOW) for place in range(2)]
                for at, both, scale in (
                    (at_q, [dot(score, key) for score in mine], 0.125),
                    (at_k, [outer(score, query) for score in mine], 0.125),
                    (at_v, [outer(prob, grad) for prob in found], 1.0),
                ):
                    merged = jnp.where(first_half, both[0], both[1]) * scale
                    qkv[rows, at] = merged.astype(LOW)

    @worker
    def project_grad(block):
        store_part(block, token_rows[...], qkv[:, block * D : (block + 1) * D])

    @worker
    def tokens_back(block):
        summed[...] += dot_right(qkv[:, block * D : (block + 1) * D], weight(block))

    @worker
    def tokens_close():
        h1[...] = summed[...].astype(LOW)
        guest_copy(GRAD).start()

    def leads_mlp_forward(value, first, second, gain, bias):
        total_branch = value.astype(F32)
        for block in range(4):
            lanes = slice(block * D, (block + 1) * D)
            out, grade = gelu_pair(dot(value, first(block)))
            lead_act[:, lanes] = out.astype(LOW)
            lead_slope[:, lanes] = grade
            total_branch = total_branch + dot(lead_act[:, lanes], second(block))
        out, normed, inv_dev = normalize(total_branch, gain, bias)
        lead_norm[...] = normed
        lead_dev[...] = jnp.broadcast_to(inv_dev, (SLAB, 128))
        pack[:, 0:D] = value
        pack[:, LEFT_OUT:RIGHT] = value
        return out

    def leads_mlp_backward(grad, first, second, gain):
        grad_sum, grad_gain, grad_bias = normalize_backward(
            grad, lead_norm[...], lead_dev[:, 0:1], gain
        )
        add_small(4, grad_gain)
        add_small(5, grad_bias)
        low_sum = grad_sum.astype(LOW)
        result = grad_sum
        for block in range(4):
            lanes = slice(block * D, (block + 1) * D)
            grad_inner = (dot_right(low_sum, second(block)) * lead_slope[:, lanes]).astype(LOW)
            pack[:, RIGHT + block * D : RIGHT + (block + 1) * D] = grad_inner
            result = result + dot_right(grad_inner, first(block))
        pack[:, LEFT_HALF:RIGHT_HALF] = lead_act[:, 2 * D :]
        pack[:, RIGHT_HALF:] = low_sum
        handed[:, 0 : 2 * D] = lead_act[:, 0 : 2 * D]
        handed[:, 2 * D :] = low_sum
        return result

    def own_weight(place):
        return flat[flat_rows(place)]

    def last_second(block):
        if block >= 2:
            return own_weight(2 + block)
        return core_in[2 * block : 2 * block + 2].reshape(D, D)

    def leads_first():
        @pl.when(me == 2)
        def _():
            lead_wait(H2, h2_slab, h2_leads, 2, 2)
            for place in range(4):
                load_own(place).wait()
            value = collected(h2_leads, 2).astype(LOW)
            pack[:, 0:D] = value
            for block in range(3):
                lead_qkv[:, block * D : (block + 1) * D] = dot(value, own_weight(block)).astype(LOW)
            docs = seg_doc[...]
            row, column = (lax.broadcasted_iota(jnp.int32, (SLAB, SLAB), i) for i in range(2))
            sort = jnp.where(row == column, 2.0, 0.0)
            for micro in range(seg_doc.shape[0]):
                pair_sort = jnp.where(
                    docs[micro : micro + 1, 0:1] == docs[micro : micro + 1, 1:2], 2.0, 1.0
                )
                near = (row // 2 == micro) & (column // 2 == micro) & (row != column)
                sort = jnp.where(near, pair_sort, sort)
            for pair in range(PAIRS):
                at = [slice(p * D + pair * 128, p * D + (pair + 1) * 128) for p in range(3)]
                query, key, val = (lead_qkv[:, lanes] for lanes in at)
                parts = []
                for place in range(2):
                    scores = dot_right(query * head_masks[place], key) * 0.125
                    scores = jnp.where(
                        sort > 1.5, scores, jnp.where(sort > 0.5, -1000000000.0, -1e30)
                    )
                    raised = jnp.exp(scores - jnp.max(scores, axis=-1, keepdims=True))
                    prob = raised / jnp.sum(raised, axis=-1, keepdims=True)
                    lead_probs[pair, place] = prob
                    parts.append(dot(prob.astype(LOW), val))
                lead_context[:, pair * 128 : (pair + 1) * 128] = jnp.where(
                    first_half, parts[0], parts[1]
                ).astype(LOW)
            summed_rows = value.astype(F32) + dot_right(lead_context[...], own_weight(3))
            out, normed, inv_dev = normalize(summed_rows, vectors[2, 0:1], vectors[2, 1:2])
            lead_norm[...] = normed
            lead_dev[...] = jnp.broadcast_to(inv_dev, (SLAB, 128))
            lead_third[...] = out.astype(LOW)
            hop_copy(THIRD, lead_third, 1).start()

        @pl.when(me == 1)
        def _():
            lead_wait(H1, h1_slab, h1_leads, 1, 2)
            leads_mlp_forward(
                collected(h1_leads, 2).astype(LOW),
                lambda block: weight(4 + block),
                lambda block: weight(8 + block),
                vectors[1, 0:1],
                vectors[1, 1:2],
            )

    def leads_second():
        @pl.when(me == 3)
        def _():
            hop_copy(THIRD, lead_third, -1).wait_recv()
            for place in range(6):
                load_own(place).wait()
            out = leads_mlp_forward(
                lead_third[...], own_weight, last_second, vectors[3, 0:1], vectors[3, 1:2]
            )
            lead_fourth[...] = out.astype(LOW)
            for step in range(1, sections):
                spread_copy(FOURTH, lead_fourth, step).start()
            lead_wait(COT, cot_slab, cot_leads, 3, sections)
            grad = leads_mlp_backward(
                collected(cot_leads, sections), own_weight, last_second, vectors[3, 0:1]
            )
            lead_grad3[...] = grad.astype(LOW)
            hop_copy(GRAD3, lead_grad3, -1).start()
            hop_copy(HAND, handed, -1).start()

    def leads_third():
        @pl.when(me == 2)
        def _():
            hop_copy(GRAD3, lead_grad3, 1).wait_recv()
            grad_sum, grad_gain, grad_bias = normalize_backward(
                lead_grad3[...].astype(F32), lead_norm[...], lead_dev[:, 0:1], vectors[2, 0:1]
            )
            add_small(4, grad_gain)
            add_small(5, grad_bias)
            low_sum = grad_sum.astype(LOW)
            pack[:, LEFT_OUT:RIGHT] = low_sum
            pack[:, RIGHT + 3 * D : LEFT_HALF] = lead_context[...]
            grad_context = dot(low_sum, own_weight(3)).astype(LOW)
            for pair in range(PAIRS):
                at = [slice(p * D + pair * 128, p * D + (pair + 1) * 128) for p in range(3)]
                query, key, val = (lead_qkv[:, lanes] for lanes in at)
                grad = grad_context[:, pair * 128 : (pair + 1) * 128]
                grads = ([], [], [])
                for place in range(2):
                    prob = lead_probs[pair, place]
                    grad_prob = dot_right(grad * head_masks[place], val)
                    inside = prob * grad_prob
                    grad_score = inside - prob * jnp.sum(inside, axis=-1, keepdims=True)
                    grad_score = grad_score.astype(LOW)
                    grads[0].append(dot(grad_score, key))
                    grads[1].append(outer(grad_score, query))
                    grads[2].append(outer(prob.astype(LOW), grad))
                for lanes, pair_grads, scale in zip(at, grads, (0.125, 0.125, 1.0)):
                    merged = jnp.where(first_half, pair_grads[0], pair_grads[1]) * scale
                    pack[:, RIGHT + lanes.start : RIGHT + lanes.stop] = merged.astype(LOW)
            result = grad_sum
            for block in range(3):
                result = result + dot_right(
                    pack[:, RIGHT + block * D : RIGHT + (block + 1) * D], own_weight(block)
                )
            lead_grad2[...] = result.astype(LOW)
            hop_copy(GRAD2, lead_grad2, -1).start()
            hop_copy(HAND, handed, 1).wait_recv()
            pack[:, LEFT_HALF:] = handed[...]

    def leads_fourth():
        @pl.when(me == 1)
        def _():
            hop_copy(GRAD2, lead_grad2, 1).wait_recv()
            grad = leads_mlp_backward(
                lead_grad2[...].astype(F32),
                lambda block: weight(4 + block),
                lambda block: weight(8 + block),
                vectors[1, 0:1],
            )
            lead_grad1[...] = grad.astype(LOW)
            hop_copy(GRAD1, lead_grad1, -1).start()
            hop_copy(HAND, handed, -1).start()

    half_lanes = pl.ds(pl.multiple_of(core * HALF_PACK, 128), HALF_PACK)
    other_lanes = pl.ds(pl.multiple_of((1 - core) * HALF_PACK, 128), HALF_PACK)
    first_peer = {"dp": group * CUBE + (y + core - 2 * y * core) * 4
                  + (x + (1 - core) * (1 - 2 * x)) * 2 + core}
    second_peer = {"dp": group * CUBE + (y + (1 - core) * (1 - 2 * y)) * 4
                   + (x + core - 2 * x * core) * 2 + core}

    def pack_copy(stage):
        chip = y * 2 + x
        first_chip = (y + core - 2 * y * core) * 2 + x + (1 - core) * (1 - 2 * x)
        if stage == 0:
            source, target, peer = pack.at[:, other_lanes], pack_in, beside_core
        elif stage == 1:
            source = target = factors.at[chip, :, half_lanes]
            peer = first_peer
        elif stage == 2:
            source = target = factors.at[chip, :, half_lanes]
            peer = second_peer
        elif stage == 3:
            source = target = factors.at[first_chip, :, half_lanes]
            peer = second_peer
        else:
            source = target = factors.at[:, :, half_lanes]
            peer = beside_core
        return remote(source, target, pack_send.at[stage], pack_recv.at[stage], peer)

    def pack_join():
        pack_copy(0).wait()

        @pl.loop(0, HALF_PACK // WIDTH)
        def _(step):
            start = pl.multiple_of(step * WIDTH, 128)
            lanes = pl.ds(pl.multiple_of(core * HALF_PACK + start, 128), WIDTH)
            mine = pack[:, lanes].astype(F32)[0:8]
            theirs = pack_in[:, pl.ds(start, WIDTH)].astype(F32)[0:8]
            low_rows = jnp.where(core == 0, mine, theirs)
            high_rows = jnp.where(core == 0, theirs, mine)
            factors[y * 2 + x, :, lanes] = jnp.concatenate([low_rows, high_rows]).astype(LOW)

        pack_copy(1).start()

    def pack_second():
        pack_copy(1).wait()
        pack_copy(2).start()
        pack_copy(3).start()

    def pack_third():
        pack_copy(2).wait()
        pack_copy(3).wait()
        pack_copy(4).start()

    def to_packs(step):
        return remote(
            factors, packs.at[group], group_pack_send.at[step], group_pack_recv.at[step],
            {"dp": lax.rem(index + step * CUBE, replicas)},
        )

    def own_pack():
        return pltpu.make_async_copy(factors, packs.at[group], group_pack_send.at[0])

    def pack_fourth():
        pack_copy(4).wait()
        own_pack().start()
        for step in range(1, groups):
            to_packs(step).start()

    def pack_last():
        own_pack().wait()
        for step in range(1, groups):
            to_packs(step).wait()

    def rows_store(place):
        source, target = ((out_rows, layer_out), (h1, grad_tokens))[place]
        return pltpu.make_async_copy(source.at[own_part], target, rows_out.at[place])

    def leads_close():
        @pl.when(me != 3)
        def _():
            spread_copy(FOURTH, lead_fourth, 1).wait_recv()

        @pl.when(me >= 2)
        def _():
            guest_copy(OUT).wait_recv()

        leads = leads_of(lead_fourth, me)
        for lead in range(2):
            rows = pl.ds(lead * seg_rows, SLAB)
            out_rows[rows] = jnp.where(
                row_of == 0, leads[lead], out_rows[rows].astype(F32)
            ).astype(LOW)
        rows_store(0).start()

        @pl.when(me == 0)
        def _():
            hop_copy(GRAD1, lead_grad1, 1).wait_recv()
            hop_copy(HAND, handed, 1).wait_recv()
            pack[:, 0:LEFT_HALF] = jnp.zeros((SLAB, LEFT_HALF), LOW)
            pack[:, LEFT_HALF:] = handed[...]

        pack_copy(0).start()

    def add(target, *sources):
        value = target[...].astype(F32)
        for source in sources:
            value = value + source[...].astype(F32)
        target[...] = value.astype(LOW)

    def landing(block):
        return blocks.at[8 + block, 0] if block < 4 else core_in.at[block - 4]

    def scatter(turn, stage):
        block, lanes = turn // 2, lanes_of(turn)
        run = blocks.at[part(block)]
        source, target, peer = (
            (run.at[:, :, 1 - core, :, lanes], landing(block).at[:, :, :, lanes], beside_core),
            (run.at[:, 1 - x, core, upper, lanes], one_a.at[block, :, :, lanes], beside_x),
            (run.at[1 - y, :, core, lower, lanes], one_b.at[block, :, :, lanes], beside_y),
            (run.at[1 - y, x, core, upper, lanes], two_a.at[block, :, lanes], beside_y),
            (run.at[y, 1 - x, core, lower, lanes], two_b.at[block, :, lanes], beside_x),
        )[stage]
        return remote(source, target, rs_send.at[turn, stage], rs_recv.at[turn, stage], peer)

    def to_line(turn):
        return remote(
            blocks.at[part(turn // 2), y, x, core, :, lanes_of(turn)],
            line_in.at[turn // 2, :, lanes_of(turn)],
            z_send.at[turn],
            z_recv.at[turn],
            {"section": HOLDER[turn // 2]},
        )

    def to_holder(turn):
        place = EARLY.index(turn // 2)
        return remote(
            blocks.at[part(turn // 2), :, :, core, :, lanes_of(turn)],
            early_in.at[place, :, :, :, lanes_of(turn)],
            z_send.at[turn],
            z_recv.at[turn],
            {"section": HOLDER[turn // 2]},
        )

    def to_group(turn, step):
        return remote(
            blocks.at[part(turn // 2), y, x, core, :, lanes_of(turn)],
            group_in.at[turn // 2, step - 1, :, lanes_of(turn)],
            group_send.at[turn, step - 1],
            group_recv.at[turn, step - 1],
            {"dp": lax.rem(index + step * CUBE, replicas)},
        )

    def gather_back(turn, stage):
        place = 2 * OWN[HOLDER[turn // 2]].index(turn // 2) + turn % 2
        run, lanes = blocks.at[part(turn // 2)], lanes_of(turn)
        ref, peer = (
            (run.at[y, x, core, upper, lanes], beside_y),
            (run.at[y, x, core, lower, lanes], beside_x),
            (run.at[:, x, core, upper, lanes], beside_x),
            (run.at[y, :, core, lower, lanes], beside_y),
            (run.at[:, :, core, :, lanes], beside_core),
        )[stage]
        return remote(ref, ref, ag_send.at[place, stage], ag_recv.at[place, stage], peer)

    def write_out(block):
        place = OWN[HOLDER[block]].index(block)
        return pltpu.make_async_copy(
            blocks.at[part(block)], total.at[place], out_sem.at[place]
        )

    @worker
    def reduce_core(block):
        scatter(2 * block, 0).start()
        scatter(2 * block + 1, 0).start()

    def is_early(turn):
        return turn // 2 in EARLY

    def in_plane(turn):
        return me == HOLDER[turn // 2] if is_early(turn) else works

    def add_four(turn, source):
        for yy in range(2):
            for xx in range(2):
                add(
                    blocks.at[part(turn // 2), yy, xx, core, :, lanes_of(turn)],
                    source.at[yy, xx, :, lanes_of(turn)],
                )

    def reduce_one(turn):
        @pl.when(works)
        def _():
            scatter(turn, 0).wait()
            add_four(turn, landing(turn // 2))
            if not is_early(turn):
                scatter(turn, 1).start()
                scatter(turn, 2).start()

        if is_early(turn):

            @pl.when(me == 1 - HOLDER[turn // 2])
            def _():
                to_holder(turn).start()

    def reduce_early(turn):
        @pl.when(me == HOLDER[turn // 2])
        def _():
            to_holder(turn).wait_recv()
            add_four(turn, early_in.at[EARLY.index(turn // 2)])
            scatter(turn, 1).start()
            scatter(turn, 2).start()

    def reduce_two(turn):
        @pl.when(in_plane(turn))
        def _():
            reduce_two_now(turn)

    def reduce_two_now(turn):
        block, lanes = turn // 2, lanes_of(turn)
        run = blocks.at[part(block)]
        scatter(turn, 1).wait()
        for yy in range(2):
            add(run.at[yy, x, core, upper, lanes], one_a.at[block, yy, :, lanes])
        scatter(turn, 3).start()
        scatter(turn, 2).wait()
        for xx in range(2):
            add(run.at[y, xx, core, lower, lanes], one_b.at[block, xx, :, lanes])
        scatter(turn, 4).start()

    def reduce_three(turn):
        @pl.when(in_plane(turn))
        def _():
            reduce_three_now(turn)

        if not is_early(turn):

            @pl.when(me == 1 - HOLDER[turn // 2])
            def _():
                to_line(turn).start()

        else:

            @pl.when(me == HOLDER[turn // 2])
            def _():
                spread_one(turn)

    def reduce_three_now(turn):
        block, lanes = turn // 2, lanes_of(turn)
        run = blocks.at[part(block)]
        scatter(turn, 3).wait()
        add(run.at[y, x, core, upper, lanes], two_a.at[block, :, lanes])
        scatter(turn, 4).wait()
        add(run.at[y, x, core, lower, lanes], two_b.at[block, :, lanes])
        if groups > 1:
            for step in range(1, groups):
                to_group(turn, step).start()
            for step in range(1, groups):
                to_group(turn, step).wait()
            for step in range(1, groups):
                copy = pltpu.make_async_copy(
                    group_in.at[block, step - 1, :, lanes], group_piece, group_load
                )
                copy.start()
                copy.wait()
                add(run.at[y, x, core, :, lanes], group_piece)

    def spread_one(turn):
        gather_back(turn, 0).start()
        gather_back(turn, 1).start()

    def reduce_line(turn):
        @pl.when(me == HOLDER[turn // 2])
        def _():
            block, lanes = turn // 2, lanes_of(turn)
            to_line(turn).wait_recv()
            add(blocks.at[part(block), y, x, core, :, lanes], line_in.at[block, :, lanes])
            spread_one(turn)

    def spread_two(turn):
        @pl.when(me == HOLDER[turn // 2])
        def _():
            gather_back(turn, 0).wait()
            gather_back(turn, 2).start()
            gather_back(turn, 1).wait()
            gather_back(turn, 3).start()

    def spread_core(turn):
        @pl.when(me == HOLDER[turn // 2])
        def _():
            gather_back(turn, 2).wait()
            gather_back(turn, 3).wait()
            gather_back(turn, 4).start()

    def spread_done(turn):
        @pl.when(me == HOLDER[turn // 2])
        def _():
            gather_back(turn, 4).wait()
            if turn % 2 == 1:
                write_out(turn // 2).start()

        @pl.when(me == 1 - HOLDER[turn // 2])
        def _():
            (to_holder if is_early(turn) else to_line)(turn).wait_send()

    tail_plan = ((spread_done, 13), (spread_core, 11), (spread_two, 9))
    late_plan = tail_plan + (
        (reduce_three, 5), (reduce_line, 7), (reduce_two, 3), (reduce_one, 1)
    )
    early_plan = tail_plan + (
        (reduce_three, 7), (reduce_two, 5), (reduce_early, 3), (reduce_one, 1)
    )

    def turns(*order):
        return tuple(2 * block + side for block in order for side in range(2))

    class Wave:
        def __init__(self, order):
            self.order, self.at = turns(*order), 0

        def tick(self, count=1):
            for _ in range(count):
                for stage, offset in late_plan:
                    if 0 <= self.at - offset < len(self.order):
                        stage(self.order[self.at - offset])
                self.at += 1

        def left(self):
            return self.at < len(self.order) + tail_plan[0][1]

    one, two = Wave((8, 9, 10, 11, 4, 5, 6, 7)), Wave((3, 0, 1, 2))

    small[...] = jnp.zeros_like(small)

    @pl.when(works)
    def _():
        guest_copy(TOKENS).wait_recv()

    for tick in range(gather_ticks):
        gather_tick(tick)
        at = tick - gather_plan[0][1]
        if at == 0:
            gather_wait_own()
            for step in range(1, sections):
                vector_copy(step).wait()
        if at < 0:
            continue
        if at % 2 == 1 and at < 6:
            project(at // 2)
        if at == 6:
            heads_forward()
        if at == 7:
            attention_close()
        if at >= 8:
            inner_block(at - 8)
    for place in range(4):
        second_block(place)
    mlp_close()

    @pl.when(works)
    def _():
        guest_copy(COTANGENT).wait_recv()

    mlp_open_backward()
    for reader, wanted in WANTED.items():
        for turn in turns(*wanted):
            gather_finish(turn, reader)

    for block in range(4):
        second_grad(block)
        reduce_core(8 + block)
        one.tick(2)
        if block == 1:
            leads_first()
    for block in range(4):
        inner_grad(block)
        reduce_core(4 + block)
        one.tick(2)
        if block == 0:
            leads_second()
        if block == 2:
            leads_third()
    leads_fourth()

    @pl.when(works)
    def _():
        pl.semaphore_signal(credit, inc=1, device_id=beside_core, device_id_type=MESH)

    one.tick(2)
    leads_close()
    attention_open_backward()
    out_grad()
    pack_join()

    @pl.when(works)
    def _():
        pl.semaphore_wait(credit, 1)

    reduce_core(3)
    one.tick(2)
    two.tick()
    heads_backward()
    pack_second()
    for block in range(3):
        project_grad(block)
        reduce_core(block)
        one.tick(2)
        two.tick(2)

    def small_copy(step):
        return remote(
            small, small_all.at[index], small_send.at[step], small_recv.at[step], replica(step)
        )

    def sum_copy(step):
        return remote(
            small_sum, smalls.at[me], sum_send.at[step], sum_recv.at[step], others[step - 1]
        )

    def own_sum():
        return pltpu.make_async_copy(small_sum, smalls.at[me], sum_send.at[0])

    @pl.loop(1, replicas)
    def _(step):
        small_copy(step).start()

    small_all[index] = small[...]
    for block in range(3):
        tokens_back(block)
        one.tick()
        two.tick()
    tokens_close()
    pack_third()

    @pl.loop(1, replicas)
    def _(step):
        small_copy(step).wait()

    small_sum[...] = jnp.sum(small_all[...], axis=0)
    for place in range(1, sections):
        sum_copy(place).start()
    own_sum().start()
    pack_fourth()
    while one.left() or two.left():
        if one.left():
            one.tick()
        if two.left():
            two.tick()

    for place in range(1, sections):
        sum_copy(place).wait()
    own_sum().wait()
    pack_last()

    for holder in (0, 1):

        @pl.when(me == holder)
        def _():
            for block in OWN[holder]:
                write_out(block).wait()

    @pl.when(me != 3)
    def _():
        lead_copy(COT, cot_slab, cot_leads, 3).wait_send()

    @pl.when(me == 0)
    def _():
        lead_copy(H1, h1_slab, h1_leads, 1).wait_send()

    @pl.when(works)
    def _():
        lead_copy(H2, h2_slab, h2_leads, 2).wait_send()
        guest_copy(OUT).wait_send()
        guest_copy(GRAD).wait_send()

    @pl.when(me >= 2)
    def _():
        guest_copy(TOKENS).wait_send()
        guest_copy(COTANGENT).wait_send()
        guest_copy(GRAD).wait_recv()

    rows_store(1).start()
    rows_store(1).wait()
    rows_store(0).wait()

    @pl.when(me == 1)
    def _():
        hop_copy(GRAD1, lead_grad1, -1).wait_send()
        hop_copy(HAND, handed, -1).wait_send()

    @pl.when(me == 2)
    def _():
        hop_copy(THIRD, lead_third, 1).wait_send()
        hop_copy(GRAD2, lead_grad2, -1).wait_send()

    @pl.when(me == 3)
    def _():
        for place in range(1, sections):
            spread_copy(FOURTH, lead_fourth, place).wait_send()
        hop_copy(GRAD3, lead_grad3, -1).wait_send()
        hop_copy(HAND, handed, -1).wait_send()


def run_layers(sections, replicas, tokens, cotangent, seg_doc, gain, bias, wide, half):
    groups = replicas // CUBE
    rows = 2 * tokens.shape[0]
    seg_rows = tokens.shape[0] // 2
    vector = (8, D)
    block = (2, 2, 2, PIECE, D)
    reduced_groups = max(groups - 1, 1)
    in_vmem = pl.BlockSpec(memory_space=pltpu.VMEM)
    anywhere = pl.BlockSpec(memory_space=pl.ANY)
    slab = pltpu.VMEM((SLAB, D), LOW)
    leads = pltpu.VMEM((sections, SLAB, D), LOW)
    low_rows = pltpu.VMEM((rows, D), LOW)
    full_rows = pltpu.VMEM((rows, D), F32)
    return pl.pallas_call(
        partial(layer_kernel, sections, replicas),
        out_shape=(
            jax.ShapeDtypeStruct(tokens.shape, LOW),
            jax.ShapeDtypeStruct(tokens.shape, LOW),
            jax.ShapeDtypeStruct((OWNED,) + block, LOW),
            jax.ShapeDtypeStruct((groups, CUBE // 2, SLAB, PACK), LOW),
            jax.ShapeDtypeStruct((sections,) + vector, F32),
            jax.ShapeDtypeStruct(
                (REDUCED if groups > 1 else 1, reduced_groups, PIECE, D), LOW
            ),
        ),
        in_specs=[anywhere] * 2 + [in_vmem] * 3 + [anywhere] * 4,
        out_specs=[anywhere] * 6,
        scratch_shapes=[
            pltpu.VMEM((REDUCED + 8,) + block, LOW),
            pltpu.VMEM((max(8 * rows, 6 * D), D), LOW),
            pltpu.VMEM((8, 2, 2, PIECE, D), LOW),
            pltpu.VMEM((REDUCED, 2, HALF, D), LOW),
            pltpu.VMEM((REDUCED, 2, HALF, D), LOW),
            pltpu.VMEM((REDUCED, HALF, D), LOW),
            pltpu.VMEM((REDUCED, HALF, D), LOW),
            pltpu.VMEM((REDUCED, PIECE, D), LOW),
            pltpu.VMEM((max(len(EARLY), 1), 2, 2, PIECE, D), LOW),
            pltpu.VMEM((sections,) + vector, F32),
            low_rows, low_rows, low_rows,
            pltpu.VMEM((rows, 3 * D), LOW),
            pltpu.VMEM((4, PAIRS, 2, seg_rows, seg_rows), F32),
            low_rows, low_rows, full_rows,
            pltpu.VMEM((rows, 128), F32),
            full_rows, full_rows,
            pltpu.VMEM((rows, 128), F32),
            full_rows, low_rows,
            slab, slab, slab, leads, leads, leads,
            slab, slab, slab, slab, slab,
            pltpu.VMEM((SLAB, 3 * D), LOW),
            pltpu.VMEM((SLAB, 3 * D), LOW),
            pltpu.VMEM((PAIRS, 2, SLAB, SLAB), F32),
            slab,
            pltpu.VMEM((SLAB, D), F32),
            pltpu.VMEM((SLAB, 128), F32),
            pltpu.VMEM((SLAB, 4 * D), LOW),
            pltpu.VMEM((SLAB, 4 * D), F32),
            pltpu.VMEM((SLAB, PACK), LOW),
            pltpu.VMEM((SLAB, HALF_PACK), LOW),
            pltpu.VMEM((CUBE // 2, SLAB, PACK), LOW),
            pltpu.VMEM(vector, F32),
            pltpu.VMEM((replicas,) + vector, F32),
            pltpu.VMEM(vector, F32),
            pltpu.VMEM((PIECE, WIDTH), LOW),
            DMA((2,)),
            DMA((4,)),
            DMA((4,)),
            DMA((2,)),
            DMA((ROUNDS,)),
            DMA((ROUNDS,)),
            DMA((ROUNDS, 5)),
            DMA((ROUNDS, 5)),
            DMA((GATHERED,)),
            DMA((2 * REDUCED, 5)),
            DMA((2 * REDUCED, 5)),
            DMA((2 * REDUCED,)),
            DMA((2 * REDUCED,)),
            DMA((2 * REDUCED, reduced_groups)),
            DMA((2 * REDUCED, reduced_groups)),
            DMA,
            DMA((2 * OWNED, 5)),
            DMA((2 * OWNED, 5)),
            DMA((OWNED,)),
            DMA((5,)),
            DMA((5,)),
            DMA((groups,)),
            DMA((groups,)),
            DMA((replicas,)),
            DMA((replicas,)),
            DMA((sections,)),
            DMA((sections,)),
            DMA((sections,)),
            DMA((sections,)),
            DMA((3,)),
            DMA((3, sections)),
            DMA((1, sections)),
            DMA((1,)),
            DMA((5,)),
            DMA((5,)),
            pltpu.SemaphoreType.REGULAR,
        ],
        compiler_params=pltpu.CompilerParams(
            collective_id=0, has_side_effects=True, vmem_limit_bytes=VMEM_BYTES
        ),
    )(
        tokens, cotangent, seg_doc, gain, bias,
        wide.reshape(2, 2, 2, PIECE, 4 * D), half.reshape(2, 2, 2, 2, PIECE, D), wide, half,
    )


VMEM_BYTES = 62 * 1024 * 1024


def close_kernel(
    total, packs, smalls, rows_in, grads_in,
    wide_out, half_out, gain_out, bias_out, rows_out, grads_out,
):
    me = lax.axis_index("section")
    step = pl.program_id(0)
    near = me < 2
    packed = packs.reshape(-1, PACK)
    summed = jnp.where(near, total[0, 0].reshape(WIDTH, D).astype(F32), 0.0)

    def wide_step(block, side):
        @pl.when(step == 2 * block + side)
        def _():
            first = (0 if block < 3 else LEFT_OUT) + side * WIDTH
            left = packed[:, first : first + WIDTH]
            right = packed[:, RIGHT + block * D : RIGHT + (block + 1) * D]
            wide_out[0] = summed + outer(left, right)

    def half_step(side):
        @pl.when(step == 8 + side)
        def _():
            first = LEFT_HALF + side * WIDTH
            half_out[0] = summed + outer(packed[:, first : first + WIDTH], packed[:, RIGHT_HALF:])

    for block in range(4):
        for side in range(2):
            wide_step(block, side)
    for side in range(4):
        half_step(side)

    @pl.when(step == 0)
    def _():
        every = jnp.sum(smalls[...], axis=0)
        mine = smalls[me]
        for row, out in ((0, gain_out), (1, bias_out)):
            value = jnp.where(me == 0, every[row : row + 1], every[2 + row : 3 + row])
            value = jnp.where(near, value, 0.0) + mine[4 + row : 5 + row]
            out[...] = value
        rows_out[...] = rows_in[...]
        grads_out[...] = grads_in[...]


def close(total, packs, smalls, rows, grads):
    def whole(shape):
        return pl.BlockSpec(shape, lambda step: (0,) * len(shape))

    return pl.pallas_call(
        close_kernel,
        grid=(2 * OWNED,),
        out_shape=(
            jax.ShapeDtypeStruct((1, D, 4 * D), F32),
            jax.ShapeDtypeStruct((1, 2 * D, D), F32),
            jax.ShapeDtypeStruct((1, D), F32),
            jax.ShapeDtypeStruct((1, D), F32),
            jax.ShapeDtypeStruct(rows.shape, LOW),
            jax.ShapeDtypeStruct(rows.shape, LOW),
        ),
        in_specs=[
            pl.BlockSpec(
                (1, 1) + total.shape[2:], lambda step: (step // 2, lax.rem(step, 2), 0, 0, 0, 0)
            ),
            whole(packs.shape),
            whole(smalls.shape),
            whole(rows.shape),
            whole(rows.shape),
        ],
        out_specs=[
            pl.BlockSpec(
                (1, WIDTH, D),
                lambda step: (
                    0,
                    jnp.where(step < 8, lax.rem(step, 2), 1),
                    jnp.minimum(step // 2, 3),
                ),
            ),
            pl.BlockSpec((1, WIDTH, D), lambda step: (0, jnp.maximum(step - 8, 0), 0)),
            whole((1, D)),
            whole((1, D)),
            whole(rows.shape),
            whole(rows.shape),
        ],
        compiler_params=pltpu.CompilerParams(vmem_limit_bytes=VMEM_BYTES),
    )(total, packs, smalls, rows, grads)


def on_device(tokens, cotangent, seg_doc, wide_in, half_out, norm_gain, norm_bias):
    sections = lax.axis_size("section")
    replicas = lax.axis_size("dp")
    rows, grads, total, packs, smalls, _ = run_layers(
        sections, replicas, tokens, cotangent, seg_doc, norm_gain, norm_bias, wide_in[0], half_out[0]
    )
    wide_grad, half_grad, gain_grad, bias_grad, layer_out, tokens_grad = close(
        total, packs, smalls, rows, grads
    )
    return layer_out, tokens_grad, wide_grad, half_grad, gain_grad, bias_grad


def solution(mesh):
    placed = (
        P(("dp", "section"), None),
        P(("dp", "section"), None),
        P("dp", None),
        P("section", None, None),
        P("section", None, None),
        P("section", None),
        P("section", None),
    )
    return jax.shard_map(
        on_device,
        mesh=mesh,
        in_specs=placed,
        out_specs=(
            P(("dp", "section"), None),
            P(("dp", "section"), None),
            P("section", None, None),
            P("section", None, None),
            P("section", None),
            P("section", None),
        ),
        check_vma=False,
    )
```

```python
from functools import partial

import jax
import jax.numpy as jnp
from jax import lax
from jax.experimental import pallas as pl
from jax.experimental.pallas import tpu as pltpu
from jax.sharding import PartitionSpec as P

D = 768
HEADS = 12
PAIRS = HEADS // 2
CUBE = 8
PIECE = D // CUBE
HALF = PIECE // 2
WIDTH = D // 2
SLAB = 16
HOLDER = (0, 0, 0, 0, 1, 1, 1, 1, 0, 0, 1, 1, 2, 2)
GATHERED = len(HOLDER)
ROUNDS = 2 * GATHERED
WANTED = {0: (4, 5, 6, 7, 10, 11), 1: (0, 1, 2, 3, 8, 9), 3: (12, 13)}
EARLY = ()
REDUCED = 12
OWN = {0: (0, 1, 2, 3, 8, 9), 1: (4, 5, 6, 7, 10, 11)}
OWNED = len(OWN[0])
LEFT_OUT, RIGHT, LEFT_HALF, RIGHT_HALF, PACK = D, 2 * D, 6 * D, 8 * D, 9 * D
HALF_PACK = PACK // 2
LOW = jnp.bfloat16
F32 = jnp.float32
DMA = pltpu.SemaphoreType.DMA
MESH = pl.DeviceIdType.MESH


def dot(left, right):
    return jnp.dot(left, right, preferred_element_type=F32)


def dot_right(left, right):
    return lax.dot_general(left, right, (((1,), (1,)), ((), ())), preferred_element_type=F32)


def outer(left, right):
    return lax.dot_general(left, right, (((0,), (0,)), ((), ())), preferred_element_type=F32)


def normalize(summed, gain, bias):
    average = jnp.mean(summed, axis=-1, keepdims=True)
    centred = summed - average
    inv_dev = lax.rsqrt(jnp.mean(centred * centred, axis=-1, keepdims=True) + 1e-05)
    normed = centred * inv_dev
    return normed * gain + bias, normed, inv_dev


def normalize_backward(grad, normed, inv_dev, gain):
    scaled = grad * gain
    mean_scaled = jnp.mean(scaled, axis=-1, keepdims=True)
    mean_normed = jnp.mean(scaled * normed, axis=-1, keepdims=True)
    grad_sum = inv_dev * (scaled - mean_scaled - normed * mean_normed)
    return (
        grad_sum,
        jnp.sum(grad * normed, axis=0, keepdims=True),
        jnp.sum(grad, axis=0, keepdims=True),
    )


def gelu_pair(value):
    bell = jnp.exp(-0.5 * value * value)
    base = 1.0 + (0.3275911 * 0.7071067811865476) * jnp.abs(value)
    guess = pl.reciprocal(base, approx=True)
    t = guess * (2.0 - base * guess)
    poly = t * (
        0.5 * 0.254829592
        + t
        * (
            0.5 * -0.284496736
            + t * (0.5 * 1.421413741 + t * (0.5 * -1.453152027 + t * (0.5 * 1.061405429)))
        )
    )
    tail = poly * bell
    below = jnp.where(value >= 0, 1.0 - tail, tail)
    return value * below, below + value * bell * 0.3989422804014327


def position():
    index = lax.axis_index("dp")
    return (lax.rem(index // 4, 2), lax.rem(index // 2, 2), lax.rem(index, 2), index // CUBE)


def remote(source, target, send, receive, device):
    return pltpu.make_async_remote_copy(
        src_ref=source,
        dst_ref=target,
        send_sem=send,
        recv_sem=receive,
        device_id=device,
        device_id_type=MESH,
    )


def layer_kernel(
    sections, replicas,
    tokens, cotangent, seg_doc, norm_gain, norm_bias, wide, half, wide_flat, half_flat,
    layer_out, grad_tokens, total, packs, smalls, group_in,
    blocks, flat, core_in, one_a, one_b, two_a, two_b, line_in, early_in, vectors,
    token_rows, cot_rows, out_rows,
    qkv, probs, context, h1, norm0, dev0, summed, norm1, dev1, branch, kept,
    cot_slab, h1_slab, h2_slab, cot_leads, h1_leads, h2_leads,
    lead_third, lead_fourth, lead_grad3, lead_grad2, lead_grad1, handed,
    lead_qkv, lead_probs, lead_context, lead_norm, lead_dev, lead_act, lead_slope,
    pack, pack_in, factors, small, small_all, small_sum, group_piece,
    rows_load, guest_send, guest_recv, rows_out,
    line_send, line_recv, cube_send, cube_recv, load_sem,
    rs_send, rs_recv, z_send, z_recv, group_send, group_recv, group_load, ag_send, ag_recv,
    out_sem, pack_send, pack_recv, group_pack_send, group_pack_recv,
    small_send, small_recv, sum_send, sum_recv,
    vector_send, vector_recv, lead_send, lead_recv, spread_send, spread_recv, hop_send, hop_recv,
    credit,
):
    me = lax.axis_index("section")
    index = lax.axis_index("dp")
    y, x, core, group = position()
    groups = replicas // CUBE
    micro_rows = tokens.shape[0]
    seg_rows = micro_rows // 2
    rows_all = 2 * micro_rows
    works = me < 2

    def cube_peer(yy, xx, cc):
        return {"dp": group * CUBE + yy * 4 + xx * 2 + cc}

    beside_x = cube_peer(y, 1 - x, core)
    beside_y = cube_peer(1 - y, x, core)
    beside_core = cube_peer(y, x, 1 - core)
    others = [{"section": lax.rem(me + step, sections)} for step in range(1, sections)]

    def replica(step):
        return {"dp": lax.rem(index + step, replicas)}

    barrier = pltpu.get_barrier_semaphore()
    for other in others:
        pl.semaphore_signal(barrier, inc=1, device_id=other, device_id_type=MESH)

    @pl.loop(1, replicas)
    def _(step):
        pl.semaphore_signal(barrier, inc=1, device_id=replica(step), device_id_type=MESH)

    own_part, guest_part = pl.ds(0, micro_rows), pl.ds(micro_rows, micro_rows)

    def load_rows(place):
        source, target = ((tokens, token_rows), (cotangent, cot_rows))[place]
        return pltpu.make_async_copy(source, target.at[own_part], rows_load.at[place])

    load_rows(0).start()
    load_rows(1).start()

    def load(block):
        if block < 8:
            source = wide.at[:, :, :, :, pl.ds((block % 4) * D, D)]
        else:
            source = half.at[block % 2]
        return pltpu.make_async_copy(source, blocks.at[block], load_sem.at[block])

    def flat_rows(place):
        return pl.ds(place * D, D)

    def load_own(place):
        if place < 4:
            source = wide_flat.at[:, pl.ds(place * D, D)]
        else:
            source = half_flat.at[flat_rows(place - 4)]
        return pltpu.make_async_copy(source, flat.at[flat_rows(place)], load_sem.at[place])

    for holder in (0, 1):

        @pl.when(me == holder)
        def _():
            for block in OWN[holder]:
                load(block).start()

    @pl.when(me >= 2)
    def _():
        for place in range(4):
            load_own(place).start()

    def load_upper(block):
        return pltpu.make_async_copy(
            half.at[block], core_in.at[pl.ds(2 * block, 2)], load_sem.at[REDUCED + block]
        )

    @pl.when(me == 2)
    def _():
        for block in range(2):
            load_upper(block).start()

    @pl.when(me == 3)
    def _():
        for place in (4, 5):
            load_own(place).start()

    pl.semaphore_wait(barrier, sections - 1 + replicas - 1)

    def guest_copy(kind):
        down = {"section": lax.rem(me + sections - 2, sections)}
        up = {"section": lax.rem(me + 2, sections)}
        source, target, device = (
            (token_rows.at[own_part], token_rows.at[guest_part], down),
            (cot_rows.at[own_part], cot_rows.at[guest_part], down),
            (out_rows.at[guest_part], out_rows.at[own_part], up),
            (h1.at[guest_part], h1.at[own_part], up),
        )[kind]
        return remote(source, target, guest_send.at[kind], guest_recv.at[kind], device)

    TOKENS, COTANGENT, OUT, GRAD = 0, 1, 2, 3

    load_rows(0).wait()
    load_rows(1).wait()

    @pl.when(me >= 2)
    def _():
        guest_copy(TOKENS).start()

    row_of = lax.broadcasted_iota(jnp.int32, (SLAB, D), 0)

    def lead_rows(ref, count):
        value = jnp.zeros((SLAB, D), F32)
        for lead in range(count):
            row = ref[lead * seg_rows : lead * seg_rows + SLAB].astype(F32)[0:1]
            value = jnp.where(row_of == lead, row, value)
        return value.astype(LOW)

    def lead_copy(kind, slab, target, reader):
        return remote(
            slab, target.at[me], lead_send.at[kind], lead_recv.at[kind, me], {"section": reader}
        )

    def lead_start(kind, slab, target, reader):
        @pl.when(me != reader)
        def _():
            lead_copy(kind, slab, target, reader).start()

        @pl.when(me == reader)
        def _():
            target[reader] = slab[...]

    def lead_wait(kind, slab, target, reader, senders):
        for section in range(senders):
            if section != reader:
                remote(
                    slab, target.at[section], lead_send.at[kind], lead_recv.at[kind, section],
                    {"section": section},
                ).wait_recv()

    def collected(target, senders):
        value = jnp.zeros((SLAB, D), F32)
        for section in range(senders):
            slab = target[section].astype(F32)
            for micro in range(section, sections, senders):
                for lead in range(2):
                    place = (micro - section) // senders * 2 + lead
                    value = jnp.where(
                        row_of == 2 * micro + lead, slab[place : place + 1], value
                    )
        return value

    def spread_copy(kind, slab, step):
        return remote(
            slab, slab, spread_send.at[kind, step], spread_recv.at[kind], others[step - 1]
        )

    def hop_copy(kind, slab, step):
        return remote(
            slab, slab, hop_send.at[kind], hop_recv.at[kind],
            {"section": lax.rem(me + step + sections, sections)},
        )

    def leads_of(slab, micro):
        value = slab[...].astype(F32)
        return [
            jnp.sum(jnp.where(row_of == 2 * micro + lead, value, 0.0), axis=0, keepdims=True)
            for lead in range(2)
        ]

    COT, H1, H2 = 0, 1, 2
    FOURTH = 0
    THIRD, GRAD3, GRAD2, HAND, GRAD1 = 0, 1, 2, 3, 4

    def vector_copy(step):
        return remote(
            vectors.at[me], vectors.at[me], vector_send.at[step], vector_recv.at[step],
            others[step - 1],
        )

    vectors[me, 0:1] = norm_gain[...]
    vectors[me, 1:2] = norm_bias[...]
    for step in range(1, sections):
        vector_copy(step).start()
    cot_slab[...] = lead_rows(cot_rows, 2)
    lead_start(COT, cot_slab, cot_leads, 3)

    upper, lower = pl.ds(0, HALF), pl.ds(HALF, HALF)

    def lanes_of(turn):
        return pl.ds((turn % 2) * WIDTH, WIDTH)

    def turns(*order):
        return tuple(2 * block + side for block in order for side in range(2))

    def place_of(block):
        if block < REDUCED:
            return blocks.at[block]
        return core_in.at[pl.ds(2 * (block - REDUCED), 2)]

    def line_copy(turn, reader):
        block, lanes = turn // 2, lanes_of(turn)
        piece = place_of(block).at[y, x, core, :, lanes]
        return remote(
            piece,
            piece,
            line_send.at[turn],
            line_recv.at[turn],
            {"section": reader},
        )

    def cube_copy(turn, stage):
        full, lanes = place_of(turn // 2), lanes_of(turn)
        ref, peer = (
            (full.at[y, x, core, upper, lanes], beside_x),
            (full.at[y, x, core, lower, lanes], beside_y),
            (full.at[y, :, core, upper, lanes], beside_y),
            (full.at[:, x, core, lower, lanes], beside_x),
            (full.at[:, :, core, :, lanes], beside_core),
        )[stage]
        return remote(ref, ref, cube_send.at[turn, stage], cube_recv.at[turn, stage], peer)

    def gather_line(turn, reader):
        @pl.when(me == reader)
        def _():
            line_copy(turn, reader).wait_recv()
            cube_copy(turn, 0).start()
            cube_copy(turn, 1).start()

    def gather_two(turn, reader):
        @pl.when(me == reader)
        def _():
            cube_copy(turn, 0).wait_recv()
            cube_copy(turn, 2).start()
            cube_copy(turn, 1).wait_recv()
            cube_copy(turn, 3).start()

    def gather_three(turn, reader):
        @pl.when(me == reader)
        def _():
            cube_copy(turn, 2).wait_recv()
            cube_copy(turn, 3).wait_recv()
            cube_copy(turn, 4).start()

    def gather_ready(turn, reader):
        @pl.when(me == reader)
        def _():
            cube_copy(turn, 4).wait_recv()

    def gather_finish(turn, reader):
        @pl.when(me == reader)
        def _():
            for stage in range(5):
                cube_copy(turn, stage).wait_send()

        @pl.when(me == HOLDER[turn // 2])
        def _():
            line_copy(turn, reader).wait_send()

    def gather_send():
        for reader, wanted in WANTED.items():

            @pl.when(me == HOLDER[wanted[0]])
            def _():
                for turn in turns(*wanted):
                    line_copy(turn, reader).start()

    gather_plan = ((gather_ready, 6), (gather_three, 4), (gather_two, 2), (gather_line, 0))
    gather_ticks = 2 * OWNED + gather_plan[0][1]

    def gather_tick(tick):
        for stage, offset in gather_plan:
            at = tick - offset
            for reader, wanted in WANTED.items():
                if 0 <= at < 2 * len(wanted):
                    stage(2 * wanted[at // 2] + at % 2, reader)

    def gather_wait_own():
        @pl.when(me == 2)
        def _():
            for block in range(2):
                load_upper(block).wait()

        for holder in (0, 1):

            @pl.when(me == holder)
            def _():
                for block in OWN[holder]:
                    load(block).wait()

    def worker(step):
        def run(*given):
            @pl.when(works)
            def _():
                step(*given)

        return run

    def weight(block):
        return blocks[block].reshape(D, D)

    def act_rows(block):
        return pl.ds(pl.multiple_of(block * rows_all, SLAB), rows_all)

    def slope_rows(block):
        return pl.ds(pl.multiple_of((4 + block) * rows_all, SLAB), rows_all)

    lane_of = lax.broadcasted_iota(jnp.int32, (1, 128), 1)
    first_half = lane_of < 64
    head_masks = (first_half.astype(LOW), (~first_half).astype(LOW))
    segs = range(4)

    def chunks(size, body):
        @pl.loop(0, rows_all // size)
        def _(step):
            body(pl.multiple_of(step * size, size), size)

    @worker
    def project(block):
        qkv[:, block * D : (block + 1) * D] = dot(token_rows[...], weight(block)).astype(LOW)

    def seg_slice(seg):
        return pl.ds(seg * seg_rows, seg_rows)

    def pair_lanes(pair):
        return [pl.ds(pl.multiple_of(part * D + pair * 128, 128), 128) for part in range(3)]

    def softmax(scores):
        raised = jnp.exp(scores - jnp.max(scores, axis=-1, keepdims=True))
        return raised / jnp.sum(raised, axis=-1, keepdims=True)

    @worker
    def heads_forward():
        @pl.loop(0, PAIRS)
        def _(pair):
            at_q, at_k, at_v = pair_lanes(pair)
            heads = [(seg, place) for seg in segs for place in range(2)]
            scores = [
                dot_right(qkv[seg_slice(seg), at_q] * head_masks[place], qkv[seg_slice(seg), at_k])
                * 0.125
                for seg, place in heads
            ]
            found = [softmax(score) for score in scores]
            for (seg, place), prob in zip(heads, found):
                probs[seg, pair, place] = prob
            mixed = [
                dot(prob.astype(LOW), qkv[seg_slice(seg), at_v])
                for (seg, place), prob in zip(heads, found)
            ]
            for seg in segs:
                context[seg_slice(seg), at_q] = jnp.where(
                    first_half, mixed[2 * seg], mixed[2 * seg + 1]
                ).astype(LOW)

    @worker
    def attention_close():
        summed[...] = dot_right(context[...], weight(3))
        gain, bias = vectors[0, 0:1], vectors[0, 1:2]

        def body(start, size):
            rows = pl.ds(start, size)
            out, normed, inv_dev = normalize(
                token_rows[rows].astype(F32) + summed[rows], gain, bias
            )
            norm0[rows] = normed
            dev0[rows] = jnp.broadcast_to(inv_dev, (size, 128))
            h1[rows] = out.astype(LOW)

        chunks(32, body)
        h1_slab[...] = lead_rows(h1, 4)
        lead_start(H1, h1_slab, h1_leads, 1)

    @worker
    def inner_block(block):
        summed[...] = dot(h1[...], weight(4 + block))

        def body(start, size):
            value, grade = gelu_pair(summed[pl.ds(start, size)])
            flat[pl.ds(block * rows_all + start, size)] = value.astype(LOW)
            flat[pl.ds((4 + block) * rows_all + start, size)] = grade.astype(LOW)

        chunks(32, body)

    @worker
    def second_block(place):
        block = lax.rem(2 * me + place, 4)
        product = dot(flat[act_rows(block)], weight(8 + block))
        if place == 0:
            branch[...] = product
        else:
            branch[...] += product

    @worker
    def mlp_close():
        gain, bias = vectors[1, 0:1], vectors[1, 1:2]

        def body(start, size):
            rows = pl.ds(start, size)
            out, normed, inv_dev = normalize(h1[rows].astype(F32) + branch[rows], gain, bias)
            norm1[rows] = normed
            dev1[rows] = jnp.broadcast_to(inv_dev, (size, 128))
            out_rows[rows] = out.astype(LOW)

        chunks(32, body)
        h2_slab[...] = lead_rows(out_rows, 4)
        lead_start(H2, h2_slab, h2_leads, 2)
        guest_copy(OUT).start()

    def add_small(row, value):
        small[row : row + 1] += value

    @worker
    def mlp_open_backward():
        gain = vectors[1, 0:1]

        def body(start, size):
            rows = pl.ds(start, size)
            place = start + lax.broadcasted_iota(jnp.int32, (size, D), 0)
            grad = jnp.where(lax.rem(place, seg_rows) == 0, 0.0, cot_rows[rows].astype(F32))
            grad_sum, grad_gain, grad_bias = normalize_backward(
                grad, norm1[rows], dev1[rows][:, 0:1], gain
            )
            branch[rows] = grad_sum
            kept[rows] = grad_sum.astype(LOW)
            add_small(2, grad_gain)
            add_small(3, grad_bias)

        chunks(32, body)

    def part(block):
        return block + 4 if block < 4 else block + 8

    def store_part(block, left, right):
        for strip in range(2):
            lanes = slice(strip * WIDTH, (strip + 1) * WIDTH)
            blocks[part(block), strip] = (
                outer(left[:, lanes], right).astype(LOW).reshape(2, 2, PIECE, D)
            )

    @worker
    def second_grad(block):
        store_part(8 + block, flat[act_rows(block)], kept[...])

    @worker
    def inner_grad(block):
        grad_act = dot_right(kept[...], weight(8 + block))
        grad_inner = (grad_act * flat[slope_rows(block)].astype(F32)).astype(LOW)
        flat[act_rows(block)] = grad_inner
        branch[...] += dot_right(flat[act_rows(block)], weight(4 + block))
        store_part(4 + block, h1[...], flat[act_rows(block)])

    @worker
    def attention_open_backward():
        gain = vectors[0, 0:1]
        leads = leads_of(lead_grad1, me) + leads_of(lead_grad1, me + 2)

        def body(start, size):
            rows = pl.ds(start, size)
            place = start + lax.broadcasted_iota(jnp.int32, (size, D), 0)
            grad = branch[rows]
            for lead in range(4):
                grad = jnp.where(place == lead * seg_rows, leads[lead], grad)
            grad = grad.astype(LOW).astype(F32)
            grad_sum, grad_gain, grad_bias = normalize_backward(
                grad, norm0[rows], dev0[rows][:, 0:1], gain
            )
            summed[rows] = grad_sum
            kept[rows] = grad_sum.astype(LOW)
            add_small(0, grad_gain)
            add_small(1, grad_bias)

        chunks(32, body)

    @worker
    def out_grad():
        store_part(3, kept[...], context[...])
        context[...] = dot(kept[...], weight(3)).astype(LOW)

    @worker
    def heads_backward():
        @pl.loop(0, PAIRS)
        def _(pair):
            at_q, at_k, at_v = pair_lanes(pair)
            heads = [(seg, place) for seg in segs for place in range(2)]
            grad_probs = [
                dot_right(
                    context[seg_slice(seg), at_q] * head_masks[place], qkv[seg_slice(seg), at_v]
                )
                for seg, place in heads
            ]
            grad_scores = []
            for (seg, place), grad_prob in zip(heads, grad_probs):
                prob = probs[seg, pair, place]
                inside = prob * grad_prob
                grad_score = inside - prob * jnp.sum(inside, axis=-1, keepdims=True)
                grad_scores.append(grad_score.astype(LOW))
            for seg in segs:
                rows = seg_slice(seg)
                query, key, grad = qkv[rows, at_q], qkv[rows, at_k], context[rows, at_q]
                mine = grad_scores[2 * seg : 2 * seg + 2]
                found = [probs[seg, pair, place].astype(LOW) for place in range(2)]
                for at, both, scale in (
                    (at_q, [dot(score, key) for score in mine], 0.125),
                    (at_k, [outer(score, query) for score in mine], 0.125),
                    (at_v, [outer(prob, grad) for prob in found], 1.0),
                ):
                    merged = jnp.where(first_half, both[0], both[1]) * scale
                    qkv[rows, at] = merged.astype(LOW)

    @worker
    def project_grad(block):
        store_part(block, token_rows[...], qkv[:, block * D : (block + 1) * D])

    @worker
    def tokens_back(block):
        summed[...] += dot_right(qkv[:, block * D : (block + 1) * D], weight(block))

    @worker
    def tokens_close():
        h1[...] = summed[...].astype(LOW)
        guest_copy(GRAD).start()

    def leads_mlp_forward(value, first, second, gain, bias):
        total_branch = value.astype(F32)
        for block in range(4):
            lanes = slice(block * D, (block + 1) * D)
            out, grade = gelu_pair(dot(value, first(block)))
            lead_act[:, lanes] = out.astype(LOW)
            lead_slope[:, lanes] = grade
            total_branch = total_branch + dot(lead_act[:, lanes], second(block))
        out, normed, inv_dev = normalize(total_branch, gain, bias)
        lead_norm[...] = normed
        lead_dev[...] = jnp.broadcast_to(inv_dev, (SLAB, 128))
        pack[:, 0:D] = value
        pack[:, LEFT_OUT:RIGHT] = value
        return out

    def leads_mlp_backward(grad, first, second, gain):
        grad_sum, grad_gain, grad_bias = normalize_backward(
            grad, lead_norm[...], lead_dev[:, 0:1], gain
        )
        add_small(4, grad_gain)
        add_small(5, grad_bias)
        low_sum = grad_sum.astype(LOW)
        result = grad_sum
        for block in range(4):
            lanes = slice(block * D, (block + 1) * D)
            grad_inner = (dot_right(low_sum, second(block)) * lead_slope[:, lanes]).astype(LOW)
            pack[:, RIGHT + block * D : RIGHT + (block + 1) * D] = grad_inner
            result = result + dot_right(grad_inner, first(block))
        pack[:, LEFT_HALF:RIGHT_HALF] = lead_act[:, 2 * D :]
        pack[:, RIGHT_HALF:] = low_sum
        handed[:, 0 : 2 * D] = lead_act[:, 0 : 2 * D]
        handed[:, 2 * D :] = low_sum
        return result

    def own_weight(place):
        return flat[flat_rows(place)]

    def last_second(block):
        if block >= 2:
            return own_weight(2 + block)
        return core_in[2 * block : 2 * block + 2].reshape(D, D)

    def leads_first():
        @pl.when(me == 2)
        def _():
            lead_wait(H2, h2_slab, h2_leads, 2, 2)
            for place in range(4):
                load_own(place).wait()
            value = collected(h2_leads, 2).astype(LOW)
            pack[:, 0:D] = value
            for block in range(3):
                lead_qkv[:, block * D : (block + 1) * D] = dot(value, own_weight(block)).astype(LOW)
            docs = seg_doc[...]
            row, column = (lax.broadcasted_iota(jnp.int32, (SLAB, SLAB), i) for i in range(2))
            sort = jnp.where(row == column, 2.0, 0.0)
            for micro in range(seg_doc.shape[0]):
                pair_sort = jnp.where(
                    docs[micro : micro + 1, 0:1] == docs[micro : micro + 1, 1:2], 2.0, 1.0
                )
                near = (row // 2 == micro) & (column // 2 == micro) & (row != column)
                sort = jnp.where(near, pair_sort, sort)
            for pair in range(PAIRS):
                at = [slice(p * D + pair * 128, p * D + (pair + 1) * 128) for p in range(3)]
                query, key, val = (lead_qkv[:, lanes] for lanes in at)
                parts = []
                for place in range(2):
                    scores = dot_right(query * head_masks[place], key) * 0.125
                    scores = jnp.where(
                        sort > 1.5, scores, jnp.where(sort > 0.5, -1000000000.0, -1e30)
                    )
                    raised = jnp.exp(scores - jnp.max(scores, axis=-1, keepdims=True))
                    prob = raised / jnp.sum(raised, axis=-1, keepdims=True)
                    lead_probs[pair, place] = prob
                    parts.append(dot(prob.astype(LOW), val))
                lead_context[:, pair * 128 : (pair + 1) * 128] = jnp.where(
                    first_half, parts[0], parts[1]
                ).astype(LOW)
            summed_rows = value.astype(F32) + dot_right(lead_context[...], own_weight(3))
            out, normed, inv_dev = normalize(summed_rows, vectors[2, 0:1], vectors[2, 1:2])
            lead_norm[...] = normed
            lead_dev[...] = jnp.broadcast_to(inv_dev, (SLAB, 128))
            lead_third[...] = out.astype(LOW)
            hop_copy(THIRD, lead_third, 1).start()

        @pl.when(me == 1)
        def _():
            lead_wait(H1, h1_slab, h1_leads, 1, 2)
            leads_mlp_forward(
                collected(h1_leads, 2).astype(LOW),
                lambda block: weight(4 + block),
                lambda block: weight(8 + block),
                vectors[1, 0:1],
                vectors[1, 1:2],
            )

    def leads_second():
        @pl.when(me == 3)
        def _():
            hop_copy(THIRD, lead_third, -1).wait_recv()
            for place in range(6):
                load_own(place).wait()
            out = leads_mlp_forward(
                lead_third[...], own_weight, last_second, vectors[3, 0:1], vectors[3, 1:2]
            )
            lead_fourth[...] = out.astype(LOW)
            for step in range(1, sections):
                spread_copy(FOURTH, lead_fourth, step).start()
            lead_wait(COT, cot_slab, cot_leads, 3, sections)
            grad = leads_mlp_backward(
                collected(cot_leads, sections), own_weight, last_second, vectors[3, 0:1]
            )
            lead_grad3[...] = grad.astype(LOW)
            hop_copy(GRAD3, lead_grad3, -1).start()
            hop_copy(HAND, handed, -1).start()

    def leads_third():
        @pl.when(me == 2)
        def _():
            hop_copy(GRAD3, lead_grad3, 1).wait_recv()
            grad_sum, grad_gain, grad_bias = normalize_backward(
                lead_grad3[...].astype(F32), lead_norm[...], lead_dev[:, 0:1], vectors[2, 0:1]
            )
            add_small(4, grad_gain)
            add_small(5, grad_bias)
            low_sum = grad_sum.astype(LOW)
            pack[:, LEFT_OUT:RIGHT] = low_sum
            pack[:, RIGHT + 3 * D : LEFT_HALF] = lead_context[...]
            grad_context = dot(low_sum, own_weight(3)).astype(LOW)
            for pair in range(PAIRS):
                at = [slice(p * D + pair * 128, p * D + (pair + 1) * 128) for p in range(3)]
                query, key, val = (lead_qkv[:, lanes] for lanes in at)
                grad = grad_context[:, pair * 128 : (pair + 1) * 128]
                grads = ([], [], [])
                for place in range(2):
                    prob = lead_probs[pair, place]
                    grad_prob = dot_right(grad * head_masks[place], val)
                    inside = prob * grad_prob
                    grad_score = inside - prob * jnp.sum(inside, axis=-1, keepdims=True)
                    grad_score = grad_score.astype(LOW)
                    grads[0].append(dot(grad_score, key))
                    grads[1].append(outer(grad_score, query))
                    grads[2].append(outer(prob.astype(LOW), grad))
                for lanes, pair_grads, scale in zip(at, grads, (0.125, 0.125, 1.0)):
                    merged = jnp.where(first_half, pair_grads[0], pair_grads[1]) * scale
                    pack[:, RIGHT + lanes.start : RIGHT + lanes.stop] = merged.astype(LOW)
            result = grad_sum
            for block in range(3):
                result = result + dot_right(
                    pack[:, RIGHT + block * D : RIGHT + (block + 1) * D], own_weight(block)
                )
            lead_grad2[...] = result.astype(LOW)
            hop_copy(GRAD2, lead_grad2, -1).start()
            hop_copy(HAND, handed, 1).wait_recv()
            pack[:, LEFT_HALF:] = handed[...]

    def leads_fourth():
        @pl.when(me == 1)
        def _():
            hop_copy(GRAD2, lead_grad2, 1).wait_recv()
            grad = leads_mlp_backward(
                lead_grad2[...].astype(F32),
                lambda block: weight(4 + block),
                lambda block: weight(8 + block),
                vectors[1, 0:1],
            )
            lead_grad1[...] = grad.astype(LOW)
            hop_copy(GRAD1, lead_grad1, -1).start()
            hop_copy(HAND, handed, -1).start()

    half_lanes = pl.ds(pl.multiple_of(core * HALF_PACK, 128), HALF_PACK)
    other_lanes = pl.ds(pl.multiple_of((1 - core) * HALF_PACK, 128), HALF_PACK)
    first_peer = {"dp": group * CUBE + (y + core - 2 * y * core) * 4
                  + (x + (1 - core) * (1 - 2 * x)) * 2 + core}
    second_peer = {"dp": group * CUBE + (y + (1 - core) * (1 - 2 * y)) * 4
                   + (x + core - 2 * x * core) * 2 + core}

    def pack_copy(stage):
        chip = y * 2 + x
        first_chip = (y + core - 2 * y * core) * 2 + x + (1 - core) * (1 - 2 * x)
        if stage == 0:
            source, target, peer = pack.at[:, other_lanes], pack_in, beside_core
        elif stage == 1:
            source = target = factors.at[chip, :, half_lanes]
            peer = first_peer
        elif stage == 2:
            source = target = factors.at[chip, :, half_lanes]
            peer = second_peer
        elif stage == 3:
            source = target = factors.at[first_chip, :, half_lanes]
            peer = second_peer
        else:
            source = target = factors.at[:, :, half_lanes]
            peer = beside_core
        return remote(source, target, pack_send.at[stage], pack_recv.at[stage], peer)

    def pack_join():
        pack_copy(0).wait()

        @pl.loop(0, HALF_PACK // WIDTH)
        def _(step):
            start = pl.multiple_of(step * WIDTH, 128)
            lanes = pl.ds(pl.multiple_of(core * HALF_PACK + start, 128), WIDTH)
            mine = pack[:, lanes].astype(F32)[0:8]
            theirs = pack_in[:, pl.ds(start, WIDTH)].astype(F32)[0:8]
            low_rows = jnp.where(core == 0, mine, theirs)
            high_rows = jnp.where(core == 0, theirs, mine)
            factors[y * 2 + x, :, lanes] = jnp.concatenate([low_rows, high_rows]).astype(LOW)

        pack_copy(1).start()

    def pack_second():
        pack_copy(1).wait()
        pack_copy(2).start()
        pack_copy(3).start()

    def pack_third():
        pack_copy(2).wait()
        pack_copy(3).wait()
        pack_copy(4).start()

    def to_packs(step):
        return remote(
            factors, packs.at[group], group_pack_send.at[step], group_pack_recv.at[step],
            {"dp": lax.rem(index + step * CUBE, replicas)},
        )

    def own_pack():
        return pltpu.make_async_copy(factors, packs.at[group], group_pack_send.at[0])

    def pack_fourth():
        pack_copy(4).wait()
        own_pack().start()
        for step in range(1, groups):
            to_packs(step).start()

    def pack_last():
        own_pack().wait()
        for step in range(1, groups):
            to_packs(step).wait()

    def rows_store(place):
        source, target = ((out_rows, layer_out), (h1, grad_tokens))[place]
        return pltpu.make_async_copy(source.at[own_part], target, rows_out.at[place])

    def leads_close():
        @pl.when(me != 3)
        def _():
            spread_copy(FOURTH, lead_fourth, 1).wait_recv()

        @pl.when(me >= 2)
        def _():
            guest_copy(OUT).wait_recv()

        leads = leads_of(lead_fourth, me)
        for lead in range(2):
            rows = pl.ds(lead * seg_rows, SLAB)
            out_rows[rows] = jnp.where(
                row_of == 0, leads[lead], out_rows[rows].astype(F32)
            ).astype(LOW)
        rows_store(0).start()

        @pl.when(me == 0)
        def _():
            hop_copy(GRAD1, lead_grad1, 1).wait_recv()
            hop_copy(HAND, handed, 1).wait_recv()
            pack[:, 0:LEFT_HALF] = jnp.zeros((SLAB, LEFT_HALF), LOW)
            pack[:, LEFT_HALF:] = handed[...]

        pack_copy(0).start()

    def add(target, *sources):
        value = target[...].astype(F32)
        for source in sources:
            value = value + source[...].astype(F32)
        target[...] = value.astype(LOW)

    def landing(block):
        return blocks.at[8 + block, 0] if block < 4 else core_in.at[block - 4]

    def scatter(turn, stage):
        block, lanes = turn // 2, lanes_of(turn)
        run = blocks.at[part(block)]
        source, target, peer = (
            (run.at[:, :, 1 - core, :, lanes], landing(block).at[:, :, :, lanes], beside_core),
            (run.at[:, 1 - x, core, upper, lanes], one_a.at[block, :, :, lanes], beside_x),
            (run.at[1 - y, :, core, lower, lanes], one_b.at[block, :, :, lanes], beside_y),
            (run.at[1 - y, x, core, upper, lanes], two_a.at[block, :, lanes], beside_y),
            (run.at[y, 1 - x, core, lower, lanes], two_b.at[block, :, lanes], beside_x),
        )[stage]
        return remote(source, target, rs_send.at[turn, stage], rs_recv.at[turn, stage], peer)

    def to_line(turn):
        return remote(
            blocks.at[part(turn // 2), y, x, core, :, lanes_of(turn)],
            line_in.at[turn // 2, :, lanes_of(turn)],
            z_send.at[turn],
            z_recv.at[turn],
            {"section": HOLDER[turn // 2]},
        )

    def to_holder(turn):
        place = EARLY.index(turn // 2)
        return remote(
            blocks.at[part(turn // 2), :, :, core, :, lanes_of(turn)],
            early_in.at[place, :, :, :, lanes_of(turn)],
            z_send.at[turn],
            z_recv.at[turn],
            {"section": HOLDER[turn // 2]},
        )

    def to_group(turn, step):
        return remote(
            blocks.at[part(turn // 2), y, x, core, :, lanes_of(turn)],
            group_in.at[turn // 2, step - 1, :, lanes_of(turn)],
            group_send.at[turn, step - 1],
            group_recv.at[turn, step - 1],
            {"dp": lax.rem(index + step * CUBE, replicas)},
        )

    def gather_back(turn, stage):
        place = 2 * OWN[HOLDER[turn // 2]].index(turn // 2) + turn % 2
        run, lanes = blocks.at[part(turn // 2)], lanes_of(turn)
        ref, peer = (
            (run.at[y, x, core, upper, lanes], beside_y),
            (run.at[y, x, core, lower, lanes], beside_x),
            (run.at[:, x, core, upper, lanes], beside_x),
            (run.at[y, :, core, lower, lanes], beside_y),
            (run.at[:, :, core, :, lanes], beside_core),
        )[stage]
        return remote(ref, ref, ag_send.at[place, stage], ag_recv.at[place, stage], peer)

    def write_out(block):
        place = OWN[HOLDER[block]].index(block)
        return pltpu.make_async_copy(
            blocks.at[part(block)], total.at[place], out_sem.at[place]
        )

    @worker
    def reduce_core(block):
        scatter(2 * block, 0).start()
        scatter(2 * block + 1, 0).start()

    def is_early(turn):
        return turn // 2 in EARLY

    def in_plane(turn):
        return me == HOLDER[turn // 2] if is_early(turn) else works

    def add_four(turn, source):
        for yy in range(2):
            for xx in range(2):
                add(
                    blocks.at[part(turn // 2), yy, xx, core, :, lanes_of(turn)],
                    source.at[yy, xx, :, lanes_of(turn)],
                )

    def reduce_one(turn):
        @pl.when(works)
        def _():
            scatter(turn, 0).wait()
            add_four(turn, landing(turn // 2))
            if not is_early(turn):
                scatter(turn, 1).start()
                scatter(turn, 2).start()

        if is_early(turn):

            @pl.when(me == 1 - HOLDER[turn // 2])
            def _():
                to_holder(turn).start()

    def reduce_early(turn):
        @pl.when(me == HOLDER[turn // 2])
        def _():
            to_holder(turn).wait_recv()
            add_four(turn, early_in.at[EARLY.index(turn // 2)])
            scatter(turn, 1).start()
            scatter(turn, 2).start()

    def reduce_two(turn):
        @pl.when(in_plane(turn))
        def _():
            reduce_two_now(turn)

    def reduce_two_now(turn):
        block, lanes = turn // 2, lanes_of(turn)
        run = blocks.at[part(block)]
        scatter(turn, 1).wait()
        for yy in range(2):
            add(run.at[yy, x, core, upper, lanes], one_a.at[block, yy, :, lanes])
        scatter(turn, 3).start()
        scatter(turn, 2).wait()
        for xx in range(2):
            add(run.at[y, xx, core, lower, lanes], one_b.at[block, xx, :, lanes])
        scatter(turn, 4).start()

    def reduce_three(turn):
        @pl.when(in_plane(turn))
        def _():
            reduce_three_now(turn)

        if not is_early(turn):

            @pl.when(me == 1 - HOLDER[turn // 2])
            def _():
                to_line(turn).start()

        else:

            @pl.when(me == HOLDER[turn // 2])
            def _():
                spread_one(turn)

    def reduce_three_now(turn):
        block, lanes = turn // 2, lanes_of(turn)
        run = blocks.at[part(block)]
        scatter(turn, 3).wait()
        add(run.at[y, x, core, upper, lanes], two_a.at[block, :, lanes])
        scatter(turn, 4).wait()
        add(run.at[y, x, core, lower, lanes], two_b.at[block, :, lanes])
        if groups > 1:
            for step in range(1, groups):
                to_group(turn, step).start()
            for step in range(1, groups):
                to_group(turn, step).wait()
            for step in range(1, groups):
                copy = pltpu.make_async_copy(
                    group_in.at[block, step - 1, :, lanes], group_piece, group_load
                )
                copy.start()
                copy.wait()
                add(run.at[y, x, core, :, lanes], group_piece)

    def spread_one(turn):
        gather_back(turn, 0).start()
        gather_back(turn, 1).start()

    def reduce_line(turn):
        @pl.when(me == HOLDER[turn // 2])
        def _():
            block, lanes = turn // 2, lanes_of(turn)
            to_line(turn).wait_recv()
            add(blocks.at[part(block), y, x, core, :, lanes], line_in.at[block, :, lanes])
            spread_one(turn)

    def spread_two(turn):
        @pl.when(me == HOLDER[turn // 2])
        def _():
            gather_back(turn, 0).wait()
            gather_back(turn, 2).start()
            gather_back(turn, 1).wait()
            gather_back(turn, 3).start()

    def spread_core(turn):
        @pl.when(me == HOLDER[turn // 2])
        def _():
            gather_back(turn, 2).wait()
            gather_back(turn, 3).wait()
            gather_back(turn, 4).start()

    def spread_done(turn):
        @pl.when(me == HOLDER[turn // 2])
        def _():
            gather_back(turn, 4).wait()
            if turn % 2 == 1:
                write_out(turn // 2).start()

        @pl.when(me == 1 - HOLDER[turn // 2])
        def _():
            (to_holder if is_early(turn) else to_line)(turn).wait_send()

    tail_plan = ((spread_done, 13), (spread_core, 11), (spread_two, 9))
    late_plan = tail_plan + (
        (reduce_three, 5), (reduce_line, 7), (reduce_two, 3), (reduce_one, 1)
    )
    early_plan = tail_plan + (
        (reduce_three, 7), (reduce_two, 5), (reduce_early, 3), (reduce_one, 1)
    )

    class Wave:
        def __init__(self, order):
            self.order, self.at = turns(*order), 0

        def tick(self, count=1):
            for _ in range(count):
                for stage, offset in late_plan:
                    if 0 <= self.at - offset < len(self.order):
                        stage(self.order[self.at - offset])
                self.at += 1

        def left(self):
            return self.at < len(self.order) + tail_plan[0][1]

    one, two = Wave((8, 9, 10, 11, 4, 5, 6, 7)), Wave((3, 0, 1, 2))

    small[...] = jnp.zeros_like(small)

    gather_wait_own()
    gather_send()

    @pl.when(me >= 2)
    def _():
        guest_copy(TOKENS).wait_send()
        guest_copy(COTANGENT).start()

    for tick in range(gather_ticks):
        gather_tick(tick)
        at = tick - gather_plan[0][1]
        if at == 0:
            for step in range(1, sections):
                vector_copy(step).wait()
        if at < 0:
            continue
        if at == 1:

            @pl.when(works)
            def _():
                guest_copy(TOKENS).wait_recv()

        if at % 2 == 1 and at < 6:
            project(at // 2)
        if at == 6:
            heads_forward()
        if at == 7:
            attention_close()
        if at >= 8:
            inner_block(at - 8)
    for place in range(4):
        second_block(place)
    mlp_close()

    @pl.when(works)
    def _():
        guest_copy(COTANGENT).wait_recv()

    mlp_open_backward()
    for reader, wanted in WANTED.items():
        for turn in turns(*wanted):
            gather_finish(turn, reader)

    for block in range(4):
        second_grad(block)
        reduce_core(8 + block)
        one.tick(2)
        if block == 1:
            leads_first()
    for block in range(4):
        inner_grad(block)
        reduce_core(4 + block)
        one.tick(2)
        if block == 0:
            leads_second()
        if block == 2:
            leads_third()
    leads_fourth()

    @pl.when(works)
    def _():
        pl.semaphore_signal(credit, inc=1, device_id=beside_core, device_id_type=MESH)

    one.tick(2)
    leads_close()
    attention_open_backward()
    out_grad()
    pack_join()

    @pl.when(works)
    def _():
        pl.semaphore_wait(credit, 1)

    reduce_core(3)
    one.tick(2)
    two.tick()
    heads_backward()
    pack_second()
    for block in range(3):
        project_grad(block)
        reduce_core(block)
        one.tick(2)
        two.tick(2)

    def small_copy(step):
        return remote(
            small, small_all.at[index], small_send.at[step], small_recv.at[step], replica(step)
        )

    def sum_copy(step):
        return remote(
            small_sum, smalls.at[me], sum_send.at[step], sum_recv.at[step], others[step - 1]
        )

    def own_sum():
        return pltpu.make_async_copy(small_sum, smalls.at[me], sum_send.at[0])

    @pl.loop(1, replicas)
    def _(step):
        small_copy(step).start()

    small_all[index] = small[...]
    for block in range(3):
        tokens_back(block)
        one.tick()
        two.tick()
    tokens_close()
    pack_third()

    @pl.loop(1, replicas)
    def _(step):
        small_copy(step).wait()

    small_sum[...] = jnp.sum(small_all[...], axis=0)
    for place in range(1, sections):
        sum_copy(place).start()
    own_sum().start()
    pack_fourth()
    while one.left() or two.left():
        if one.left():
            one.tick()
        if two.left():
            two.tick()

    for place in range(1, sections):
        sum_copy(place).wait()
    own_sum().wait()
    pack_last()

    for holder in (0, 1):

        @pl.when(me == holder)
        def _():
            for block in OWN[holder]:
                write_out(block).wait()

    @pl.when(me != 3)
    def _():
        lead_copy(COT, cot_slab, cot_leads, 3).wait_send()

    @pl.when(me == 0)
    def _():
        lead_copy(H1, h1_slab, h1_leads, 1).wait_send()

    @pl.when(works)
    def _():
        lead_copy(H2, h2_slab, h2_leads, 2).wait_send()
        guest_copy(OUT).wait_send()
        guest_copy(GRAD).wait_send()

    @pl.when(me >= 2)
    def _():
        guest_copy(COTANGENT).wait_send()
        guest_copy(GRAD).wait_recv()

    rows_store(1).start()
    rows_store(1).wait()
    rows_store(0).wait()

    @pl.when(me == 1)
    def _():
        hop_copy(GRAD1, lead_grad1, -1).wait_send()
        hop_copy(HAND, handed, -1).wait_send()

    @pl.when(me == 2)
    def _():
        hop_copy(THIRD, lead_third, 1).wait_send()
        hop_copy(GRAD2, lead_grad2, -1).wait_send()

    @pl.when(me == 3)
    def _():
        for place in range(1, sections):
            spread_copy(FOURTH, lead_fourth, place).wait_send()
        hop_copy(GRAD3, lead_grad3, -1).wait_send()
        hop_copy(HAND, handed, -1).wait_send()


def run_layers(sections, replicas, tokens, cotangent, seg_doc, gain, bias, wide, half):
    groups = replicas // CUBE
    rows = 2 * tokens.shape[0]
    seg_rows = tokens.shape[0] // 2
    vector = (8, D)
    block = (2, 2, 2, PIECE, D)
    reduced_groups = max(groups - 1, 1)
    in_vmem = pl.BlockSpec(memory_space=pltpu.VMEM)
    anywhere = pl.BlockSpec(memory_space=pl.ANY)
    slab = pltpu.VMEM((SLAB, D), LOW)
    leads = pltpu.VMEM((sections, SLAB, D), LOW)
    low_rows = pltpu.VMEM((rows, D), LOW)
    full_rows = pltpu.VMEM((rows, D), F32)
    return pl.pallas_call(
        partial(layer_kernel, sections, replicas),
        out_shape=(
            jax.ShapeDtypeStruct(tokens.shape, LOW),
            jax.ShapeDtypeStruct(tokens.shape, LOW),
            jax.ShapeDtypeStruct((OWNED,) + block, LOW),
            jax.ShapeDtypeStruct((groups, CUBE // 2, SLAB, PACK), LOW),
            jax.ShapeDtypeStruct((sections,) + vector, F32),
            jax.ShapeDtypeStruct(
                (REDUCED if groups > 1 else 1, reduced_groups, PIECE, D), LOW
            ),
        ),
        in_specs=[anywhere] * 2 + [in_vmem] * 3 + [anywhere] * 4,
        out_specs=[anywhere] * 6,
        scratch_shapes=[
            pltpu.VMEM((REDUCED + 8,) + block, LOW),
            pltpu.VMEM((max(8 * rows, 6 * D), D), LOW),
            pltpu.VMEM((8, 2, 2, PIECE, D), LOW),
            pltpu.VMEM((REDUCED, 2, HALF, D), LOW),
            pltpu.VMEM((REDUCED, 2, HALF, D), LOW),
            pltpu.VMEM((REDUCED, HALF, D), LOW),
            pltpu.VMEM((REDUCED, HALF, D), LOW),
            pltpu.VMEM((REDUCED, PIECE, D), LOW),
            pltpu.VMEM((max(len(EARLY), 1), 2, 2, PIECE, D), LOW),
            pltpu.VMEM((sections,) + vector, F32),
            low_rows, low_rows, low_rows,
            pltpu.VMEM((rows, 3 * D), LOW),
            pltpu.VMEM((4, PAIRS, 2, seg_rows, seg_rows), F32),
            low_rows, low_rows, full_rows,
            pltpu.VMEM((rows, 128), F32),
            full_rows, full_rows,
            pltpu.VMEM((rows, 128), F32),
            full_rows, low_rows,
            slab, slab, slab, leads, leads, leads,
            slab, slab, slab, slab, slab,
            pltpu.VMEM((SLAB, 3 * D), LOW),
            pltpu.VMEM((SLAB, 3 * D), LOW),
            pltpu.VMEM((PAIRS, 2, SLAB, SLAB), F32),
            slab,
            pltpu.VMEM((SLAB, D), F32),
            pltpu.VMEM((SLAB, 128), F32),
            pltpu.VMEM((SLAB, 4 * D), LOW),
            pltpu.VMEM((SLAB, 4 * D), F32),
            pltpu.VMEM((SLAB, PACK), LOW),
            pltpu.VMEM((SLAB, HALF_PACK), LOW),
            pltpu.VMEM((CUBE // 2, SLAB, PACK), LOW),
            pltpu.VMEM(vector, F32),
            pltpu.VMEM((replicas,) + vector, F32),
            pltpu.VMEM(vector, F32),
            pltpu.VMEM((PIECE, WIDTH), LOW),
            DMA((2,)),
            DMA((4,)),
            DMA((4,)),
            DMA((2,)),
            DMA((ROUNDS,)),
            DMA((ROUNDS,)),
            DMA((ROUNDS, 5)),
            DMA((ROUNDS, 5)),
            DMA((GATHERED,)),
            DMA((2 * REDUCED, 5)),
            DMA((2 * REDUCED, 5)),
            DMA((2 * REDUCED,)),
            DMA((2 * REDUCED,)),
            DMA((2 * REDUCED, reduced_groups)),
            DMA((2 * REDUCED, reduced_groups)),
            DMA,
            DMA((2 * OWNED, 5)),
            DMA((2 * OWNED, 5)),
            DMA((OWNED,)),
            DMA((5,)),
            DMA((5,)),
            DMA((groups,)),
            DMA((groups,)),
            DMA((replicas,)),
            DMA((replicas,)),
            DMA((sections,)),
            DMA((sections,)),
            DMA((sections,)),
            DMA((sections,)),
            DMA((3,)),
            DMA((3, sections)),
            DMA((1, sections)),
            DMA((1,)),
            DMA((5,)),
            DMA((5,)),
            pltpu.SemaphoreType.REGULAR,
        ],
        compiler_params=pltpu.CompilerParams(
            collective_id=0, has_side_effects=True, vmem_limit_bytes=VMEM_BYTES
        ),
    )(
        tokens, cotangent, seg_doc, gain, bias,
        wide.reshape(2, 2, 2, PIECE, 4 * D), half.reshape(2, 2, 2, 2, PIECE, D), wide, half,
    )


VMEM_BYTES = 62 * 1024 * 1024


def close_kernel(
    total, packs, smalls, rows_in, grads_in,
    wide_out, half_out, gain_out, bias_out, rows_out, grads_out,
):
    me = lax.axis_index("section")
    step = pl.program_id(0)
    near = me < 2
    packed = packs.reshape(-1, PACK)
    summed = jnp.where(near, total[0, 0].reshape(WIDTH, D).astype(F32), 0.0)

    def wide_step(block, side):
        @pl.when(step == 2 * block + side)
        def _():
            first = (0 if block < 3 else LEFT_OUT) + side * WIDTH
            left = packed[:, first : first + WIDTH]
            right = packed[:, RIGHT + block * D : RIGHT + (block + 1) * D]
            wide_out[0] = summed + outer(left, right)

    def half_step(side):
        @pl.when(step == 8 + side)
        def _():
            first = LEFT_HALF + side * WIDTH
            half_out[0] = summed + outer(packed[:, first : first + WIDTH], packed[:, RIGHT_HALF:])

    for block in range(4):
        for side in range(2):
            wide_step(block, side)
    for side in range(4):
        half_step(side)

    @pl.when(step == 0)
    def _():
        every = jnp.sum(smalls[...], axis=0)
        mine = smalls[me]
        for row, out in ((0, gain_out), (1, bias_out)):
            value = jnp.where(me == 0, every[row : row + 1], every[2 + row : 3 + row])
            value = jnp.where(near, value, 0.0) + mine[4 + row : 5 + row]
            out[...] = value
        rows_out[...] = rows_in[...]
        grads_out[...] = grads_in[...]


def close(total, packs, smalls, rows, grads):
    def whole(shape):
        return pl.BlockSpec(shape, lambda step: (0,) * len(shape))

    return pl.pallas_call(
        close_kernel,
        grid=(2 * OWNED,),
        out_shape=(
            jax.ShapeDtypeStruct((1, D, 4 * D), F32),
            jax.ShapeDtypeStruct((1, 2 * D, D), F32),
            jax.ShapeDtypeStruct((1, D), F32),
            jax.ShapeDtypeStruct((1, D), F32),
            jax.ShapeDtypeStruct(rows.shape, LOW),
            jax.ShapeDtypeStruct(rows.shape, LOW),
        ),
        in_specs=[
            pl.BlockSpec(
                (1, 1) + total.shape[2:], lambda step: (step // 2, lax.rem(step, 2), 0, 0, 0, 0)
            ),
            whole(packs.shape),
            whole(smalls.shape),
            whole(rows.shape),
            whole(rows.shape),
        ],
        out_specs=[
            pl.BlockSpec(
                (1, WIDTH, D),
                lambda step: (
                    0,
                    jnp.where(step < 8, lax.rem(step, 2), 1),
                    jnp.minimum(step // 2, 3),
                ),
            ),
            pl.BlockSpec((1, WIDTH, D), lambda step: (0, jnp.maximum(step - 8, 0), 0)),
            whole((1, D)),
            whole((1, D)),
            whole(rows.shape),
            whole(rows.shape),
        ],
        compiler_params=pltpu.CompilerParams(vmem_limit_bytes=VMEM_BYTES),
    )(total, packs, smalls, rows, grads)


def on_device(tokens, cotangent, seg_doc, wide_in, half_out, norm_gain, norm_bias):
    sections = lax.axis_size("section")
    replicas = lax.axis_size("dp")
    rows, grads, total, packs, smalls, _ = run_layers(
        sections, replicas, tokens, cotangent, seg_doc, norm_gain, norm_bias, wide_in[0], half_out[0]
    )
    wide_grad, half_grad, gain_grad, bias_grad, layer_out, tokens_grad = close(
        total, packs, smalls, rows, grads
    )
    return layer_out, tokens_grad, wide_grad, half_grad, gain_grad, bias_grad


def solution(mesh):
    placed = (
        P(("dp", "section"), None),
        P(("dp", "section"), None),
        P("dp", None),
        P("section", None, None),
        P("section", None, None),
        P("section", None),
        P("section", None),
    )
    return jax.shard_map(
        on_device,
        mesh=mesh,
        in_specs=placed,
        out_specs=(
            P(("dp", "section"), None),
            P(("dp", "section"), None),
            P("section", None, None),
            P("section", None, None),
            P("section", None),
            P("section", None),
        ),
        check_vma=False,
    )
```

```python
from functools import partial

import jax
import jax.numpy as jnp
from jax import lax
from jax.experimental import pallas as pl
from jax.experimental.pallas import tpu as pltpu
from jax.sharding import PartitionSpec as P

D = 768
HEADS = 12
PAIRS = HEADS // 2
CUBE = 8
PIECE = D // CUBE
HALF = PIECE // 2
WIDTH = D // 2
SLAB = 16
HOLDER = (0, 0, 0, 0, 1, 1, 1, 1, 0, 0, 1, 1, 2, 2)
GATHERED = len(HOLDER)
ROUNDS = 2 * GATHERED
WANTED = {0: (4, 5, 6, 7, 10, 11), 1: (0, 1, 2, 3, 8, 9), 3: (12, 13)}
WAVES = ((8, 9, 10, 11, 4, 5, 6, 7), (3, 0, 1, 2))
SLOT = {
    2 * block + side: (2 * place + side) % 4
    for wanted in WANTED.values()
    for place, block in enumerate(wanted)
    for side in range(2)
}
SUM_SLOT = {
    2 * block + side: 4 * wave + (2 * place + side) % 4
    for wave, order in enumerate(WAVES)
    for place, block in enumerate(order)
    for side in range(2)
}
EARLY = ()
REDUCED = 12
OWN = {0: (0, 1, 2, 3, 8, 9), 1: (4, 5, 6, 7, 10, 11)}
OWNED = len(OWN[0])
LEFT_OUT, RIGHT, LEFT_HALF, RIGHT_HALF, PACK = D, 2 * D, 6 * D, 8 * D, 9 * D
HALF_PACK = PACK // 2
LOW = jnp.bfloat16
F32 = jnp.float32
DMA = pltpu.SemaphoreType.DMA
MESH = pl.DeviceIdType.MESH


def dot(left, right):
    return jnp.dot(left, right, preferred_element_type=F32)


def dot_right(left, right):
    return lax.dot_general(left, right, (((1,), (1,)), ((), ())), preferred_element_type=F32)


def outer(left, right):
    return lax.dot_general(left, right, (((0,), (0,)), ((), ())), preferred_element_type=F32)


def normalize(summed, gain, bias):
    average = jnp.mean(summed, axis=-1, keepdims=True)
    centred = summed - average
    inv_dev = lax.rsqrt(jnp.mean(centred * centred, axis=-1, keepdims=True) + 1e-05)
    normed = centred * inv_dev
    return normed * gain + bias, normed, inv_dev


def normalize_backward(grad, normed, inv_dev, gain):
    scaled = grad * gain
    mean_scaled = jnp.mean(scaled, axis=-1, keepdims=True)
    mean_normed = jnp.mean(scaled * normed, axis=-1, keepdims=True)
    grad_sum = inv_dev * (scaled - mean_scaled - normed * mean_normed)
    return (
        grad_sum,
        jnp.sum(grad * normed, axis=0, keepdims=True),
        jnp.sum(grad, axis=0, keepdims=True),
    )


def gelu_pair(value):
    bell = jnp.exp(-0.5 * value * value)
    base = 1.0 + (0.3275911 * 0.7071067811865476) * jnp.abs(value)
    guess = pl.reciprocal(base, approx=True)
    t = guess * (2.0 - base * guess)
    poly = t * (
        0.5 * 0.254829592
        + t
        * (
            0.5 * -0.284496736
            + t * (0.5 * 1.421413741 + t * (0.5 * -1.453152027 + t * (0.5 * 1.061405429)))
        )
    )
    tail = poly * bell
    below = jnp.where(value >= 0, 1.0 - tail, tail)
    return value * below, below + value * bell * 0.3989422804014327


def position():
    index = lax.axis_index("dp")
    return (lax.rem(index // 4, 2), lax.rem(index // 2, 2), lax.rem(index, 2), index // CUBE)


def remote(source, target, send, receive, device):
    return pltpu.make_async_remote_copy(
        src_ref=source,
        dst_ref=target,
        send_sem=send,
        recv_sem=receive,
        device_id=device,
        device_id_type=MESH,
    )


def layer_kernel(
    sections, replicas,
    tokens, cotangent, seg_doc, norm_gain, norm_bias, wide, half, wide_flat, half_flat,
    layer_out, grad_tokens, total, packs, smalls, group_in,
    blocks, flat, core_in, one_a, one_b, two_a, two_b, line_in, early_in, vectors,
    token_rows, cot_rows, out_rows,
    qkv, probs, context, h1, norm0, dev0, summed, norm1, dev1, branch, kept,
    cot_slab, h1_slab, h2_slab, cot_leads, h1_leads, h2_leads,
    lead_third, lead_fourth, lead_grad3, lead_grad2, lead_grad1, handed,
    lead_qkv, lead_probs, lead_context, lead_norm, lead_dev, lead_act, lead_slope,
    pack, pack_in, factors, small, small_all, small_sum, group_piece,
    rows_load, guest_send, guest_recv, rows_out,
    line_send, line_recv, cube_send, cube_recv, load_sem,
    core_send, core_recv, rs_send, rs_recv, z_send, z_recv, group_send, group_recv, group_load, ag_send, ag_recv,
    out_sem, pack_send, pack_recv, group_pack_send, group_pack_recv,
    small_send, small_recv, sum_send, sum_recv,
    vector_send, vector_recv, lead_send, lead_recv, spread_send, spread_recv, hop_send, hop_recv,
    credit,
):
    me = lax.axis_index("section")
    index = lax.axis_index("dp")
    y, x, core, group = position()
    groups = replicas // CUBE
    micro_rows = tokens.shape[0]
    seg_rows = micro_rows // 2
    rows_all = 2 * micro_rows
    works = me < 2

    def cube_peer(yy, xx, cc):
        return {"dp": group * CUBE + yy * 4 + xx * 2 + cc}

    beside_x = cube_peer(y, 1 - x, core)
    beside_y = cube_peer(1 - y, x, core)
    beside_core = cube_peer(y, x, 1 - core)
    others = [{"section": lax.rem(me + step, sections)} for step in range(1, sections)]

    def replica(step):
        return {"dp": lax.rem(index + step, replicas)}

    barrier = pltpu.get_barrier_semaphore()
    for other in others:
        pl.semaphore_signal(barrier, inc=1, device_id=other, device_id_type=MESH)

    @pl.loop(1, replicas)
    def _(step):
        pl.semaphore_signal(barrier, inc=1, device_id=replica(step), device_id_type=MESH)

    own_part, guest_part = pl.ds(0, micro_rows), pl.ds(micro_rows, micro_rows)

    def load_rows(place):
        source, target = ((tokens, token_rows), (cotangent, cot_rows))[place]
        return pltpu.make_async_copy(source, target.at[own_part], rows_load.at[place])

    load_rows(0).start()
    load_rows(1).start()

    def load(block):
        if block < 8:
            source = wide.at[:, :, :, :, pl.ds((block % 4) * D, D)]
        else:
            source = half.at[block % 2]
        return pltpu.make_async_copy(source, blocks.at[block], load_sem.at[block])

    def flat_rows(place):
        return pl.ds(place * D, D)

    def load_own(place):
        if place < 4:
            source = wide_flat.at[:, pl.ds(place * D, D)]
        else:
            source = half_flat.at[flat_rows(place - 4)]
        return pltpu.make_async_copy(source, flat.at[flat_rows(place)], load_sem.at[place])

    for holder in (0, 1):

        @pl.when(me == holder)
        def _():
            for block in OWN[holder]:
                load(block).start()

    @pl.when(me >= 2)
    def _():
        for place in range(4):
            load_own(place).start()

    def load_upper(block):
        return pltpu.make_async_copy(
            half.at[block], core_in.at[pl.ds(2 * block, 2)], load_sem.at[REDUCED + block]
        )

    @pl.when(me == 2)
    def _():
        for block in range(2):
            load_upper(block).start()

    @pl.when(me == 3)
    def _():
        for place in (4, 5):
            load_own(place).start()

    pl.semaphore_wait(barrier, sections - 1 + replicas - 1)

    def guest_copy(kind):
        down = {"section": lax.rem(me + sections - 2, sections)}
        up = {"section": lax.rem(me + 2, sections)}
        source, target, device = (
            (token_rows.at[own_part], token_rows.at[guest_part], down),
            (cot_rows.at[own_part], cot_rows.at[guest_part], down),
            (out_rows.at[guest_part], out_rows.at[own_part], up),
            (h1.at[guest_part], h1.at[own_part], up),
        )[kind]
        return remote(source, target, guest_send.at[kind], guest_recv.at[kind], device)

    TOKENS, COTANGENT, OUT, GRAD = 0, 1, 2, 3

    load_rows(0).wait()
    load_rows(1).wait()

    @pl.when(me >= 2)
    def _():
        guest_copy(TOKENS).start()

    row_of = lax.broadcasted_iota(jnp.int32, (SLAB, D), 0)

    def lead_rows(ref, count):
        value = jnp.zeros((SLAB, D), F32)
        for lead in range(count):
            row = ref[lead * seg_rows : lead * seg_rows + SLAB].astype(F32)[0:1]
            value = jnp.where(row_of == lead, row, value)
        return value.astype(LOW)

    def lead_copy(kind, slab, target, reader):
        return remote(
            slab, target.at[me], lead_send.at[kind], lead_recv.at[kind, me], {"section": reader}
        )

    def lead_start(kind, slab, target, reader):
        @pl.when(me != reader)
        def _():
            lead_copy(kind, slab, target, reader).start()

        @pl.when(me == reader)
        def _():
            target[reader] = slab[...]

    def lead_wait(kind, slab, target, reader, senders):
        for section in range(senders):
            if section != reader:
                remote(
                    slab, target.at[section], lead_send.at[kind], lead_recv.at[kind, section],
                    {"section": section},
                ).wait_recv()

    def collected(target, senders):
        value = jnp.zeros((SLAB, D), F32)
        for section in range(senders):
            slab = target[section].astype(F32)
            for micro in range(section, sections, senders):
                for lead in range(2):
                    place = (micro - section) // senders * 2 + lead
                    value = jnp.where(
                        row_of == 2 * micro + lead, slab[place : place + 1], value
                    )
        return value

    def spread_copy(kind, slab, step):
        return remote(
            slab, slab, spread_send.at[kind, step], spread_recv.at[kind], others[step - 1]
        )

    def hop_copy(kind, slab, step):
        return remote(
            slab, slab, hop_send.at[kind], hop_recv.at[kind],
            {"section": lax.rem(me + step + sections, sections)},
        )

    def leads_of(slab, micro):
        value = slab[...].astype(F32)
        return [
            jnp.sum(jnp.where(row_of == 2 * micro + lead, value, 0.0), axis=0, keepdims=True)
            for lead in range(2)
        ]

    COT, H1, H2 = 0, 1, 2
    FOURTH = 0
    THIRD, GRAD3, GRAD2, HAND, GRAD1 = 0, 1, 2, 3, 4

    def vector_copy(step):
        return remote(
            vectors.at[me], vectors.at[me], vector_send.at[step], vector_recv.at[step],
            others[step - 1],
        )

    vectors[me, 0:1] = norm_gain[...]
    vectors[me, 1:2] = norm_bias[...]
    for step in range(1, sections):
        vector_copy(step).start()
    cot_slab[...] = lead_rows(cot_rows, 2)
    lead_start(COT, cot_slab, cot_leads, 3)

    upper, lower = pl.ds(0, HALF), pl.ds(HALF, HALF)

    def lanes_of(turn):
        return pl.ds((turn % 2) * WIDTH, WIDTH)

    def turns(*order):
        return tuple(2 * block + side for block in order for side in range(2))

    def place_of(block):
        if block < REDUCED:
            return blocks.at[block]
        return core_in.at[pl.ds(2 * (block - REDUCED), 2)]

    def line_copy(turn, reader):
        block, lanes = turn // 2, lanes_of(turn)
        piece = place_of(block).at[y, x, core, :, lanes]
        return remote(
            piece,
            piece,
            line_send.at[turn],
            line_recv.at[turn],
            {"section": reader},
        )

    def cube_copy(turn, stage):
        full, lanes = place_of(turn // 2), lanes_of(turn)
        ref, peer = (
            (full.at[y, x, core, upper, lanes], beside_x),
            (full.at[y, x, core, lower, lanes], beside_y),
            (full.at[y, :, core, upper, lanes], beside_y),
            (full.at[:, x, core, lower, lanes], beside_x),
            (full.at[:, :, core, :, lanes], beside_core),
        )[stage]
        slot = SLOT[turn]
        return remote(ref, ref, cube_send.at[slot, stage], cube_recv.at[slot, stage], peer)

    def gather_line(turn, reader):
        @pl.when(me == reader)
        def _():
            line_copy(turn, reader).wait_recv()
            cube_copy(turn, 0).start()
            cube_copy(turn, 1).start()

    def gather_two(turn, reader):
        @pl.when(me == reader)
        def _():
            cube_copy(turn, 0).wait()
            cube_copy(turn, 2).start()
            cube_copy(turn, 1).wait()
            cube_copy(turn, 3).start()

    def gather_three(turn, reader):
        @pl.when(me == reader)
        def _():
            cube_copy(turn, 2).wait()
            cube_copy(turn, 3).wait()
            cube_copy(turn, 4).start()

    def gather_ready(turn, reader):
        @pl.when(me == reader)
        def _():
            cube_copy(turn, 4).wait()

    def gather_finish(turn, reader):
        @pl.when(me == HOLDER[turn // 2])
        def _():
            line_copy(turn, reader).wait_send()

    def gather_send():
        for reader, wanted in WANTED.items():

            @pl.when(me == HOLDER[wanted[0]])
            def _():
                for turn in turns(*wanted):
                    line_copy(turn, reader).start()

    gather_plan = ((gather_ready, 6), (gather_three, 4), (gather_two, 2), (gather_line, 0))
    gather_ticks = 2 * OWNED + gather_plan[0][1]

    def gather_tick(tick):
        for stage, offset in gather_plan:
            at = tick - offset
            for reader, wanted in WANTED.items():
                if 0 <= at < 2 * len(wanted):
                    stage(2 * wanted[at // 2] + at % 2, reader)

    def gather_wait_own():
        @pl.when(me == 2)
        def _():
            for block in range(2):
                load_upper(block).wait()

        for holder in (0, 1):

            @pl.when(me == holder)
            def _():
                for block in OWN[holder]:
                    load(block).wait()

    def worker(step):
        def run(*given):
            @pl.when(works)
            def _():
                step(*given)

        return run

    def weight(block):
        return blocks[block].reshape(D, D)

    def act_rows(block):
        return pl.ds(pl.multiple_of(block * rows_all, SLAB), rows_all)

    def slope_rows(block):
        return pl.ds(pl.multiple_of((4 + block) * rows_all, SLAB), rows_all)

    lane_of = lax.broadcasted_iota(jnp.int32, (1, 128), 1)
    first_half = lane_of < 64
    head_masks = (first_half.astype(LOW), (~first_half).astype(LOW))
    segs = range(4)

    def chunks(size, body):
        @pl.loop(0, rows_all // size)
        def _(step):
            body(pl.multiple_of(step * size, size), size)

    @worker
    def project(block):
        qkv[:, block * D : (block + 1) * D] = dot(token_rows[...], weight(block)).astype(LOW)

    def seg_slice(seg):
        return pl.ds(seg * seg_rows, seg_rows)

    def pair_lanes(pair):
        return [pl.ds(pl.multiple_of(part * D + pair * 128, 128), 128) for part in range(3)]

    def softmax(scores):
        raised = jnp.exp(scores - jnp.max(scores, axis=-1, keepdims=True))
        return raised / jnp.sum(raised, axis=-1, keepdims=True)

    @worker
    def heads_forward(first, last):
        @pl.loop(first, last)
        def _(pair):
            at_q, at_k, at_v = pair_lanes(pair)
            heads = [(seg, place) for seg in segs for place in range(2)]
            scores = [
                dot_right(qkv[seg_slice(seg), at_q] * head_masks[place], qkv[seg_slice(seg), at_k])
                * 0.125
                for seg, place in heads
            ]
            found = [softmax(score) for score in scores]
            for (seg, place), prob in zip(heads, found):
                probs[seg, pair, place] = prob
            mixed = [
                dot(prob.astype(LOW), qkv[seg_slice(seg), at_v])
                for (seg, place), prob in zip(heads, found)
            ]
            for seg in segs:
                context[seg_slice(seg), at_q] = jnp.where(
                    first_half, mixed[2 * seg], mixed[2 * seg + 1]
                ).astype(LOW)

    @worker
    def attention_close():
        summed[...] = dot_right(context[...], weight(3))
        gain, bias = vectors[0, 0:1], vectors[0, 1:2]

        def body(start, size):
            rows = pl.ds(start, size)
            out, normed, inv_dev = normalize(
                token_rows[rows].astype(F32) + summed[rows], gain, bias
            )
            norm0[rows] = normed
            dev0[rows] = jnp.broadcast_to(inv_dev, (size, 128))
            h1[rows] = out.astype(LOW)

        chunks(32, body)
        h1_slab[...] = lead_rows(h1, 4)
        lead_start(H1, h1_slab, h1_leads, 1)

    @worker
    def inner_block(block):
        summed[...] = dot(h1[...], weight(4 + block))

        def body(start, size):
            value, grade = gelu_pair(summed[pl.ds(start, size)])
            flat[pl.ds(block * rows_all + start, size)] = value.astype(LOW)
            flat[pl.ds((4 + block) * rows_all + start, size)] = grade.astype(LOW)

        chunks(32, body)

    @worker
    def second_block(place):
        block = lax.rem(2 * me + place, 4)
        product = dot(flat[act_rows(block)], weight(8 + block))
        if place == 0:
            branch[...] = product
        else:
            branch[...] += product

    @worker
    def mlp_close():
        gain, bias = vectors[1, 0:1], vectors[1, 1:2]

        def body(start, size):
            rows = pl.ds(start, size)
            out, normed, inv_dev = normalize(h1[rows].astype(F32) + branch[rows], gain, bias)
            norm1[rows] = normed
            dev1[rows] = jnp.broadcast_to(inv_dev, (size, 128))
            out_rows[rows] = out.astype(LOW)

        chunks(32, body)
        h2_slab[...] = lead_rows(out_rows, 4)
        lead_start(H2, h2_slab, h2_leads, 2)
        guest_copy(OUT).start()

    def add_small(row, value):
        small[row : row + 1] += value

    @worker
    def mlp_open_backward():
        gain = vectors[1, 0:1]

        def body(start, size):
            rows = pl.ds(start, size)
            place = start + lax.broadcasted_iota(jnp.int32, (size, D), 0)
            grad = jnp.where(lax.rem(place, seg_rows) == 0, 0.0, cot_rows[rows].astype(F32))
            grad_sum, grad_gain, grad_bias = normalize_backward(
                grad, norm1[rows], dev1[rows][:, 0:1], gain
            )
            branch[rows] = grad_sum
            kept[rows] = grad_sum.astype(LOW)
            add_small(2, grad_gain)
            add_small(3, grad_bias)

        chunks(32, body)

    def part(block):
        return block + 4 if block < 4 else block + 8

    def store_part(block, left, right):
        for strip in range(2):
            lanes = slice(strip * WIDTH, (strip + 1) * WIDTH)
            blocks[part(block), strip] = (
                outer(left[:, lanes], right).astype(LOW).reshape(2, 2, PIECE, D)
            )

    @worker
    def second_grad(block):
        store_part(8 + block, flat[act_rows(block)], kept[...])

    @worker
    def inner_grad(block):
        grad_act = dot_right(kept[...], weight(8 + block))
        grad_inner = (grad_act * flat[slope_rows(block)].astype(F32)).astype(LOW)
        flat[act_rows(block)] = grad_inner
        branch[...] += dot_right(flat[act_rows(block)], weight(4 + block))
        store_part(4 + block, h1[...], flat[act_rows(block)])

    @worker
    def attention_open_backward():
        gain = vectors[0, 0:1]
        leads = leads_of(lead_grad1, me) + leads_of(lead_grad1, me + 2)

        def body(start, size):
            rows = pl.ds(start, size)
            place = start + lax.broadcasted_iota(jnp.int32, (size, D), 0)
            grad = branch[rows]
            for lead in range(4):
                grad = jnp.where(place == lead * seg_rows, leads[lead], grad)
            grad = grad.astype(LOW).astype(F32)
            grad_sum, grad_gain, grad_bias = normalize_backward(
                grad, norm0[rows], dev0[rows][:, 0:1], gain
            )
            summed[rows] = grad_sum
            kept[rows] = grad_sum.astype(LOW)
            add_small(0, grad_gain)
            add_small(1, grad_bias)

        chunks(32, body)

    @worker
    def out_grad():
        store_part(3, kept[...], context[...])
        context[...] = dot(kept[...], weight(3)).astype(LOW)

    @worker
    def heads_backward(first, last):
        @pl.loop(first, last)
        def _(pair):
            at_q, at_k, at_v = pair_lanes(pair)
            heads = [(seg, place) for seg in segs for place in range(2)]
            grad_probs = [
                dot_right(
                    context[seg_slice(seg), at_q] * head_masks[place], qkv[seg_slice(seg), at_v]
                )
                for seg, place in heads
            ]
            grad_scores = []
            for (seg, place), grad_prob in zip(heads, grad_probs):
                prob = probs[seg, pair, place]
                inside = prob * grad_prob
                grad_score = inside - prob * jnp.sum(inside, axis=-1, keepdims=True)
                grad_scores.append(grad_score.astype(LOW))
            for seg in segs:
                rows = seg_slice(seg)
                query, key, grad = qkv[rows, at_q], qkv[rows, at_k], context[rows, at_q]
                mine = grad_scores[2 * seg : 2 * seg + 2]
                found = [probs[seg, pair, place].astype(LOW) for place in range(2)]
                for at, both, scale in (
                    (at_q, [dot(score, key) for score in mine], 0.125),
                    (at_k, [outer(score, query) for score in mine], 0.125),
                    (at_v, [outer(prob, grad) for prob in found], 1.0),
                ):
                    merged = jnp.where(first_half, both[0], both[1]) * scale
                    qkv[rows, at] = merged.astype(LOW)

    @worker
    def project_grad(block):
        store_part(block, token_rows[...], qkv[:, block * D : (block + 1) * D])

    @worker
    def tokens_back(block):
        summed[...] += dot_right(qkv[:, block * D : (block + 1) * D], weight(block))

    @worker
    def tokens_close():
        h1[...] = summed[...].astype(LOW)
        guest_copy(GRAD).start()

    def leads_mlp_forward(value, first, second, gain, bias):
        total_branch = value.astype(F32)
        for block in range(4):
            lanes = slice(block * D, (block + 1) * D)
            out, grade = gelu_pair(dot(value, first(block)))
            lead_act[:, lanes] = out.astype(LOW)
            lead_slope[:, lanes] = grade
            total_branch = total_branch + dot(lead_act[:, lanes], second(block))
        out, normed, inv_dev = normalize(total_branch, gain, bias)
        lead_norm[...] = normed
        lead_dev[...] = jnp.broadcast_to(inv_dev, (SLAB, 128))
        pack[:, 0:D] = value
        pack[:, LEFT_OUT:RIGHT] = value
        return out

    def leads_mlp_backward(grad, first, second, gain):
        grad_sum, grad_gain, grad_bias = normalize_backward(
            grad, lead_norm[...], lead_dev[:, 0:1], gain
        )
        add_small(4, grad_gain)
        add_small(5, grad_bias)
        low_sum = grad_sum.astype(LOW)
        result = grad_sum
        for block in range(4):
            lanes = slice(block * D, (block + 1) * D)
            grad_inner = (dot_right(low_sum, second(block)) * lead_slope[:, lanes]).astype(LOW)
            pack[:, RIGHT + block * D : RIGHT + (block + 1) * D] = grad_inner
            result = result + dot_right(grad_inner, first(block))
        pack[:, LEFT_HALF:RIGHT_HALF] = lead_act[:, 2 * D :]
        pack[:, RIGHT_HALF:] = low_sum
        handed[:, 0 : 2 * D] = lead_act[:, 0 : 2 * D]
        handed[:, 2 * D :] = low_sum
        return result

    def own_weight(place):
        return flat[flat_rows(place)]

    def last_second(block):
        if block >= 2:
            return own_weight(2 + block)
        return core_in[2 * block : 2 * block + 2].reshape(D, D)

    def leads_first():
        @pl.when(me == 2)
        def _():
            lead_wait(H2, h2_slab, h2_leads, 2, 2)
            for place in range(4):
                load_own(place).wait()
            value = collected(h2_leads, 2).astype(LOW)
            pack[:, 0:D] = value
            for block in range(3):
                lead_qkv[:, block * D : (block + 1) * D] = dot(value, own_weight(block)).astype(LOW)
            docs = seg_doc[...]
            row, column = (lax.broadcasted_iota(jnp.int32, (SLAB, SLAB), i) for i in range(2))
            sort = jnp.where(row == column, 2.0, 0.0)
            for micro in range(seg_doc.shape[0]):
                pair_sort = jnp.where(
                    docs[micro : micro + 1, 0:1] == docs[micro : micro + 1, 1:2], 2.0, 1.0
                )
                near = (row // 2 == micro) & (column // 2 == micro) & (row != column)
                sort = jnp.where(near, pair_sort, sort)
            for pair in range(PAIRS):
                at = [slice(p * D + pair * 128, p * D + (pair + 1) * 128) for p in range(3)]
                query, key, val = (lead_qkv[:, lanes] for lanes in at)
                parts = []
                for place in range(2):
                    scores = dot_right(query * head_masks[place], key) * 0.125
                    scores = jnp.where(
                        sort > 1.5, scores, jnp.where(sort > 0.5, -1000000000.0, -1e30)
                    )
                    raised = jnp.exp(scores - jnp.max(scores, axis=-1, keepdims=True))
                    prob = raised / jnp.sum(raised, axis=-1, keepdims=True)
                    lead_probs[pair, place] = prob
                    parts.append(dot(prob.astype(LOW), val))
                lead_context[:, pair * 128 : (pair + 1) * 128] = jnp.where(
                    first_half, parts[0], parts[1]
                ).astype(LOW)
            summed_rows = value.astype(F32) + dot_right(lead_context[...], own_weight(3))
            out, normed, inv_dev = normalize(summed_rows, vectors[2, 0:1], vectors[2, 1:2])
            lead_norm[...] = normed
            lead_dev[...] = jnp.broadcast_to(inv_dev, (SLAB, 128))
            lead_third[...] = out.astype(LOW)
            hop_copy(THIRD, lead_third, 1).start()

        @pl.when(me == 1)
        def _():
            lead_wait(H1, h1_slab, h1_leads, 1, 2)
            leads_mlp_forward(
                collected(h1_leads, 2).astype(LOW),
                lambda block: weight(4 + block),
                lambda block: weight(8 + block),
                vectors[1, 0:1],
                vectors[1, 1:2],
            )

    def leads_second():
        @pl.when(me == 3)
        def _():
            hop_copy(THIRD, lead_third, -1).wait_recv()
            for place in range(6):
                load_own(place).wait()
            out = leads_mlp_forward(
                lead_third[...], own_weight, last_second, vectors[3, 0:1], vectors[3, 1:2]
            )
            lead_fourth[...] = out.astype(LOW)
            for step in range(1, sections):
                spread_copy(FOURTH, lead_fourth, step).start()
            lead_wait(COT, cot_slab, cot_leads, 3, sections)
            grad = leads_mlp_backward(
                collected(cot_leads, sections), own_weight, last_second, vectors[3, 0:1]
            )
            lead_grad3[...] = grad.astype(LOW)
            hop_copy(GRAD3, lead_grad3, -1).start()
            hop_copy(HAND, handed, -1).start()

    def leads_third():
        @pl.when(me == 2)
        def _():
            hop_copy(GRAD3, lead_grad3, 1).wait_recv()
            grad_sum, grad_gain, grad_bias = normalize_backward(
                lead_grad3[...].astype(F32), lead_norm[...], lead_dev[:, 0:1], vectors[2, 0:1]
            )
            add_small(4, grad_gain)
            add_small(5, grad_bias)
            low_sum = grad_sum.astype(LOW)
            pack[:, LEFT_OUT:RIGHT] = low_sum
            pack[:, RIGHT + 3 * D : LEFT_HALF] = lead_context[...]
            grad_context = dot(low_sum, own_weight(3)).astype(LOW)
            for pair in range(PAIRS):
                at = [slice(p * D + pair * 128, p * D + (pair + 1) * 128) for p in range(3)]
                query, key, val = (lead_qkv[:, lanes] for lanes in at)
                grad = grad_context[:, pair * 128 : (pair + 1) * 128]
                grads = ([], [], [])
                for place in range(2):
                    prob = lead_probs[pair, place]
                    grad_prob = dot_right(grad * head_masks[place], val)
                    inside = prob * grad_prob
                    grad_score = inside - prob * jnp.sum(inside, axis=-1, keepdims=True)
                    grad_score = grad_score.astype(LOW)
                    grads[0].append(dot(grad_score, key))
                    grads[1].append(outer(grad_score, query))
                    grads[2].append(outer(prob.astype(LOW), grad))
                for lanes, pair_grads, scale in zip(at, grads, (0.125, 0.125, 1.0)):
                    merged = jnp.where(first_half, pair_grads[0], pair_grads[1]) * scale
                    pack[:, RIGHT + lanes.start : RIGHT + lanes.stop] = merged.astype(LOW)
            result = grad_sum
            for block in range(3):
                result = result + dot_right(
                    pack[:, RIGHT + block * D : RIGHT + (block + 1) * D], own_weight(block)
                )
            lead_grad2[...] = result.astype(LOW)
            hop_copy(GRAD2, lead_grad2, -1).start()
            hop_copy(HAND, handed, 1).wait_recv()
            pack[:, LEFT_HALF:] = handed[...]

    def leads_fourth():
        @pl.when(me == 1)
        def _():
            hop_copy(GRAD2, lead_grad2, 1).wait_recv()
            grad = leads_mlp_backward(
                lead_grad2[...].astype(F32),
                lambda block: weight(4 + block),
                lambda block: weight(8 + block),
                vectors[1, 0:1],
            )
            lead_grad1[...] = grad.astype(LOW)
            hop_copy(GRAD1, lead_grad1, -1).start()
            hop_copy(HAND, handed, -1).start()

    half_lanes = pl.ds(pl.multiple_of(core * HALF_PACK, 128), HALF_PACK)
    other_lanes = pl.ds(pl.multiple_of((1 - core) * HALF_PACK, 128), HALF_PACK)
    first_peer = {"dp": group * CUBE + (y + core - 2 * y * core) * 4
                  + (x + (1 - core) * (1 - 2 * x)) * 2 + core}
    second_peer = {"dp": group * CUBE + (y + (1 - core) * (1 - 2 * y)) * 4
                   + (x + core - 2 * x * core) * 2 + core}

    def pack_copy(stage):
        chip = y * 2 + x
        first_chip = (y + core - 2 * y * core) * 2 + x + (1 - core) * (1 - 2 * x)
        if stage == 0:
            source, target, peer = pack.at[:, other_lanes], pack_in, beside_core
        elif stage == 1:
            source = target = factors.at[chip, :, half_lanes]
            peer = first_peer
        elif stage == 2:
            source = target = factors.at[chip, :, half_lanes]
            peer = second_peer
        elif stage == 3:
            source = target = factors.at[first_chip, :, half_lanes]
            peer = second_peer
        else:
            source = target = factors.at[:, :, half_lanes]
            peer = beside_core
        return remote(source, target, pack_send.at[stage], pack_recv.at[stage], peer)

    def pack_join():
        pack_copy(0).wait()

        @pl.loop(0, HALF_PACK // WIDTH)
        def _(step):
            start = pl.multiple_of(step * WIDTH, 128)
            lanes = pl.ds(pl.multiple_of(core * HALF_PACK + start, 128), WIDTH)
            mine = pack[:, lanes].astype(F32)[0:8]
            theirs = pack_in[:, pl.ds(start, WIDTH)].astype(F32)[0:8]
            low_rows = jnp.where(core == 0, mine, theirs)
            high_rows = jnp.where(core == 0, theirs, mine)
            factors[y * 2 + x, :, lanes] = jnp.concatenate([low_rows, high_rows]).astype(LOW)

        pack_copy(1).start()

    def pack_second():
        pack_copy(1).wait()
        pack_copy(2).start()
        pack_copy(3).start()

    def pack_third():
        pack_copy(2).wait()
        pack_copy(3).wait()
        pack_copy(4).start()

    def to_packs(step):
        return remote(
            factors, packs.at[group], group_pack_send.at[step], group_pack_recv.at[step],
            {"dp": lax.rem(index + step * CUBE, replicas)},
        )

    def own_pack():
        return pltpu.make_async_copy(factors, packs.at[group], group_pack_send.at[0])

    def pack_fourth():
        pack_copy(4).wait()
        own_pack().start()
        for step in range(1, groups):
            to_packs(step).start()

    def pack_last():
        own_pack().wait()
        for step in range(1, groups):
            to_packs(step).wait()

    def rows_store(place):
        source, target = ((out_rows, layer_out), (h1, grad_tokens))[place]
        return pltpu.make_async_copy(source.at[own_part], target, rows_out.at[place])

    def leads_close():
        @pl.when(me != 3)
        def _():
            spread_copy(FOURTH, lead_fourth, 1).wait_recv()

        @pl.when(me >= 2)
        def _():
            guest_copy(OUT).wait_recv()

        leads = leads_of(lead_fourth, me)
        for lead in range(2):
            rows = pl.ds(lead * seg_rows, SLAB)
            out_rows[rows] = jnp.where(
                row_of == 0, leads[lead], out_rows[rows].astype(F32)
            ).astype(LOW)
        rows_store(0).start()

        @pl.when(me == 0)
        def _():
            hop_copy(GRAD1, lead_grad1, 1).wait_recv()
            hop_copy(HAND, handed, 1).wait_recv()
            pack[:, 0:LEFT_HALF] = jnp.zeros((SLAB, LEFT_HALF), LOW)
            pack[:, LEFT_HALF:] = handed[...]

        pack_copy(0).start()

    def add(target, *sources):
        value = target[...].astype(F32)
        for source in sources:
            value = value + source[...].astype(F32)
        target[...] = value.astype(LOW)

    def landing(block):
        return blocks.at[8 + block, 0] if block < 4 else core_in.at[block - 4]

    def scatter(turn, stage):
        block, lanes = turn // 2, lanes_of(turn)
        run = blocks.at[part(block)]
        source, target, peer = (
            (run.at[:, :, 1 - core, :, lanes], landing(block).at[:, :, :, lanes], beside_core),
            (run.at[:, 1 - x, core, upper, lanes], one_a.at[block, :, :, lanes], beside_x),
            (run.at[1 - y, :, core, lower, lanes], one_b.at[block, :, :, lanes], beside_y),
            (run.at[1 - y, x, core, upper, lanes], two_a.at[block, :, lanes], beside_y),
            (run.at[y, 1 - x, core, lower, lanes], two_b.at[block, :, lanes], beside_x),
        )[stage]
        if stage == 0:
            return remote(source, target, core_send.at[turn], core_recv.at[turn], peer)
        slot = SUM_SLOT[turn]
        return remote(source, target, rs_send.at[slot, stage], rs_recv.at[slot, stage], peer)

    def to_line(turn):
        return remote(
            blocks.at[part(turn // 2), y, x, core, :, lanes_of(turn)],
            line_in.at[turn // 2, :, lanes_of(turn)],
            z_send.at[turn],
            z_recv.at[turn],
            {"section": HOLDER[turn // 2]},
        )

    def to_holder(turn):
        place = EARLY.index(turn // 2)
        return remote(
            blocks.at[part(turn // 2), :, :, core, :, lanes_of(turn)],
            early_in.at[place, :, :, :, lanes_of(turn)],
            z_send.at[turn],
            z_recv.at[turn],
            {"section": HOLDER[turn // 2]},
        )

    def to_group(turn, step):
        return remote(
            blocks.at[part(turn // 2), y, x, core, :, lanes_of(turn)],
            group_in.at[turn // 2, step - 1, :, lanes_of(turn)],
            group_send.at[turn, step - 1],
            group_recv.at[turn, step - 1],
            {"dp": lax.rem(index + step * CUBE, replicas)},
        )

    def gather_back(turn, stage):
        slot = SUM_SLOT[turn]
        run, lanes = blocks.at[part(turn // 2)], lanes_of(turn)
        ref, peer = (
            (run.at[y, x, core, upper, lanes], beside_y),
            (run.at[y, x, core, lower, lanes], beside_x),
            (run.at[:, x, core, upper, lanes], beside_x),
            (run.at[y, :, core, lower, lanes], beside_y),
            (run.at[:, :, core, :, lanes], beside_core),
        )[stage]
        return remote(ref, ref, ag_send.at[slot, stage], ag_recv.at[slot, stage], peer)

    def write_out(block):
        place = OWN[HOLDER[block]].index(block)
        return pltpu.make_async_copy(
            blocks.at[part(block)], total.at[place], out_sem.at[place]
        )

    @worker
    def reduce_core(block):
        scatter(2 * block, 0).start()
        scatter(2 * block + 1, 0).start()

    def is_early(turn):
        return turn // 2 in EARLY

    def in_plane(turn):
        return me == HOLDER[turn // 2] if is_early(turn) else works

    def add_four(turn, source):
        for yy in range(2):
            for xx in range(2):
                add(
                    blocks.at[part(turn // 2), yy, xx, core, :, lanes_of(turn)],
                    source.at[yy, xx, :, lanes_of(turn)],
                )

    def reduce_one(turn):
        @pl.when(works)
        def _():
            scatter(turn, 0).wait()
            add_four(turn, landing(turn // 2))
            if not is_early(turn):
                scatter(turn, 1).start()
                scatter(turn, 2).start()

        if is_early(turn):

            @pl.when(me == 1 - HOLDER[turn // 2])
            def _():
                to_holder(turn).start()

    def reduce_early(turn):
        @pl.when(me == HOLDER[turn // 2])
        def _():
            to_holder(turn).wait_recv()
            add_four(turn, early_in.at[EARLY.index(turn // 2)])
            scatter(turn, 1).start()
            scatter(turn, 2).start()

    def reduce_two(turn):
        @pl.when(in_plane(turn))
        def _():
            reduce_two_now(turn)

    def reduce_two_now(turn):
        block, lanes = turn // 2, lanes_of(turn)
        run = blocks.at[part(block)]
        scatter(turn, 1).wait()
        for yy in range(2):
            add(run.at[yy, x, core, upper, lanes], one_a.at[block, yy, :, lanes])
        scatter(turn, 3).start()
        scatter(turn, 2).wait()
        for xx in range(2):
            add(run.at[y, xx, core, lower, lanes], one_b.at[block, xx, :, lanes])
        scatter(turn, 4).start()

    def reduce_three(turn):
        @pl.when(in_plane(turn))
        def _():
            reduce_three_now(turn)

        if not is_early(turn):

            @pl.when(me == 1 - HOLDER[turn // 2])
            def _():
                to_line(turn).start()

        else:

            @pl.when(me == HOLDER[turn // 2])
            def _():
                spread_one(turn)

    def reduce_three_now(turn):
        block, lanes = turn // 2, lanes_of(turn)
        run = blocks.at[part(block)]
        scatter(turn, 3).wait()
        add(run.at[y, x, core, upper, lanes], two_a.at[block, :, lanes])
        scatter(turn, 4).wait()
        add(run.at[y, x, core, lower, lanes], two_b.at[block, :, lanes])
        if groups > 1:
            for step in range(1, groups):
                to_group(turn, step).start()
            for step in range(1, groups):
                to_group(turn, step).wait()
            for step in range(1, groups):
                copy = pltpu.make_async_copy(
                    group_in.at[block, step - 1, :, lanes], group_piece, group_load
                )
                copy.start()
                copy.wait()
                add(run.at[y, x, core, :, lanes], group_piece)

    def spread_one(turn):
        gather_back(turn, 0).start()
        gather_back(turn, 1).start()

    def reduce_line(turn):
        @pl.when(me == HOLDER[turn // 2])
        def _():
            block, lanes = turn // 2, lanes_of(turn)
            to_line(turn).wait_recv()
            add(blocks.at[part(block), y, x, core, :, lanes], line_in.at[block, :, lanes])
            spread_one(turn)

    def spread_two(turn):
        @pl.when(me == HOLDER[turn // 2])
        def _():
            gather_back(turn, 0).wait()
            gather_back(turn, 2).start()
            gather_back(turn, 1).wait()
            gather_back(turn, 3).start()

    def spread_core(turn):
        @pl.when(me == HOLDER[turn // 2])
        def _():
            gather_back(turn, 2).wait()
            gather_back(turn, 3).wait()
            gather_back(turn, 4).start()

    def spread_done(turn):
        @pl.when(me == HOLDER[turn // 2])
        def _():
            gather_back(turn, 4).wait()
            if turn % 2 == 1:
                write_out(turn // 2).start()

        @pl.when(me == 1 - HOLDER[turn // 2])
        def _():
            (to_holder if is_early(turn) else to_line)(turn).wait_send()

    tail_plan = ((spread_done, 13), (spread_core, 11), (spread_two, 9))
    late_plan = tail_plan + (
        (reduce_three, 5), (reduce_line, 7), (reduce_two, 3), (reduce_one, 1)
    )
    early_plan = tail_plan + (
        (reduce_three, 7), (reduce_two, 5), (reduce_early, 3), (reduce_one, 1)
    )

    class Wave:
        def __init__(self, order):
            self.order, self.at = turns(*order), 0

        def tick(self, count=1):
            for _ in range(count):
                for stage, offset in late_plan:
                    if 0 <= self.at - offset < len(self.order):
                        stage(self.order[self.at - offset])
                self.at += 1

        def left(self):
            return self.at < len(self.order) + tail_plan[0][1]

    one, two = Wave(WAVES[0]), Wave(WAVES[1])

    small[...] = jnp.zeros_like(small)

    gather_wait_own()
    gather_send()

    @pl.when(me >= 2)
    def _():
        guest_copy(TOKENS).wait_send()
        guest_copy(COTANGENT).start()

    for tick in range(gather_ticks):
        gather_tick(tick)
        at = tick - gather_plan[0][1]
        if at == 0:
            for step in range(1, sections):
                vector_copy(step).wait()
        if at < 0:
            continue
        if at == 1:

            @pl.when(works)
            def _():
                guest_copy(TOKENS).wait_recv()

        if at % 2 == 1 and at < 6:
            project(at // 2)
        if at == 5:
            heads_forward(0, 2)
        if at == 6:
            heads_forward(2, 4)
        if at == 7:
            heads_forward(4, 6)
            attention_close()
        if at >= 8:
            inner_block(at - 8)
    for place in range(4):
        second_block(place)
    mlp_close()

    @pl.when(works)
    def _():
        guest_copy(COTANGENT).wait_recv()

    mlp_open_backward()
    for reader, wanted in WANTED.items():
        for turn in turns(*wanted):
            gather_finish(turn, reader)

    for block in range(4):
        second_grad(block)
        reduce_core(8 + block)
        if block > 0:
            one.tick()
    leads_first()
    for block in range(4):
        inner_grad(block)
        reduce_core(4 + block)
        one.tick(2)
        if block == 1:
            leads_second()
    leads_third()
    leads_fourth()

    @pl.when(works)
    def _():
        pl.semaphore_signal(credit, inc=1, device_id=beside_core, device_id_type=MESH)

    one.tick()
    leads_close()
    attention_open_backward()
    one.tick()
    out_grad()

    @pl.when(works)
    def _():
        pl.semaphore_wait(credit, 1)

    reduce_core(3)
    one.tick()
    heads_backward(0, 2)
    one.tick()
    two.tick()
    heads_backward(2, 4)
    one.tick()
    two.tick()
    heads_backward(4, 6)
    one.tick()
    pack_join()
    for block in range(3):
        project_grad(block)
        reduce_core(block)
        one.tick(2)
        two.tick(2)
        if block == 1:
            pack_second()

    def small_copy(step):
        return remote(
            small, small_all.at[index], small_send.at[step], small_recv.at[step], replica(step)
        )

    def sum_copy(step):
        return remote(
            small_sum, smalls.at[me], sum_send.at[step], sum_recv.at[step], others[step - 1]
        )

    def own_sum():
        return pltpu.make_async_copy(small_sum, smalls.at[me], sum_send.at[0])

    @pl.loop(1, replicas)
    def _(step):
        small_copy(step).start()

    small_all[index] = small[...]
    for block in range(3):
        tokens_back(block)
        one.tick()
        two.tick()
    tokens_close()
    pack_third()

    @pl.loop(1, replicas)
    def _(step):
        small_copy(step).wait()

    small_sum[...] = jnp.sum(small_all[...], axis=0)
    for place in range(1, sections):
        sum_copy(place).start()
    own_sum().start()
    pack_fourth()
    while one.left() or two.left():
        if one.left():
            one.tick()
        if two.left():
            two.tick()

    for place in range(1, sections):
        sum_copy(place).wait()
    own_sum().wait()
    pack_last()

    for holder in (0, 1):

        @pl.when(me == holder)
        def _():
            for block in OWN[holder]:
                write_out(block).wait()

    @pl.when(me != 3)
    def _():
        lead_copy(COT, cot_slab, cot_leads, 3).wait_send()

    @pl.when(me == 0)
    def _():
        lead_copy(H1, h1_slab, h1_leads, 1).wait_send()

    @pl.when(works)
    def _():
        lead_copy(H2, h2_slab, h2_leads, 2).wait_send()
        guest_copy(OUT).wait_send()
        guest_copy(GRAD).wait_send()

    @pl.when(me >= 2)
    def _():
        guest_copy(COTANGENT).wait_send()
        guest_copy(GRAD).wait_recv()

    rows_store(1).start()
    rows_store(1).wait()
    rows_store(0).wait()

    @pl.when(me == 1)
    def _():
        hop_copy(GRAD1, lead_grad1, -1).wait_send()
        hop_copy(HAND, handed, -1).wait_send()

    @pl.when(me == 2)
    def _():
        hop_copy(THIRD, lead_third, 1).wait_send()
        hop_copy(GRAD2, lead_grad2, -1).wait_send()

    @pl.when(me == 3)
    def _():
        for place in range(1, sections):
            spread_copy(FOURTH, lead_fourth, place).wait_send()
        hop_copy(GRAD3, lead_grad3, -1).wait_send()
        hop_copy(HAND, handed, -1).wait_send()


def run_layers(sections, replicas, tokens, cotangent, seg_doc, gain, bias, wide, half):
    groups = replicas // CUBE
    rows = 2 * tokens.shape[0]
    seg_rows = tokens.shape[0] // 2
    vector = (8, D)
    block = (2, 2, 2, PIECE, D)
    reduced_groups = max(groups - 1, 1)
    in_vmem = pl.BlockSpec(memory_space=pltpu.VMEM)
    anywhere = pl.BlockSpec(memory_space=pl.ANY)
    slab = pltpu.VMEM((SLAB, D), LOW)
    leads = pltpu.VMEM((sections, SLAB, D), LOW)
    low_rows = pltpu.VMEM((rows, D), LOW)
    full_rows = pltpu.VMEM((rows, D), F32)
    return pl.pallas_call(
        partial(layer_kernel, sections, replicas),
        out_shape=(
            jax.ShapeDtypeStruct(tokens.shape, LOW),
            jax.ShapeDtypeStruct(tokens.shape, LOW),
            jax.ShapeDtypeStruct((OWNED,) + block, LOW),
            jax.ShapeDtypeStruct((groups, CUBE // 2, SLAB, PACK), LOW),
            jax.ShapeDtypeStruct((sections,) + vector, F32),
            jax.ShapeDtypeStruct(
                (REDUCED if groups > 1 else 1, reduced_groups, PIECE, D), LOW
            ),
        ),
        in_specs=[anywhere] * 2 + [in_vmem] * 3 + [anywhere] * 4,
        out_specs=[anywhere] * 6,
        scratch_shapes=[
            pltpu.VMEM((REDUCED + 8,) + block, LOW),
            pltpu.VMEM((max(8 * rows, 6 * D), D), LOW),
            pltpu.VMEM((8, 2, 2, PIECE, D), LOW),
            pltpu.VMEM((REDUCED, 2, HALF, D), LOW),
            pltpu.VMEM((REDUCED, 2, HALF, D), LOW),
            pltpu.VMEM((REDUCED, HALF, D), LOW),
            pltpu.VMEM((REDUCED, HALF, D), LOW),
            pltpu.VMEM((REDUCED, PIECE, D), LOW),
            pltpu.VMEM((max(len(EARLY), 1), 2, 2, PIECE, D), LOW),
            pltpu.VMEM((sections,) + vector, F32),
            low_rows, low_rows, low_rows,
            pltpu.VMEM((rows, 3 * D), LOW),
            pltpu.VMEM((4, PAIRS, 2, seg_rows, seg_rows), F32),
            low_rows, low_rows, full_rows,
            pltpu.VMEM((rows, 128), F32),
            full_rows, full_rows,
            pltpu.VMEM((rows, 128), F32),
            full_rows, low_rows,
            slab, slab, slab, leads, leads, leads,
            slab, slab, slab, slab, slab,
            pltpu.VMEM((SLAB, 3 * D), LOW),
            pltpu.VMEM((SLAB, 3 * D), LOW),
            pltpu.VMEM((PAIRS, 2, SLAB, SLAB), F32),
            slab,
            pltpu.VMEM((SLAB, D), F32),
            pltpu.VMEM((SLAB, 128), F32),
            pltpu.VMEM((SLAB, 4 * D), LOW),
            pltpu.VMEM((SLAB, 4 * D), F32),
            pltpu.VMEM((SLAB, PACK), LOW),
            pltpu.VMEM((SLAB, HALF_PACK), LOW),
            pltpu.VMEM((CUBE // 2, SLAB, PACK), LOW),
            pltpu.VMEM(vector, F32),
            pltpu.VMEM((replicas,) + vector, F32),
            pltpu.VMEM(vector, F32),
            pltpu.VMEM((PIECE, WIDTH), LOW),
            DMA((2,)),
            DMA((4,)),
            DMA((4,)),
            DMA((2,)),
            DMA((ROUNDS,)),
            DMA((ROUNDS,)),
            DMA((4, 5)),
            DMA((4, 5)),
            DMA((GATHERED,)),
            DMA((2 * REDUCED,)),
            DMA((2 * REDUCED,)),
            DMA((8, 5)),
            DMA((8, 5)),
            DMA((2 * REDUCED,)),
            DMA((2 * REDUCED,)),
            DMA((2 * REDUCED if groups > 1 else 1, reduced_groups)),
            DMA((2 * REDUCED if groups > 1 else 1, reduced_groups)),
            DMA,
            DMA((8, 5)),
            DMA((8, 5)),
            DMA((OWNED,)),
            DMA((5,)),
            DMA((5,)),
            DMA((groups,)),
            DMA((groups,)),
            DMA((replicas,)),
            DMA((replicas,)),
            DMA((sections,)),
            DMA((sections,)),
            DMA((sections,)),
            DMA((sections,)),
            DMA((3,)),
            DMA((3, sections)),
            DMA((1, sections)),
            DMA((1,)),
            DMA((5,)),
            DMA((5,)),
            pltpu.SemaphoreType.REGULAR,
        ],
        compiler_params=pltpu.CompilerParams(
            collective_id=0, has_side_effects=True, vmem_limit_bytes=VMEM_BYTES
        ),
    )(
        tokens, cotangent, seg_doc, gain, bias,
        wide.reshape(2, 2, 2, PIECE, 4 * D), half.reshape(2, 2, 2, 2, PIECE, D), wide, half,
    )


VMEM_BYTES = 62 * 1024 * 1024


def close_kernel(
    total, packs, smalls, rows_in, grads_in,
    wide_out, half_out, gain_out, bias_out, rows_out, grads_out,
    blocks, packed, result, rows, grads, block_sem, result_sem, pack_sem, rows_sem, back_sem,
):
    me = lax.axis_index("section")
    near = me < 2
    groups = packs.shape[0]
    pack_copy = pltpu.make_async_copy(packs, packed, pack_sem)
    loads = [
        pltpu.make_async_copy(total.at[place], blocks.at[place], block_sem.at[place])
        for place in range(OWNED)
    ]
    passing = [
        (
            pltpu.make_async_copy(source, buffer, rows_sem.at[i]),
            pltpu.make_async_copy(buffer, target, back_sem.at[i]),
        )
        for i, (source, buffer, target) in enumerate(
            ((rows_in, rows, rows_out), (grads_in, grads, grads_out))
        )
    ]
    pack_copy.start()
    for load in loads:
        load.start()
    for arrive, _ in passing:
        arrive.start()

    every = jnp.sum(smalls[...], axis=0)
    mine = smalls[me]
    for row, out in ((0, gain_out), (1, bias_out)):
        value = jnp.where(me == 0, every[row : row + 1], every[2 + row : 3 + row])
        out[...] = jnp.where(near, value, 0.0) + mine[4 + row : 5 + row]

    pack_copy.wait()
    factors = packed[...].reshape(groups * CUBE // 2 * SLAB, PACK)
    stores = []
    for place in range(OWNED):
        if place < 4:
            left = factors[:, 0:D] if place < 3 else factors[:, LEFT_OUT:RIGHT]
            right = factors[:, RIGHT + place * D : RIGHT + (place + 1) * D]
            target = wide_out.at[0, :, pl.ds(place * D, D)]
        else:
            left = factors[:, LEFT_HALF + (place - 4) * D : LEFT_HALF + (place - 3) * D]
            right = factors[:, RIGHT_HALF:]
            target = half_out.at[0, pl.ds((place - 4) * D, D)]
        loads[place].wait()
        for strip in range(2):
            rows_of = pl.ds(strip * WIDTH, WIDTH)
            summed = blocks[place, strip].reshape(WIDTH, D).astype(F32)
            result[place, rows_of] = jnp.where(near, summed, 0.0) + outer(
                left[:, strip * WIDTH : (strip + 1) * WIDTH], right
            )
        store = pltpu.make_async_copy(result.at[place], target, result_sem.at[place])
        store.start()
        stores.append(store)
    for arrive, leave in passing:
        arrive.wait()
        leave.start()
    for store in stores:
        store.wait()
    for _, leave in passing:
        leave.wait()


def close(total, packs, smalls, rows, grads):
    in_vmem = pl.BlockSpec(memory_space=pltpu.VMEM)
    anywhere = pl.BlockSpec(memory_space=pl.ANY)
    return pl.pallas_call(
        close_kernel,
        out_shape=(
            jax.ShapeDtypeStruct((1, D, 4 * D), F32),
            jax.ShapeDtypeStruct((1, 2 * D, D), F32),
            jax.ShapeDtypeStruct((1, D), F32),
            jax.ShapeDtypeStruct((1, D), F32),
            jax.ShapeDtypeStruct(rows.shape, LOW),
            jax.ShapeDtypeStruct(rows.shape, LOW),
        ),
        in_specs=[anywhere, anywhere, in_vmem, anywhere, anywhere],
        out_specs=[anywhere, anywhere, in_vmem, in_vmem, anywhere, anywhere],
        scratch_shapes=[
            pltpu.VMEM(total.shape, LOW),
            pltpu.VMEM(packs.shape, LOW),
            pltpu.VMEM((OWNED, D, D), F32),
            pltpu.VMEM(rows.shape, LOW),
            pltpu.VMEM(rows.shape, LOW),
            DMA((OWNED,)),
            DMA((OWNED,)),
            DMA,
            DMA((2,)),
            DMA((2,)),
        ],
        compiler_params=pltpu.CompilerParams(vmem_limit_bytes=VMEM_BYTES),
    )(total, packs, smalls, rows, grads)


def on_device(tokens, cotangent, seg_doc, wide_in, half_out, norm_gain, norm_bias):
    sections = lax.axis_size("section")
    replicas = lax.axis_size("dp")
    rows, grads, total, packs, smalls, _ = run_layers(
        sections, replicas, tokens, cotangent, seg_doc, norm_gain, norm_bias, wide_in[0], half_out[0]
    )
    wide_grad, half_grad, gain_grad, bias_grad, layer_out, tokens_grad = close(
        total, packs, smalls, rows, grads
    )
    return layer_out, tokens_grad, wide_grad, half_grad, gain_grad, bias_grad


def solution(mesh):
    placed = (
        P(("dp", "section"), None),
        P(("dp", "section"), None),
        P("dp", None),
        P("section", None, None),
        P("section", None, None),
        P("section", None),
        P("section", None),
    )
    return jax.shard_map(
        on_device,
        mesh=mesh,
        in_specs=placed,
        out_specs=(
            P(("dp", "section"), None),
            P(("dp", "section"), None),
            P("section", None, None),
            P("section", None, None),
            P("section", None),
            P("section", None),
        ),
        check_vma=False,
    )
```

```python
from functools import partial

import jax
import jax.numpy as jnp
from jax import lax
from jax.experimental import pallas as pl
from jax.experimental.pallas import tpu as pltpu
from jax.sharding import PartitionSpec as P

D = 768
HEADS = 12
PAIRS = HEADS // 2
CUBE = 8
PIECE = D // CUBE
HALF = PIECE // 2
WIDTH = D // 2
SLAB = 16
HOLDER = (0, 0, 0, 0, 1, 1, 1, 1, 0, 0, 1, 1, 2, 2)
GATHERED = len(HOLDER)
ROUNDS = 2 * GATHERED
REDUCED = 12
OWN = {0: (0, 1, 2, 3, 8, 9), 1: (4, 5, 6, 7, 10, 11)}
OWNED = len(OWN[0])
WANTED = {0: (4, 5, 6, 7, 10, 11), 1: (0, 1, 2, 3, 8, 9), 3: (12, 13)}
WAVES = ((8, 9, 10, 11, 4, 5, 6, 7), (3, 0, 1, 2))
EARLY = ()
SPACING = (4, 2)
EARLY_AT = (9, 5)
SLOT = {
    2 * block + side: (2 * place + side) % 4
    for wanted in WANTED.values()
    for place, block in enumerate(wanted)
    for side in range(2)
}


def sum_slots(orders):
    slots, base = {}, 0
    for spacing, order in zip(SPACING, orders):
        late = [block for block in order if block not in EARLY]
        for place, block in enumerate(late):
            for side in range(2):
                slots[2 * block + side] = base + (2 * place + side) % (2 * spacing)
        base += 2 * spacing
    for place, block in enumerate(EARLY):
        for side in range(2):
            slots[2 * block + side] = base + 2 * place + side
    return slots


SUM_SLOT = sum_slots(WAVES)
BACK_SLOT = {}
for holder in OWN:
    BACK_SLOT |= {
        turn: slot
        for turn, slot in sum_slots(
            [[b for b in order if HOLDER[b] == holder] for order in WAVES]
        ).items()
        if HOLDER[turn // 2] == holder
    }
SLOTS = 2 * sum(SPACING) + 2 * len(EARLY)
EARLY_PLACE = {
    block: [other for other in EARLY if HOLDER[other] == HOLDER[block]].index(block)
    for block in EARLY
}
EARLY_PLACES = max(EARLY_PLACE.values(), default=0) + 1
LEFT_OUT, RIGHT, LEFT_HALF, RIGHT_HALF, PACK = D, 2 * D, 6 * D, 8 * D, 9 * D
HALF_PACK = PACK // 2
LOW = jnp.bfloat16
F32 = jnp.float32
DMA = pltpu.SemaphoreType.DMA
MESH = pl.DeviceIdType.MESH


def dot(left, right):
    return jnp.dot(left, right, preferred_element_type=F32)


def dot_right(left, right):
    return lax.dot_general(left, right, (((1,), (1,)), ((), ())), preferred_element_type=F32)


def outer(left, right):
    return lax.dot_general(left, right, (((0,), (0,)), ((), ())), preferred_element_type=F32)


def normalize(summed, gain, bias):
    average = jnp.mean(summed, axis=-1, keepdims=True)
    centred = summed - average
    inv_dev = lax.rsqrt(jnp.mean(centred * centred, axis=-1, keepdims=True) + 1e-05)
    normed = centred * inv_dev
    return normed * gain + bias, normed, inv_dev


def normalize_backward(grad, normed, inv_dev, gain):
    scaled = grad * gain
    mean_scaled = jnp.mean(scaled, axis=-1, keepdims=True)
    mean_normed = jnp.mean(scaled * normed, axis=-1, keepdims=True)
    grad_sum = inv_dev * (scaled - mean_scaled - normed * mean_normed)
    return (
        grad_sum,
        jnp.sum(grad * normed, axis=0, keepdims=True),
        jnp.sum(grad, axis=0, keepdims=True),
    )


def gelu_pair(value):
    bell = jnp.exp(-0.5 * value * value)
    base = 1.0 + (0.3275911 * 0.7071067811865476) * jnp.abs(value)
    guess = pl.reciprocal(base, approx=True)
    t = guess * (2.0 - base * guess)
    poly = t * (
        0.5 * 0.254829592
        + t
        * (
            0.5 * -0.284496736
            + t * (0.5 * 1.421413741 + t * (0.5 * -1.453152027 + t * (0.5 * 1.061405429)))
        )
    )
    tail = poly * bell
    below = jnp.where(value >= 0, 1.0 - tail, tail)
    return value * below, below + value * bell * 0.3989422804014327


def position():
    index = lax.axis_index("dp")
    return (lax.rem(index // 4, 2), lax.rem(index // 2, 2), lax.rem(index, 2), index // CUBE)


def remote(source, target, send, receive, device):
    return pltpu.make_async_remote_copy(
        src_ref=source,
        dst_ref=target,
        send_sem=send,
        recv_sem=receive,
        device_id=device,
        device_id_type=MESH,
    )


def layer_kernel(
    sections, replicas,
    tokens, cotangent, seg_doc, norm_gain, norm_bias, wide, half, wide_flat, half_flat,
    layer_out, grad_tokens, total, packs, smalls, group_in,
    blocks, flat, core_in, one_a, one_b, two_a, two_b, line_in, early_in, vectors,
    token_rows, cot_rows, out_rows,
    qkv, probs, context, h1, norm0, dev0, summed, norm1, dev1, branch, kept,
    cot_slab, h1_slab, h2_slab, cot_leads, h1_leads, h2_leads,
    lead_third, lead_fourth, lead_grad3, lead_grad2, lead_grad1, handed,
    lead_qkv, lead_probs, lead_context, lead_norm, lead_dev, lead_act, lead_slope,
    pack, pack_in, factors, small, small_all, small_sum, group_piece,
    rows_load, guest_send, guest_recv, rows_out,
    line_send, line_recv, cube_send, cube_recv, load_sem,
    core_send, core_recv, rs_send, rs_recv, z_send, z_recv, group_send, group_recv, group_load, ag_send, ag_recv,
    out_sem, pack_send, pack_recv, group_pack_send, group_pack_recv,
    small_send, small_recv, sum_send, sum_recv,
    vector_send, vector_recv, lead_send, lead_recv, spread_send, spread_recv, hop_send, hop_recv,
    credit, clear_x, clear_y,
):
    me = lax.axis_index("section")
    index = lax.axis_index("dp")
    y, x, core, group = position()
    groups = replicas // CUBE
    micro_rows = tokens.shape[0]
    seg_rows = micro_rows // 2
    rows_all = 2 * micro_rows
    works = me < 2

    def cube_peer(yy, xx, cc):
        return {"dp": group * CUBE + yy * 4 + xx * 2 + cc}

    beside_x = cube_peer(y, 1 - x, core)
    beside_y = cube_peer(1 - y, x, core)
    beside_core = cube_peer(y, x, 1 - core)
    others = [{"section": lax.rem(me + step, sections)} for step in range(1, sections)]

    def replica(step):
        return {"dp": lax.rem(index + step, replicas)}

    barrier = pltpu.get_barrier_semaphore()
    for other in others:
        pl.semaphore_signal(barrier, inc=1, device_id=other, device_id_type=MESH)

    @pl.loop(1, replicas)
    def _(step):
        pl.semaphore_signal(barrier, inc=1, device_id=replica(step), device_id_type=MESH)

    own_part, guest_part = pl.ds(0, micro_rows), pl.ds(micro_rows, micro_rows)

    def load_rows(place):
        source, target = ((tokens, token_rows), (cotangent, cot_rows))[place]
        return pltpu.make_async_copy(source, target.at[own_part], rows_load.at[place])

    load_rows(0).start()
    load_rows(1).start()

    def load(block):
        if block < 8:
            source = wide.at[:, :, :, :, pl.ds((block % 4) * D, D)]
        else:
            source = half.at[block % 2]
        return pltpu.make_async_copy(source, blocks.at[block], load_sem.at[block])

    def flat_rows(place):
        return pl.ds(place * D, D)

    def load_own(place):
        if place < 4:
            source = wide_flat.at[:, pl.ds(place * D, D)]
        else:
            source = half_flat.at[flat_rows(place - 4)]
        return pltpu.make_async_copy(source, flat.at[flat_rows(place)], load_sem.at[place])

    for holder in (0, 1):

        @pl.when(me == holder)
        def _():
            for block in OWN[holder]:
                load(block).start()

    @pl.when(me >= 2)
    def _():
        for place in range(4):
            load_own(place).start()

    def load_upper(block):
        return pltpu.make_async_copy(
            half.at[block], core_in.at[pl.ds(2 * block, 2)], load_sem.at[REDUCED + block]
        )

    @pl.when(me == 2)
    def _():
        for block in range(2):
            load_upper(block).start()

    @pl.when(me == 3)
    def _():
        for place in (4, 5):
            load_own(place).start()

    pl.semaphore_wait(barrier, sections - 1 + replicas - 1)

    def guest_copy(kind):
        down = {"section": lax.rem(me + sections - 2, sections)}
        up = {"section": lax.rem(me + 2, sections)}
        source, target, device = (
            (token_rows.at[own_part], token_rows.at[guest_part], down),
            (cot_rows.at[own_part], cot_rows.at[guest_part], down),
            (out_rows.at[guest_part], out_rows.at[own_part], up),
            (h1.at[guest_part], h1.at[own_part], up),
        )[kind]
        return remote(source, target, guest_send.at[kind], guest_recv.at[kind], device)

    TOKENS, COTANGENT, OUT, GRAD = 0, 1, 2, 3

    load_rows(0).wait()
    load_rows(1).wait()

    @pl.when(me >= 2)
    def _():
        guest_copy(TOKENS).start()

    row_of = lax.broadcasted_iota(jnp.int32, (SLAB, D), 0)

    def lead_rows(ref, count):
        value = jnp.zeros((SLAB, D), F32)
        for lead in range(count):
            row = ref[lead * seg_rows : lead * seg_rows + SLAB].astype(F32)[0:1]
            value = jnp.where(row_of == lead, row, value)
        return value.astype(LOW)

    def lead_copy(kind, slab, target, reader):
        return remote(
            slab, target.at[me], lead_send.at[kind], lead_recv.at[kind, me], {"section": reader}
        )

    def lead_start(kind, slab, target, reader):
        @pl.when(me != reader)
        def _():
            lead_copy(kind, slab, target, reader).start()

        @pl.when(me == reader)
        def _():
            target[reader] = slab[...]

    def lead_wait(kind, slab, target, reader, senders):
        for section in range(senders):
            if section != reader:
                remote(
                    slab, target.at[section], lead_send.at[kind], lead_recv.at[kind, section],
                    {"section": section},
                ).wait_recv()

    def collected(target, senders):
        value = jnp.zeros((SLAB, D), F32)
        for section in range(senders):
            slab = target[section].astype(F32)
            for micro in range(section, sections, senders):
                for lead in range(2):
                    place = (micro - section) // senders * 2 + lead
                    value = jnp.where(
                        row_of == 2 * micro + lead, slab[place : place + 1], value
                    )
        return value

    def spread_copy(kind, slab, step):
        return remote(
            slab, slab, spread_send.at[kind, step], spread_recv.at[kind], others[step - 1]
        )

    def hop_copy(kind, slab, step):
        return remote(
            slab, slab, hop_send.at[kind], hop_recv.at[kind],
            {"section": lax.rem(me + step + sections, sections)},
        )

    def leads_of(slab, micro):
        value = slab[...].astype(F32)
        return [
            jnp.sum(jnp.where(row_of == 2 * micro + lead, value, 0.0), axis=0, keepdims=True)
            for lead in range(2)
        ]

    COT, H1, H2 = 0, 1, 2
    FOURTH = 0
    THIRD, GRAD3, GRAD2, HAND, GRAD1 = 0, 1, 2, 3, 4

    def vector_copy(step):
        return remote(
            vectors.at[me], vectors.at[me], vector_send.at[step], vector_recv.at[step],
            others[step - 1],
        )

    vectors[me, 0:1] = norm_gain[...]
    vectors[me, 1:2] = norm_bias[...]
    for step in range(1, sections):
        vector_copy(step).start()
    cot_slab[...] = lead_rows(cot_rows, 2)
    lead_start(COT, cot_slab, cot_leads, 3)

    upper, lower = pl.ds(0, HALF), pl.ds(HALF, HALF)

    def lanes_of(turn):
        return pl.ds((turn % 2) * WIDTH, WIDTH)

    def turns(*order):
        return tuple(2 * block + side for block in order for side in range(2))

    def place_of(block):
        if block < REDUCED:
            return blocks.at[block]
        return core_in.at[pl.ds(2 * (block - REDUCED), 2)]

    def line_copy(turn, reader):
        block, lanes = turn // 2, lanes_of(turn)
        piece = place_of(block).at[y, x, core, :, lanes]
        return remote(
            piece,
            piece,
            line_send.at[turn],
            line_recv.at[turn],
            {"section": reader},
        )

    def cube_copy(turn, stage):
        full, lanes = place_of(turn // 2), lanes_of(turn)
        ref, peer = (
            (full.at[y, x, core, upper, lanes], beside_x),
            (full.at[y, x, core, lower, lanes], beside_y),
            (full.at[y, :, core, upper, lanes], beside_y),
            (full.at[:, x, core, lower, lanes], beside_x),
            (full.at[:, :, core, :, lanes], beside_core),
        )[stage]
        slot = SLOT[turn]
        return remote(ref, ref, cube_send.at[slot, stage], cube_recv.at[slot, stage], peer)

    def gather_line(turn, reader):
        @pl.when(me == reader)
        def _():
            line_copy(turn, reader).wait_recv()
            cube_copy(turn, 0).start()
            cube_copy(turn, 1).start()

    def gather_two(turn, reader):
        @pl.when(me == reader)
        def _():
            cube_copy(turn, 0).wait()
            cube_copy(turn, 2).start()
            cube_copy(turn, 1).wait()
            cube_copy(turn, 3).start()

    def gather_three(turn, reader):
        @pl.when(me == reader)
        def _():
            cube_copy(turn, 2).wait()
            cube_copy(turn, 3).wait()
            cube_copy(turn, 4).start()

    def gather_ready(turn, reader):
        @pl.when(me == reader)
        def _():
            cube_copy(turn, 4).wait()

    def gather_finish(turn, reader):
        @pl.when(me == HOLDER[turn // 2])
        def _():
            line_copy(turn, reader).wait_send()

    def gather_send():
        for reader, wanted in WANTED.items():

            @pl.when(me == HOLDER[wanted[0]])
            def _():
                for turn in turns(*wanted):
                    line_copy(turn, reader).start()

    gather_plan = ((gather_ready, 6), (gather_three, 4), (gather_two, 2), (gather_line, 0))
    gather_ticks = 2 * OWNED + gather_plan[0][1]

    def gather_tick(tick):
        for stage, offset in gather_plan:
            at = tick - offset
            for reader, wanted in WANTED.items():
                if 0 <= at < 2 * len(wanted):
                    stage(2 * wanted[at // 2] + at % 2, reader)

    def gather_wait_own():
        @pl.when(me == 2)
        def _():
            for block in range(2):
                load_upper(block).wait()

        for holder in (0, 1):

            @pl.when(me == holder)
            def _():
                for block in OWN[holder]:
                    load(block).wait()

    def worker(step):
        def run(*given):
            @pl.when(works)
            def _():
                step(*given)

        return run

    def weight(block):
        return blocks[block].reshape(D, D)

    def act_rows(block):
        return pl.ds(pl.multiple_of(block * rows_all, SLAB), rows_all)

    def slope_rows(block):
        return pl.ds(pl.multiple_of((4 + block) * rows_all, SLAB), rows_all)

    lane_of = lax.broadcasted_iota(jnp.int32, (1, 128), 1)
    first_half = lane_of < 64
    head_masks = (first_half.astype(LOW), (~first_half).astype(LOW))
    segs = range(4)

    def chunks(size, body):
        @pl.loop(0, rows_all // size)
        def _(step):
            body(pl.multiple_of(step * size, size), size)

    @worker
    def project(block):
        qkv[:, block * D : (block + 1) * D] = dot(token_rows[...], weight(block)).astype(LOW)

    def seg_slice(seg):
        return pl.ds(seg * seg_rows, seg_rows)

    def pair_lanes(pair):
        return [pl.ds(pl.multiple_of(part * D + pair * 128, 128), 128) for part in range(3)]

    def softmax(scores):
        raised = jnp.exp(scores - jnp.max(scores, axis=-1, keepdims=True))
        return raised / jnp.sum(raised, axis=-1, keepdims=True)

    @worker
    def heads_forward(first, last):
        @pl.loop(first, last)
        def _(pair):
            at_q, at_k, at_v = pair_lanes(pair)
            heads = [(seg, place) for seg in segs for place in range(2)]
            scores = [
                dot_right(qkv[seg_slice(seg), at_q] * head_masks[place], qkv[seg_slice(seg), at_k])
                * 0.125
                for seg, place in heads
            ]
            found = [softmax(score) for score in scores]
            for (seg, place), prob in zip(heads, found):
                probs[seg, pair, place] = prob
            mixed = [
                dot(prob.astype(LOW), qkv[seg_slice(seg), at_v])
                for (seg, place), prob in zip(heads, found)
            ]
            for seg in segs:
                context[seg_slice(seg), at_q] = jnp.where(
                    first_half, mixed[2 * seg], mixed[2 * seg + 1]
                ).astype(LOW)

    @worker
    def attention_close():
        summed[...] = dot_right(context[...], weight(3))
        gain, bias = vectors[0, 0:1], vectors[0, 1:2]

        def body(start, size):
            rows = pl.ds(start, size)
            out, normed, inv_dev = normalize(
                token_rows[rows].astype(F32) + summed[rows], gain, bias
            )
            norm0[rows] = normed
            dev0[rows] = jnp.broadcast_to(inv_dev, (size, 128))
            h1[rows] = out.astype(LOW)

        chunks(32, body)
        h1_slab[...] = lead_rows(h1, 4)
        lead_start(H1, h1_slab, h1_leads, 1)

    @worker
    def inner_block(block):
        summed[...] = dot(h1[...], weight(4 + block))

        def body(start, size):
            value, grade = gelu_pair(summed[pl.ds(start, size)])
            flat[pl.ds(block * rows_all + start, size)] = value.astype(LOW)
            flat[pl.ds((4 + block) * rows_all + start, size)] = grade.astype(LOW)

        chunks(32, body)

    @worker
    def second_block(place):
        block = lax.rem(2 * me + place, 4)
        product = dot(flat[act_rows(block)], weight(8 + block))
        if place == 0:
            branch[...] = product
        else:
            branch[...] += product

    @worker
    def mlp_close():
        gain, bias = vectors[1, 0:1], vectors[1, 1:2]

        def body(start, size):
            rows = pl.ds(start, size)
            out, normed, inv_dev = normalize(h1[rows].astype(F32) + branch[rows], gain, bias)
            norm1[rows] = normed
            dev1[rows] = jnp.broadcast_to(inv_dev, (size, 128))
            out_rows[rows] = out.astype(LOW)

        chunks(32, body)
        h2_slab[...] = lead_rows(out_rows, 4)
        lead_start(H2, h2_slab, h2_leads, 2)

    @worker
    def rows_leave():
        guest_copy(OUT).start()

    def add_small(row, value):
        small[row : row + 1] += value

    @worker
    def mlp_open_backward():
        gain = vectors[1, 0:1]

        def body(start, size):
            rows = pl.ds(start, size)
            place = start + lax.broadcasted_iota(jnp.int32, (size, D), 0)
            grad = jnp.where(lax.rem(place, seg_rows) == 0, 0.0, cot_rows[rows].astype(F32))
            grad_sum, grad_gain, grad_bias = normalize_backward(
                grad, norm1[rows], dev1[rows][:, 0:1], gain
            )
            branch[rows] = grad_sum
            kept[rows] = grad_sum.astype(LOW)
            add_small(2, grad_gain)
            add_small(3, grad_bias)

        chunks(32, body)

    def part(block):
        return block + 4 if block < 4 else block + 8

    def store_part(block, left, right):
        for strip in range(2):
            lanes = slice(strip * WIDTH, (strip + 1) * WIDTH)
            blocks[part(block), strip] = (
                outer(left[:, lanes], right).astype(LOW).reshape(2, 2, PIECE, D)
            )

    @worker
    def second_grad(block):
        store_part(8 + block, flat[act_rows(block)], kept[...])

    @worker
    def inner_grad(block):
        grad_act = dot_right(kept[...], weight(8 + block))
        grad_inner = (grad_act * flat[slope_rows(block)].astype(F32)).astype(LOW)
        flat[act_rows(block)] = grad_inner
        branch[...] += dot_right(flat[act_rows(block)], weight(4 + block))
        store_part(4 + block, h1[...], flat[act_rows(block)])

    @worker
    def attention_open_backward():
        gain = vectors[0, 0:1]
        leads = leads_of(lead_grad1, me) + leads_of(lead_grad1, me + 2)

        def body(start, size):
            rows = pl.ds(start, size)
            place = start + lax.broadcasted_iota(jnp.int32, (size, D), 0)
            grad = branch[rows]
            for lead in range(4):
                grad = jnp.where(place == lead * seg_rows, leads[lead], grad)
            grad = grad.astype(LOW).astype(F32)
            grad_sum, grad_gain, grad_bias = normalize_backward(
                grad, norm0[rows], dev0[rows][:, 0:1], gain
            )
            summed[rows] = grad_sum
            kept[rows] = grad_sum.astype(LOW)
            add_small(0, grad_gain)
            add_small(1, grad_bias)

        chunks(32, body)

    @worker
    def out_grad():
        store_part(3, kept[...], context[...])
        context[...] = dot(kept[...], weight(3)).astype(LOW)

    @worker
    def heads_backward(first, last):
        @pl.loop(first, last)
        def _(pair):
            at_q, at_k, at_v = pair_lanes(pair)
            heads = [(seg, place) for seg in segs for place in range(2)]
            grad_probs = [
                dot_right(
                    context[seg_slice(seg), at_q] * head_masks[place], qkv[seg_slice(seg), at_v]
                )
                for seg, place in heads
            ]
            grad_scores = []
            for (seg, place), grad_prob in zip(heads, grad_probs):
                prob = probs[seg, pair, place]
                inside = prob * grad_prob
                grad_score = inside - prob * jnp.sum(inside, axis=-1, keepdims=True)
                grad_scores.append(grad_score.astype(LOW))
            for seg in segs:
                rows = seg_slice(seg)
                query, key, grad = qkv[rows, at_q], qkv[rows, at_k], context[rows, at_q]
                mine = grad_scores[2 * seg : 2 * seg + 2]
                found = [probs[seg, pair, place].astype(LOW) for place in range(2)]
                for at, both, scale in (
                    (at_q, [dot(score, key) for score in mine], 0.125),
                    (at_k, [outer(score, query) for score in mine], 0.125),
                    (at_v, [outer(prob, grad) for prob in found], 1.0),
                ):
                    merged = jnp.where(first_half, both[0], both[1]) * scale
                    qkv[rows, at] = merged.astype(LOW)

    @worker
    def project_grad(block):
        store_part(block, token_rows[...], qkv[:, block * D : (block + 1) * D])

    @worker
    def tokens_back(block):
        summed[...] += dot_right(qkv[:, block * D : (block + 1) * D], weight(block))

    @worker
    def tokens_close():
        h1[...] = summed[...].astype(LOW)
        guest_copy(GRAD).start()

    def leads_mlp_forward(value, first, second, gain, bias):
        total_branch = value.astype(F32)
        for block in range(4):
            lanes = slice(block * D, (block + 1) * D)
            out, grade = gelu_pair(dot(value, first(block)))
            lead_act[:, lanes] = out.astype(LOW)
            lead_slope[:, lanes] = grade
            total_branch = total_branch + dot(lead_act[:, lanes], second(block))
        out, normed, inv_dev = normalize(total_branch, gain, bias)
        lead_norm[...] = normed
        lead_dev[...] = jnp.broadcast_to(inv_dev, (SLAB, 128))
        pack[:, 0:D] = value
        pack[:, LEFT_OUT:RIGHT] = value
        return out

    def leads_mlp_backward(grad, first, second, gain):
        grad_sum, grad_gain, grad_bias = normalize_backward(
            grad, lead_norm[...], lead_dev[:, 0:1], gain
        )
        add_small(4, grad_gain)
        add_small(5, grad_bias)
        low_sum = grad_sum.astype(LOW)
        result = grad_sum
        for block in range(4):
            lanes = slice(block * D, (block + 1) * D)
            grad_inner = (dot_right(low_sum, second(block)) * lead_slope[:, lanes]).astype(LOW)
            pack[:, RIGHT + block * D : RIGHT + (block + 1) * D] = grad_inner
            result = result + dot_right(grad_inner, first(block))
        pack[:, LEFT_HALF:RIGHT_HALF] = lead_act[:, 2 * D :]
        pack[:, RIGHT_HALF:] = low_sum
        handed[:, 0 : 2 * D] = lead_act[:, 0 : 2 * D]
        handed[:, 2 * D :] = low_sum
        return result

    def own_weight(place):
        return flat[flat_rows(place)]

    def last_second(block):
        if block >= 2:
            return own_weight(2 + block)
        return core_in[2 * block : 2 * block + 2].reshape(D, D)

    def leads_first():
        @pl.when(me == 2)
        def _():
            lead_wait(H2, h2_slab, h2_leads, 2, 2)
            for place in range(4):
                load_own(place).wait()
            value = collected(h2_leads, 2).astype(LOW)
            pack[:, 0:D] = value
            for block in range(3):
                lead_qkv[:, block * D : (block + 1) * D] = dot(value, own_weight(block)).astype(LOW)
            docs = seg_doc[...]
            row, column = (lax.broadcasted_iota(jnp.int32, (SLAB, SLAB), i) for i in range(2))
            sort = jnp.where(row == column, 2.0, 0.0)
            for micro in range(seg_doc.shape[0]):
                pair_sort = jnp.where(
                    docs[micro : micro + 1, 0:1] == docs[micro : micro + 1, 1:2], 2.0, 1.0
                )
                near = (row // 2 == micro) & (column // 2 == micro) & (row != column)
                sort = jnp.where(near, pair_sort, sort)
            for pair in range(PAIRS):
                at = [slice(p * D + pair * 128, p * D + (pair + 1) * 128) for p in range(3)]
                query, key, val = (lead_qkv[:, lanes] for lanes in at)
                parts = []
                for place in range(2):
                    scores = dot_right(query * head_masks[place], key) * 0.125
                    scores = jnp.where(
                        sort > 1.5, scores, jnp.where(sort > 0.5, -1000000000.0, -1e30)
                    )
                    raised = jnp.exp(scores - jnp.max(scores, axis=-1, keepdims=True))
                    prob = raised / jnp.sum(raised, axis=-1, keepdims=True)
                    lead_probs[pair, place] = prob
                    parts.append(dot(prob.astype(LOW), val))
                lead_context[:, pair * 128 : (pair + 1) * 128] = jnp.where(
                    first_half, parts[0], parts[1]
                ).astype(LOW)
            summed_rows = value.astype(F32) + dot_right(lead_context[...], own_weight(3))
            out, normed, inv_dev = normalize(summed_rows, vectors[2, 0:1], vectors[2, 1:2])
            lead_norm[...] = normed
            lead_dev[...] = jnp.broadcast_to(inv_dev, (SLAB, 128))
            lead_third[...] = out.astype(LOW)
            hop_copy(THIRD, lead_third, 1).start()

        @pl.when(me == 1)
        def _():
            lead_wait(H1, h1_slab, h1_leads, 1, 2)
            leads_mlp_forward(
                collected(h1_leads, 2).astype(LOW),
                lambda block: weight(4 + block),
                lambda block: weight(8 + block),
                vectors[1, 0:1],
                vectors[1, 1:2],
            )

    def leads_second():
        @pl.when(me == 3)
        def _():
            hop_copy(THIRD, lead_third, -1).wait_recv()
            for place in range(6):
                load_own(place).wait()
            out = leads_mlp_forward(
                lead_third[...], own_weight, last_second, vectors[3, 0:1], vectors[3, 1:2]
            )
            lead_fourth[...] = out.astype(LOW)
            for step in range(1, sections):
                spread_copy(FOURTH, lead_fourth, step).start()
            lead_wait(COT, cot_slab, cot_leads, 3, sections)
            grad = leads_mlp_backward(
                collected(cot_leads, sections), own_weight, last_second, vectors[3, 0:1]
            )
            lead_grad3[...] = grad.astype(LOW)
            hop_copy(GRAD3, lead_grad3, -1).start()
            hop_copy(HAND, handed, -1).start()

    def leads_third():
        @pl.when(me == 2)
        def _():
            hop_copy(GRAD3, lead_grad3, 1).wait_recv()
            grad_sum, grad_gain, grad_bias = normalize_backward(
                lead_grad3[...].astype(F32), lead_norm[...], lead_dev[:, 0:1], vectors[2, 0:1]
            )
            add_small(4, grad_gain)
            add_small(5, grad_bias)
            low_sum = grad_sum.astype(LOW)
            pack[:, LEFT_OUT:RIGHT] = low_sum
            pack[:, RIGHT + 3 * D : LEFT_HALF] = lead_context[...]
            grad_context = dot(low_sum, own_weight(3)).astype(LOW)
            for pair in range(PAIRS):
                at = [slice(p * D + pair * 128, p * D + (pair + 1) * 128) for p in range(3)]
                query, key, val = (lead_qkv[:, lanes] for lanes in at)
                grad = grad_context[:, pair * 128 : (pair + 1) * 128]
                grads = ([], [], [])
                for place in range(2):
                    prob = lead_probs[pair, place]
                    grad_prob = dot_right(grad * head_masks[place], val)
                    inside = prob * grad_prob
                    grad_score = inside - prob * jnp.sum(inside, axis=-1, keepdims=True)
                    grad_score = grad_score.astype(LOW)
                    grads[0].append(dot(grad_score, key))
                    grads[1].append(outer(grad_score, query))
                    grads[2].append(outer(prob.astype(LOW), grad))
                for lanes, pair_grads, scale in zip(at, grads, (0.125, 0.125, 1.0)):
                    merged = jnp.where(first_half, pair_grads[0], pair_grads[1]) * scale
                    pack[:, RIGHT + lanes.start : RIGHT + lanes.stop] = merged.astype(LOW)
            result = grad_sum
            for block in range(3):
                result = result + dot_right(
                    pack[:, RIGHT + block * D : RIGHT + (block + 1) * D], own_weight(block)
                )
            lead_grad2[...] = result.astype(LOW)
            hop_copy(GRAD2, lead_grad2, -1).start()
            hop_copy(HAND, handed, 1).wait_recv()
            pack[:, LEFT_HALF:] = handed[...]

    def leads_fourth():
        @pl.when(me == 1)
        def _():
            hop_copy(GRAD2, lead_grad2, 1).wait_recv()
            grad = leads_mlp_backward(
                lead_grad2[...].astype(F32),
                lambda block: weight(4 + block),
                lambda block: weight(8 + block),
                vectors[1, 0:1],
            )
            lead_grad1[...] = grad.astype(LOW)
            hop_copy(GRAD1, lead_grad1, -1).start()
            hop_copy(HAND, handed, -1).start()

    half_lanes = pl.ds(pl.multiple_of(core * HALF_PACK, 128), HALF_PACK)
    other_lanes = pl.ds(pl.multiple_of((1 - core) * HALF_PACK, 128), HALF_PACK)
    first_peer = {"dp": group * CUBE + (y + core - 2 * y * core) * 4
                  + (x + (1 - core) * (1 - 2 * x)) * 2 + core}
    second_peer = {"dp": group * CUBE + (y + (1 - core) * (1 - 2 * y)) * 4
                   + (x + core - 2 * x * core) * 2 + core}

    def pack_copy(stage):
        chip = y * 2 + x
        first_chip = (y + core - 2 * y * core) * 2 + x + (1 - core) * (1 - 2 * x)
        if stage == 0:
            source, target, peer = pack.at[:, other_lanes], pack_in, beside_core
        elif stage == 1:
            source = target = factors.at[chip, :, half_lanes]
            peer = first_peer
        elif stage == 2:
            source = target = factors.at[chip, :, half_lanes]
            peer = second_peer
        elif stage == 3:
            source = target = factors.at[first_chip, :, half_lanes]
            peer = second_peer
        else:
            source = target = factors.at[:, :, half_lanes]
            peer = beside_core
        return remote(source, target, pack_send.at[stage], pack_recv.at[stage], peer)

    def pack_join():
        pack_copy(0).wait()

        @pl.loop(0, HALF_PACK // WIDTH)
        def _(step):
            start = pl.multiple_of(step * WIDTH, 128)
            lanes = pl.ds(pl.multiple_of(core * HALF_PACK + start, 128), WIDTH)
            mine = pack[:, lanes].astype(F32)[0:8]
            theirs = pack_in[:, pl.ds(start, WIDTH)].astype(F32)[0:8]
            low_rows = jnp.where(core == 0, mine, theirs)
            high_rows = jnp.where(core == 0, theirs, mine)
            factors[y * 2 + x, :, lanes] = jnp.concatenate([low_rows, high_rows]).astype(LOW)

        pack_copy(1).start()

    def pack_second():
        pack_copy(1).wait()
        pack_copy(2).start()
        pack_copy(3).start()

    def pack_third():
        pack_copy(2).wait()
        pack_copy(3).wait()
        pack_copy(4).start()

    def to_packs(step):
        return remote(
            factors, packs.at[group], group_pack_send.at[step], group_pack_recv.at[step],
            {"dp": lax.rem(index + step * CUBE, replicas)},
        )

    def own_pack():
        return pltpu.make_async_copy(factors, packs.at[group], group_pack_send.at[0])

    def pack_fourth():
        pack_copy(4).wait()
        own_pack().start()
        for step in range(1, groups):
            to_packs(step).start()

    def pack_last():
        own_pack().wait()
        for step in range(1, groups):
            to_packs(step).wait()

    def rows_store(place):
        source, target = ((out_rows, layer_out), (h1, grad_tokens))[place]
        return pltpu.make_async_copy(source.at[own_part], target, rows_out.at[place])

    def leads_close():
        @pl.when(me != 3)
        def _():
            spread_copy(FOURTH, lead_fourth, 1).wait_recv()

        @pl.when(me >= 2)
        def _():
            guest_copy(OUT).wait_recv()

        leads = leads_of(lead_fourth, me)
        for lead in range(2):
            rows = pl.ds(lead * seg_rows, SLAB)
            out_rows[rows] = jnp.where(
                row_of == 0, leads[lead], out_rows[rows].astype(F32)
            ).astype(LOW)
        rows_store(0).start()

        @pl.when(me == 0)
        def _():
            hop_copy(GRAD1, lead_grad1, 1).wait_recv()
            hop_copy(HAND, handed, 1).wait_recv()
            pack[:, 0:LEFT_HALF] = jnp.zeros((SLAB, LEFT_HALF), LOW)
            pack[:, LEFT_HALF:] = handed[...]

        pack_copy(0).start()

    def add(target, *sources):
        value = target[...].astype(F32)
        for source in sources:
            value = value + source[...].astype(F32)
        target[...] = value.astype(LOW)

    def landing(block):
        return blocks.at[8 + block, 0] if block < 4 else core_in.at[block - 4]

    def scatter(turn, stage):
        slot = SUM_SLOT[turn]
        block, lanes = turn // 2, lanes_of(turn)
        run = blocks.at[part(block)]
        source, target, peer = (
            (run.at[:, :, 1 - core, :, lanes], landing(block).at[:, :, :, lanes], beside_core),
            (run.at[:, 1 - x, core, upper, lanes], one_a.at[slot], beside_x),
            (run.at[1 - y, :, core, lower, lanes], one_b.at[slot], beside_y),
            (run.at[1 - y, x, core, upper, lanes], two_a.at[slot], beside_y),
            (run.at[y, 1 - x, core, lower, lanes], two_b.at[slot], beside_x),
        )[stage]
        if stage == 0:
            return remote(source, target, core_send.at[turn], core_recv.at[turn], peer)
        return remote(source, target, rs_send.at[slot, stage], rs_recv.at[slot, stage], peer)

    def to_line(turn):
        return remote(
            blocks.at[part(turn // 2), y, x, core, :, lanes_of(turn)],
            line_in.at[turn // 2, :, lanes_of(turn)],
            z_send.at[turn],
            z_recv.at[turn],
            {"section": HOLDER[turn // 2]},
        )

    def to_holder(turn):
        place = EARLY_PLACE[turn // 2]
        return remote(
            blocks.at[part(turn // 2), :, :, core, :, lanes_of(turn)],
            early_in.at[place, :, :, :, lanes_of(turn)],
            z_send.at[turn],
            z_recv.at[turn],
            {"section": HOLDER[turn // 2]},
        )

    def to_group(turn, step):
        return remote(
            blocks.at[part(turn // 2), y, x, core, :, lanes_of(turn)],
            group_in.at[turn // 2, step - 1, :, lanes_of(turn)],
            group_send.at[turn, step - 1],
            group_recv.at[turn, step - 1],
            {"dp": lax.rem(index + step * CUBE, replicas)},
        )

    def gather_back(turn, stage):
        slot = BACK_SLOT[turn]
        run, lanes = blocks.at[part(turn // 2)], lanes_of(turn)
        ref, peer = (
            (run.at[y, x, core, upper, lanes], beside_y),
            (run.at[y, x, core, lower, lanes], beside_x),
            (run.at[:, x, core, upper, lanes], beside_x),
            (run.at[y, :, core, lower, lanes], beside_y),
            (run.at[:, :, core, :, lanes], beside_core),
        )[stage]
        return remote(ref, ref, ag_send.at[slot, stage], ag_recv.at[slot, stage], peer)

    def write_out(block):
        place = OWN[HOLDER[block]].index(block)
        return pltpu.make_async_copy(
            blocks.at[part(block)], total.at[place], out_sem.at[place]
        )

    @worker
    def reduce_core(block):
        scatter(2 * block, 0).start()
        scatter(2 * block + 1, 0).start()

    def is_early(turn):
        return turn // 2 in EARLY

    def in_plane(turn):
        return me == HOLDER[turn // 2] if is_early(turn) else works

    def add_four(turn, source):
        for yy in range(2):
            for xx in range(2):
                add(
                    blocks.at[part(turn // 2), yy, xx, core, :, lanes_of(turn)],
                    source.at[yy, xx, :, lanes_of(turn)],
                )

    def reduce_one(turn):
        @pl.when(works)
        def _():
            scatter(turn, 0).wait()
            add_four(turn, landing(turn // 2))
            if not is_early(turn):
                scatter(turn, 1).start()
                scatter(turn, 2).start()

        if is_early(turn):

            @pl.when(me == 1 - HOLDER[turn // 2])
            def _():
                to_holder(turn).start()

    def reduce_early(turn):
        @pl.when(me == HOLDER[turn // 2])
        def _():
            to_holder(turn).wait_recv()
            add_four(turn, early_in.at[EARLY_PLACE[turn // 2]])
            scatter(turn, 1).start()
            scatter(turn, 2).start()

    def reduce_two(turn):
        @pl.when(in_plane(turn))
        def _():
            reduce_two_now(turn)

    def reduce_two_now(turn):
        block, lanes = turn // 2, lanes_of(turn)
        run = blocks.at[part(block)]
        scatter(turn, 1).wait()
        for yy in range(2):
            add(run.at[yy, x, core, upper, lanes], one_a.at[SUM_SLOT[turn], yy])
        scatter(turn, 3).start()
        scatter(turn, 2).wait()
        for xx in range(2):
            add(run.at[y, xx, core, lower, lanes], one_b.at[SUM_SLOT[turn], xx])
        scatter(turn, 4).start()

    def reduce_three(turn):
        @pl.when(in_plane(turn))
        def _():
            reduce_three_now(turn)

        @pl.when(me == HOLDER[turn // 2])
        def _():
            for clear, peer in ((clear_y, beside_y), (clear_x, beside_x)):
                pl.semaphore_signal(clear, inc=1, device_id=peer, device_id_type=MESH)

        if not is_early(turn):

            @pl.when(me == 1 - HOLDER[turn // 2])
            def _():
                to_line(turn).start()

    def reduce_three_now(turn):
        block, lanes = turn // 2, lanes_of(turn)
        run = blocks.at[part(block)]
        scatter(turn, 3).wait()
        add(run.at[y, x, core, upper, lanes], two_a.at[SUM_SLOT[turn]])
        scatter(turn, 4).wait()
        add(run.at[y, x, core, lower, lanes], two_b.at[SUM_SLOT[turn]])
        if groups > 1:
            for step in range(1, groups):
                to_group(turn, step).start()
            for step in range(1, groups):
                to_group(turn, step).wait()
            for step in range(1, groups):
                copy = pltpu.make_async_copy(
                    group_in.at[block, step - 1, :, lanes], group_piece, group_load
                )
                copy.start()
                copy.wait()
                add(run.at[y, x, core, :, lanes], group_piece)

    def spread_one(turn):
        pl.semaphore_wait(clear_y, 1)
        gather_back(turn, 0).start()
        pl.semaphore_wait(clear_x, 1)
        gather_back(turn, 1).start()

    def spread_early(turn):
        @pl.when(me == HOLDER[turn // 2])
        def _():
            spread_one(turn)

    def reduce_line(turn):
        @pl.when(me == HOLDER[turn // 2])
        def _():
            block, lanes = turn // 2, lanes_of(turn)
            to_line(turn).wait_recv()
            add(blocks.at[part(block), y, x, core, :, lanes], line_in.at[block, :, lanes])
            spread_one(turn)

    def spread_two(turn):
        @pl.when(me == HOLDER[turn // 2])
        def _():
            gather_back(turn, 0).wait()
            gather_back(turn, 2).start()
            gather_back(turn, 1).wait()
            gather_back(turn, 3).start()

    def spread_core(turn):
        @pl.when(me == HOLDER[turn // 2])
        def _():
            gather_back(turn, 2).wait()
            gather_back(turn, 3).wait()
            gather_back(turn, 4).start()

    def spread_done(turn):
        @pl.when(me == HOLDER[turn // 2])
        def _():
            gather_back(turn, 4).wait()
            if turn % 2 == 1:
                write_out(turn // 2).start()

        @pl.when(me == 1 - HOLDER[turn // 2])
        def _():
            (to_holder if is_early(turn) else to_line)(turn).wait_send()

    late_stages = (
        reduce_one, reduce_two, reduce_three, reduce_line, spread_two, spread_core, spread_done,
    )
    early_stages = (
        reduce_one, reduce_early, reduce_two, reduce_three, spread_early, spread_two, spread_core,
        spread_done,
    )

    class Wave:
        def __init__(self, order, spacing, early_at):
            self.order, self.at = turns(*order), 0
            late = range(1, 1 + 7 * spacing, spacing)
            early = (1,) + tuple(range(early_at, early_at + 7 * spacing, spacing))
            self.plans = [
                tuple(zip(early_stages, early) if is_early(turn) else zip(late_stages, late))
                for turn in self.order
            ]
            self.last = max(i + plan[-1][1] for i, plan in enumerate(self.plans))

        def tick(self, count=1):
            for _ in range(count):
                due = []
                for place, turn in enumerate(self.order):
                    for stage, offset in self.plans[place]:
                        if place + offset == self.at:
                            due.append((offset, stage, turn))
                for _, stage, turn in sorted(due, key=lambda item: -item[0]):
                    stage(turn)
                self.at += 1

        def left(self):
            return self.at <= self.last

    one, two = (Wave(*given) for given in zip(WAVES, SPACING, EARLY_AT))

    small[...] = jnp.zeros_like(small)

    gather_wait_own()
    gather_send()

    @pl.when(me >= 2)
    def _():
        guest_copy(TOKENS).wait_send()
        guest_copy(COTANGENT).start()

    for tick in range(gather_ticks):
        gather_tick(tick)
        at = tick - gather_plan[0][1]
        if at == 0:
            for step in range(1, sections):
                vector_copy(step).wait()
        if at < 0:
            continue
        if at == 1:

            @pl.when(works)
            def _():
                guest_copy(TOKENS).wait_recv()

        if at % 2 == 1 and at < 6:
            project(at // 2)
        if at == 5:
            heads_forward(0, 2)
        if at == 6:
            heads_forward(2, 4)
        if at == 7:
            heads_forward(4, 6)
            attention_close()
        if at >= 8:
            inner_block(at - 8)
    for place in range(4):
        second_block(place)
    mlp_close()

    @pl.when(works)
    def _():
        guest_copy(COTANGENT).wait_recv()

    mlp_open_backward()
    for reader, wanted in WANTED.items():
        for turn in turns(*wanted):
            gather_finish(turn, reader)

    for block in range(4):
        second_grad(block)
        reduce_core(8 + block)
    one.tick(5)
    for block in range(2):
        inner_grad(block)
        reduce_core(4 + block)
    leads_first()
    one.tick(4)
    for block in range(2, 4):
        inner_grad(block)
        reduce_core(4 + block)
    leads_second()
    rows_leave()
    one.tick(4)
    leads_third()
    one.tick(4)
    leads_fourth()

    @pl.when(works)
    def _():
        pl.semaphore_signal(credit, inc=1, device_id=beside_core, device_id_type=MESH)

    leads_close()
    attention_open_backward()
    out_grad()

    @pl.when(works)
    def _():
        pl.semaphore_wait(credit, 1)

    reduce_core(3)
    one.tick(4)
    heads_backward(0, 2)
    two.tick(2)
    heads_backward(2, 4)
    one.tick()
    two.tick()
    heads_backward(4, 6)
    one.tick()
    pack_join()
    for block in range(3):
        project_grad(block)
        reduce_core(block)
        one.tick()
        two.tick(2)
        if block == 1:
            pack_second()

    def small_copy(step):
        return remote(
            small, small_all.at[index], small_send.at[step], small_recv.at[step], replica(step)
        )

    def sum_copy(step):
        return remote(
            small_sum, smalls.at[me], sum_send.at[step], sum_recv.at[step], others[step - 1]
        )

    def own_sum():
        return pltpu.make_async_copy(small_sum, smalls.at[me], sum_send.at[0])

    @pl.loop(1, replicas)
    def _(step):
        small_copy(step).start()

    small_all[index] = small[...]
    for block in range(3):
        tokens_back(block)
        one.tick()
        two.tick()
    tokens_close()
    pack_third()

    @pl.loop(1, replicas)
    def _(step):
        small_copy(step).wait()

    small_sum[...] = jnp.sum(small_all[...], axis=0)
    for place in range(1, sections):
        sum_copy(place).start()
    own_sum().start()
    pack_fourth()
    while one.left() or two.left():
        if one.left():
            one.tick()
        if two.left():
            two.tick()

    for place in range(1, sections):
        sum_copy(place).wait()
    own_sum().wait()
    pack_last()

    for holder in (0, 1):

        @pl.when(me == holder)
        def _():
            for block in OWN[holder]:
                write_out(block).wait()

    @pl.when(me != 3)
    def _():
        lead_copy(COT, cot_slab, cot_leads, 3).wait_send()

    @pl.when(me == 0)
    def _():
        lead_copy(H1, h1_slab, h1_leads, 1).wait_send()

    @pl.when(works)
    def _():
        lead_copy(H2, h2_slab, h2_leads, 2).wait_send()
        guest_copy(OUT).wait_send()
        guest_copy(GRAD).wait_send()

    @pl.when(me >= 2)
    def _():
        guest_copy(COTANGENT).wait_send()
        guest_copy(GRAD).wait_recv()

    rows_store(1).start()
    rows_store(1).wait()
    rows_store(0).wait()

    @pl.when(me == 1)
    def _():
        hop_copy(GRAD1, lead_grad1, -1).wait_send()
        hop_copy(HAND, handed, -1).wait_send()

    @pl.when(me == 2)
    def _():
        hop_copy(THIRD, lead_third, 1).wait_send()
        hop_copy(GRAD2, lead_grad2, -1).wait_send()

    @pl.when(me == 3)
    def _():
        for place in range(1, sections):
            spread_copy(FOURTH, lead_fourth, place).wait_send()
        hop_copy(GRAD3, lead_grad3, -1).wait_send()
        hop_copy(HAND, handed, -1).wait_send()


def run_layers(sections, replicas, tokens, cotangent, seg_doc, gain, bias, wide, half):
    groups = replicas // CUBE
    rows = 2 * tokens.shape[0]
    seg_rows = tokens.shape[0] // 2
    vector = (8, D)
    block = (2, 2, 2, PIECE, D)
    reduced_groups = max(groups - 1, 1)
    in_vmem = pl.BlockSpec(memory_space=pltpu.VMEM)
    anywhere = pl.BlockSpec(memory_space=pl.ANY)
    slab = pltpu.VMEM((SLAB, D), LOW)
    leads = pltpu.VMEM((sections, SLAB, D), LOW)
    low_rows = pltpu.VMEM((rows, D), LOW)
    full_rows = pltpu.VMEM((rows, D), F32)
    return pl.pallas_call(
        partial(layer_kernel, sections, replicas),
        out_shape=(
            jax.ShapeDtypeStruct(tokens.shape, LOW),
            jax.ShapeDtypeStruct(tokens.shape, LOW),
            jax.ShapeDtypeStruct((OWNED,) + block, LOW),
            jax.ShapeDtypeStruct((groups, CUBE // 2, SLAB, PACK), LOW),
            jax.ShapeDtypeStruct((sections,) + vector, F32),
            jax.ShapeDtypeStruct(
                (REDUCED if groups > 1 else 1, reduced_groups, PIECE, D), LOW
            ),
        ),
        in_specs=[anywhere] * 2 + [in_vmem] * 3 + [anywhere] * 4,
        out_specs=[anywhere] * 6,
        scratch_shapes=[
            pltpu.VMEM((REDUCED + 8,) + block, LOW),
            pltpu.VMEM((max(8 * rows, 6 * D), D), LOW),
            pltpu.VMEM((8, 2, 2, PIECE, D), LOW),
            pltpu.VMEM((SLOTS, 2, HALF, WIDTH), LOW),
            pltpu.VMEM((SLOTS, 2, HALF, WIDTH), LOW),
            pltpu.VMEM((SLOTS, HALF, WIDTH), LOW),
            pltpu.VMEM((SLOTS, HALF, WIDTH), LOW),
            pltpu.VMEM((REDUCED, PIECE, D), LOW),
            pltpu.VMEM((EARLY_PLACES, 2, 2, PIECE, D), LOW),
            pltpu.VMEM((sections,) + vector, F32),
            low_rows, low_rows, low_rows,
            pltpu.VMEM((rows, 3 * D), LOW),
            pltpu.VMEM((4, PAIRS, 2, seg_rows, seg_rows), F32),
            low_rows, low_rows, full_rows,
            pltpu.VMEM((rows, 128), F32),
            full_rows, full_rows,
            pltpu.VMEM((rows, 128), F32),
            full_rows, low_rows,
            slab, slab, slab, leads, leads, leads,
            slab, slab, slab, slab, slab,
            pltpu.VMEM((SLAB, 3 * D), LOW),
            pltpu.VMEM((SLAB, 3 * D), LOW),
            pltpu.VMEM((PAIRS, 2, SLAB, SLAB), F32),
            slab,
            pltpu.VMEM((SLAB, D), F32),
            pltpu.VMEM((SLAB, 128), F32),
            pltpu.VMEM((SLAB, 4 * D), LOW),
            pltpu.VMEM((SLAB, 4 * D), F32),
            pltpu.VMEM((SLAB, PACK), LOW),
            pltpu.VMEM((SLAB, HALF_PACK), LOW),
            pltpu.VMEM((CUBE // 2, SLAB, PACK), LOW),
            pltpu.VMEM(vector, F32),
            pltpu.VMEM((replicas,) + vector, F32),
            pltpu.VMEM(vector, F32),
            pltpu.VMEM((PIECE, WIDTH), LOW),
            DMA((2,)),
            DMA((4,)),
            DMA((4,)),
            DMA((2,)),
            DMA((ROUNDS,)),
            DMA((ROUNDS,)),
            DMA((4, 5)),
            DMA((4, 5)),
            DMA((GATHERED,)),
            DMA((2 * REDUCED,)),
            DMA((2 * REDUCED,)),
            DMA((SLOTS, 5)),
            DMA((SLOTS, 5)),
            DMA((2 * REDUCED,)),
            DMA((2 * REDUCED,)),
            DMA((2 * REDUCED if groups > 1 else 1, reduced_groups)),
            DMA((2 * REDUCED if groups > 1 else 1, reduced_groups)),
            DMA,
            DMA((SLOTS, 5)),
            DMA((SLOTS, 5)),
            DMA((OWNED,)),
            DMA((5,)),
            DMA((5,)),
            DMA((groups,)),
            DMA((groups,)),
            DMA((replicas,)),
            DMA((replicas,)),
            DMA((sections,)),
            DMA((sections,)),
            DMA((sections,)),
            DMA((sections,)),
            DMA((3,)),
            DMA((3, sections)),
            DMA((1, sections)),
            DMA((1,)),
            DMA((5,)),
            DMA((5,)),
            pltpu.SemaphoreType.REGULAR,
            pltpu.SemaphoreType.REGULAR,
            pltpu.SemaphoreType.REGULAR,
        ],
        compiler_params=pltpu.CompilerParams(
            collective_id=0, has_side_effects=True, vmem_limit_bytes=VMEM_BYTES
        ),
    )(
        tokens, cotangent, seg_doc, gain, bias,
        wide.reshape(2, 2, 2, PIECE, 4 * D), half.reshape(2, 2, 2, 2, PIECE, D), wide, half,
    )


VMEM_BYTES = 62 * 1024 * 1024


def close_kernel(
    total, packs, smalls, rows_in, grads_in,
    wide_out, half_out, gain_out, bias_out, rows_out, grads_out,
    blocks, packed, result, rows, grads, block_sem, result_sem, pack_sem, rows_sem, back_sem,
):
    me = lax.axis_index("section")
    near = me < 2
    groups = packs.shape[0]
    pack_copy = pltpu.make_async_copy(packs, packed, pack_sem)
    loads = [
        pltpu.make_async_copy(total.at[place], blocks.at[place], block_sem.at[place])
        for place in range(OWNED)
    ]
    passing = [
        (
            pltpu.make_async_copy(source, buffer, rows_sem.at[i]),
            pltpu.make_async_copy(buffer, target, back_sem.at[i]),
        )
        for i, (source, buffer, target) in enumerate(
            ((rows_in, rows, rows_out), (grads_in, grads, grads_out))
        )
    ]
    pack_copy.start()
    for load in loads:
        load.start()
    for arrive, _ in passing:
        arrive.start()

    every = jnp.sum(smalls[...], axis=0)
    mine = smalls[me]
    for row, out in ((0, gain_out), (1, bias_out)):
        value = jnp.where(me == 0, every[row : row + 1], every[2 + row : 3 + row])
        out[...] = jnp.where(near, value, 0.0) + mine[4 + row : 5 + row]

    pack_copy.wait()
    factors = packed[...].reshape(groups * CUBE // 2 * SLAB, PACK)
    stores = []
    for place in range(OWNED):
        if place < 4:
            left = factors[:, 0:D] if place < 3 else factors[:, LEFT_OUT:RIGHT]
            right = factors[:, RIGHT + place * D : RIGHT + (place + 1) * D]
            target = wide_out.at[0, :, pl.ds(place * D, D)]
        else:
            left = factors[:, LEFT_HALF + (place - 4) * D : LEFT_HALF + (place - 3) * D]
            right = factors[:, RIGHT_HALF:]
            target = half_out.at[0, pl.ds((place - 4) * D, D)]
        loads[place].wait()
        for strip in range(2):
            rows_of = pl.ds(strip * WIDTH, WIDTH)
            summed = blocks[place, strip].reshape(WIDTH, D).astype(F32)
            result[place, rows_of] = jnp.where(near, summed, 0.0) + outer(
                left[:, strip * WIDTH : (strip + 1) * WIDTH], right
            )
        store = pltpu.make_async_copy(result.at[place], target, result_sem.at[place])
        store.start()
        stores.append(store)
    for arrive, leave in passing:
        arrive.wait()
        leave.start()
    for store in stores:
        store.wait()
    for _, leave in passing:
        leave.wait()


def close(total, packs, smalls, rows, grads):
    in_vmem = pl.BlockSpec(memory_space=pltpu.VMEM)
    anywhere = pl.BlockSpec(memory_space=pl.ANY)
    return pl.pallas_call(
        close_kernel,
        out_shape=(
            jax.ShapeDtypeStruct((1, D, 4 * D), F32),
            jax.ShapeDtypeStruct((1, 2 * D, D), F32),
            jax.ShapeDtypeStruct((1, D), F32),
            jax.ShapeDtypeStruct((1, D), F32),
            jax.ShapeDtypeStruct(rows.shape, LOW),
            jax.ShapeDtypeStruct(rows.shape, LOW),
        ),
        in_specs=[anywhere, anywhere, in_vmem, anywhere, anywhere],
        out_specs=[anywhere, anywhere, in_vmem, in_vmem, anywhere, anywhere],
        scratch_shapes=[
            pltpu.VMEM(total.shape, LOW),
            pltpu.VMEM(packs.shape, LOW),
            pltpu.VMEM((OWNED, D, D), F32),
            pltpu.VMEM(rows.shape, LOW),
            pltpu.VMEM(rows.shape, LOW),
            DMA((OWNED,)),
            DMA((OWNED,)),
            DMA,
            DMA((2,)),
            DMA((2,)),
        ],
        compiler_params=pltpu.CompilerParams(vmem_limit_bytes=VMEM_BYTES),
    )(total, packs, smalls, rows, grads)


def on_device(tokens, cotangent, seg_doc, wide_in, half_out, norm_gain, norm_bias):
    sections = lax.axis_size("section")
    replicas = lax.axis_size("dp")
    rows, grads, total, packs, smalls, _ = run_layers(
        sections, replicas, tokens, cotangent, seg_doc, norm_gain, norm_bias, wide_in[0], half_out[0]
    )
    wide_grad, half_grad, gain_grad, bias_grad, layer_out, tokens_grad = close(
        total, packs, smalls, rows, grads
    )
    return layer_out, tokens_grad, wide_grad, half_grad, gain_grad, bias_grad


def solution(mesh):
    placed = (
        P(("dp", "section"), None),
        P(("dp", "section"), None),
        P("dp", None),
        P("section", None, None),
        P("section", None, None),
        P("section", None),
        P("section", None),
    )
    return jax.shard_map(
        on_device,
        mesh=mesh,
        in_specs=placed,
        out_specs=(
            P(("dp", "section"), None),
            P(("dp", "section"), None),
            P("section", None, None),
            P("section", None, None),
            P("section", None),
            P("section", None),
        ),
        check_vma=False,
    )
```

```python
from functools import partial

import jax
import jax.numpy as jnp
from jax import lax
from jax.experimental import pallas as pl
from jax.experimental.pallas import tpu as pltpu
from jax.sharding import PartitionSpec as P

D = 768
HEADS = 12
PAIRS = HEADS // 2
CUBE = 8
PIECE = D // CUBE
HALF = PIECE // 2
WIDTH = D // 2
SLAB = 16
HOLDER = (0, 0, 0, 0, 1, 1, 1, 1, 0, 0, 1, 1, 2, 2)
GATHERED = len(HOLDER)
ROUNDS = 2 * GATHERED
REDUCED = 12
OWN = {0: (0, 1, 2, 3, 8, 9), 1: (4, 5, 6, 7, 10, 11)}
OWNED = len(OWN[0])
WANTED = {0: (4, 5, 6, 7, 10, 11), 1: (0, 1, 2, 3, 8, 9), 3: (12, 13)}
WAVES = ((8, 9, 10, 11, 4, 5, 6, 7), (3, 0, 1, 2))
EARLY = (8, 10)
SPACING = (4, 2)
EARLY_AT = (13, 5)
SLOT = {
    2 * block + side: (2 * place + side) % 4
    for wanted in WANTED.values()
    for place, block in enumerate(wanted)
    for side in range(2)
}


def sum_slots(orders):
    slots, base = {}, 0
    for spacing, order in zip(SPACING, orders):
        late = [block for block in order if block not in EARLY]
        for place, block in enumerate(late):
            for side in range(2):
                slots[2 * block + side] = base + (2 * place + side) % (2 * spacing)
        base += 2 * spacing
    for place, block in enumerate(EARLY):
        for side in range(2):
            slots[2 * block + side] = base + 2 * place + side
    return slots


SUM_SLOT = sum_slots(WAVES)
BACK_SLOT = {}
for holder in OWN:
    BACK_SLOT |= {
        turn: slot
        for turn, slot in sum_slots(
            [[b for b in order if HOLDER[b] == holder] for order in WAVES]
        ).items()
        if HOLDER[turn // 2] == holder
    }
SLOTS = 2 * sum(SPACING) + 2 * len(EARLY)
EARLY_PLACE = {
    block: [other for other in EARLY if HOLDER[other] == HOLDER[block]].index(block)
    for block in EARLY
}
EARLY_PLACES = max(EARLY_PLACE.values(), default=0) + 1
LEFT_OUT, RIGHT, LEFT_HALF, RIGHT_HALF, PACK = D, 2 * D, 6 * D, 8 * D, 9 * D
HALF_PACK = PACK // 2
LOW = jnp.bfloat16
F32 = jnp.float32
DMA = pltpu.SemaphoreType.DMA
MESH = pl.DeviceIdType.MESH


def dot(left, right):
    return jnp.dot(left, right, preferred_element_type=F32)


def dot_right(left, right):
    return lax.dot_general(left, right, (((1,), (1,)), ((), ())), preferred_element_type=F32)


def outer(left, right):
    return lax.dot_general(left, right, (((0,), (0,)), ((), ())), preferred_element_type=F32)


def normalize(summed, gain, bias):
    average = jnp.mean(summed, axis=-1, keepdims=True)
    centred = summed - average
    inv_dev = lax.rsqrt(jnp.mean(centred * centred, axis=-1, keepdims=True) + 1e-05)
    normed = centred * inv_dev
    return normed * gain + bias, normed, inv_dev


def normalize_backward(grad, normed, inv_dev, gain):
    scaled = grad * gain
    mean_scaled = jnp.mean(scaled, axis=-1, keepdims=True)
    mean_normed = jnp.mean(scaled * normed, axis=-1, keepdims=True)
    grad_sum = inv_dev * (scaled - mean_scaled - normed * mean_normed)
    return (
        grad_sum,
        jnp.sum(grad * normed, axis=0, keepdims=True),
        jnp.sum(grad, axis=0, keepdims=True),
    )


def gelu_pair(value):
    bell = jnp.exp(-0.5 * value * value)
    base = 1.0 + (0.3275911 * 0.7071067811865476) * jnp.abs(value)
    guess = pl.reciprocal(base, approx=True)
    t = guess * (2.0 - base * guess)
    poly = t * (
        0.5 * 0.254829592
        + t
        * (
            0.5 * -0.284496736
            + t * (0.5 * 1.421413741 + t * (0.5 * -1.453152027 + t * (0.5 * 1.061405429)))
        )
    )
    tail = poly * bell
    below = jnp.where(value >= 0, 1.0 - tail, tail)
    return value * below, below + value * bell * 0.3989422804014327


def position():
    index = lax.axis_index("dp")
    return (lax.rem(index // 4, 2), lax.rem(index // 2, 2), lax.rem(index, 2), index // CUBE)


def remote(source, target, send, receive, device):
    return pltpu.make_async_remote_copy(
        src_ref=source,
        dst_ref=target,
        send_sem=send,
        recv_sem=receive,
        device_id=device,
        device_id_type=MESH,
    )


def layer_kernel(
    sections, replicas,
    tokens, cotangent, seg_doc, norm_gain, norm_bias, wide, half, wide_flat, half_flat,
    layer_out, grad_tokens, total, packs, smalls, group_in,
    blocks, flat, core_in, one_a, one_b, two_a, two_b, line_in, early_in, vectors,
    token_rows, cot_rows, out_rows,
    qkv, probs, context, h1, norm0, dev0, summed, norm1, dev1, branch, kept,
    cot_slab, h1_slab, h2_slab, cot_leads, h1_leads, h2_leads,
    lead_third, lead_fourth, lead_grad3, lead_grad2, lead_grad1, handed,
    lead_qkv, lead_probs, lead_context, lead_norm, lead_dev, lead_act, lead_slope,
    pack, pack_in, factors, small, small_all, small_sum, group_piece,
    rows_load, guest_send, guest_recv, rows_out,
    line_send, line_recv, cube_send, cube_recv, load_sem,
    core_send, core_recv, rs_send, rs_recv, z_send, z_recv, group_send, group_recv, group_load, ag_send, ag_recv,
    out_sem, pack_send, pack_recv, group_pack_send, group_pack_recv,
    small_send, small_recv, sum_send, sum_recv,
    vector_send, vector_recv, lead_send, lead_recv, spread_send, spread_recv, hop_send, hop_recv,
    credit, clear_x, clear_y,
):
    me = lax.axis_index("section")
    index = lax.axis_index("dp")
    y, x, core, group = position()
    groups = replicas // CUBE
    micro_rows = tokens.shape[0]
    seg_rows = micro_rows // 2
    rows_all = 2 * micro_rows
    works = me < 2

    def cube_peer(yy, xx, cc):
        return {"dp": group * CUBE + yy * 4 + xx * 2 + cc}

    beside_x = cube_peer(y, 1 - x, core)
    beside_y = cube_peer(1 - y, x, core)
    beside_core = cube_peer(y, x, 1 - core)
    others = [{"section": lax.rem(me + step, sections)} for step in range(1, sections)]

    def replica(step):
        return {"dp": lax.rem(index + step, replicas)}

    barrier = pltpu.get_barrier_semaphore()
    for other in others:
        pl.semaphore_signal(barrier, inc=1, device_id=other, device_id_type=MESH)

    @pl.loop(1, replicas)
    def _(step):
        pl.semaphore_signal(barrier, inc=1, device_id=replica(step), device_id_type=MESH)

    own_part, guest_part = pl.ds(0, micro_rows), pl.ds(micro_rows, micro_rows)

    def load_rows(place):
        source, target = ((tokens, token_rows), (cotangent, cot_rows))[place]
        return pltpu.make_async_copy(source, target.at[own_part], rows_load.at[place])

    load_rows(0).start()
    load_rows(1).start()

    def load(block):
        if block < 8:
            source = wide.at[:, :, :, :, pl.ds((block % 4) * D, D)]
        else:
            source = half.at[block % 2]
        return pltpu.make_async_copy(source, blocks.at[block], load_sem.at[block])

    def flat_rows(place):
        return pl.ds(place * D, D)

    def load_own(place):
        if place < 4:
            source = wide_flat.at[:, pl.ds(place * D, D)]
        else:
            source = half_flat.at[flat_rows(place - 4)]
        return pltpu.make_async_copy(source, flat.at[flat_rows(place)], load_sem.at[place])

    for holder in (0, 1):

        @pl.when(me == holder)
        def _():
            for block in OWN[holder]:
                load(block).start()

    @pl.when(me >= 2)
    def _():
        for place in range(4):
            load_own(place).start()

    def load_upper(block):
        return pltpu.make_async_copy(
            half.at[block], core_in.at[pl.ds(2 * block, 2)], load_sem.at[REDUCED + block]
        )

    @pl.when(me == 2)
    def _():
        for block in range(2):
            load_upper(block).start()

    @pl.when(me == 3)
    def _():
        for place in (4, 5):
            load_own(place).start()

    pl.semaphore_wait(barrier, sections - 1 + replicas - 1)

    def guest_copy(kind):
        down = {"section": lax.rem(me + sections - 2, sections)}
        up = {"section": lax.rem(me + 2, sections)}
        source, target, device = (
            (token_rows.at[own_part], token_rows.at[guest_part], down),
            (cot_rows.at[own_part], cot_rows.at[guest_part], down),
            (out_rows.at[guest_part], out_rows.at[own_part], up),
            (h1.at[guest_part], h1.at[own_part], up),
        )[kind]
        return remote(source, target, guest_send.at[kind], guest_recv.at[kind], device)

    TOKENS, COTANGENT, OUT, GRAD = 0, 1, 2, 3

    load_rows(0).wait()
    load_rows(1).wait()

    @pl.when(me >= 2)
    def _():
        guest_copy(TOKENS).start()

    row_of = lax.broadcasted_iota(jnp.int32, (SLAB, D), 0)

    def lead_rows(ref, count):
        value = jnp.zeros((SLAB, D), F32)
        for lead in range(count):
            row = ref[lead * seg_rows : lead * seg_rows + SLAB].astype(F32)[0:1]
            value = jnp.where(row_of == lead, row, value)
        return value.astype(LOW)

    def lead_copy(kind, slab, target, reader):
        return remote(
            slab, target.at[me], lead_send.at[kind], lead_recv.at[kind, me], {"section": reader}
        )

    def lead_start(kind, slab, target, reader):
        @pl.when(me != reader)
        def _():
            lead_copy(kind, slab, target, reader).start()

        @pl.when(me == reader)
        def _():
            target[reader] = slab[...]

    def lead_wait(kind, slab, target, reader, senders):
        for section in range(senders):
            if section != reader:
                remote(
                    slab, target.at[section], lead_send.at[kind], lead_recv.at[kind, section],
                    {"section": section},
                ).wait_recv()

    def collected(target, senders):
        value = jnp.zeros((SLAB, D), F32)
        for section in range(senders):
            slab = target[section].astype(F32)
            for micro in range(section, sections, senders):
                for lead in range(2):
                    place = (micro - section) // senders * 2 + lead
                    value = jnp.where(
                        row_of == 2 * micro + lead, slab[place : place + 1], value
                    )
        return value

    def spread_copy(kind, slab, step):
        return remote(
            slab, slab, spread_send.at[kind, step], spread_recv.at[kind], others[step - 1]
        )

    def hop_copy(kind, slab, step):
        return remote(
            slab, slab, hop_send.at[kind], hop_recv.at[kind],
            {"section": lax.rem(me + step + sections, sections)},
        )

    def leads_of(slab, micro):
        value = slab[...].astype(F32)
        return [
            jnp.sum(jnp.where(row_of == 2 * micro + lead, value, 0.0), axis=0, keepdims=True)
            for lead in range(2)
        ]

    COT, H1, H2 = 0, 1, 2
    FOURTH = 0
    THIRD, GRAD3, GRAD2, HAND, GRAD1 = 0, 1, 2, 3, 4

    def vector_copy(step):
        return remote(
            vectors.at[me], vectors.at[me], vector_send.at[step], vector_recv.at[step],
            others[step - 1],
        )

    vectors[me, 0:1] = norm_gain[...]
    vectors[me, 1:2] = norm_bias[...]
    for step in range(1, sections):
        vector_copy(step).start()
    cot_slab[...] = lead_rows(cot_rows, 2)
    lead_start(COT, cot_slab, cot_leads, 3)

    upper, lower = pl.ds(0, HALF), pl.ds(HALF, HALF)

    def lanes_of(turn):
        return pl.ds((turn % 2) * WIDTH, WIDTH)

    def turns(*order):
        return tuple(2 * block + side for block in order for side in range(2))

    def place_of(block):
        if block < REDUCED:
            return blocks.at[block]
        return core_in.at[pl.ds(2 * (block - REDUCED), 2)]

    def line_copy(turn, reader):
        block, lanes = turn // 2, lanes_of(turn)
        piece = place_of(block).at[y, x, core, :, lanes]
        return remote(
            piece,
            piece,
            line_send.at[turn],
            line_recv.at[turn],
            {"section": reader},
        )

    def cube_copy(turn, stage):
        full, lanes = place_of(turn // 2), lanes_of(turn)
        ref, peer = (
            (full.at[y, x, core, upper, lanes], beside_x),
            (full.at[y, x, core, lower, lanes], beside_y),
            (full.at[y, :, core, upper, lanes], beside_y),
            (full.at[:, x, core, lower, lanes], beside_x),
            (full.at[:, :, core, :, lanes], beside_core),
        )[stage]
        slot = SLOT[turn]
        return remote(ref, ref, cube_send.at[slot, stage], cube_recv.at[slot, stage], peer)

    def gather_line(turn, reader):
        @pl.when(me == reader)
        def _():
            line_copy(turn, reader).wait_recv()
            cube_copy(turn, 0).start()
            cube_copy(turn, 1).start()

    def gather_two(turn, reader):
        @pl.when(me == reader)
        def _():
            cube_copy(turn, 0).wait()
            cube_copy(turn, 2).start()
            cube_copy(turn, 1).wait()
            cube_copy(turn, 3).start()

    def gather_three(turn, reader):
        @pl.when(me == reader)
        def _():
            cube_copy(turn, 2).wait()
            cube_copy(turn, 3).wait()
            cube_copy(turn, 4).start()

    def gather_ready(turn, reader):
        @pl.when(me == reader)
        def _():
            cube_copy(turn, 4).wait()

    def gather_finish(turn, reader):
        @pl.when(me == HOLDER[turn // 2])
        def _():
            line_copy(turn, reader).wait_send()

    def gather_send():
        for reader, wanted in WANTED.items():

            @pl.when(me == HOLDER[wanted[0]])
            def _():
                for turn in turns(*wanted):
                    line_copy(turn, reader).start()

    gather_plan = ((gather_ready, 6), (gather_three, 4), (gather_two, 2), (gather_line, 0))
    gather_ticks = 2 * OWNED + gather_plan[0][1]

    def gather_tick(tick):
        for stage, offset in gather_plan:
            at = tick - offset
            for reader, wanted in WANTED.items():
                if 0 <= at < 2 * len(wanted):
                    stage(2 * wanted[at // 2] + at % 2, reader)

    def gather_wait_own():
        @pl.when(me == 2)
        def _():
            for block in range(2):
                load_upper(block).wait()

        for holder in (0, 1):

            @pl.when(me == holder)
            def _():
                for block in OWN[holder]:
                    load(block).wait()

    def worker(step):
        def run(*given):
            @pl.when(works)
            def _():
                step(*given)

        return run

    def weight(block):
        return blocks[block].reshape(D, D)

    def act_rows(block):
        return pl.ds(pl.multiple_of(block * rows_all, SLAB), rows_all)

    def slope_rows(block):
        return pl.ds(pl.multiple_of((4 + block) * rows_all, SLAB), rows_all)

    lane_of = lax.broadcasted_iota(jnp.int32, (1, 128), 1)
    first_half = lane_of < 64
    head_masks = (first_half.astype(LOW), (~first_half).astype(LOW))
    segs = range(4)

    def chunks(size, body):
        @pl.loop(0, rows_all // size)
        def _(step):
            body(pl.multiple_of(step * size, size), size)

    @worker
    def project(block):
        qkv[:, block * D : (block + 1) * D] = dot(token_rows[...], weight(block)).astype(LOW)

    def seg_slice(seg):
        return pl.ds(seg * seg_rows, seg_rows)

    def pair_lanes(pair):
        return [pl.ds(pl.multiple_of(part * D + pair * 128, 128), 128) for part in range(3)]

    def softmax(scores):
        raised = jnp.exp(scores - jnp.max(scores, axis=-1, keepdims=True))
        return raised / jnp.sum(raised, axis=-1, keepdims=True)

    @worker
    def heads_forward(first, last):
        @pl.loop(first, last)
        def _(pair):
            at_q, at_k, at_v = pair_lanes(pair)
            heads = [(seg, place) for seg in segs for place in range(2)]
            scores = [
                dot_right(qkv[seg_slice(seg), at_q] * head_masks[place], qkv[seg_slice(seg), at_k])
                * 0.125
                for seg, place in heads
            ]
            found = [softmax(score) for score in scores]
            for (seg, place), prob in zip(heads, found):
                probs[seg, pair, place] = prob
            mixed = [
                dot(prob.astype(LOW), qkv[seg_slice(seg), at_v])
                for (seg, place), prob in zip(heads, found)
            ]
            for seg in segs:
                context[seg_slice(seg), at_q] = jnp.where(
                    first_half, mixed[2 * seg], mixed[2 * seg + 1]
                ).astype(LOW)

    @worker
    def attention_close():
        summed[...] = dot_right(context[...], weight(3))
        gain, bias = vectors[0, 0:1], vectors[0, 1:2]

        def body(start, size):
            rows = pl.ds(start, size)
            out, normed, inv_dev = normalize(
                token_rows[rows].astype(F32) + summed[rows], gain, bias
            )
            norm0[rows] = normed
            dev0[rows] = jnp.broadcast_to(inv_dev, (size, 128))
            h1[rows] = out.astype(LOW)
            branch[rows] = jnp.zeros((size, D), F32)

        chunks(32, body)
        h1_slab[...] = lead_rows(h1, 4)
        lead_start(H1, h1_slab, h1_leads, 1)

    @worker
    def inner_blocks(first, last):
        count = 2
        size = rows_all // count

        @pl.loop(first, last)
        def _(place):
            block = lax.rem(2 * me + place, 4)
            for step in range(count):
                rows = pl.ds(step * size, size)
                start = pl.multiple_of(block * rows_all + step * size, SLAB)
                value, grade = gelu_pair(dot(h1[rows], weight(4 + block)))
                flat[pl.ds(start, size)] = value.astype(LOW)
                flat[pl.ds(pl.multiple_of(4 * rows_all + start, SLAB), size)] = grade.astype(LOW)
                branch[rows] += dot(flat[pl.ds(start, size)], weight(8 + block))

    @worker
    def mlp_close():
        gain, bias = vectors[1, 0:1], vectors[1, 1:2]

        def body(start, size):
            rows = pl.ds(start, size)
            out, normed, inv_dev = normalize(h1[rows].astype(F32) + branch[rows], gain, bias)
            norm1[rows] = normed
            dev1[rows] = jnp.broadcast_to(inv_dev, (size, 128))
            out_rows[rows] = out.astype(LOW)

        chunks(32, body)
        h2_slab[...] = lead_rows(out_rows, 4)
        lead_start(H2, h2_slab, h2_leads, 2)

    @worker
    def rows_leave():
        guest_copy(OUT).start()

    def add_small(row, value):
        small[row : row + 1] += value

    @worker
    def mlp_open_backward():
        gain = vectors[1, 0:1]

        def body(start, size):
            rows = pl.ds(start, size)
            place = start + lax.broadcasted_iota(jnp.int32, (size, D), 0)
            grad = jnp.where(lax.rem(place, seg_rows) == 0, 0.0, cot_rows[rows].astype(F32))
            grad_sum, grad_gain, grad_bias = normalize_backward(
                grad, norm1[rows], dev1[rows][:, 0:1], gain
            )
            branch[rows] = grad_sum
            kept[rows] = grad_sum.astype(LOW)
            add_small(2, grad_gain)
            add_small(3, grad_bias)

        chunks(32, body)

    def part(block):
        return block + 4 if block < 4 else block + 8

    def store_part(block, left, right):
        for strip in range(2):
            lanes = slice(strip * WIDTH, (strip + 1) * WIDTH)
            blocks[part(block), strip] = (
                outer(left[:, lanes], right).astype(LOW).reshape(2, 2, PIECE, D)
            )

    @worker
    def second_grad(block):
        store_part(8 + block, flat[act_rows(block)], kept[...])

    @worker
    def inner_grad(block):
        grad_act = dot_right(kept[...], weight(8 + block))
        grad_inner = (grad_act * flat[slope_rows(block)].astype(F32)).astype(LOW)
        flat[act_rows(block)] = grad_inner
        branch[...] += dot_right(flat[act_rows(block)], weight(4 + block))
        store_part(4 + block, h1[...], flat[act_rows(block)])

    @worker
    def attention_open_backward():
        gain = vectors[0, 0:1]
        leads = leads_of(lead_grad1, me) + leads_of(lead_grad1, me + 2)

        def body(start, size):
            rows = pl.ds(start, size)
            place = start + lax.broadcasted_iota(jnp.int32, (size, D), 0)
            grad = branch[rows]
            for lead in range(4):
                grad = jnp.where(place == lead * seg_rows, leads[lead], grad)
            grad = grad.astype(LOW).astype(F32)
            grad_sum, grad_gain, grad_bias = normalize_backward(
                grad, norm0[rows], dev0[rows][:, 0:1], gain
            )
            summed[rows] = grad_sum
            kept[rows] = grad_sum.astype(LOW)
            add_small(0, grad_gain)
            add_small(1, grad_bias)

        chunks(32, body)

    @worker
    def out_grad():
        store_part(3, kept[...], context[...])
        context[...] = dot(kept[...], weight(3)).astype(LOW)

    @worker
    def heads_backward(first, last):
        @pl.loop(first, last)
        def _(pair):
            at_q, at_k, at_v = pair_lanes(pair)
            heads = [(seg, place) for seg in segs for place in range(2)]
            grad_probs = [
                dot_right(
                    context[seg_slice(seg), at_q] * head_masks[place], qkv[seg_slice(seg), at_v]
                )
                for seg, place in heads
            ]
            grad_scores = []
            for (seg, place), grad_prob in zip(heads, grad_probs):
                prob = probs[seg, pair, place]
                inside = prob * grad_prob
                grad_score = inside - prob * jnp.sum(inside, axis=-1, keepdims=True)
                grad_scores.append(grad_score.astype(LOW))
            for seg in segs:
                rows = seg_slice(seg)
                query, key, grad = qkv[rows, at_q], qkv[rows, at_k], context[rows, at_q]
                mine = grad_scores[2 * seg : 2 * seg + 2]
                found = [probs[seg, pair, place].astype(LOW) for place in range(2)]
                for at, both, scale in (
                    (at_q, [dot(score, key) for score in mine], 0.125),
                    (at_k, [outer(score, query) for score in mine], 0.125),
                    (at_v, [outer(prob, grad) for prob in found], 1.0),
                ):
                    merged = jnp.where(first_half, both[0], both[1]) * scale
                    qkv[rows, at] = merged.astype(LOW)

    @worker
    def project_grad(block):
        store_part(block, token_rows[...], qkv[:, block * D : (block + 1) * D])

    @worker
    def tokens_back(block):
        summed[...] += dot_right(qkv[:, block * D : (block + 1) * D], weight(block))

    @worker
    def tokens_close():
        h1[...] = summed[...].astype(LOW)
        guest_copy(GRAD).start()

    def leads_mlp_forward(value, first, second, gain, bias):
        total_branch = value.astype(F32)
        for block in range(4):
            lanes = slice(block * D, (block + 1) * D)
            out, grade = gelu_pair(dot(value, first(block)))
            lead_act[:, lanes] = out.astype(LOW)
            lead_slope[:, lanes] = grade
            total_branch = total_branch + dot(lead_act[:, lanes], second(block))
        out, normed, inv_dev = normalize(total_branch, gain, bias)
        lead_norm[...] = normed
        lead_dev[...] = jnp.broadcast_to(inv_dev, (SLAB, 128))
        pack[:, 0:D] = value
        pack[:, LEFT_OUT:RIGHT] = value
        return out

    def leads_mlp_backward(grad, first, second, gain):
        grad_sum, grad_gain, grad_bias = normalize_backward(
            grad, lead_norm[...], lead_dev[:, 0:1], gain
        )
        add_small(4, grad_gain)
        add_small(5, grad_bias)
        low_sum = grad_sum.astype(LOW)
        result = grad_sum
        for block in range(4):
            lanes = slice(block * D, (block + 1) * D)
            grad_inner = (dot_right(low_sum, second(block)) * lead_slope[:, lanes]).astype(LOW)
            pack[:, RIGHT + block * D : RIGHT + (block + 1) * D] = grad_inner
            result = result + dot_right(grad_inner, first(block))
        pack[:, LEFT_HALF:RIGHT_HALF] = lead_act[:, 2 * D :]
        pack[:, RIGHT_HALF:] = low_sum
        handed[:, 0 : 2 * D] = lead_act[:, 0 : 2 * D]
        handed[:, 2 * D :] = low_sum
        return result

    def own_weight(place):
        return flat[flat_rows(place)]

    def last_second(block):
        if block >= 2:
            return own_weight(2 + block)
        return core_in[2 * block : 2 * block + 2].reshape(D, D)

    def leads_first():
        @pl.when(me == 2)
        def _():
            lead_wait(H2, h2_slab, h2_leads, 2, 2)
            for place in range(4):
                load_own(place).wait()
            value = collected(h2_leads, 2).astype(LOW)
            pack[:, 0:D] = value
            for block in range(3):
                lead_qkv[:, block * D : (block + 1) * D] = dot(value, own_weight(block)).astype(LOW)
            docs = seg_doc[...]
            row, column = (lax.broadcasted_iota(jnp.int32, (SLAB, SLAB), i) for i in range(2))
            sort = jnp.where(row == column, 2.0, 0.0)
            for micro in range(seg_doc.shape[0]):
                pair_sort = jnp.where(
                    docs[micro : micro + 1, 0:1] == docs[micro : micro + 1, 1:2], 2.0, 1.0
                )
                near = (row // 2 == micro) & (column // 2 == micro) & (row != column)
                sort = jnp.where(near, pair_sort, sort)
            for pair in range(PAIRS):
                at = [slice(p * D + pair * 128, p * D + (pair + 1) * 128) for p in range(3)]
                query, key, val = (lead_qkv[:, lanes] for lanes in at)
                parts = []
                for place in range(2):
                    scores = dot_right(query * head_masks[place], key) * 0.125
                    scores = jnp.where(
                        sort > 1.5, scores, jnp.where(sort > 0.5, -1000000000.0, -1e30)
                    )
                    raised = jnp.exp(scores - jnp.max(scores, axis=-1, keepdims=True))
                    prob = raised / jnp.sum(raised, axis=-1, keepdims=True)
                    lead_probs[pair, place] = prob
                    parts.append(dot(prob.astype(LOW), val))
                lead_context[:, pair * 128 : (pair + 1) * 128] = jnp.where(
                    first_half, parts[0], parts[1]
                ).astype(LOW)
            summed_rows = value.astype(F32) + dot_right(lead_context[...], own_weight(3))
            out, normed, inv_dev = normalize(summed_rows, vectors[2, 0:1], vectors[2, 1:2])
            lead_norm[...] = normed
            lead_dev[...] = jnp.broadcast_to(inv_dev, (SLAB, 128))
            lead_third[...] = out.astype(LOW)
            hop_copy(THIRD, lead_third, 1).start()

        @pl.when(me == 1)
        def _():
            lead_wait(H1, h1_slab, h1_leads, 1, 2)
            leads_mlp_forward(
                collected(h1_leads, 2).astype(LOW),
                lambda block: weight(4 + block),
                lambda block: weight(8 + block),
                vectors[1, 0:1],
                vectors[1, 1:2],
            )

    def leads_second():
        @pl.when(me == 3)
        def _():
            hop_copy(THIRD, lead_third, -1).wait_recv()
            for place in range(6):
                load_own(place).wait()
            out = leads_mlp_forward(
                lead_third[...], own_weight, last_second, vectors[3, 0:1], vectors[3, 1:2]
            )
            lead_fourth[...] = out.astype(LOW)
            for step in range(1, sections):
                spread_copy(FOURTH, lead_fourth, step).start()
            lead_wait(COT, cot_slab, cot_leads, 3, sections)
            grad = leads_mlp_backward(
                collected(cot_leads, sections), own_weight, last_second, vectors[3, 0:1]
            )
            lead_grad3[...] = grad.astype(LOW)
            hop_copy(GRAD3, lead_grad3, -1).start()
            hop_copy(HAND, handed, -1).start()

    def leads_third():
        @pl.when(me == 2)
        def _():
            hop_copy(GRAD3, lead_grad3, 1).wait_recv()
            grad_sum, grad_gain, grad_bias = normalize_backward(
                lead_grad3[...].astype(F32), lead_norm[...], lead_dev[:, 0:1], vectors[2, 0:1]
            )
            add_small(4, grad_gain)
            add_small(5, grad_bias)
            low_sum = grad_sum.astype(LOW)
            pack[:, LEFT_OUT:RIGHT] = low_sum
            pack[:, RIGHT + 3 * D : LEFT_HALF] = lead_context[...]
            grad_context = dot(low_sum, own_weight(3)).astype(LOW)
            for pair in range(PAIRS):
                at = [slice(p * D + pair * 128, p * D + (pair + 1) * 128) for p in range(3)]
                query, key, val = (lead_qkv[:, lanes] for lanes in at)
                grad = grad_context[:, pair * 128 : (pair + 1) * 128]
                grads = ([], [], [])
                for place in range(2):
                    prob = lead_probs[pair, place]
                    grad_prob = dot_right(grad * head_masks[place], val)
                    inside = prob * grad_prob
                    grad_score = inside - prob * jnp.sum(inside, axis=-1, keepdims=True)
                    grad_score = grad_score.astype(LOW)
                    grads[0].append(dot(grad_score, key))
                    grads[1].append(outer(grad_score, query))
                    grads[2].append(outer(prob.astype(LOW), grad))
                for lanes, pair_grads, scale in zip(at, grads, (0.125, 0.125, 1.0)):
                    merged = jnp.where(first_half, pair_grads[0], pair_grads[1]) * scale
                    pack[:, RIGHT + lanes.start : RIGHT + lanes.stop] = merged.astype(LOW)
            result = grad_sum
            for block in range(3):
                result = result + dot_right(
                    pack[:, RIGHT + block * D : RIGHT + (block + 1) * D], own_weight(block)
                )
            lead_grad2[...] = result.astype(LOW)
            hop_copy(GRAD2, lead_grad2, -1).start()
            hop_copy(HAND, handed, 1).wait_recv()
            pack[:, LEFT_HALF:] = handed[...]

    def leads_fourth():
        @pl.when(me == 1)
        def _():
            hop_copy(GRAD2, lead_grad2, 1).wait_recv()
            grad = leads_mlp_backward(
                lead_grad2[...].astype(F32),
                lambda block: weight(4 + block),
                lambda block: weight(8 + block),
                vectors[1, 0:1],
            )
            lead_grad1[...] = grad.astype(LOW)
            hop_copy(GRAD1, lead_grad1, -1).start()
            hop_copy(HAND, handed, -1).start()

    half_lanes = pl.ds(pl.multiple_of(core * HALF_PACK, 128), HALF_PACK)
    other_lanes = pl.ds(pl.multiple_of((1 - core) * HALF_PACK, 128), HALF_PACK)
    first_peer = {"dp": group * CUBE + (y + core - 2 * y * core) * 4
                  + (x + (1 - core) * (1 - 2 * x)) * 2 + core}
    second_peer = {"dp": group * CUBE + (y + (1 - core) * (1 - 2 * y)) * 4
                   + (x + core - 2 * x * core) * 2 + core}

    def pack_copy(stage):
        chip = y * 2 + x
        first_chip = (y + core - 2 * y * core) * 2 + x + (1 - core) * (1 - 2 * x)
        if stage == 0:
            source, target, peer = pack.at[:, other_lanes], pack_in, beside_core
        elif stage == 1:
            source = target = factors.at[chip, :, half_lanes]
            peer = first_peer
        elif stage == 2:
            source = target = factors.at[chip, :, half_lanes]
            peer = second_peer
        elif stage == 3:
            source = target = factors.at[first_chip, :, half_lanes]
            peer = second_peer
        else:
            source = target = factors.at[:, :, half_lanes]
            peer = beside_core
        return remote(source, target, pack_send.at[stage], pack_recv.at[stage], peer)

    def pack_join():
        pack_copy(0).wait()

        @pl.loop(0, HALF_PACK // WIDTH)
        def _(step):
            start = pl.multiple_of(step * WIDTH, 128)
            lanes = pl.ds(pl.multiple_of(core * HALF_PACK + start, 128), WIDTH)
            mine = pack[:, lanes].astype(F32)[0:8]
            theirs = pack_in[:, pl.ds(start, WIDTH)].astype(F32)[0:8]
            low_rows = jnp.where(core == 0, mine, theirs)
            high_rows = jnp.where(core == 0, theirs, mine)
            factors[y * 2 + x, :, lanes] = jnp.concatenate([low_rows, high_rows]).astype(LOW)

        pack_copy(1).start()

    def pack_second():
        pack_copy(1).wait()
        pack_copy(2).start()
        pack_copy(3).start()

    def pack_third():
        pack_copy(2).wait()
        pack_copy(3).wait()
        pack_copy(4).start()

    def to_packs(step):
        return remote(
            factors, packs.at[group], group_pack_send.at[step], group_pack_recv.at[step],
            {"dp": lax.rem(index + step * CUBE, replicas)},
        )

    def own_pack():
        return pltpu.make_async_copy(factors, packs.at[group], group_pack_send.at[0])

    def pack_fourth():
        pack_copy(4).wait()
        own_pack().start()
        for step in range(1, groups):
            to_packs(step).start()

    def pack_last():
        own_pack().wait()
        for step in range(1, groups):
            to_packs(step).wait()

    def rows_store(place):
        source, target = ((out_rows, layer_out), (h1, grad_tokens))[place]
        return pltpu.make_async_copy(source.at[own_part], target, rows_out.at[place])

    def leads_close():
        @pl.when(me != 3)
        def _():
            spread_copy(FOURTH, lead_fourth, 1).wait_recv()

        @pl.when(me >= 2)
        def _():
            guest_copy(OUT).wait_recv()

        leads = leads_of(lead_fourth, me)
        for lead in range(2):
            rows = pl.ds(lead * seg_rows, SLAB)
            out_rows[rows] = jnp.where(
                row_of == 0, leads[lead], out_rows[rows].astype(F32)
            ).astype(LOW)
        rows_store(0).start()

        @pl.when(me == 0)
        def _():
            hop_copy(GRAD1, lead_grad1, 1).wait_recv()
            hop_copy(HAND, handed, 1).wait_recv()
            pack[:, 0:LEFT_HALF] = jnp.zeros((SLAB, LEFT_HALF), LOW)
            pack[:, LEFT_HALF:] = handed[...]

        pack_copy(0).start()

    def add(target, source):
        target[...] = target[...] + source[...]

    def landing(block):
        return blocks.at[8 + block, 0] if block < 4 else core_in.at[block - 4]

    def scatter(turn, stage):
        slot = SUM_SLOT[turn]
        block, lanes = turn // 2, lanes_of(turn)
        run = blocks.at[part(block)]
        source, target, peer = (
            (run.at[:, :, 1 - core, :, lanes], landing(block).at[:, :, :, lanes], beside_core),
            (run.at[:, 1 - x, core, upper, lanes], one_a.at[slot], beside_x),
            (run.at[1 - y, :, core, lower, lanes], one_b.at[slot], beside_y),
            (run.at[1 - y, x, core, upper, lanes], two_a.at[slot], beside_y),
            (run.at[y, 1 - x, core, lower, lanes], two_b.at[slot], beside_x),
        )[stage]
        if stage == 0:
            return remote(source, target, core_send.at[turn], core_recv.at[turn], peer)
        return remote(source, target, rs_send.at[slot, stage], rs_recv.at[slot, stage], peer)

    def to_line(turn):
        return remote(
            blocks.at[part(turn // 2), y, x, core, :, lanes_of(turn)],
            line_in.at[turn // 2, :, lanes_of(turn)],
            z_send.at[turn],
            z_recv.at[turn],
            {"section": HOLDER[turn // 2]},
        )

    def to_holder(turn):
        place = EARLY_PLACE[turn // 2]
        return remote(
            blocks.at[part(turn // 2), :, :, core, :, lanes_of(turn)],
            early_in.at[place, :, :, :, lanes_of(turn)],
            z_send.at[turn],
            z_recv.at[turn],
            {"section": HOLDER[turn // 2]},
        )

    def to_group(turn, step):
        return remote(
            blocks.at[part(turn // 2), y, x, core, :, lanes_of(turn)],
            group_in.at[turn // 2, step - 1, :, lanes_of(turn)],
            group_send.at[turn, step - 1],
            group_recv.at[turn, step - 1],
            {"dp": lax.rem(index + step * CUBE, replicas)},
        )

    def gather_back(turn, stage):
        slot = BACK_SLOT[turn]
        run, lanes = blocks.at[part(turn // 2)], lanes_of(turn)
        ref, peer = (
            (run.at[y, x, core, upper, lanes], beside_y),
            (run.at[y, x, core, lower, lanes], beside_x),
            (run.at[:, x, core, upper, lanes], beside_x),
            (run.at[y, :, core, lower, lanes], beside_y),
            (run.at[:, :, core, :, lanes], beside_core),
        )[stage]
        return remote(ref, ref, ag_send.at[slot, stage], ag_recv.at[slot, stage], peer)

    def write_out(block):
        place = OWN[HOLDER[block]].index(block)
        return pltpu.make_async_copy(
            blocks.at[part(block)], total.at[place], out_sem.at[place]
        )

    @worker
    def reduce_core(block):
        scatter(2 * block, 0).start()
        scatter(2 * block + 1, 0).start()

    def wave_of(turn):
        return 0 if turn // 2 in WAVES[0] else 1

    def is_early(turn):
        return turn // 2 in EARLY

    def in_plane(turn):
        return me == HOLDER[turn // 2] if is_early(turn) else works

    def add_four(turn, source):
        for yy in range(2):
            for xx in range(2):
                add(
                    blocks.at[part(turn // 2), yy, xx, core, :, lanes_of(turn)],
                    source.at[yy, xx, :, lanes_of(turn)],
                )

    def reduce_one(turn):
        @pl.when(works)
        def _():
            scatter(turn, 0).wait()
            add_four(turn, landing(turn // 2))
            if not is_early(turn):
                scatter(turn, 1).start()
                scatter(turn, 2).start()

        if is_early(turn):

            @pl.when(me == 1 - HOLDER[turn // 2])
            def _():
                to_holder(turn).start()

    def reduce_early(turn):
        @pl.when(me == HOLDER[turn // 2])
        def _():
            to_holder(turn).wait_recv()
            add_four(turn, early_in.at[EARLY_PLACE[turn // 2]])
            scatter(turn, 1).start()
            scatter(turn, 2).start()

    def reduce_two(turn):
        @pl.when(in_plane(turn))
        def _():
            reduce_two_now(turn)

    def reduce_two_now(turn):
        block, lanes = turn // 2, lanes_of(turn)
        run = blocks.at[part(block)]
        scatter(turn, 1).wait()
        for yy in range(2):
            add(run.at[yy, x, core, upper, lanes], one_a.at[SUM_SLOT[turn], yy])
        scatter(turn, 3).start()
        scatter(turn, 2).wait()
        for xx in range(2):
            add(run.at[y, xx, core, lower, lanes], one_b.at[SUM_SLOT[turn], xx])
        scatter(turn, 4).start()

    def reduce_three(turn):
        @pl.when(in_plane(turn))
        def _():
            reduce_three_now(turn)

        @pl.when(me == HOLDER[turn // 2])
        def _():
            for clear, peer in ((clear_y, beside_y), (clear_x, beside_x)):
                pl.semaphore_signal(
                    clear.at[wave_of(turn)], inc=1, device_id=peer, device_id_type=MESH
                )

        if not is_early(turn):

            @pl.when(me == 1 - HOLDER[turn // 2])
            def _():
                to_line(turn).start()

    def reduce_three_now(turn):
        block, lanes = turn // 2, lanes_of(turn)
        run = blocks.at[part(block)]
        scatter(turn, 3).wait()
        add(run.at[y, x, core, upper, lanes], two_a.at[SUM_SLOT[turn]])
        scatter(turn, 4).wait()
        add(run.at[y, x, core, lower, lanes], two_b.at[SUM_SLOT[turn]])
        if groups > 1:
            for step in range(1, groups):
                to_group(turn, step).start()
            for step in range(1, groups):
                to_group(turn, step).wait()
            for step in range(1, groups):
                copy = pltpu.make_async_copy(
                    group_in.at[block, step - 1, :, lanes], group_piece, group_load
                )
                copy.start()
                copy.wait()
                add(run.at[y, x, core, :, lanes], group_piece)

    def spread_one(turn):
        pl.semaphore_wait(clear_y.at[wave_of(turn)], 1)
        gather_back(turn, 0).start()
        pl.semaphore_wait(clear_x.at[wave_of(turn)], 1)
        gather_back(turn, 1).start()

    def spread_early(turn):
        @pl.when(me == HOLDER[turn // 2])
        def _():
            spread_one(turn)

    def reduce_line(turn):
        @pl.when(me == HOLDER[turn // 2])
        def _():
            block, lanes = turn // 2, lanes_of(turn)
            to_line(turn).wait_recv()
            add(blocks.at[part(block), y, x, core, :, lanes], line_in.at[block, :, lanes])
            spread_one(turn)

    def spread_two(turn):
        @pl.when(me == HOLDER[turn // 2])
        def _():
            gather_back(turn, 0).wait()
            gather_back(turn, 2).start()
            gather_back(turn, 1).wait()
            gather_back(turn, 3).start()

    def spread_core(turn):
        @pl.when(me == HOLDER[turn // 2])
        def _():
            gather_back(turn, 2).wait()
            gather_back(turn, 3).wait()
            gather_back(turn, 4).start()

    def spread_done(turn):
        @pl.when(me == HOLDER[turn // 2])
        def _():
            gather_back(turn, 4).wait()
            if turn % 2 == 1:
                write_out(turn // 2).start()

        @pl.when(me == 1 - HOLDER[turn // 2])
        def _():
            (to_holder if is_early(turn) else to_line)(turn).wait_send()

    late_stages = (
        reduce_one, reduce_two, reduce_three, reduce_line, spread_two, spread_core, spread_done,
    )
    early_stages = (
        reduce_one, reduce_early, reduce_two, reduce_three, spread_early, spread_two, spread_core,
        spread_done,
    )

    class Wave:
        def __init__(self, order, spacing, early_at):
            self.order, self.at = turns(*order), 0
            late = range(1, 1 + 7 * spacing, spacing)
            early = (1,) + tuple(range(early_at, early_at + 7 * spacing, spacing))
            self.plans = [
                tuple(zip(early_stages, early) if is_early(turn) else zip(late_stages, late))
                for turn in self.order
            ]
            self.last = max(i + plan[-1][1] for i, plan in enumerate(self.plans))

        def tick(self, count=1):
            for _ in range(count):
                due = []
                for place, turn in enumerate(self.order):
                    for stage, offset in self.plans[place]:
                        if place + offset == self.at:
                            due.append((offset, stage, turn))
                for _, stage, turn in sorted(due, key=lambda item: -item[0]):
                    stage(turn)
                self.at += 1

        def left(self):
            return self.at <= self.last

    one, two = (Wave(*given) for given in zip(WAVES, SPACING, EARLY_AT))

    small[...] = jnp.zeros_like(small)

    gather_wait_own()
    gather_send()

    @pl.when(me >= 2)
    def _():
        guest_copy(TOKENS).wait_send()
        guest_copy(COTANGENT).start()

    for tick in range(gather_ticks):
        gather_tick(tick)
        at = tick - gather_plan[0][1]
        if at == 0:
            for step in range(1, sections):
                vector_copy(step).wait()
        if at < 0:
            continue
        if at == 1:

            @pl.when(works)
            def _():
                guest_copy(TOKENS).wait_recv()

        if at % 2 == 1 and at < 6:
            project(at // 2)
        if at == 5:
            heads_forward(0, 2)
        if at == 6:
            heads_forward(2, 4)
        if at == 7:
            heads_forward(4, 6)
            attention_close()
        if at == 9:
            inner_blocks(0, 1)
        if at == 10:
            inner_blocks(1, 2)
    inner_blocks(2, 4)
    mlp_close()

    @pl.when(works)
    def _():
        guest_copy(COTANGENT).wait_recv()

    mlp_open_backward()
    for reader, wanted in WANTED.items():
        for turn in turns(*wanted):
            gather_finish(turn, reader)

    for block in range(4):
        second_grad(block)
        reduce_core(8 + block)
    one.tick(5)
    for block in range(2):
        inner_grad(block)
        reduce_core(4 + block)
    leads_first()
    one.tick(4)
    for block in range(2, 4):
        inner_grad(block)
        reduce_core(4 + block)
    leads_second()
    rows_leave()
    one.tick(4)
    leads_third()
    one.tick(4)
    leads_fourth()

    @pl.when(works)
    def _():
        pl.semaphore_signal(credit, inc=1, device_id=beside_core, device_id_type=MESH)

    leads_close()
    attention_open_backward()
    out_grad()

    @pl.when(works)
    def _():
        pl.semaphore_wait(credit, 1)

    reduce_core(3)
    one.tick(4)
    heads_backward(0, 2)
    two.tick(2)
    heads_backward(2, 4)
    one.tick()
    two.tick()
    heads_backward(4, 6)
    one.tick()
    pack_join()
    for block in range(3):
        project_grad(block)
        reduce_core(block)
        one.tick()
        two.tick(2)
        if block == 1:
            pack_second()

    def small_copy(step):
        return remote(
            small, small_all.at[index], small_send.at[step], small_recv.at[step], replica(step)
        )

    def sum_copy(step):
        return remote(
            small_sum, smalls.at[me], sum_send.at[step], sum_recv.at[step], others[step - 1]
        )

    def own_sum():
        return pltpu.make_async_copy(small_sum, smalls.at[me], sum_send.at[0])

    @pl.loop(1, replicas)
    def _(step):
        small_copy(step).start()

    small_all[index] = small[...]
    for block in range(3):
        tokens_back(block)
        one.tick()
        two.tick()
    tokens_close()
    pack_third()

    @pl.loop(1, replicas)
    def _(step):
        small_copy(step).wait()

    small_sum[...] = jnp.sum(small_all[...], axis=0)
    for place in range(1, sections):
        sum_copy(place).start()
    own_sum().start()
    pack_fourth()
    while one.left() or two.left():
        if one.left():
            one.tick()
        if two.left():
            two.tick()

    for place in range(1, sections):
        sum_copy(place).wait()
    own_sum().wait()
    pack_last()

    for holder in (0, 1):

        @pl.when(me == holder)
        def _():
            for block in OWN[holder]:
                write_out(block).wait()

    @pl.when(me != 3)
    def _():
        lead_copy(COT, cot_slab, cot_leads, 3).wait_send()

    @pl.when(me == 0)
    def _():
        lead_copy(H1, h1_slab, h1_leads, 1).wait_send()

    @pl.when(works)
    def _():
        lead_copy(H2, h2_slab, h2_leads, 2).wait_send()
        guest_copy(OUT).wait_send()
        guest_copy(GRAD).wait_send()

    @pl.when(me >= 2)
    def _():
        guest_copy(COTANGENT).wait_send()
        guest_copy(GRAD).wait_recv()

    rows_store(1).start()
    rows_store(1).wait()
    rows_store(0).wait()

    @pl.when(me == 1)
    def _():
        hop_copy(GRAD1, lead_grad1, -1).wait_send()
        hop_copy(HAND, handed, -1).wait_send()

    @pl.when(me == 2)
    def _():
        hop_copy(THIRD, lead_third, 1).wait_send()
        hop_copy(GRAD2, lead_grad2, -1).wait_send()

    @pl.when(me == 3)
    def _():
        for place in range(1, sections):
            spread_copy(FOURTH, lead_fourth, place).wait_send()
        hop_copy(GRAD3, lead_grad3, -1).wait_send()
        hop_copy(HAND, handed, -1).wait_send()


def run_layers(sections, replicas, tokens, cotangent, seg_doc, gain, bias, wide, half):
    groups = replicas // CUBE
    rows = 2 * tokens.shape[0]
    seg_rows = tokens.shape[0] // 2
    vector = (8, D)
    block = (2, 2, 2, PIECE, D)
    reduced_groups = max(groups - 1, 1)
    in_vmem = pl.BlockSpec(memory_space=pltpu.VMEM)
    anywhere = pl.BlockSpec(memory_space=pl.ANY)
    slab = pltpu.VMEM((SLAB, D), LOW)
    leads = pltpu.VMEM((sections, SLAB, D), LOW)
    low_rows = pltpu.VMEM((rows, D), LOW)
    full_rows = pltpu.VMEM((rows, D), F32)
    return pl.pallas_call(
        partial(layer_kernel, sections, replicas),
        out_shape=(
            jax.ShapeDtypeStruct(tokens.shape, LOW),
            jax.ShapeDtypeStruct(tokens.shape, LOW),
            jax.ShapeDtypeStruct((OWNED,) + block, LOW),
            jax.ShapeDtypeStruct((groups, CUBE // 2, SLAB, PACK), LOW),
            jax.ShapeDtypeStruct((sections,) + vector, F32),
            jax.ShapeDtypeStruct(
                (REDUCED if groups > 1 else 1, reduced_groups, PIECE, D), LOW
            ),
        ),
        in_specs=[anywhere] * 2 + [in_vmem] * 3 + [anywhere] * 4,
        out_specs=[anywhere] * 6,
        scratch_shapes=[
            pltpu.VMEM((REDUCED + 8,) + block, LOW),
            pltpu.VMEM((max(8 * rows, 6 * D), D), LOW),
            pltpu.VMEM((8, 2, 2, PIECE, D), LOW),
            pltpu.VMEM((SLOTS, 2, HALF, WIDTH), LOW),
            pltpu.VMEM((SLOTS, 2, HALF, WIDTH), LOW),
            pltpu.VMEM((SLOTS, HALF, WIDTH), LOW),
            pltpu.VMEM((SLOTS, HALF, WIDTH), LOW),
            pltpu.VMEM((REDUCED, PIECE, D), LOW),
            pltpu.VMEM((EARLY_PLACES, 2, 2, PIECE, D), LOW),
            pltpu.VMEM((sections,) + vector, F32),
            low_rows, low_rows, low_rows,
            pltpu.VMEM((rows, 3 * D), LOW),
            pltpu.VMEM((4, PAIRS, 2, seg_rows, seg_rows), F32),
            low_rows, low_rows, full_rows,
            pltpu.VMEM((rows, 128), F32),
            full_rows, full_rows,
            pltpu.VMEM((rows, 128), F32),
            full_rows, low_rows,
            slab, slab, slab, leads, leads, leads,
            slab, slab, slab, slab, slab,
            pltpu.VMEM((SLAB, 3 * D), LOW),
            pltpu.VMEM((SLAB, 3 * D), LOW),
            pltpu.VMEM((PAIRS, 2, SLAB, SLAB), F32),
            slab,
            pltpu.VMEM((SLAB, D), F32),
            pltpu.VMEM((SLAB, 128), F32),
            pltpu.VMEM((SLAB, 4 * D), LOW),
            pltpu.VMEM((SLAB, 4 * D), F32),
            pltpu.VMEM((SLAB, PACK), LOW),
            pltpu.VMEM((SLAB, HALF_PACK), LOW),
            pltpu.VMEM((CUBE // 2, SLAB, PACK), LOW),
            pltpu.VMEM(vector, F32),
            pltpu.VMEM((replicas,) + vector, F32),
            pltpu.VMEM(vector, F32),
            pltpu.VMEM((PIECE, WIDTH), LOW),
            DMA((2,)),
            DMA((4,)),
            DMA((4,)),
            DMA((2,)),
            DMA((ROUNDS,)),
            DMA((ROUNDS,)),
            DMA((4, 5)),
            DMA((4, 5)),
            DMA((GATHERED,)),
            DMA((2 * REDUCED,)),
            DMA((2 * REDUCED,)),
            DMA((SLOTS, 5)),
            DMA((SLOTS, 5)),
            DMA((2 * REDUCED,)),
            DMA((2 * REDUCED,)),
            DMA((2 * REDUCED if groups > 1 else 1, reduced_groups)),
            DMA((2 * REDUCED if groups > 1 else 1, reduced_groups)),
            DMA,
            DMA((SLOTS, 5)),
            DMA((SLOTS, 5)),
            DMA((OWNED,)),
            DMA((5,)),
            DMA((5,)),
            DMA((groups,)),
            DMA((groups,)),
            DMA((replicas,)),
            DMA((replicas,)),
            DMA((sections,)),
            DMA((sections,)),
            DMA((sections,)),
            DMA((sections,)),
            DMA((3,)),
            DMA((3, sections)),
            DMA((1, sections)),
            DMA((1,)),
            DMA((5,)),
            DMA((5,)),
            pltpu.SemaphoreType.REGULAR,
            pltpu.SemaphoreType.REGULAR((len(WAVES),)),
            pltpu.SemaphoreType.REGULAR((len(WAVES),)),
        ],
        compiler_params=pltpu.CompilerParams(
            collective_id=0, has_side_effects=True, vmem_limit_bytes=VMEM_BYTES
        ),
    )(
        tokens, cotangent, seg_doc, gain, bias,
        wide.reshape(2, 2, 2, PIECE, 4 * D), half.reshape(2, 2, 2, 2, PIECE, D), wide, half,
    )


VMEM_BYTES = 62 * 1024 * 1024


def close_kernel(
    total, packs, smalls, rows_in, grads_in,
    wide_out, half_out, gain_out, bias_out, rows_out, grads_out,
    blocks, packed, result, rows, grads, block_sem, result_sem, pack_sem, rows_sem, back_sem,
):
    me = lax.axis_index("section")
    near = me < 2
    groups = packs.shape[0]
    pack_copy = pltpu.make_async_copy(packs, packed, pack_sem)
    loads = [
        pltpu.make_async_copy(total.at[place], blocks.at[place], block_sem.at[place])
        for place in range(OWNED)
    ]
    passing = [
        (
            pltpu.make_async_copy(source, buffer, rows_sem.at[i]),
            pltpu.make_async_copy(buffer, target, back_sem.at[i]),
        )
        for i, (source, buffer, target) in enumerate(
            ((rows_in, rows, rows_out), (grads_in, grads, grads_out))
        )
    ]
    pack_copy.start()
    for load in loads:
        load.start()
    for arrive, _ in passing:
        arrive.start()

    every = jnp.sum(smalls[...], axis=0)
    mine = smalls[me]
    for row, out in ((0, gain_out), (1, bias_out)):
        value = jnp.where(me == 0, every[row : row + 1], every[2 + row : 3 + row])
        out[...] = jnp.where(near, value, 0.0) + mine[4 + row : 5 + row]

    pack_copy.wait()
    factors = packed[...].reshape(groups * CUBE // 2 * SLAB, PACK)
    stores = []
    for place in range(OWNED):
        if place < 4:
            left = factors[:, 0:D] if place < 3 else factors[:, LEFT_OUT:RIGHT]
            right = factors[:, RIGHT + place * D : RIGHT + (place + 1) * D]
            target = wide_out.at[0, :, pl.ds(place * D, D)]
        else:
            left = factors[:, LEFT_HALF + (place - 4) * D : LEFT_HALF + (place - 3) * D]
            right = factors[:, RIGHT_HALF:]
            target = half_out.at[0, pl.ds((place - 4) * D, D)]
        loads[place].wait()
        for strip in range(2):
            rows_of = pl.ds(strip * WIDTH, WIDTH)
            summed = blocks[place, strip].reshape(WIDTH, D).astype(F32)
            result[place, rows_of] = jnp.where(near, summed, 0.0) + outer(
                left[:, strip * WIDTH : (strip + 1) * WIDTH], right
            )
        store = pltpu.make_async_copy(result.at[place], target, result_sem.at[place])
        store.start()
        stores.append(store)
    for arrive, leave in passing:
        arrive.wait()
        leave.start()
    for store in stores:
        store.wait()
    for _, leave in passing:
        leave.wait()


def close(total, packs, smalls, rows, grads):
    in_vmem = pl.BlockSpec(memory_space=pltpu.VMEM)
    anywhere = pl.BlockSpec(memory_space=pl.ANY)
    return pl.pallas_call(
        close_kernel,
        out_shape=(
            jax.ShapeDtypeStruct((1, D, 4 * D), F32),
            jax.ShapeDtypeStruct((1, 2 * D, D), F32),
            jax.ShapeDtypeStruct((1, D), F32),
            jax.ShapeDtypeStruct((1, D), F32),
            jax.ShapeDtypeStruct(rows.shape, LOW),
            jax.ShapeDtypeStruct(rows.shape, LOW),
        ),
        in_specs=[anywhere, anywhere, in_vmem, anywhere, anywhere],
        out_specs=[anywhere, anywhere, in_vmem, in_vmem, anywhere, anywhere],
        scratch_shapes=[
            pltpu.VMEM(total.shape, LOW),
            pltpu.VMEM(packs.shape, LOW),
            pltpu.VMEM((OWNED, D, D), F32),
            pltpu.VMEM(rows.shape, LOW),
            pltpu.VMEM(rows.shape, LOW),
            DMA((OWNED,)),
            DMA((OWNED,)),
            DMA,
            DMA((2,)),
            DMA((2,)),
        ],
        compiler_params=pltpu.CompilerParams(vmem_limit_bytes=VMEM_BYTES),
    )(total, packs, smalls, rows, grads)


def on_device(tokens, cotangent, seg_doc, wide_in, half_out, norm_gain, norm_bias):
    sections = lax.axis_size("section")
    replicas = lax.axis_size("dp")
    rows, grads, total, packs, smalls, _ = run_layers(
        sections, replicas, tokens, cotangent, seg_doc, norm_gain, norm_bias, wide_in[0], half_out[0]
    )
    wide_grad, half_grad, gain_grad, bias_grad, layer_out, tokens_grad = close(
        total, packs, smalls, rows, grads
    )
    return layer_out, tokens_grad, wide_grad, half_grad, gain_grad, bias_grad


def solution(mesh):
    placed = (
        P(("dp", "section"), None),
        P(("dp", "section"), None),
        P("dp", None),
        P("section", None, None),
        P("section", None, None),
        P("section", None),
        P("section", None),
    )
    return jax.shard_map(
        on_device,
        mesh=mesh,
        in_specs=placed,
        out_specs=(
            P(("dp", "section"), None),
            P(("dp", "section"), None),
            P("section", None, None),
            P("section", None, None),
            P("section", None),
            P("section", None),
        ),
        check_vma=False,
    )
```

```python
from functools import partial

import jax
import jax.numpy as jnp
from jax import lax
from jax.experimental import pallas as pl
from jax.experimental.pallas import tpu as pltpu
from jax.sharding import PartitionSpec as P

D = 768
HEADS = 12
PAIRS = HEADS // 2
CUBE = 8
PIECE = D // CUBE
HALF = PIECE // 2
WIDTH = D // 2
SLAB = 16
HOLDER = (0, 0, 0, 0, 1, 1, 1, 1, 0, 0, 1, 1, 2, 2)
GATHERED = len(HOLDER)
ROUNDS = 2 * GATHERED
REDUCED = 12
OWN = {0: (0, 1, 2, 3, 8, 9), 1: (4, 5, 6, 7, 10, 11)}
OWNED = len(OWN[0])
WANTED = {0: (4, 5, 6, 7, 10, 11), 1: (0, 1, 2, 3, 8, 9), 3: (12, 13)}
WAVES = ((8, 9, 10, 11, 4, 5, 6, 7), (3, 0, 1, 2))
EARLY = (8, 10)
SPACING = (4, 2)
EARLY_AT = (13, 5)
SLOT = {
    2 * block + side: (2 * place + side) % 4
    for wanted in WANTED.values()
    for place, block in enumerate(wanted)
    for side in range(2)
}


def sum_slots(orders):
    slots, base = {}, 0
    for spacing, order in zip(SPACING, orders):
        late = [block for block in order if block not in EARLY]
        for place, block in enumerate(late):
            for side in range(2):
                slots[2 * block + side] = base + (2 * place + side) % (2 * spacing)
        base += 2 * spacing
    for place, block in enumerate(EARLY):
        for side in range(2):
            slots[2 * block + side] = base + 2 * place + side
    return slots


SUM_SLOT = sum_slots(WAVES)
BACK_SLOT = {}
for holder in OWN:
    BACK_SLOT |= {
        turn: slot
        for turn, slot in sum_slots(
            [[b for b in order if HOLDER[b] == holder] for order in WAVES]
        ).items()
        if HOLDER[turn // 2] == holder
    }
SLOTS = 2 * sum(SPACING) + 2 * len(EARLY)
EARLY_PLACE = {
    block: [other for other in EARLY if HOLDER[other] == HOLDER[block]].index(block)
    for block in EARLY
}
EARLY_PLACES = max(EARLY_PLACE.values(), default=0) + 1
LEFT_OUT, RIGHT, LEFT_HALF, RIGHT_HALF, PACK = D, 2 * D, 6 * D, 8 * D, 9 * D
HALF_PACK = PACK // 2
LOW = jnp.bfloat16
F32 = jnp.float32
DMA = pltpu.SemaphoreType.DMA
MESH = pl.DeviceIdType.MESH


def dot(left, right):
    return jnp.dot(left, right, preferred_element_type=F32)


def dot_right(left, right):
    return lax.dot_general(left, right, (((1,), (1,)), ((), ())), preferred_element_type=F32)


def outer(left, right):
    return lax.dot_general(left, right, (((0,), (0,)), ((), ())), preferred_element_type=F32)


def normalize(summed, gain, bias):
    average = jnp.mean(summed, axis=-1, keepdims=True)
    centred = summed - average
    inv_dev = lax.rsqrt(jnp.mean(centred * centred, axis=-1, keepdims=True) + 1e-05)
    normed = centred * inv_dev
    return normed * gain + bias, normed, inv_dev


def normalize_backward(grad, normed, inv_dev, gain):
    scaled = grad * gain
    mean_scaled = jnp.mean(scaled, axis=-1, keepdims=True)
    mean_normed = jnp.mean(scaled * normed, axis=-1, keepdims=True)
    grad_sum = inv_dev * (scaled - mean_scaled - normed * mean_normed)
    return (
        grad_sum,
        jnp.sum(grad * normed, axis=0, keepdims=True),
        jnp.sum(grad, axis=0, keepdims=True),
    )


def gelu_pair(value):
    bell = jnp.exp(-0.5 * value * value)
    base = 1.0 + (0.3275911 * 0.7071067811865476) * jnp.abs(value)
    guess = pl.reciprocal(base, approx=True)
    t = guess * (2.0 - base * guess)
    poly = t * (
        0.5 * 0.254829592
        + t
        * (
            0.5 * -0.284496736
            + t * (0.5 * 1.421413741 + t * (0.5 * -1.453152027 + t * (0.5 * 1.061405429)))
        )
    )
    tail = poly * bell
    below = jnp.where(value >= 0, 1.0 - tail, tail)
    return value * below, below + value * bell * 0.3989422804014327


def position():
    index = lax.axis_index("dp")
    return (lax.rem(index // 4, 2), lax.rem(index // 2, 2), lax.rem(index, 2), index // CUBE)


def remote(source, target, send, receive, device):
    return pltpu.make_async_remote_copy(
        src_ref=source,
        dst_ref=target,
        send_sem=send,
        recv_sem=receive,
        device_id=device,
        device_id_type=MESH,
    )


def layer_kernel(
    sections, replicas,
    tokens, cotangent, seg_doc, norm_gain, norm_bias, wide, half, wide_flat, half_flat,
    layer_out, grad_tokens, total, packs, smalls, group_in,
    blocks, flat, core_in, one_a, one_b, two_a, two_b, line_in, early_in, vectors,
    token_rows, cot_rows, out_rows,
    qkv, probs, context, h1, norm0, dev0, summed, norm1, dev1, branch, kept,
    cot_slab, h1_slab, h2_slab, cot_leads, h1_leads, h2_leads,
    lead_third, lead_fourth, lead_grad3, lead_grad2, lead_grad1, handed,
    lead_qkv, lead_probs, lead_context, lead_norm, lead_dev, lead_act, lead_slope,
    pack, pack_in, factors, small, small_all, small_sum, group_piece,
    rows_load, guest_send, guest_recv, rows_out,
    line_send, line_recv, cube_send, cube_recv, load_sem,
    core_send, core_recv, rs_send, rs_recv, z_send, z_recv, group_send, group_recv, group_load, ag_send, ag_recv,
    out_sem, pack_send, pack_recv, group_pack_send, group_pack_recv,
    small_send, small_recv, sum_send, sum_recv,
    vector_send, vector_recv, lead_send, lead_recv, spread_send, spread_recv, hop_send, hop_recv,
    credit, clear_x, clear_y,
):
    me = lax.axis_index("section")
    index = lax.axis_index("dp")
    y, x, core, group = position()
    groups = replicas // CUBE
    micro_rows = tokens.shape[0]
    seg_rows = micro_rows // 2
    rows_all = 2 * micro_rows
    works = me < 2

    def cube_peer(yy, xx, cc):
        return {"dp": group * CUBE + yy * 4 + xx * 2 + cc}

    beside_x = cube_peer(y, 1 - x, core)
    beside_y = cube_peer(1 - y, x, core)
    beside_core = cube_peer(y, x, 1 - core)
    others = [{"section": lax.rem(me + step, sections)} for step in range(1, sections)]

    def replica(step):
        return {"dp": lax.rem(index + step, replicas)}

    barrier = pltpu.get_barrier_semaphore()
    for other in others:
        pl.semaphore_signal(barrier, inc=1, device_id=other, device_id_type=MESH)

    @pl.loop(1, replicas)
    def _(step):
        pl.semaphore_signal(barrier, inc=1, device_id=replica(step), device_id_type=MESH)

    own_part, guest_part = pl.ds(0, micro_rows), pl.ds(micro_rows, micro_rows)

    def load_rows(place):
        source, target = ((tokens, token_rows), (cotangent, cot_rows))[place]
        return pltpu.make_async_copy(source, target.at[own_part], rows_load.at[place])

    load_rows(0).start()
    load_rows(1).start()

    def load(block):
        if block < 8:
            source = wide.at[:, :, :, :, pl.ds((block % 4) * D, D)]
        else:
            source = half.at[block % 2]
        return pltpu.make_async_copy(source, blocks.at[block], load_sem.at[block])

    def flat_rows(place):
        return pl.ds(place * D, D)

    def load_own(place):
        if place < 4:
            source = wide_flat.at[:, pl.ds(place * D, D)]
        else:
            source = half_flat.at[flat_rows(place - 4)]
        return pltpu.make_async_copy(source, flat.at[flat_rows(place)], load_sem.at[place])

    for holder in (0, 1):

        @pl.when(me == holder)
        def _():
            for block in OWN[holder]:
                load(block).start()

    @pl.when(me >= 2)
    def _():
        for place in range(4):
            load_own(place).start()

    def load_upper(block):
        return pltpu.make_async_copy(
            half.at[block], core_in.at[pl.ds(2 * block, 2)], load_sem.at[REDUCED + block]
        )

    @pl.when(me == 2)
    def _():
        for block in range(2):
            load_upper(block).start()

    @pl.when(me == 3)
    def _():
        for place in (4, 5):
            load_own(place).start()

    pl.semaphore_wait(barrier, sections - 1 + replicas - 1)

    def guest_copy(kind):
        down = {"section": lax.rem(me + sections - 2, sections)}
        up = {"section": lax.rem(me + 2, sections)}
        source, target, device = (
            (token_rows.at[own_part], token_rows.at[guest_part], down),
            (cot_rows.at[own_part], cot_rows.at[guest_part], down),
            (out_rows.at[guest_part], out_rows.at[own_part], up),
            (h1.at[guest_part], h1.at[own_part], up),
        )[kind]
        return remote(source, target, guest_send.at[kind], guest_recv.at[kind], device)

    TOKENS, COTANGENT, OUT, GRAD = 0, 1, 2, 3

    load_rows(0).wait()
    load_rows(1).wait()

    @pl.when(me >= 2)
    def _():
        guest_copy(TOKENS).start()

    row_of = lax.broadcasted_iota(jnp.int32, (SLAB, D), 0)

    def lead_rows(ref, count):
        value = jnp.zeros((SLAB, D), F32)
        for lead in range(count):
            row = ref[lead * seg_rows : lead * seg_rows + SLAB].astype(F32)[0:1]
            value = jnp.where(row_of == lead, row, value)
        return value.astype(LOW)

    def lead_copy(kind, slab, target, reader):
        return remote(
            slab, target.at[me], lead_send.at[kind], lead_recv.at[kind, me], {"section": reader}
        )

    def lead_start(kind, slab, target, reader):
        @pl.when(me != reader)
        def _():
            lead_copy(kind, slab, target, reader).start()

        @pl.when(me == reader)
        def _():
            target[reader] = slab[...]

    def lead_wait(kind, slab, target, reader, senders):
        for section in range(senders):
            if section != reader:
                remote(
                    slab, target.at[section], lead_send.at[kind], lead_recv.at[kind, section],
                    {"section": section},
                ).wait_recv()

    def collected(target, senders):
        value = jnp.zeros((SLAB, D), F32)
        for section in range(senders):
            slab = target[section].astype(F32)
            for micro in range(section, sections, senders):
                for lead in range(2):
                    place = (micro - section) // senders * 2 + lead
                    value = jnp.where(
                        row_of == 2 * micro + lead, slab[place : place + 1], value
                    )
        return value

    def spread_copy(kind, slab, step):
        return remote(
            slab, slab, spread_send.at[kind, step], spread_recv.at[kind], others[step - 1]
        )

    def hop_copy(kind, slab, step):
        return remote(
            slab, slab, hop_send.at[kind], hop_recv.at[kind],
            {"section": lax.rem(me + step + sections, sections)},
        )

    def leads_of(slab, micro):
        value = slab[...].astype(F32)
        return [
            jnp.sum(jnp.where(row_of == 2 * micro + lead, value, 0.0), axis=0, keepdims=True)
            for lead in range(2)
        ]

    COT, H1, H2 = 0, 1, 2
    FOURTH = 0
    THIRD, GRAD3, GRAD2, HAND, GRAD1 = 0, 1, 2, 3, 4

    def vector_copy(step):
        return remote(
            vectors.at[me], vectors.at[me], vector_send.at[step], vector_recv.at[step],
            others[step - 1],
        )

    vectors[me, 0:1] = norm_gain[...]
    vectors[me, 1:2] = norm_bias[...]
    for step in range(1, sections):
        vector_copy(step).start()
    cot_slab[...] = lead_rows(cot_rows, 2)
    lead_start(COT, cot_slab, cot_leads, 3)

    upper, lower = pl.ds(0, HALF), pl.ds(HALF, HALF)

    def lanes_of(turn):
        return pl.ds((turn % 2) * WIDTH, WIDTH)

    def turns(*order):
        return tuple(2 * block + side for block in order for side in range(2))

    def place_of(block):
        if block < REDUCED:
            return blocks.at[block]
        return core_in.at[pl.ds(2 * (block - REDUCED), 2)]

    def line_copy(turn, reader):
        block, lanes = turn // 2, lanes_of(turn)
        piece = place_of(block).at[y, x, core, :, lanes]
        return remote(
            piece,
            piece,
            line_send.at[turn],
            line_recv.at[turn],
            {"section": reader},
        )

    def cube_copy(turn, stage):
        full, lanes = place_of(turn // 2), lanes_of(turn)
        ref, peer = (
            (full.at[y, x, core, upper, lanes], beside_x),
            (full.at[y, x, core, lower, lanes], beside_y),
            (full.at[y, :, core, upper, lanes], beside_y),
            (full.at[:, x, core, lower, lanes], beside_x),
            (full.at[:, :, core, :, lanes], beside_core),
        )[stage]
        slot = SLOT[turn]
        return remote(ref, ref, cube_send.at[slot, stage], cube_recv.at[slot, stage], peer)

    def gather_line(turn, reader):
        @pl.when(me == reader)
        def _():
            line_copy(turn, reader).wait_recv()
            cube_copy(turn, 0).start()
            cube_copy(turn, 1).start()

    def gather_two(turn, reader):
        @pl.when(me == reader)
        def _():
            cube_copy(turn, 0).wait()
            cube_copy(turn, 2).start()
            cube_copy(turn, 1).wait()
            cube_copy(turn, 3).start()

    def gather_three(turn, reader):
        @pl.when(me == reader)
        def _():
            cube_copy(turn, 2).wait()
            cube_copy(turn, 3).wait()
            cube_copy(turn, 4).start()

    def gather_ready(turn, reader):
        @pl.when(me == reader)
        def _():
            cube_copy(turn, 4).wait()

    def gather_finish(turn, reader):
        @pl.when(me == HOLDER[turn // 2])
        def _():
            line_copy(turn, reader).wait_send()

    def gather_send():
        for reader, wanted in WANTED.items():

            @pl.when(me == HOLDER[wanted[0]])
            def _():
                for turn in turns(*wanted):
                    line_copy(turn, reader).start()

    gather_plan = ((gather_ready, 6), (gather_three, 4), (gather_two, 2), (gather_line, 0))
    gather_ticks = 2 * OWNED + gather_plan[0][1]

    def gather_tick(tick):
        for stage, offset in gather_plan:
            at = tick - offset
            for reader, wanted in WANTED.items():
                if 0 <= at < 2 * len(wanted):
                    stage(2 * wanted[at // 2] + at % 2, reader)

    def gather_wait_own():
        @pl.when(me == 2)
        def _():
            for block in range(2):
                load_upper(block).wait()

        for holder in (0, 1):

            @pl.when(me == holder)
            def _():
                for block in OWN[holder]:
                    load(block).wait()

    def worker(step):
        def run(*given):
            @pl.when(works)
            def _():
                step(*given)

        return run

    def weight(block):
        return blocks[block].reshape(D, D)

    def act_rows(block):
        return pl.ds(pl.multiple_of(block * rows_all, SLAB), rows_all)

    def slope_rows(block):
        return pl.ds(pl.multiple_of((4 + block) * rows_all, SLAB), rows_all)

    lane_of = lax.broadcasted_iota(jnp.int32, (1, 128), 1)
    first_half = lane_of < 64
    head_masks = (first_half.astype(LOW), (~first_half).astype(LOW))
    segs = range(4)

    def chunks(size, body):
        @pl.loop(0, rows_all // size)
        def _(step):
            body(pl.multiple_of(step * size, size), size)

    @worker
    def project(block):
        qkv[:, block * D : (block + 1) * D] = dot(token_rows[...], weight(block)).astype(LOW)

    def seg_slice(seg):
        return pl.ds(seg * seg_rows, seg_rows)

    def pair_lanes(pair):
        return [pl.ds(pl.multiple_of(part * D + pair * 128, 128), 128) for part in range(3)]

    def softmax(scores):
        raised = jnp.exp(scores - jnp.max(scores, axis=-1, keepdims=True))
        return raised / jnp.sum(raised, axis=-1, keepdims=True)

    @worker
    def heads_forward(first, last):
        @pl.loop(first, last)
        def _(pair):
            at_q, at_k, at_v = pair_lanes(pair)
            heads = [(seg, place) for seg in segs for place in range(2)]
            scores = [
                dot_right(qkv[seg_slice(seg), at_q] * head_masks[place], qkv[seg_slice(seg), at_k])
                * 0.125
                for seg, place in heads
            ]
            found = [softmax(score) for score in scores]
            for (seg, place), prob in zip(heads, found):
                probs[seg, pair, place] = prob
            mixed = [
                dot(prob.astype(LOW), qkv[seg_slice(seg), at_v])
                for (seg, place), prob in zip(heads, found)
            ]
            for seg in segs:
                context[seg_slice(seg), at_q] = jnp.where(
                    first_half, mixed[2 * seg], mixed[2 * seg + 1]
                ).astype(LOW)

    @worker
    def attention_close():
        summed[...] = dot_right(context[...], weight(3))
        gain, bias = vectors[0, 0:1], vectors[0, 1:2]

        def body(start, size):
            rows = pl.ds(start, size)
            out, normed, inv_dev = normalize(
                token_rows[rows].astype(F32) + summed[rows], gain, bias
            )
            norm0[rows] = normed
            dev0[rows] = jnp.broadcast_to(inv_dev, (size, 128))
            h1[rows] = out.astype(LOW)
            branch[rows] = jnp.zeros((size, D), F32)

        chunks(128, body)
        h1_slab[...] = lead_rows(h1, 4)
        lead_start(H1, h1_slab, h1_leads, 1)

    @worker
    def inner_blocks(first, last):
        count = 2
        size = rows_all // count

        @pl.loop(first, last)
        def _(place):
            block = lax.rem(2 * me + place, 4)
            for step in range(count):
                rows = pl.ds(step * size, size)
                start = pl.multiple_of(block * rows_all + step * size, SLAB)
                value, grade = gelu_pair(dot(h1[rows], weight(4 + block)))
                flat[pl.ds(start, size)] = value.astype(LOW)
                flat[pl.ds(pl.multiple_of(4 * rows_all + start, SLAB), size)] = grade.astype(LOW)
                branch[rows] += dot(flat[pl.ds(start, size)], weight(8 + block))

    @worker
    def mlp_close():
        gain, bias = vectors[1, 0:1], vectors[1, 1:2]

        def body(start, size):
            rows = pl.ds(start, size)
            out, normed, inv_dev = normalize(h1[rows].astype(F32) + branch[rows], gain, bias)
            norm1[rows] = normed
            dev1[rows] = jnp.broadcast_to(inv_dev, (size, 128))
            out_rows[rows] = out.astype(LOW)

        chunks(128, body)
        h2_slab[...] = lead_rows(out_rows, 4)
        lead_start(H2, h2_slab, h2_leads, 2)

    @worker
    def rows_leave():
        guest_copy(OUT).start()

    def add_small(row, value):
        small[row : row + 1] += value

    @worker
    def mlp_open_backward():
        gain = vectors[1, 0:1]

        def body(start, size):
            rows = pl.ds(start, size)
            place = start + lax.broadcasted_iota(jnp.int32, (size, D), 0)
            grad = jnp.where(lax.rem(place, seg_rows) == 0, 0.0, cot_rows[rows].astype(F32))
            grad_sum, grad_gain, grad_bias = normalize_backward(
                grad, norm1[rows], dev1[rows][:, 0:1], gain
            )
            branch[rows] = grad_sum
            kept[rows] = grad_sum.astype(LOW)
            add_small(2, grad_gain)
            add_small(3, grad_bias)

        chunks(128, body)

    def part(block):
        return block + 4 if block < 4 else block + 8

    def store_part(block, left, right):
        for strip in range(2):
            lanes = slice(strip * WIDTH, (strip + 1) * WIDTH)
            blocks[part(block), strip] = (
                outer(left[:, lanes], right).astype(LOW).reshape(2, 2, PIECE, D)
            )

    @worker
    def second_grad(block):
        store_part(8 + block, flat[act_rows(block)], kept[...])

    @worker
    def inner_grad(block):
        grad_act = dot_right(kept[...], weight(8 + block))
        grad_inner = (grad_act * flat[slope_rows(block)].astype(F32)).astype(LOW)
        flat[act_rows(block)] = grad_inner
        branch[...] += dot_right(flat[act_rows(block)], weight(4 + block))
        store_part(4 + block, h1[...], flat[act_rows(block)])

    @worker
    def attention_open_backward():
        gain = vectors[0, 0:1]
        leads = leads_of(lead_grad1, me) + leads_of(lead_grad1, me + 2)

        def body(start, size):
            rows = pl.ds(start, size)
            place = start + lax.broadcasted_iota(jnp.int32, (size, D), 0)
            grad = branch[rows]
            for lead in range(4):
                grad = jnp.where(place == lead * seg_rows, leads[lead], grad)
            grad = grad.astype(LOW).astype(F32)
            grad_sum, grad_gain, grad_bias = normalize_backward(
                grad, norm0[rows], dev0[rows][:, 0:1], gain
            )
            summed[rows] = grad_sum
            kept[rows] = grad_sum.astype(LOW)
            add_small(0, grad_gain)
            add_small(1, grad_bias)

        chunks(128, body)

    @worker
    def out_grad():
        store_part(3, kept[...], context[...])
        context[...] = dot(kept[...], weight(3)).astype(LOW)

    @worker
    def heads_backward(first, last):
        @pl.loop(first, last)
        def _(pair):
            at_q, at_k, at_v = pair_lanes(pair)
            heads = [(seg, place) for seg in segs for place in range(2)]
            grad_probs = [
                dot_right(
                    context[seg_slice(seg), at_q] * head_masks[place], qkv[seg_slice(seg), at_v]
                )
                for seg, place in heads
            ]
            grad_scores = []
            for (seg, place), grad_prob in zip(heads, grad_probs):
                prob = probs[seg, pair, place]
                inside = prob * grad_prob
                grad_score = inside - prob * jnp.sum(inside, axis=-1, keepdims=True)
                grad_scores.append(grad_score.astype(LOW))
            for seg in segs:
                rows = seg_slice(seg)
                query, key, grad = qkv[rows, at_q], qkv[rows, at_k], context[rows, at_q]
                mine = grad_scores[2 * seg : 2 * seg + 2]
                found = [probs[seg, pair, place].astype(LOW) for place in range(2)]
                for at, both, scale in (
                    (at_q, [dot(score, key) for score in mine], 0.125),
                    (at_k, [outer(score, query) for score in mine], 0.125),
                    (at_v, [outer(prob, grad) for prob in found], 1.0),
                ):
                    merged = jnp.where(first_half, both[0], both[1]) * scale
                    qkv[rows, at] = merged.astype(LOW)

    @worker
    def project_grad(block):
        store_part(block, token_rows[...], qkv[:, block * D : (block + 1) * D])

    @worker
    def tokens_back(block):
        summed[...] += dot_right(qkv[:, block * D : (block + 1) * D], weight(block))

    @worker
    def tokens_close():
        h1[...] = summed[...].astype(LOW)
        guest_copy(GRAD).start()

    def leads_mlp_forward(value, first, second, gain, bias):
        total_branch = value.astype(F32)
        for block in range(4):
            lanes = slice(block * D, (block + 1) * D)
            out, grade = gelu_pair(dot(value, first(block)))
            lead_act[:, lanes] = out.astype(LOW)
            lead_slope[:, lanes] = grade
            total_branch = total_branch + dot(lead_act[:, lanes], second(block))
        out, normed, inv_dev = normalize(total_branch, gain, bias)
        lead_norm[...] = normed
        lead_dev[...] = jnp.broadcast_to(inv_dev, (SLAB, 128))
        pack[:, 0:D] = value
        pack[:, LEFT_OUT:RIGHT] = value
        return out

    def leads_mlp_backward(grad, first, second, gain):
        grad_sum, grad_gain, grad_bias = normalize_backward(
            grad, lead_norm[...], lead_dev[:, 0:1], gain
        )
        add_small(4, grad_gain)
        add_small(5, grad_bias)
        low_sum = grad_sum.astype(LOW)
        result = grad_sum
        for block in range(4):
            lanes = slice(block * D, (block + 1) * D)
            grad_inner = (dot_right(low_sum, second(block)) * lead_slope[:, lanes]).astype(LOW)
            pack[:, RIGHT + block * D : RIGHT + (block + 1) * D] = grad_inner
            result = result + dot_right(grad_inner, first(block))
        pack[:, LEFT_HALF:RIGHT_HALF] = lead_act[:, 2 * D :]
        pack[:, RIGHT_HALF:] = low_sum
        handed[:, 0 : 2 * D] = lead_act[:, 0 : 2 * D]
        handed[:, 2 * D :] = low_sum
        return result

    def own_weight(place):
        return flat[flat_rows(place)]

    def last_second(block):
        if block >= 2:
            return own_weight(2 + block)
        return core_in[2 * block : 2 * block + 2].reshape(D, D)

    def leads_first():
        @pl.when(me == 2)
        def _():
            lead_wait(H2, h2_slab, h2_leads, 2, 2)
            for place in range(4):
                load_own(place).wait()
            value = collected(h2_leads, 2).astype(LOW)
            pack[:, 0:D] = value
            for block in range(3):
                lead_qkv[:, block * D : (block + 1) * D] = dot(value, own_weight(block)).astype(LOW)
            docs = seg_doc[...]
            row, column = (lax.broadcasted_iota(jnp.int32, (SLAB, SLAB), i) for i in range(2))
            sort = jnp.where(row == column, 2.0, 0.0)
            for micro in range(seg_doc.shape[0]):
                pair_sort = jnp.where(
                    docs[micro : micro + 1, 0:1] == docs[micro : micro + 1, 1:2], 2.0, 1.0
                )
                near = (row // 2 == micro) & (column // 2 == micro) & (row != column)
                sort = jnp.where(near, pair_sort, sort)
            for pair in range(PAIRS):
                at = [slice(p * D + pair * 128, p * D + (pair + 1) * 128) for p in range(3)]
                query, key, val = (lead_qkv[:, lanes] for lanes in at)
                parts = []
                for place in range(2):
                    scores = dot_right(query * head_masks[place], key) * 0.125
                    scores = jnp.where(
                        sort > 1.5, scores, jnp.where(sort > 0.5, -1000000000.0, -1e30)
                    )
                    raised = jnp.exp(scores - jnp.max(scores, axis=-1, keepdims=True))
                    prob = raised / jnp.sum(raised, axis=-1, keepdims=True)
                    lead_probs[pair, place] = prob
                    parts.append(dot(prob.astype(LOW), val))
                lead_context[:, pair * 128 : (pair + 1) * 128] = jnp.where(
                    first_half, parts[0], parts[1]
                ).astype(LOW)
            summed_rows = value.astype(F32) + dot_right(lead_context[...], own_weight(3))
            out, normed, inv_dev = normalize(summed_rows, vectors[2, 0:1], vectors[2, 1:2])
            lead_norm[...] = normed
            lead_dev[...] = jnp.broadcast_to(inv_dev, (SLAB, 128))
            lead_third[...] = out.astype(LOW)
            hop_copy(THIRD, lead_third, 1).start()

        @pl.when(me == 1)
        def _():
            lead_wait(H1, h1_slab, h1_leads, 1, 2)
            leads_mlp_forward(
                collected(h1_leads, 2).astype(LOW),
                lambda block: weight(4 + block),
                lambda block: weight(8 + block),
                vectors[1, 0:1],
                vectors[1, 1:2],
            )

    def leads_second():
        @pl.when(me == 3)
        def _():
            hop_copy(THIRD, lead_third, -1).wait_recv()
            for place in range(6):
                load_own(place).wait()
            out = leads_mlp_forward(
                lead_third[...], own_weight, last_second, vectors[3, 0:1], vectors[3, 1:2]
            )
            lead_fourth[...] = out.astype(LOW)
            for step in range(1, sections):
                spread_copy(FOURTH, lead_fourth, step).start()
            lead_wait(COT, cot_slab, cot_leads, 3, sections)
            grad = leads_mlp_backward(
                collected(cot_leads, sections), own_weight, last_second, vectors[3, 0:1]
            )
            lead_grad3[...] = grad.astype(LOW)
            hop_copy(GRAD3, lead_grad3, -1).start()
            hop_copy(HAND, handed, -1).start()

    def leads_third():
        @pl.when(me == 2)
        def _():
            hop_copy(GRAD3, lead_grad3, 1).wait_recv()
            grad_sum, grad_gain, grad_bias = normalize_backward(
                lead_grad3[...].astype(F32), lead_norm[...], lead_dev[:, 0:1], vectors[2, 0:1]
            )
            add_small(4, grad_gain)
            add_small(5, grad_bias)
            low_sum = grad_sum.astype(LOW)
            pack[:, LEFT_OUT:RIGHT] = low_sum
            pack[:, RIGHT + 3 * D : LEFT_HALF] = lead_context[...]
            grad_context = dot(low_sum, own_weight(3)).astype(LOW)
            for pair in range(PAIRS):
                at = [slice(p * D + pair * 128, p * D + (pair + 1) * 128) for p in range(3)]
                query, key, val = (lead_qkv[:, lanes] for lanes in at)
                grad = grad_context[:, pair * 128 : (pair + 1) * 128]
                grads = ([], [], [])
                for place in range(2):
                    prob = lead_probs[pair, place]
                    grad_prob = dot_right(grad * head_masks[place], val)
                    inside = prob * grad_prob
                    grad_score = inside - prob * jnp.sum(inside, axis=-1, keepdims=True)
                    grad_score = grad_score.astype(LOW)
                    grads[0].append(dot(grad_score, key))
                    grads[1].append(outer(grad_score, query))
                    grads[2].append(outer(prob.astype(LOW), grad))
                for lanes, pair_grads, scale in zip(at, grads, (0.125, 0.125, 1.0)):
                    merged = jnp.where(first_half, pair_grads[0], pair_grads[1]) * scale
                    pack[:, RIGHT + lanes.start : RIGHT + lanes.stop] = merged.astype(LOW)
            result = grad_sum
            for block in range(3):
                result = result + dot_right(
                    pack[:, RIGHT + block * D : RIGHT + (block + 1) * D], own_weight(block)
                )
            lead_grad2[...] = result.astype(LOW)
            hop_copy(GRAD2, lead_grad2, -1).start()
            hop_copy(HAND, handed, 1).wait_recv()
            pack[:, LEFT_HALF:] = handed[...]

    def leads_fourth():
        @pl.when(me == 1)
        def _():
            hop_copy(GRAD2, lead_grad2, 1).wait_recv()
            grad = leads_mlp_backward(
                lead_grad2[...].astype(F32),
                lambda block: weight(4 + block),
                lambda block: weight(8 + block),
                vectors[1, 0:1],
            )
            lead_grad1[...] = grad.astype(LOW)
            hop_copy(GRAD1, lead_grad1, -1).start()
            hop_copy(HAND, handed, -1).start()

    half_lanes = pl.ds(pl.multiple_of(core * HALF_PACK, 128), HALF_PACK)
    other_lanes = pl.ds(pl.multiple_of((1 - core) * HALF_PACK, 128), HALF_PACK)
    first_peer = {"dp": group * CUBE + (y + core - 2 * y * core) * 4
                  + (x + (1 - core) * (1 - 2 * x)) * 2 + core}
    second_peer = {"dp": group * CUBE + (y + (1 - core) * (1 - 2 * y)) * 4
                   + (x + core - 2 * x * core) * 2 + core}

    def pack_copy(stage):
        chip = y * 2 + x
        first_chip = (y + core - 2 * y * core) * 2 + x + (1 - core) * (1 - 2 * x)
        if stage == 0:
            source, target, peer = pack.at[:, other_lanes], pack_in, beside_core
        elif stage == 1:
            source = target = factors.at[chip, :, half_lanes]
            peer = first_peer
        elif stage == 2:
            source = target = factors.at[chip, :, half_lanes]
            peer = second_peer
        elif stage == 3:
            source = target = factors.at[first_chip, :, half_lanes]
            peer = second_peer
        else:
            source = target = factors.at[:, :, half_lanes]
            peer = beside_core
        return remote(source, target, pack_send.at[stage], pack_recv.at[stage], peer)

    def pack_join():
        pack_copy(0).wait()

        @pl.loop(0, HALF_PACK // WIDTH)
        def _(step):
            start = pl.multiple_of(step * WIDTH, 128)
            lanes = pl.ds(pl.multiple_of(core * HALF_PACK + start, 128), WIDTH)
            mine = pack[:, lanes].astype(F32)[0:8]
            theirs = pack_in[:, pl.ds(start, WIDTH)].astype(F32)[0:8]
            low_rows = jnp.where(core == 0, mine, theirs)
            high_rows = jnp.where(core == 0, theirs, mine)
            factors[y * 2 + x, :, lanes] = jnp.concatenate([low_rows, high_rows]).astype(LOW)

        pack_copy(1).start()

    def pack_second():
        pack_copy(1).wait()
        pack_copy(2).start()
        pack_copy(3).start()

    def pack_third():
        pack_copy(2).wait()
        pack_copy(3).wait()
        pack_copy(4).start()

    def to_packs(step):
        return remote(
            factors, packs.at[group], group_pack_send.at[step], group_pack_recv.at[step],
            {"dp": lax.rem(index + step * CUBE, replicas)},
        )

    def own_pack():
        return pltpu.make_async_copy(factors, packs.at[group], group_pack_send.at[0])

    def pack_fourth():
        pack_copy(4).wait()
        own_pack().start()
        for step in range(1, groups):
            to_packs(step).start()

    def pack_last():
        own_pack().wait()
        for step in range(1, groups):
            to_packs(step).wait()

    def rows_store(place):
        source, target = ((out_rows, layer_out), (h1, grad_tokens))[place]
        return pltpu.make_async_copy(source.at[own_part], target, rows_out.at[place])

    def leads_close():
        @pl.when(me != 3)
        def _():
            spread_copy(FOURTH, lead_fourth, 1).wait_recv()

        @pl.when(me >= 2)
        def _():
            guest_copy(OUT).wait_recv()

        leads = leads_of(lead_fourth, me)
        for lead in range(2):
            rows = pl.ds(lead * seg_rows, SLAB)
            out_rows[rows] = jnp.where(
                row_of == 0, leads[lead], out_rows[rows].astype(F32)
            ).astype(LOW)
        rows_store(0).start()

        @pl.when(me == 0)
        def _():
            hop_copy(GRAD1, lead_grad1, 1).wait_recv()
            hop_copy(HAND, handed, 1).wait_recv()
            pack[:, 0:LEFT_HALF] = jnp.zeros((SLAB, LEFT_HALF), LOW)
            pack[:, LEFT_HALF:] = handed[...]

        pack_copy(0).start()

    def add(target, source):
        target[...] = target[...] + source[...]

    def landing(block):
        return blocks.at[8 + block, 0] if block < 4 else core_in.at[block - 4]

    def scatter(turn, stage):
        slot = SUM_SLOT[turn]
        block, lanes = turn // 2, lanes_of(turn)
        run = blocks.at[part(block)]
        source, target, peer = (
            (run.at[:, :, 1 - core, :, lanes], landing(block).at[:, :, :, lanes], beside_core),
            (run.at[:, 1 - x, core, upper, lanes], one_a.at[slot], beside_x),
            (run.at[1 - y, :, core, lower, lanes], one_b.at[slot], beside_y),
            (run.at[1 - y, x, core, upper, lanes], two_a.at[slot], beside_y),
            (run.at[y, 1 - x, core, lower, lanes], two_b.at[slot], beside_x),
        )[stage]
        if stage == 0:
            return remote(source, target, core_send.at[turn], core_recv.at[turn], peer)
        return remote(source, target, rs_send.at[slot, stage], rs_recv.at[slot, stage], peer)

    def to_line(turn):
        return remote(
            blocks.at[part(turn // 2), y, x, core, :, lanes_of(turn)],
            line_in.at[turn // 2, :, lanes_of(turn)],
            z_send.at[turn],
            z_recv.at[turn],
            {"section": HOLDER[turn // 2]},
        )

    def to_holder(turn):
        place = EARLY_PLACE[turn // 2]
        return remote(
            blocks.at[part(turn // 2), :, :, core, :, lanes_of(turn)],
            early_in.at[place, :, :, :, lanes_of(turn)],
            z_send.at[turn],
            z_recv.at[turn],
            {"section": HOLDER[turn // 2]},
        )

    def to_group(turn, step):
        return remote(
            blocks.at[part(turn // 2), y, x, core, :, lanes_of(turn)],
            group_in.at[turn // 2, step - 1, :, lanes_of(turn)],
            group_send.at[turn, step - 1],
            group_recv.at[turn, step - 1],
            {"dp": lax.rem(index + step * CUBE, replicas)},
        )

    def gather_back(turn, stage):
        slot = BACK_SLOT[turn]
        run, lanes = blocks.at[part(turn // 2)], lanes_of(turn)
        ref, peer = (
            (run.at[y, x, core, upper, lanes], beside_y),
            (run.at[y, x, core, lower, lanes], beside_x),
            (run.at[:, x, core, upper, lanes], beside_x),
            (run.at[y, :, core, lower, lanes], beside_y),
            (run.at[:, :, core, :, lanes], beside_core),
        )[stage]
        return remote(ref, ref, ag_send.at[slot, stage], ag_recv.at[slot, stage], peer)

    def write_out(block):
        place = OWN[HOLDER[block]].index(block)
        return pltpu.make_async_copy(
            blocks.at[part(block)], total.at[place], out_sem.at[place]
        )

    @worker
    def reduce_core(block):
        scatter(2 * block, 0).start()
        scatter(2 * block + 1, 0).start()

    def wave_of(turn):
        return 0 if turn // 2 in WAVES[0] else 1

    def is_early(turn):
        return turn // 2 in EARLY

    def in_plane(turn):
        return me == HOLDER[turn // 2] if is_early(turn) else works

    def add_four(turn, source):
        for yy in range(2):
            for xx in range(2):
                add(
                    blocks.at[part(turn // 2), yy, xx, core, :, lanes_of(turn)],
                    source.at[yy, xx, :, lanes_of(turn)],
                )

    def reduce_one(turn):
        @pl.when(works)
        def _():
            scatter(turn, 0).wait()
            add_four(turn, landing(turn // 2))
            if not is_early(turn):
                scatter(turn, 1).start()
                scatter(turn, 2).start()

        if is_early(turn):

            @pl.when(me == 1 - HOLDER[turn // 2])
            def _():
                to_holder(turn).start()

    def reduce_early(turn):
        @pl.when(me == HOLDER[turn // 2])
        def _():
            to_holder(turn).wait_recv()
            add_four(turn, early_in.at[EARLY_PLACE[turn // 2]])
            scatter(turn, 1).start()
            scatter(turn, 2).start()

    def reduce_two(turn):
        @pl.when(in_plane(turn))
        def _():
            reduce_two_now(turn)

    def reduce_two_now(turn):
        block, lanes = turn // 2, lanes_of(turn)
        run = blocks.at[part(block)]
        scatter(turn, 1).wait()
        for yy in range(2):
            add(run.at[yy, x, core, upper, lanes], one_a.at[SUM_SLOT[turn], yy])
        scatter(turn, 3).start()
        scatter(turn, 2).wait()
        for xx in range(2):
            add(run.at[y, xx, core, lower, lanes], one_b.at[SUM_SLOT[turn], xx])
        scatter(turn, 4).start()

    def reduce_three(turn):
        @pl.when(in_plane(turn))
        def _():
            reduce_three_now(turn)

        @pl.when(me == HOLDER[turn // 2])
        def _():
            for clear, peer in ((clear_y, beside_y), (clear_x, beside_x)):
                pl.semaphore_signal(
                    clear.at[wave_of(turn)], inc=1, device_id=peer, device_id_type=MESH
                )

        if not is_early(turn):

            @pl.when(me == 1 - HOLDER[turn // 2])
            def _():
                to_line(turn).start()

    def reduce_three_now(turn):
        block, lanes = turn // 2, lanes_of(turn)
        run = blocks.at[part(block)]
        scatter(turn, 3).wait()
        add(run.at[y, x, core, upper, lanes], two_a.at[SUM_SLOT[turn]])
        scatter(turn, 4).wait()
        add(run.at[y, x, core, lower, lanes], two_b.at[SUM_SLOT[turn]])
        if groups > 1:
            for step in range(1, groups):
                to_group(turn, step).start()
            for step in range(1, groups):
                to_group(turn, step).wait()
            for step in range(1, groups):
                copy = pltpu.make_async_copy(
                    group_in.at[block, step - 1, :, lanes], group_piece, group_load
                )
                copy.start()
                copy.wait()
                add(run.at[y, x, core, :, lanes], group_piece)

    def spread_one(turn):
        pl.semaphore_wait(clear_y.at[wave_of(turn)], 1)
        gather_back(turn, 0).start()
        pl.semaphore_wait(clear_x.at[wave_of(turn)], 1)
        gather_back(turn, 1).start()

    def spread_early(turn):
        @pl.when(me == HOLDER[turn // 2])
        def _():
            spread_one(turn)

    def reduce_line(turn):
        @pl.when(me == HOLDER[turn // 2])
        def _():
            block, lanes = turn // 2, lanes_of(turn)
            to_line(turn).wait_recv()
            add(blocks.at[part(block), y, x, core, :, lanes], line_in.at[block, :, lanes])
            spread_one(turn)

    def spread_two(turn):
        @pl.when(me == HOLDER[turn // 2])
        def _():
            gather_back(turn, 0).wait()
            gather_back(turn, 2).start()
            gather_back(turn, 1).wait()
            gather_back(turn, 3).start()

    def spread_core(turn):
        @pl.when(me == HOLDER[turn // 2])
        def _():
            gather_back(turn, 2).wait()
            gather_back(turn, 3).wait()
            gather_back(turn, 4).start()

    def spread_done(turn):
        @pl.when(me == HOLDER[turn // 2])
        def _():
            gather_back(turn, 4).wait()
            if turn % 2 == 1:
                write_out(turn // 2).start()

        @pl.when(me == 1 - HOLDER[turn // 2])
        def _():
            (to_holder if is_early(turn) else to_line)(turn).wait_send()

    late_stages = (
        reduce_one, reduce_two, reduce_three, reduce_line, spread_two, spread_core, spread_done,
    )
    early_stages = (
        reduce_one, reduce_early, reduce_two, reduce_three, spread_early, spread_two, spread_core,
        spread_done,
    )

    class Wave:
        def __init__(self, order, spacing, early_at):
            self.order, self.at = turns(*order), 0
            late = range(1, 1 + 7 * spacing, spacing)
            early = (1,) + tuple(range(early_at, early_at + 7 * spacing, spacing))
            self.plans = [
                tuple(zip(early_stages, early) if is_early(turn) else zip(late_stages, late))
                for turn in self.order
            ]
            self.last = max(i + plan[-1][1] for i, plan in enumerate(self.plans))

        def tick(self, count=1):
            for _ in range(count):
                due = []
                for place, turn in enumerate(self.order):
                    for stage, offset in self.plans[place]:
                        if place + offset == self.at:
                            due.append((offset, stage, turn))
                for _, stage, turn in sorted(due, key=lambda item: -item[0]):
                    stage(turn)
                self.at += 1

        def left(self):
            return self.at <= self.last

    one, two = (Wave(*given) for given in zip(WAVES, SPACING, EARLY_AT))

    small[...] = jnp.zeros_like(small)

    gather_wait_own()
    gather_send()

    @pl.when(me >= 2)
    def _():
        guest_copy(TOKENS).wait_send()
        guest_copy(COTANGENT).start()

    for tick in range(gather_ticks):
        gather_tick(tick)
        at = tick - gather_plan[0][1]
        if at == 0:
            for step in range(1, sections):
                vector_copy(step).wait()
        if at < 0:
            continue
        if at == 1:

            @pl.when(works)
            def _():
                guest_copy(TOKENS).wait_recv()

        if at % 2 == 1 and at < 6:
            project(at // 2)
        if at == 5:
            heads_forward(0, 2)
        if at == 6:
            heads_forward(2, 4)
        if at == 7:
            heads_forward(4, 6)
            attention_close()
        if at == 9:
            inner_blocks(0, 1)
        if at == 10:
            inner_blocks(1, 2)
    inner_blocks(2, 4)
    mlp_close()

    @pl.when(works)
    def _():
        guest_copy(COTANGENT).wait_recv()

    mlp_open_backward()
    for reader, wanted in WANTED.items():
        for turn in turns(*wanted):
            gather_finish(turn, reader)

    for block in range(4):
        second_grad(block)
        reduce_core(8 + block)
    one.tick(5)
    for block in range(2):
        inner_grad(block)
        reduce_core(4 + block)
    leads_first()
    one.tick(4)
    for block in range(2, 4):
        inner_grad(block)
        reduce_core(4 + block)
    leads_second()
    rows_leave()
    one.tick(4)
    leads_third()
    one.tick(4)
    leads_fourth()

    @pl.when(works)
    def _():
        pl.semaphore_signal(credit, inc=1, device_id=beside_core, device_id_type=MESH)

    leads_close()
    attention_open_backward()
    out_grad()

    @pl.when(works)
    def _():
        pl.semaphore_wait(credit, 1)

    reduce_core(3)
    one.tick(4)
    heads_backward(0, 2)
    two.tick(2)
    heads_backward(2, 4)
    one.tick()
    two.tick()
    heads_backward(4, 6)
    one.tick()
    pack_join()
    for block in range(3):
        project_grad(block)
        reduce_core(block)
        one.tick()
        two.tick(2)
        if block == 1:
            pack_second()

    def small_copy(step):
        return remote(
            small, small_all.at[index], small_send.at[step], small_recv.at[step], replica(step)
        )

    def sum_copy(step):
        return remote(
            small_sum, smalls.at[me], sum_send.at[step], sum_recv.at[step], others[step - 1]
        )

    def own_sum():
        return pltpu.make_async_copy(small_sum, smalls.at[me], sum_send.at[0])

    @pl.loop(1, replicas)
    def _(step):
        small_copy(step).start()

    small_all[index] = small[...]
    for block in range(3):
        tokens_back(block)
        one.tick()
        two.tick()
    tokens_close()
    pack_third()

    @pl.loop(1, replicas)
    def _(step):
        small_copy(step).wait()

    small_sum[...] = jnp.sum(small_all[...], axis=0)
    for place in range(1, sections):
        sum_copy(place).start()
    own_sum().start()
    pack_fourth()
    while one.left() or two.left():
        if one.left():
            one.tick()
        if two.left():
            two.tick()

    for place in range(1, sections):
        sum_copy(place).wait()
    own_sum().wait()
    pack_last()

    for holder in (0, 1):

        @pl.when(me == holder)
        def _():
            for block in OWN[holder]:
                write_out(block).wait()

    @pl.when(me != 3)
    def _():
        lead_copy(COT, cot_slab, cot_leads, 3).wait_send()

    @pl.when(me == 0)
    def _():
        lead_copy(H1, h1_slab, h1_leads, 1).wait_send()

    @pl.when(works)
    def _():
        lead_copy(H2, h2_slab, h2_leads, 2).wait_send()
        guest_copy(OUT).wait_send()
        guest_copy(GRAD).wait_send()

    @pl.when(me >= 2)
    def _():
        guest_copy(COTANGENT).wait_send()
        guest_copy(GRAD).wait_recv()

    rows_store(1).start()
    rows_store(1).wait()
    rows_store(0).wait()

    @pl.when(me == 1)
    def _():
        hop_copy(GRAD1, lead_grad1, -1).wait_send()
        hop_copy(HAND, handed, -1).wait_send()

    @pl.when(me == 2)
    def _():
        hop_copy(THIRD, lead_third, 1).wait_send()
        hop_copy(GRAD2, lead_grad2, -1).wait_send()

    @pl.when(me == 3)
    def _():
        for place in range(1, sections):
            spread_copy(FOURTH, lead_fourth, place).wait_send()
        hop_copy(GRAD3, lead_grad3, -1).wait_send()
        hop_copy(HAND, handed, -1).wait_send()


def run_layers(sections, replicas, tokens, cotangent, seg_doc, gain, bias, wide, half):
    groups = replicas // CUBE
    rows = 2 * tokens.shape[0]
    seg_rows = tokens.shape[0] // 2
    vector = (8, D)
    block = (2, 2, 2, PIECE, D)
    reduced_groups = max(groups - 1, 1)
    in_vmem = pl.BlockSpec(memory_space=pltpu.VMEM)
    anywhere = pl.BlockSpec(memory_space=pl.ANY)
    slab = pltpu.VMEM((SLAB, D), LOW)
    leads = pltpu.VMEM((sections, SLAB, D), LOW)
    low_rows = pltpu.VMEM((rows, D), LOW)
    full_rows = pltpu.VMEM((rows, D), F32)
    return pl.pallas_call(
        partial(layer_kernel, sections, replicas),
        out_shape=(
            jax.ShapeDtypeStruct(tokens.shape, LOW),
            jax.ShapeDtypeStruct(tokens.shape, LOW),
            jax.ShapeDtypeStruct((OWNED,) + block, LOW),
            jax.ShapeDtypeStruct((groups, CUBE // 2, SLAB, PACK), LOW),
            jax.ShapeDtypeStruct((sections,) + vector, F32),
            jax.ShapeDtypeStruct(
                (REDUCED if groups > 1 else 1, reduced_groups, PIECE, D), LOW
            ),
        ),
        in_specs=[anywhere] * 2 + [in_vmem] * 3 + [anywhere] * 4,
        out_specs=[anywhere] * 6,
        scratch_shapes=[
            pltpu.VMEM((REDUCED + 8,) + block, LOW),
            pltpu.VMEM((max(8 * rows, 6 * D), D), LOW),
            pltpu.VMEM((8, 2, 2, PIECE, D), LOW),
            pltpu.VMEM((SLOTS, 2, HALF, WIDTH), LOW),
            pltpu.VMEM((SLOTS, 2, HALF, WIDTH), LOW),
            pltpu.VMEM((SLOTS, HALF, WIDTH), LOW),
            pltpu.VMEM((SLOTS, HALF, WIDTH), LOW),
            pltpu.VMEM((REDUCED, PIECE, D), LOW),
            pltpu.VMEM((EARLY_PLACES, 2, 2, PIECE, D), LOW),
            pltpu.VMEM((sections,) + vector, F32),
            low_rows, low_rows, low_rows,
            pltpu.VMEM((rows, 3 * D), LOW),
            pltpu.VMEM((4, PAIRS, 2, seg_rows, seg_rows), F32),
            low_rows, low_rows, full_rows,
            pltpu.VMEM((rows, 128), F32),
            full_rows, full_rows,
            pltpu.VMEM((rows, 128), F32),
            full_rows, low_rows,
            slab, slab, slab, leads, leads, leads,
            slab, slab, slab, slab, slab,
            pltpu.VMEM((SLAB, 3 * D), LOW),
            pltpu.VMEM((SLAB, 3 * D), LOW),
            pltpu.VMEM((PAIRS, 2, SLAB, SLAB), F32),
            slab,
            pltpu.VMEM((SLAB, D), F32),
            pltpu.VMEM((SLAB, 128), F32),
            pltpu.VMEM((SLAB, 4 * D), LOW),
            pltpu.VMEM((SLAB, 4 * D), F32),
            pltpu.VMEM((SLAB, PACK), LOW),
            pltpu.VMEM((SLAB, HALF_PACK), LOW),
            pltpu.VMEM((CUBE // 2, SLAB, PACK), LOW),
            pltpu.VMEM(vector, F32),
            pltpu.VMEM((replicas,) + vector, F32),
            pltpu.VMEM(vector, F32),
            pltpu.VMEM((PIECE, WIDTH), LOW),
            DMA((2,)),
            DMA((4,)),
            DMA((4,)),
            DMA((2,)),
            DMA((ROUNDS,)),
            DMA((ROUNDS,)),
            DMA((4, 5)),
            DMA((4, 5)),
            DMA((GATHERED,)),
            DMA((2 * REDUCED,)),
            DMA((2 * REDUCED,)),
            DMA((SLOTS, 5)),
            DMA((SLOTS, 5)),
            DMA((2 * REDUCED,)),
            DMA((2 * REDUCED,)),
            DMA((2 * REDUCED if groups > 1 else 1, reduced_groups)),
            DMA((2 * REDUCED if groups > 1 else 1, reduced_groups)),
            DMA,
            DMA((SLOTS, 5)),
            DMA((SLOTS, 5)),
            DMA((OWNED,)),
            DMA((5,)),
            DMA((5,)),
            DMA((groups,)),
            DMA((groups,)),
            DMA((replicas,)),
            DMA((replicas,)),
            DMA((sections,)),
            DMA((sections,)),
            DMA((sections,)),
            DMA((sections,)),
            DMA((3,)),
            DMA((3, sections)),
            DMA((1, sections)),
            DMA((1,)),
            DMA((5,)),
            DMA((5,)),
            pltpu.SemaphoreType.REGULAR,
            pltpu.SemaphoreType.REGULAR((len(WAVES),)),
            pltpu.SemaphoreType.REGULAR((len(WAVES),)),
        ],
        compiler_params=pltpu.CompilerParams(
            collective_id=0, has_side_effects=True, vmem_limit_bytes=VMEM_BYTES
        ),
    )(
        tokens, cotangent, seg_doc, gain, bias,
        wide.reshape(2, 2, 2, PIECE, 4 * D), half.reshape(2, 2, 2, 2, PIECE, D), wide, half,
    )


VMEM_BYTES = 62 * 1024 * 1024


def close_kernel(
    total, packs, smalls, rows_in, grads_in,
    wide_out, half_out, gain_out, bias_out, rows_out, grads_out,
    blocks, packed, result, rows, grads, block_sem, result_sem, pack_sem, rows_sem, back_sem,
):
    me = lax.axis_index("section")
    near = me < 2
    groups = packs.shape[0]
    pack_copy = pltpu.make_async_copy(packs, packed, pack_sem)
    loads = [
        pltpu.make_async_copy(total.at[place], blocks.at[place], block_sem.at[place])
        for place in range(OWNED)
    ]
    passing = [
        (
            pltpu.make_async_copy(source, buffer, rows_sem.at[i]),
            pltpu.make_async_copy(buffer, target, back_sem.at[i]),
        )
        for i, (source, buffer, target) in enumerate(
            ((rows_in, rows, rows_out), (grads_in, grads, grads_out))
        )
    ]
    pack_copy.start()
    for load in loads:
        load.start()
    for arrive, _ in passing:
        arrive.start()

    every = jnp.sum(smalls[...], axis=0)
    mine = smalls[me]
    for row, out in ((0, gain_out), (1, bias_out)):
        value = jnp.where(me == 0, every[row : row + 1], every[2 + row : 3 + row])
        out[...] = jnp.where(near, value, 0.0) + mine[4 + row : 5 + row]

    pack_copy.wait()
    factors = packed[...].reshape(groups * CUBE // 2 * SLAB, PACK)
    stores = []
    for place in range(OWNED):
        if place < 4:
            left = factors[:, 0:D] if place < 3 else factors[:, LEFT_OUT:RIGHT]
            right = factors[:, RIGHT + place * D : RIGHT + (place + 1) * D]
            target = wide_out.at[0, :, pl.ds(place * D, D)]
        else:
            left = factors[:, LEFT_HALF + (place - 4) * D : LEFT_HALF + (place - 3) * D]
            right = factors[:, RIGHT_HALF:]
            target = half_out.at[0, pl.ds((place - 4) * D, D)]
        loads[place].wait()
        for strip in range(2):
            rows_of = pl.ds(strip * WIDTH, WIDTH)
            summed = blocks[place, strip].reshape(WIDTH, D).astype(F32)
            result[place, rows_of] = jnp.where(near, summed, 0.0) + outer(
                left[:, strip * WIDTH : (strip + 1) * WIDTH], right
            )
        store = pltpu.make_async_copy(result.at[place], target, result_sem.at[place])
        store.start()
        stores.append(store)
    for arrive, leave in passing:
        arrive.wait()
        leave.start()
    for store in stores:
        store.wait()
    for _, leave in passing:
        leave.wait()


def close(total, packs, smalls, rows, grads):
    in_vmem = pl.BlockSpec(memory_space=pltpu.VMEM)
    anywhere = pl.BlockSpec(memory_space=pl.ANY)
    return pl.pallas_call(
        close_kernel,
        out_shape=(
            jax.ShapeDtypeStruct((1, D, 4 * D), F32),
            jax.ShapeDtypeStruct((1, 2 * D, D), F32),
            jax.ShapeDtypeStruct((1, D), F32),
            jax.ShapeDtypeStruct((1, D), F32),
            jax.ShapeDtypeStruct(rows.shape, LOW),
            jax.ShapeDtypeStruct(rows.shape, LOW),
        ),
        in_specs=[anywhere, anywhere, in_vmem, anywhere, anywhere],
        out_specs=[anywhere, anywhere, in_vmem, in_vmem, anywhere, anywhere],
        scratch_shapes=[
            pltpu.VMEM(total.shape, LOW),
            pltpu.VMEM(packs.shape, LOW),
            pltpu.VMEM((OWNED, D, D), F32),
            pltpu.VMEM(rows.shape, LOW),
            pltpu.VMEM(rows.shape, LOW),
            DMA((OWNED,)),
            DMA((OWNED,)),
            DMA,
            DMA((2,)),
            DMA((2,)),
        ],
        compiler_params=pltpu.CompilerParams(vmem_limit_bytes=VMEM_BYTES),
    )(total, packs, smalls, rows, grads)


def on_device(tokens, cotangent, seg_doc, wide_in, half_out, norm_gain, norm_bias):
    sections = lax.axis_size("section")
    replicas = lax.axis_size("dp")
    rows, grads, total, packs, smalls, _ = run_layers(
        sections, replicas, tokens, cotangent, seg_doc, norm_gain, norm_bias, wide_in[0], half_out[0]
    )
    wide_grad, half_grad, gain_grad, bias_grad, layer_out, tokens_grad = close(
        total, packs, smalls, rows, grads
    )
    return layer_out, tokens_grad, wide_grad, half_grad, gain_grad, bias_grad


def solution(mesh):
    placed = (
        P(("dp", "section"), None),
        P(("dp", "section"), None),
        P("dp", None),
        P("section", None, None),
        P("section", None, None),
        P("section", None),
        P("section", None),
    )
    return jax.shard_map(
        on_device,
        mesh=mesh,
        in_specs=placed,
        out_specs=(
            P(("dp", "section"), None),
            P(("dp", "section"), None),
            P("section", None, None),
            P("section", None, None),
            P("section", None),
            P("section", None),
        ),
        check_vma=False,
    )
```

```python
from functools import partial

import jax
import jax.numpy as jnp
from jax import lax
from jax.experimental import pallas as pl
from jax.experimental.pallas import tpu as pltpu
from jax.sharding import PartitionSpec as P

D = 768
HEADS = 12
PAIRS = HEADS // 2
CUBE = 8
PIECE = D // CUBE
HALF = PIECE // 2
WIDTH = D // 2
SLAB = 16
HOLDER = (0, 0, 0, 0, 1, 1, 1, 1, 0, 0, 1, 1, 2, 2)
GATHERED = len(HOLDER)
ROUNDS = 2 * GATHERED
REDUCED = 12
OWN = {0: (0, 1, 2, 3, 8, 9), 1: (4, 5, 6, 7, 10, 11)}
OWNED = len(OWN[0])
WANTED = {0: (4, 5, 6, 7, 10, 11), 1: (0, 1, 2, 3, 8, 9), 3: (12, 13)}
WAVES = ((8, 9, 10, 11, 4, 5, 6, 7), (3, 0, 1, 2))
EARLY = (8, 10)
SPACING = (4, 2)
EARLY_AT = (13, 5)
SLOT = {
    2 * block + side: (2 * place + side) % 4
    for wanted in WANTED.values()
    for place, block in enumerate(wanted)
    for side in range(2)
}


def sum_slots(orders):
    slots, base = {}, 0
    for spacing, order in zip(SPACING, orders):
        late = [block for block in order if block not in EARLY]
        for place, block in enumerate(late):
            for side in range(2):
                slots[2 * block + side] = base + (2 * place + side) % (2 * spacing)
        base += 2 * spacing
    for place, block in enumerate(EARLY):
        for side in range(2):
            slots[2 * block + side] = base + 2 * place + side
    return slots


SUM_SLOT = sum_slots(WAVES)
BACK_SLOT = {}
for holder in OWN:
    BACK_SLOT |= {
        turn: slot
        for turn, slot in sum_slots(
            [[b for b in order if HOLDER[b] == holder] for order in WAVES]
        ).items()
        if HOLDER[turn // 2] == holder
    }
SLOTS = 2 * sum(SPACING) + 2 * len(EARLY)
EARLY_PLACE = {
    block: [other for other in EARLY if HOLDER[other] == HOLDER[block]].index(block)
    for block in EARLY
}
EARLY_PLACES = max(EARLY_PLACE.values(), default=0) + 1
LEFT_OUT, RIGHT, LEFT_HALF, RIGHT_HALF, PACK = D, 2 * D, 6 * D, 8 * D, 9 * D
HALF_PACK = PACK // 2
LOW = jnp.bfloat16
F32 = jnp.float32
DMA = pltpu.SemaphoreType.DMA
MESH = pl.DeviceIdType.MESH


def dot(left, right):
    return jnp.dot(left, right, preferred_element_type=F32)


def dot_right(left, right):
    return lax.dot_general(left, right, (((1,), (1,)), ((), ())), preferred_element_type=F32)


def outer(left, right):
    return lax.dot_general(left, right, (((0,), (0,)), ((), ())), preferred_element_type=F32)


def normalize(summed, gain, bias):
    average = jnp.mean(summed, axis=-1, keepdims=True)
    centred = summed - average
    inv_dev = lax.rsqrt(jnp.mean(centred * centred, axis=-1, keepdims=True) + 1e-05)
    normed = centred * inv_dev
    return normed * gain + bias, normed, inv_dev


def normalize_backward(grad, normed, inv_dev, gain):
    scaled = grad * gain
    mean_scaled = jnp.mean(scaled, axis=-1, keepdims=True)
    mean_normed = jnp.mean(scaled * normed, axis=-1, keepdims=True)
    grad_sum = inv_dev * (scaled - mean_scaled - normed * mean_normed)
    return (
        grad_sum,
        jnp.sum(grad * normed, axis=0, keepdims=True),
        jnp.sum(grad, axis=0, keepdims=True),
    )


def gelu_pair(value):
    bell = jnp.exp(-0.5 * value * value)
    base = 1.0 + (0.3275911 * 0.7071067811865476) * jnp.abs(value)
    guess = pl.reciprocal(base, approx=True)
    t = guess * (2.0 - base * guess)
    poly = t * (
        0.5 * 0.254829592
        + t
        * (
            0.5 * -0.284496736
            + t * (0.5 * 1.421413741 + t * (0.5 * -1.453152027 + t * (0.5 * 1.061405429)))
        )
    )
    tail = poly * bell
    below = jnp.where(value >= 0, 1.0 - tail, tail)
    return value * below, below + value * bell * 0.3989422804014327


def position():
    index = lax.axis_index("dp")
    return (lax.rem(index // 4, 2), lax.rem(index // 2, 2), lax.rem(index, 2), index // CUBE)


def remote(source, target, send, receive, device):
    return pltpu.make_async_remote_copy(
        src_ref=source,
        dst_ref=target,
        send_sem=send,
        recv_sem=receive,
        device_id=device,
        device_id_type=MESH,
    )


def layer_kernel(
    sections, replicas,
    tokens, cotangent, seg_doc, norm_gain, norm_bias, wide, half, wide_flat, half_flat,
    layer_out, grad_tokens, total, packs, smalls, group_in,
    blocks, flat, core_in, one_a, one_b, two_a, two_b, line_in, early_in, vectors,
    token_rows, cot_rows, out_rows,
    qkv, probs, context, h1, norm0, dev0, summed, norm1, dev1, branch, kept,
    cot_slab, h1_slab, h2_slab, cot_leads, h1_leads, h2_leads,
    lead_third, lead_fourth, lead_grad3, lead_grad2, lead_grad1, handed,
    lead_qkv, lead_probs, lead_context, lead_norm, lead_dev, lead_act, lead_slope,
    doc_rows, pack, pack_in, factors, small, small_all, small_sum, group_piece,
    rows_load, guest_send, guest_recv, rows_out,
    line_send, line_recv, cube_send, cube_recv, load_sem,
    core_send, core_recv, rs_send, rs_recv, z_send, z_recv, group_send, group_recv, group_load, ag_send, ag_recv,
    out_sem, pack_send, pack_recv, group_pack_send, group_pack_recv,
    small_send, small_recv, sum_send, sum_recv,
    vector_send, vector_recv, lead_send, lead_recv, spread_send, spread_recv, hop_send, hop_recv,
    credit, clear_x, clear_y,
):
    me = lax.axis_index("section")
    index = lax.axis_index("dp")
    y, x, core, group = position()
    groups = replicas // CUBE
    micro_rows = tokens.shape[0]
    seg_rows = micro_rows // 2
    rows_all = 2 * micro_rows
    works = me < 2

    def cube_peer(yy, xx, cc):
        return {"dp": group * CUBE + yy * 4 + xx * 2 + cc}

    beside_x = cube_peer(y, 1 - x, core)
    beside_y = cube_peer(1 - y, x, core)
    beside_core = cube_peer(y, x, 1 - core)
    others = [{"section": lax.rem(me + step, sections)} for step in range(1, sections)]

    def replica(step):
        return {"dp": lax.rem(index + step, replicas)}

    barrier = pltpu.get_barrier_semaphore()
    for other in others:
        pl.semaphore_signal(barrier, inc=1, device_id=other, device_id_type=MESH)

    @pl.loop(1, replicas)
    def _(step):
        pl.semaphore_signal(barrier, inc=1, device_id=replica(step), device_id_type=MESH)

    own_part, guest_part = pl.ds(0, micro_rows), pl.ds(micro_rows, micro_rows)

    def load_rows(place):
        source, target = ((tokens, token_rows), (cotangent, cot_rows))[place]
        return pltpu.make_async_copy(source, target.at[own_part], rows_load.at[place])

    load_rows(0).start()
    load_rows(1).start()

    def load(block):
        if block < 8:
            source = wide.at[:, :, :, :, pl.ds((block % 4) * D, D)]
        else:
            source = half.at[block % 2]
        return pltpu.make_async_copy(source, blocks.at[block], load_sem.at[block])

    def flat_rows(place):
        return pl.ds(place * D, D)

    def load_own(place):
        if place < 4:
            source = wide_flat.at[:, pl.ds(place * D, D)]
        else:
            source = half_flat.at[flat_rows(place - 4)]
        return pltpu.make_async_copy(source, flat.at[flat_rows(place)], load_sem.at[place])

    for holder in (0, 1):

        @pl.when(me == holder)
        def _():
            for block in OWN[holder]:
                load(block).start()

    @pl.when(me >= 2)
    def _():
        for place in range(4):
            load_own(place).start()

    def load_upper(block):
        return pltpu.make_async_copy(
            half.at[block], core_in.at[pl.ds(2 * block, 2)], load_sem.at[REDUCED + block]
        )

    @pl.when(me == 2)
    def _():
        for block in range(2):
            load_upper(block).start()

    @pl.when(me == 3)
    def _():
        for place in (4, 5):
            load_own(place).start()

    pl.semaphore_wait(barrier, sections - 1 + replicas - 1)

    def guest_copy(kind):
        down = {"section": lax.rem(me + sections - 2, sections)}
        up = {"section": lax.rem(me + 2, sections)}
        source, target, device = (
            (token_rows.at[own_part], token_rows.at[guest_part], down),
            (cot_rows.at[own_part], cot_rows.at[guest_part], down),
            (out_rows.at[guest_part], out_rows.at[own_part], up),
            (h1.at[guest_part], h1.at[own_part], up),
        )[kind]
        return remote(source, target, guest_send.at[kind], guest_recv.at[kind], device)

    TOKENS, COTANGENT, OUT, GRAD = 0, 1, 2, 3

    load_rows(0).wait()
    load_rows(1).wait()

    @pl.when(me >= 2)
    def _():
        guest_copy(TOKENS).start()

    row_of = lax.broadcasted_iota(jnp.int32, (SLAB, D), 0)

    def lead_rows(ref, count):
        value = jnp.zeros((SLAB, D), F32)
        for lead in range(count):
            row = ref[lead * seg_rows : lead * seg_rows + SLAB].astype(F32)[0:1]
            value = jnp.where(row_of == lead, row, value)
        return value.astype(LOW)

    def lead_copy(kind, slab, target, reader):
        return remote(
            slab, target.at[me], lead_send.at[kind], lead_recv.at[kind, me], {"section": reader}
        )

    def lead_start(kind, slab, target, reader):
        @pl.when(me != reader)
        def _():
            lead_copy(kind, slab, target, reader).start()

        @pl.when(me == reader)
        def _():
            target[reader] = slab[...]

    def lead_wait(kind, slab, target, reader, senders):
        for section in range(senders):
            if section != reader:
                remote(
                    slab, target.at[section], lead_send.at[kind], lead_recv.at[kind, section],
                    {"section": section},
                ).wait_recv()

    def collected(target, senders):
        value = jnp.zeros((SLAB, D), F32)
        for section in range(senders):
            slab = target[section].astype(F32)
            for micro in range(section, sections, senders):
                for lead in range(2):
                    place = (micro - section) // senders * 2 + lead
                    value = jnp.where(
                        row_of == 2 * micro + lead, slab[place : place + 1], value
                    )
        return value

    def spread_copy(kind, slab, step):
        return remote(
            slab, slab, spread_send.at[kind, step], spread_recv.at[kind], others[step - 1]
        )

    def hop_copy(kind, slab, step):
        return remote(
            slab, slab, hop_send.at[kind], hop_recv.at[kind],
            {"section": lax.rem(me + step + sections, sections)},
        )

    def leads_of(slab, micro):
        value = slab[...].astype(F32)
        return [
            jnp.sum(jnp.where(row_of == 2 * micro + lead, value, 0.0), axis=0, keepdims=True)
            for lead in range(2)
        ]

    COT, H1, H2 = 0, 1, 2
    FOURTH = 0
    THIRD, GRAD3, GRAD2, HAND, GRAD1 = 0, 1, 2, 3, 4

    def vector_copy(step):
        return remote(
            vectors.at[me], vectors.at[me], vector_send.at[step], vector_recv.at[step],
            others[step - 1],
        )

    vectors[me, 0:1] = norm_gain[...]
    vectors[me, 1:2] = norm_bias[...]
    for step in range(1, sections):
        vector_copy(step).start()
    cot_slab[...] = lead_rows(cot_rows, 2)
    lead_start(COT, cot_slab, cot_leads, 3)

    upper, lower = pl.ds(0, HALF), pl.ds(HALF, HALF)

    def lanes_of(turn):
        return pl.ds((turn % 2) * WIDTH, WIDTH)

    def turns(*order):
        return tuple(2 * block + side for block in order for side in range(2))

    def place_of(block):
        if block < REDUCED:
            return blocks.at[block]
        return core_in.at[pl.ds(2 * (block - REDUCED), 2)]

    def line_copy(turn, reader):
        block, lanes = turn // 2, lanes_of(turn)
        piece = place_of(block).at[y, x, core, :, lanes]
        return remote(
            piece,
            piece,
            line_send.at[turn],
            line_recv.at[turn],
            {"section": reader},
        )

    def cube_copy(turn, stage):
        full, lanes = place_of(turn // 2), lanes_of(turn)
        ref, peer = (
            (full.at[y, x, core, upper, lanes], beside_x),
            (full.at[y, x, core, lower, lanes], beside_y),
            (full.at[y, :, core, upper, lanes], beside_y),
            (full.at[:, x, core, lower, lanes], beside_x),
            (full.at[:, :, core, :, lanes], beside_core),
        )[stage]
        slot = SLOT[turn]
        return remote(ref, ref, cube_send.at[slot, stage], cube_recv.at[slot, stage], peer)

    def gather_line(turn, reader):
        @pl.when(me == reader)
        def _():
            line_copy(turn, reader).wait_recv()
            cube_copy(turn, 0).start()
            cube_copy(turn, 1).start()

    def gather_two(turn, reader):
        @pl.when(me == reader)
        def _():
            cube_copy(turn, 0).wait()
            cube_copy(turn, 2).start()
            cube_copy(turn, 1).wait()
            cube_copy(turn, 3).start()

    def gather_three(turn, reader):
        @pl.when(me == reader)
        def _():
            cube_copy(turn, 2).wait()
            cube_copy(turn, 3).wait()
            cube_copy(turn, 4).start()

    def gather_ready(turn, reader):
        @pl.when(me == reader)
        def _():
            cube_copy(turn, 4).wait()

    def gather_finish(turn, reader):
        @pl.when(me == HOLDER[turn // 2])
        def _():
            line_copy(turn, reader).wait_send()

    def gather_send():
        for reader, wanted in WANTED.items():

            @pl.when(me == HOLDER[wanted[0]])
            def _():
                for turn in turns(*wanted):
                    line_copy(turn, reader).start()

    gather_plan = ((gather_ready, 6), (gather_three, 4), (gather_two, 2), (gather_line, 0))
    gather_ticks = 2 * OWNED + gather_plan[0][1]

    def gather_tick(tick):
        for stage, offset in gather_plan:
            at = tick - offset
            for reader, wanted in WANTED.items():
                if 0 <= at < 2 * len(wanted):
                    stage(2 * wanted[at // 2] + at % 2, reader)

    def gather_wait_own():
        @pl.when(me == 2)
        def _():
            for block in range(2):
                load_upper(block).wait()

        for holder in (0, 1):

            @pl.when(me == holder)
            def _():
                for block in OWN[holder]:
                    load(block).wait()

    def worker(step):
        def run(*given):
            @pl.when(works)
            def _():
                step(*given)

        return run

    def weight(block):
        return blocks[block].reshape(D, D)

    def act_rows(block):
        return pl.ds(pl.multiple_of(block * rows_all, SLAB), rows_all)

    def slope_rows(block):
        return pl.ds(pl.multiple_of((4 + block) * rows_all, SLAB), rows_all)

    lane_of = lax.broadcasted_iota(jnp.int32, (1, 128), 1)
    first_half = lane_of < 64
    head_masks = (first_half.astype(LOW), (~first_half).astype(LOW))
    segs = range(4)

    def chunks(size, body):
        @pl.loop(0, rows_all // size)
        def _(step):
            body(pl.multiple_of(step * size, size), size)

    @worker
    def project(block):
        qkv[:, block * D : (block + 1) * D] = dot(token_rows[...], weight(block)).astype(LOW)

    def seg_slice(seg):
        return pl.ds(seg * seg_rows, seg_rows)

    def pair_lanes(pair):
        return [pl.ds(pl.multiple_of(part * D + pair * 128, 128), 128) for part in range(3)]

    def softmax(scores):
        raised = jnp.exp(scores - jnp.max(scores, axis=-1, keepdims=True))
        return raised / jnp.sum(raised, axis=-1, keepdims=True)

    @worker
    def heads_forward(first, last):
        @pl.loop(first, last, unroll=2)
        def _(pair):
            at_q, at_k, at_v = pair_lanes(pair)
            heads = [(seg, place) for seg in segs for place in range(2)]
            scores = [
                dot_right(qkv[seg_slice(seg), at_q] * head_masks[place], qkv[seg_slice(seg), at_k])
                * 0.125
                for seg, place in heads
            ]
            found = [softmax(score) for score in scores]
            for (seg, place), prob in zip(heads, found):
                probs[seg, pair, place] = prob
            mixed = [
                dot(prob.astype(LOW), qkv[seg_slice(seg), at_v])
                for (seg, place), prob in zip(heads, found)
            ]
            for seg in segs:
                context[seg_slice(seg), at_q] = jnp.where(
                    first_half, mixed[2 * seg], mixed[2 * seg + 1]
                ).astype(LOW)

    @worker
    def attention_close():
        summed[...] = dot_right(context[...], weight(3))
        gain, bias = vectors[0, 0:1], vectors[0, 1:2]

        def body(start, size):
            rows = pl.ds(start, size)
            out, normed, inv_dev = normalize(
                token_rows[rows].astype(F32) + summed[rows], gain, bias
            )
            norm0[rows] = normed
            dev0[rows] = jnp.broadcast_to(inv_dev, (size, 128))
            h1[rows] = out.astype(LOW)
            branch[rows] = jnp.zeros((size, D), F32)

        chunks(256, body)
        h1_slab[...] = lead_rows(h1, 4)
        lead_start(H1, h1_slab, h1_leads, 1)

    @worker
    def inner_blocks(first, last):
        count = 2
        size = rows_all // count

        @pl.loop(first, last)
        def _(place):
            block = lax.rem(2 * me + place, 4)
            for step in range(count):
                rows = pl.ds(step * size, size)
                start = pl.multiple_of(block * rows_all + step * size, SLAB)
                value, grade = gelu_pair(dot(h1[rows], weight(4 + block)))
                flat[pl.ds(start, size)] = value.astype(LOW)
                flat[pl.ds(pl.multiple_of(4 * rows_all + start, SLAB), size)] = grade.astype(LOW)
                branch[rows] += dot(flat[pl.ds(start, size)], weight(8 + block))

    @worker
    def mlp_close():
        gain, bias = vectors[1, 0:1], vectors[1, 1:2]

        def body(start, size):
            rows = pl.ds(start, size)
            out, normed, inv_dev = normalize(h1[rows].astype(F32) + branch[rows], gain, bias)
            norm1[rows] = normed
            dev1[rows] = jnp.broadcast_to(inv_dev, (size, 128))
            out_rows[rows] = out.astype(LOW)

        chunks(256, body)
        h2_slab[...] = lead_rows(out_rows, 4)
        lead_start(H2, h2_slab, h2_leads, 2)

    @worker
    def rows_leave():
        guest_copy(OUT).start()

    def add_small(row, value):
        small[row : row + 1] += value

    @worker
    def mlp_open_backward():
        gain = vectors[1, 0:1]

        def body(start, size):
            rows = pl.ds(start, size)
            place = start + lax.broadcasted_iota(jnp.int32, (size, D), 0)
            grad = jnp.where(lax.rem(place, seg_rows) == 0, 0.0, cot_rows[rows].astype(F32))
            grad_sum, grad_gain, grad_bias = normalize_backward(
                grad, norm1[rows], dev1[rows][:, 0:1], gain
            )
            branch[rows] = grad_sum
            kept[rows] = grad_sum.astype(LOW)
            add_small(2, grad_gain)
            add_small(3, grad_bias)

        chunks(256, body)

    def part(block):
        return block + 4 if block < 4 else block + 8

    def store_part(block, left, right):
        for strip in range(2):
            lanes = slice(strip * WIDTH, (strip + 1) * WIDTH)
            blocks[part(block), strip] = (
                outer(left[:, lanes], right).astype(LOW).reshape(2, 2, PIECE, D)
            )

    @worker
    def second_grad(block):
        store_part(8 + block, flat[act_rows(block)], kept[...])

    @worker
    def inner_grad(block):
        grad_act = dot_right(kept[...], weight(8 + block))
        grad_inner = (grad_act * flat[slope_rows(block)].astype(F32)).astype(LOW)
        flat[act_rows(block)] = grad_inner
        branch[...] += dot_right(flat[act_rows(block)], weight(4 + block))
        store_part(4 + block, h1[...], flat[act_rows(block)])

    @worker
    def attention_open_backward():
        gain = vectors[0, 0:1]
        leads = leads_of(lead_grad1, me) + leads_of(lead_grad1, me + 2)

        def body(start, size):
            rows = pl.ds(start, size)
            place = start + lax.broadcasted_iota(jnp.int32, (size, D), 0)
            grad = branch[rows]
            for lead in range(4):
                grad = jnp.where(place == lead * seg_rows, leads[lead], grad)
            grad = grad.astype(LOW).astype(F32)
            grad_sum, grad_gain, grad_bias = normalize_backward(
                grad, norm0[rows], dev0[rows][:, 0:1], gain
            )
            summed[rows] = grad_sum
            kept[rows] = grad_sum.astype(LOW)
            add_small(0, grad_gain)
            add_small(1, grad_bias)

        chunks(256, body)

    @worker
    def out_grad():
        store_part(3, kept[...], context[...])
        context[...] = dot(kept[...], weight(3)).astype(LOW)

    @worker
    def heads_backward(first, last):
        @pl.loop(first, last, unroll=2)
        def _(pair):
            at_q, at_k, at_v = pair_lanes(pair)
            heads = [(seg, place) for seg in segs for place in range(2)]
            grad_probs = [
                dot_right(
                    context[seg_slice(seg), at_q] * head_masks[place], qkv[seg_slice(seg), at_v]
                )
                for seg, place in heads
            ]
            grad_scores = []
            for (seg, place), grad_prob in zip(heads, grad_probs):
                prob = probs[seg, pair, place]
                inside = prob * grad_prob
                grad_score = inside - prob * jnp.sum(inside, axis=-1, keepdims=True)
                grad_scores.append(grad_score.astype(LOW))
            for seg in segs:
                rows = seg_slice(seg)
                query, key, grad = qkv[rows, at_q], qkv[rows, at_k], context[rows, at_q]
                mine = grad_scores[2 * seg : 2 * seg + 2]
                found = [probs[seg, pair, place].astype(LOW) for place in range(2)]
                for at, both, scale in (
                    (at_q, [dot(score, key) for score in mine], 0.125),
                    (at_k, [outer(score, query) for score in mine], 0.125),
                    (at_v, [outer(prob, grad) for prob in found], 1.0),
                ):
                    merged = jnp.where(first_half, both[0], both[1]) * scale
                    qkv[rows, at] = merged.astype(LOW)

    @worker
    def project_grad(block):
        store_part(block, token_rows[...], qkv[:, block * D : (block + 1) * D])

    @worker
    def tokens_back(block):
        summed[...] += dot_right(qkv[:, block * D : (block + 1) * D], weight(block))

    @worker
    def tokens_close():
        h1[...] = summed[...].astype(LOW)
        guest_copy(GRAD).start()

    def leads_mlp_forward(value, first, second, gain, bias):
        total_branch = value.astype(F32)
        for block in range(4):
            lanes = slice(block * D, (block + 1) * D)
            out, grade = gelu_pair(dot(value, first(block)))
            lead_act[:, lanes] = out.astype(LOW)
            lead_slope[:, lanes] = grade
            total_branch = total_branch + dot(lead_act[:, lanes], second(block))
        out, normed, inv_dev = normalize(total_branch, gain, bias)
        lead_norm[...] = normed
        lead_dev[...] = jnp.broadcast_to(inv_dev, (SLAB, 128))
        pack[:, 0:D] = value
        pack[:, LEFT_OUT:RIGHT] = value
        return out

    def leads_mlp_backward(grad, first, second, gain):
        grad_sum, grad_gain, grad_bias = normalize_backward(
            grad, lead_norm[...], lead_dev[:, 0:1], gain
        )
        add_small(4, grad_gain)
        add_small(5, grad_bias)
        low_sum = grad_sum.astype(LOW)
        result = grad_sum
        for block in range(4):
            lanes = slice(block * D, (block + 1) * D)
            grad_inner = (dot_right(low_sum, second(block)) * lead_slope[:, lanes]).astype(LOW)
            pack[:, RIGHT + block * D : RIGHT + (block + 1) * D] = grad_inner
            result = result + dot_right(grad_inner, first(block))
        pack[:, LEFT_HALF:RIGHT_HALF] = lead_act[:, 2 * D :]
        pack[:, RIGHT_HALF:] = low_sum
        handed[:, 0 : 2 * D] = lead_act[:, 0 : 2 * D]
        handed[:, 2 * D :] = low_sum
        return result

    def own_weight(place):
        return flat[flat_rows(place)]

    def last_second(block):
        if block >= 2:
            return own_weight(2 + block)
        return core_in[2 * block : 2 * block + 2].reshape(D, D)

    def leads_first():
        @pl.when(me == 2)
        def _():
            lead_wait(H2, h2_slab, h2_leads, 2, 2)
            for place in range(4):
                load_own(place).wait()
            value = collected(h2_leads, 2).astype(LOW)
            pack[:, 0:D] = value
            for block in range(3):
                lead_qkv[:, block * D : (block + 1) * D] = dot(value, own_weight(block)).astype(LOW)
            doc_copy = pltpu.make_async_copy(seg_doc, doc_rows, rows_load.at[2])
            doc_copy.start()
            doc_copy.wait()
            docs = doc_rows[...]
            row, column = (lax.broadcasted_iota(jnp.int32, (SLAB, SLAB), i) for i in range(2))
            sort = jnp.where(row == column, 2.0, 0.0)
            for micro in range(seg_doc.shape[0]):
                pair_sort = jnp.where(
                    docs[micro : micro + 1, 0:1] == docs[micro : micro + 1, 1:2], 2.0, 1.0
                )
                near = (row // 2 == micro) & (column // 2 == micro) & (row != column)
                sort = jnp.where(near, pair_sort, sort)
            for pair in range(PAIRS):
                at = [slice(p * D + pair * 128, p * D + (pair + 1) * 128) for p in range(3)]
                query, key, val = (lead_qkv[:, lanes] for lanes in at)
                parts = []
                for place in range(2):
                    scores = dot_right(query * head_masks[place], key) * 0.125
                    scores = jnp.where(
                        sort > 1.5, scores, jnp.where(sort > 0.5, -1000000000.0, -1e30)
                    )
                    raised = jnp.exp(scores - jnp.max(scores, axis=-1, keepdims=True))
                    prob = raised / jnp.sum(raised, axis=-1, keepdims=True)
                    lead_probs[pair, place] = prob
                    parts.append(dot(prob.astype(LOW), val))
                lead_context[:, pair * 128 : (pair + 1) * 128] = jnp.where(
                    first_half, parts[0], parts[1]
                ).astype(LOW)
            summed_rows = value.astype(F32) + dot_right(lead_context[...], own_weight(3))
            out, normed, inv_dev = normalize(summed_rows, vectors[2, 0:1], vectors[2, 1:2])
            lead_norm[...] = normed
            lead_dev[...] = jnp.broadcast_to(inv_dev, (SLAB, 128))
            lead_third[...] = out.astype(LOW)
            hop_copy(THIRD, lead_third, 1).start()

        @pl.when(me == 1)
        def _():
            lead_wait(H1, h1_slab, h1_leads, 1, 2)
            leads_mlp_forward(
                collected(h1_leads, 2).astype(LOW),
                lambda block: weight(4 + block),
                lambda block: weight(8 + block),
                vectors[1, 0:1],
                vectors[1, 1:2],
            )

    def leads_second():
        @pl.when(me == 3)
        def _():
            hop_copy(THIRD, lead_third, -1).wait_recv()
            for place in range(6):
                load_own(place).wait()
            out = leads_mlp_forward(
                lead_third[...], own_weight, last_second, vectors[3, 0:1], vectors[3, 1:2]
            )
            lead_fourth[...] = out.astype(LOW)
            for step in range(1, sections):
                spread_copy(FOURTH, lead_fourth, step).start()
            lead_wait(COT, cot_slab, cot_leads, 3, sections)
            grad = leads_mlp_backward(
                collected(cot_leads, sections), own_weight, last_second, vectors[3, 0:1]
            )
            lead_grad3[...] = grad.astype(LOW)
            hop_copy(GRAD3, lead_grad3, -1).start()
            hop_copy(HAND, handed, -1).start()

    def leads_third():
        @pl.when(me == 2)
        def _():
            hop_copy(GRAD3, lead_grad3, 1).wait_recv()
            grad_sum, grad_gain, grad_bias = normalize_backward(
                lead_grad3[...].astype(F32), lead_norm[...], lead_dev[:, 0:1], vectors[2, 0:1]
            )
            add_small(4, grad_gain)
            add_small(5, grad_bias)
            low_sum = grad_sum.astype(LOW)
            pack[:, LEFT_OUT:RIGHT] = low_sum
            pack[:, RIGHT + 3 * D : LEFT_HALF] = lead_context[...]
            grad_context = dot(low_sum, own_weight(3)).astype(LOW)
            for pair in range(PAIRS):
                at = [slice(p * D + pair * 128, p * D + (pair + 1) * 128) for p in range(3)]
                query, key, val = (lead_qkv[:, lanes] for lanes in at)
                grad = grad_context[:, pair * 128 : (pair + 1) * 128]
                grads = ([], [], [])
                for place in range(2):
                    prob = lead_probs[pair, place]
                    grad_prob = dot_right(grad * head_masks[place], val)
                    inside = prob * grad_prob
                    grad_score = inside - prob * jnp.sum(inside, axis=-1, keepdims=True)
                    grad_score = grad_score.astype(LOW)
                    grads[0].append(dot(grad_score, key))
                    grads[1].append(outer(grad_score, query))
                    grads[2].append(outer(prob.astype(LOW), grad))
                for lanes, pair_grads, scale in zip(at, grads, (0.125, 0.125, 1.0)):
                    merged = jnp.where(first_half, pair_grads[0], pair_grads[1]) * scale
                    pack[:, RIGHT + lanes.start : RIGHT + lanes.stop] = merged.astype(LOW)
            result = grad_sum
            for block in range(3):
                result = result + dot_right(
                    pack[:, RIGHT + block * D : RIGHT + (block + 1) * D], own_weight(block)
                )
            lead_grad2[...] = result.astype(LOW)
            hop_copy(GRAD2, lead_grad2, -1).start()
            hop_copy(HAND, handed, 1).wait_recv()
            pack[:, LEFT_HALF:] = handed[...]

    def leads_fourth():
        @pl.when(me == 1)
        def _():
            hop_copy(GRAD2, lead_grad2, 1).wait_recv()
            grad = leads_mlp_backward(
                lead_grad2[...].astype(F32),
                lambda block: weight(4 + block),
                lambda block: weight(8 + block),
                vectors[1, 0:1],
            )
            lead_grad1[...] = grad.astype(LOW)
            hop_copy(GRAD1, lead_grad1, -1).start()
            hop_copy(HAND, handed, -1).start()

    half_lanes = pl.ds(pl.multiple_of(core * HALF_PACK, 128), HALF_PACK)
    other_lanes = pl.ds(pl.multiple_of((1 - core) * HALF_PACK, 128), HALF_PACK)
    first_peer = {"dp": group * CUBE + (y + core - 2 * y * core) * 4
                  + (x + (1 - core) * (1 - 2 * x)) * 2 + core}
    second_peer = {"dp": group * CUBE + (y + (1 - core) * (1 - 2 * y)) * 4
                   + (x + core - 2 * x * core) * 2 + core}

    def pack_copy(stage):
        chip = y * 2 + x
        first_chip = (y + core - 2 * y * core) * 2 + x + (1 - core) * (1 - 2 * x)
        if stage == 0:
            source, target, peer = pack.at[:, other_lanes], pack_in, beside_core
        elif stage == 1:
            source = target = factors.at[chip, :, half_lanes]
            peer = first_peer
        elif stage == 2:
            source = target = factors.at[chip, :, half_lanes]
            peer = second_peer
        elif stage == 3:
            source = target = factors.at[first_chip, :, half_lanes]
            peer = second_peer
        else:
            source = target = factors.at[:, :, half_lanes]
            peer = beside_core
        return remote(source, target, pack_send.at[stage], pack_recv.at[stage], peer)

    def pack_join():
        pack_copy(0).wait()

        @pl.loop(0, HALF_PACK // WIDTH)
        def _(step):
            start = pl.multiple_of(step * WIDTH, 128)
            lanes = pl.ds(pl.multiple_of(core * HALF_PACK + start, 128), WIDTH)
            mine = pack[:, lanes].astype(F32)[0:8]
            theirs = pack_in[:, pl.ds(start, WIDTH)].astype(F32)[0:8]
            low_rows = jnp.where(core == 0, mine, theirs)
            high_rows = jnp.where(core == 0, theirs, mine)
            factors[y * 2 + x, :, lanes] = jnp.concatenate([low_rows, high_rows]).astype(LOW)

        pack_copy(1).start()

    def pack_second():
        pack_copy(1).wait()
        pack_copy(2).start()
        pack_copy(3).start()

    def pack_third():
        pack_copy(2).wait()
        pack_copy(3).wait()
        pack_copy(4).start()

    def to_packs(step):
        return remote(
            factors, packs.at[group], group_pack_send.at[step], group_pack_recv.at[step],
            {"dp": lax.rem(index + step * CUBE, replicas)},
        )

    def own_pack():
        return pltpu.make_async_copy(factors, packs.at[group], group_pack_send.at[0])

    def pack_fourth():
        pack_copy(4).wait()
        own_pack().start()
        for step in range(1, groups):
            to_packs(step).start()

    def pack_last():
        own_pack().wait()
        for step in range(1, groups):
            to_packs(step).wait()

    def rows_store(place):
        source, target = ((out_rows, layer_out), (h1, grad_tokens))[place]
        return pltpu.make_async_copy(source.at[own_part], target, rows_out.at[place])

    def leads_close():
        @pl.when(me != 3)
        def _():
            spread_copy(FOURTH, lead_fourth, 1).wait_recv()

        @pl.when(me >= 2)
        def _():
            guest_copy(OUT).wait_recv()

        leads = leads_of(lead_fourth, me)
        for lead in range(2):
            rows = pl.ds(lead * seg_rows, SLAB)
            out_rows[rows] = jnp.where(
                row_of == 0, leads[lead], out_rows[rows].astype(F32)
            ).astype(LOW)
        rows_store(0).start()

        @pl.when(me == 0)
        def _():
            hop_copy(GRAD1, lead_grad1, 1).wait_recv()
            hop_copy(HAND, handed, 1).wait_recv()
            pack[:, 0:LEFT_HALF] = jnp.zeros((SLAB, LEFT_HALF), LOW)
            pack[:, LEFT_HALF:] = handed[...]

        pack_copy(0).start()

    def add(target, source):
        target[...] = target[...] + source[...]

    def landing(block):
        return blocks.at[8 + block, 0] if block < 4 else core_in.at[block - 4]

    def scatter(turn, stage):
        slot = SUM_SLOT[turn]
        block, lanes = turn // 2, lanes_of(turn)
        run = blocks.at[part(block)]
        source, target, peer = (
            (run.at[:, :, 1 - core, :, lanes], landing(block).at[:, :, :, lanes], beside_core),
            (run.at[:, 1 - x, core, upper, lanes], one_a.at[slot], beside_x),
            (run.at[1 - y, :, core, lower, lanes], one_b.at[slot], beside_y),
            (run.at[1 - y, x, core, upper, lanes], two_a.at[slot], beside_y),
            (run.at[y, 1 - x, core, lower, lanes], two_b.at[slot], beside_x),
        )[stage]
        if stage == 0:
            return remote(source, target, core_send.at[turn], core_recv.at[turn], peer)
        return remote(source, target, rs_send.at[slot, stage], rs_recv.at[slot, stage], peer)

    def to_line(turn):
        return remote(
            blocks.at[part(turn // 2), y, x, core, :, lanes_of(turn)],
            line_in.at[turn // 2, :, lanes_of(turn)],
            z_send.at[turn],
            z_recv.at[turn],
            {"section": HOLDER[turn // 2]},
        )

    def to_holder(turn):
        place = EARLY_PLACE[turn // 2]
        return remote(
            blocks.at[part(turn // 2), :, :, core, :, lanes_of(turn)],
            early_in.at[place, :, :, :, lanes_of(turn)],
            z_send.at[turn],
            z_recv.at[turn],
            {"section": HOLDER[turn // 2]},
        )

    def to_group(turn, step):
        return remote(
            blocks.at[part(turn // 2), y, x, core, :, lanes_of(turn)],
            group_in.at[turn // 2, step - 1, :, lanes_of(turn)],
            group_send.at[turn, step - 1],
            group_recv.at[turn, step - 1],
            {"dp": lax.rem(index + step * CUBE, replicas)},
        )

    def gather_back(turn, stage):
        slot = BACK_SLOT[turn]
        run, lanes = blocks.at[part(turn // 2)], lanes_of(turn)
        ref, peer = (
            (run.at[y, x, core, upper, lanes], beside_y),
            (run.at[y, x, core, lower, lanes], beside_x),
            (run.at[:, x, core, upper, lanes], beside_x),
            (run.at[y, :, core, lower, lanes], beside_y),
            (run.at[:, :, core, :, lanes], beside_core),
        )[stage]
        return remote(ref, ref, ag_send.at[slot, stage], ag_recv.at[slot, stage], peer)

    def write_out(block):
        place = OWN[HOLDER[block]].index(block)
        return pltpu.make_async_copy(
            blocks.at[part(block)], total.at[place], out_sem.at[place]
        )

    @worker
    def reduce_core(block):
        scatter(2 * block, 0).start()
        scatter(2 * block + 1, 0).start()

    def wave_of(turn):
        return 0 if turn // 2 in WAVES[0] else 1

    def is_early(turn):
        return turn // 2 in EARLY

    def in_plane(turn):
        return me == HOLDER[turn // 2] if is_early(turn) else works

    def add_four(turn, source):
        for yy in range(2):
            for xx in range(2):
                add(
                    blocks.at[part(turn // 2), yy, xx, core, :, lanes_of(turn)],
                    source.at[yy, xx, :, lanes_of(turn)],
                )

    def reduce_one(turn):
        @pl.when(works)
        def _():
            scatter(turn, 0).wait()
            add_four(turn, landing(turn // 2))
            if not is_early(turn):
                scatter(turn, 1).start()
                scatter(turn, 2).start()

        if is_early(turn):

            @pl.when(me == 1 - HOLDER[turn // 2])
            def _():
                to_holder(turn).start()

    def reduce_early(turn):
        @pl.when(me == HOLDER[turn // 2])
        def _():
            to_holder(turn).wait_recv()
            add_four(turn, early_in.at[EARLY_PLACE[turn // 2]])
            scatter(turn, 1).start()
            scatter(turn, 2).start()

    def reduce_two(turn):
        @pl.when(in_plane(turn))
        def _():
            reduce_two_now(turn)

    def reduce_two_now(turn):
        block, lanes = turn // 2, lanes_of(turn)
        run = blocks.at[part(block)]
        scatter(turn, 1).wait()
        for yy in range(2):
            add(run.at[yy, x, core, upper, lanes], one_a.at[SUM_SLOT[turn], yy])
        scatter(turn, 3).start()
        scatter(turn, 2).wait()
        for xx in range(2):
            add(run.at[y, xx, core, lower, lanes], one_b.at[SUM_SLOT[turn], xx])
        scatter(turn, 4).start()

    def reduce_three(turn):
        @pl.when(in_plane(turn))
        def _():
            reduce_three_now(turn)

        @pl.when(me == HOLDER[turn // 2])
        def _():
            for clear, peer in ((clear_y, beside_y), (clear_x, beside_x)):
                pl.semaphore_signal(
                    clear.at[wave_of(turn)], inc=1, device_id=peer, device_id_type=MESH
                )

        if not is_early(turn):

            @pl.when(me == 1 - HOLDER[turn // 2])
            def _():
                to_line(turn).start()

    def reduce_three_now(turn):
        block, lanes = turn // 2, lanes_of(turn)
        run = blocks.at[part(block)]
        scatter(turn, 3).wait()
        add(run.at[y, x, core, upper, lanes], two_a.at[SUM_SLOT[turn]])
        scatter(turn, 4).wait()
        add(run.at[y, x, core, lower, lanes], two_b.at[SUM_SLOT[turn]])
        if groups > 1:
            for step in range(1, groups):
                to_group(turn, step).start()
            for step in range(1, groups):
                to_group(turn, step).wait()
            for step in range(1, groups):
                copy = pltpu.make_async_copy(
                    group_in.at[block, step - 1, :, lanes], group_piece, group_load
                )
                copy.start()
                copy.wait()
                add(run.at[y, x, core, :, lanes], group_piece)

    def spread_one(turn):
        pl.semaphore_wait(clear_y.at[wave_of(turn)], 1)
        gather_back(turn, 0).start()
        pl.semaphore_wait(clear_x.at[wave_of(turn)], 1)
        gather_back(turn, 1).start()

    def spread_early(turn):
        @pl.when(me == HOLDER[turn // 2])
        def _():
            spread_one(turn)

    def reduce_line(turn):
        @pl.when(me == HOLDER[turn // 2])
        def _():
            block, lanes = turn // 2, lanes_of(turn)
            to_line(turn).wait_recv()
            add(blocks.at[part(block), y, x, core, :, lanes], line_in.at[block, :, lanes])
            spread_one(turn)

    def spread_two(turn):
        @pl.when(me == HOLDER[turn // 2])
        def _():
            gather_back(turn, 0).wait()
            gather_back(turn, 2).start()
            gather_back(turn, 1).wait()
            gather_back(turn, 3).start()

    def spread_core(turn):
        @pl.when(me == HOLDER[turn // 2])
        def _():
            gather_back(turn, 2).wait()
            gather_back(turn, 3).wait()
            gather_back(turn, 4).start()

    def spread_done(turn):
        @pl.when(me == HOLDER[turn // 2])
        def _():
            gather_back(turn, 4).wait()
            if turn % 2 == 1:
                write_out(turn // 2).start()

        @pl.when(me == 1 - HOLDER[turn // 2])
        def _():
            (to_holder if is_early(turn) else to_line)(turn).wait_send()

    late_stages = (
        reduce_one, reduce_two, reduce_three, reduce_line, spread_two, spread_core, spread_done,
    )
    early_stages = (
        reduce_one, reduce_early, reduce_two, reduce_three, spread_early, spread_two, spread_core,
        spread_done,
    )

    class Wave:
        def __init__(self, order, spacing, early_at):
            self.order, self.at = turns(*order), 0
            late = range(1, 1 + 7 * spacing, spacing)
            early = (1,) + tuple(range(early_at, early_at + 7 * spacing, spacing))
            self.plans = [
                tuple(zip(early_stages, early) if is_early(turn) else zip(late_stages, late))
                for turn in self.order
            ]
            self.last = max(i + plan[-1][1] for i, plan in enumerate(self.plans))

        def tick(self, count=1):
            for _ in range(count):
                due = []
                for place, turn in enumerate(self.order):
                    for stage, offset in self.plans[place]:
                        if place + offset == self.at:
                            due.append((offset, stage, turn))
                for _, stage, turn in sorted(due, key=lambda item: -item[0]):
                    stage(turn)
                self.at += 1

        def left(self):
            return self.at <= self.last

    one, two = (Wave(*given) for given in zip(WAVES, SPACING, EARLY_AT))

    small[...] = jnp.zeros_like(small)

    gather_wait_own()
    gather_send()

    @pl.when(me >= 2)
    def _():
        guest_copy(TOKENS).wait_send()
        guest_copy(COTANGENT).start()

    for tick in range(gather_ticks):
        gather_tick(tick)
        at = tick - gather_plan[0][1]
        if at == 0:
            for step in range(1, sections):
                vector_copy(step).wait()
        if at < 0:
            continue
        if at == 1:

            @pl.when(works)
            def _():
                guest_copy(TOKENS).wait_recv()

        if at % 2 == 1 and at < 6:
            project(at // 2)
        if at == 5:
            heads_forward(0, 2)
        if at == 6:
            heads_forward(2, 4)
        if at == 7:
            heads_forward(4, 6)
            attention_close()
        if at == 9:
            inner_blocks(0, 1)
        if at == 10:
            inner_blocks(1, 2)
    inner_blocks(2, 4)
    mlp_close()

    @pl.when(works)
    def _():
        guest_copy(COTANGENT).wait_recv()

    mlp_open_backward()
    for reader, wanted in WANTED.items():
        for turn in turns(*wanted):
            gather_finish(turn, reader)

    for block in range(4):
        second_grad(block)
        reduce_core(8 + block)
    one.tick(5)
    for block in range(2):
        inner_grad(block)
        reduce_core(4 + block)
    leads_first()
    one.tick(4)
    for block in range(2, 4):
        inner_grad(block)
        reduce_core(4 + block)
    leads_second()
    rows_leave()
    one.tick(4)
    leads_third()
    one.tick(4)
    leads_fourth()

    @pl.when(works)
    def _():
        pl.semaphore_signal(credit, inc=1, device_id=beside_core, device_id_type=MESH)

    leads_close()
    attention_open_backward()
    out_grad()

    @pl.when(works)
    def _():
        pl.semaphore_wait(credit, 1)

    reduce_core(3)
    one.tick(4)
    heads_backward(0, 2)
    two.tick(2)
    heads_backward(2, 4)
    one.tick()
    two.tick()
    heads_backward(4, 6)
    one.tick()
    pack_join()
    for block in range(3):
        project_grad(block)
        reduce_core(block)
        one.tick()
        two.tick(2)
        if block == 1:
            pack_second()

    def small_copy(step):
        return remote(
            small, small_all.at[index], small_send.at[step], small_recv.at[step], replica(step)
        )

    def sum_copy(step):
        return remote(
            small_sum, smalls.at[me], sum_send.at[step], sum_recv.at[step], others[step - 1]
        )

    def own_sum():
        return pltpu.make_async_copy(small_sum, smalls.at[me], sum_send.at[0])

    @pl.loop(1, replicas)
    def _(step):
        small_copy(step).start()

    small_all[index] = small[...]
    for block in range(3):
        tokens_back(block)
        one.tick()
        two.tick()
    tokens_close()
    pack_third()

    @pl.loop(1, replicas)
    def _(step):
        small_copy(step).wait()

    small_sum[...] = jnp.sum(small_all[...], axis=0)
    for place in range(1, sections):
        sum_copy(place).start()
    own_sum().start()
    pack_fourth()
    while one.left() or two.left():
        if one.left():
            one.tick()
        if two.left():
            two.tick()

    for place in range(1, sections):
        sum_copy(place).wait()
    own_sum().wait()
    pack_last()

    for holder in (0, 1):

        @pl.when(me == holder)
        def _():
            for block in OWN[holder]:
                write_out(block).wait()

    @pl.when(me != 3)
    def _():
        lead_copy(COT, cot_slab, cot_leads, 3).wait_send()

    @pl.when(me == 0)
    def _():
        lead_copy(H1, h1_slab, h1_leads, 1).wait_send()

    @pl.when(works)
    def _():
        lead_copy(H2, h2_slab, h2_leads, 2).wait_send()
        guest_copy(OUT).wait_send()
        guest_copy(GRAD).wait_send()

    @pl.when(me >= 2)
    def _():
        guest_copy(COTANGENT).wait_send()
        guest_copy(GRAD).wait_recv()

    rows_store(1).start()
    rows_store(1).wait()
    rows_store(0).wait()

    @pl.when(me == 1)
    def _():
        hop_copy(GRAD1, lead_grad1, -1).wait_send()
        hop_copy(HAND, handed, -1).wait_send()

    @pl.when(me == 2)
    def _():
        hop_copy(THIRD, lead_third, 1).wait_send()
        hop_copy(GRAD2, lead_grad2, -1).wait_send()

    @pl.when(me == 3)
    def _():
        for place in range(1, sections):
            spread_copy(FOURTH, lead_fourth, place).wait_send()
        hop_copy(GRAD3, lead_grad3, -1).wait_send()
        hop_copy(HAND, handed, -1).wait_send()


def run_layers(sections, replicas, tokens, cotangent, seg_doc, gain, bias, wide, half):
    groups = replicas // CUBE
    rows = 2 * tokens.shape[0]
    seg_rows = tokens.shape[0] // 2
    vector = (8, D)
    block = (2, 2, 2, PIECE, D)
    reduced_groups = max(groups - 1, 1)
    in_vmem = pl.BlockSpec(memory_space=pltpu.VMEM)
    anywhere = pl.BlockSpec(memory_space=pl.ANY)
    slab = pltpu.VMEM((SLAB, D), LOW)
    leads = pltpu.VMEM((sections, SLAB, D), LOW)
    low_rows = pltpu.VMEM((rows, D), LOW)
    full_rows = pltpu.VMEM((rows, D), F32)
    return pl.pallas_call(
        partial(layer_kernel, sections, replicas),
        out_shape=(
            jax.ShapeDtypeStruct(tokens.shape, LOW),
            jax.ShapeDtypeStruct(tokens.shape, LOW),
            jax.ShapeDtypeStruct((OWNED,) + block, LOW),
            jax.ShapeDtypeStruct((groups, CUBE // 2, SLAB, PACK), LOW),
            jax.ShapeDtypeStruct((sections,) + vector, F32),
            jax.ShapeDtypeStruct(
                (REDUCED if groups > 1 else 1, reduced_groups, PIECE, D), LOW
            ),
        ),
        in_specs=[anywhere] * 3 + [in_vmem] * 2 + [anywhere] * 4,
        out_specs=[anywhere] * 6,
        scratch_shapes=[
            pltpu.VMEM((REDUCED + 8,) + block, LOW),
            pltpu.VMEM((max(8 * rows, 6 * D), D), LOW),
            pltpu.VMEM((8, 2, 2, PIECE, D), LOW),
            pltpu.VMEM((SLOTS, 2, HALF, WIDTH), LOW),
            pltpu.VMEM((SLOTS, 2, HALF, WIDTH), LOW),
            pltpu.VMEM((SLOTS, HALF, WIDTH), LOW),
            pltpu.VMEM((SLOTS, HALF, WIDTH), LOW),
            pltpu.VMEM((REDUCED, PIECE, D), LOW),
            pltpu.VMEM((EARLY_PLACES, 2, 2, PIECE, D), LOW),
            pltpu.VMEM((sections,) + vector, F32),
            low_rows, low_rows, low_rows,
            pltpu.VMEM((rows, 3 * D), LOW),
            pltpu.VMEM((4, PAIRS, 2, seg_rows, seg_rows), F32),
            low_rows, low_rows, full_rows,
            pltpu.VMEM((rows, 128), F32),
            full_rows, full_rows,
            pltpu.VMEM((rows, 128), F32),
            full_rows, low_rows,
            slab, slab, slab, leads, leads, leads,
            slab, slab, slab, slab, slab,
            pltpu.VMEM((SLAB, 3 * D), LOW),
            pltpu.VMEM((SLAB, 3 * D), LOW),
            pltpu.VMEM((PAIRS, 2, SLAB, SLAB), F32),
            slab,
            pltpu.VMEM((SLAB, D), F32),
            pltpu.VMEM((SLAB, 128), F32),
            pltpu.VMEM((SLAB, 4 * D), LOW),
            pltpu.VMEM((SLAB, 4 * D), F32),
            pltpu.VMEM(seg_doc.shape, jnp.int32),
            pltpu.VMEM((SLAB, PACK), LOW),
            pltpu.VMEM((SLAB, HALF_PACK), LOW),
            pltpu.VMEM((CUBE // 2, SLAB, PACK), LOW),
            pltpu.VMEM(vector, F32),
            pltpu.VMEM((replicas,) + vector, F32),
            pltpu.VMEM(vector, F32),
            pltpu.VMEM((PIECE, WIDTH), LOW),
            DMA((3,)),
            DMA((4,)),
            DMA((4,)),
            DMA((2,)),
            DMA((ROUNDS,)),
            DMA((ROUNDS,)),
            DMA((4, 5)),
            DMA((4, 5)),
            DMA((GATHERED,)),
            DMA((2 * REDUCED,)),
            DMA((2 * REDUCED,)),
            DMA((SLOTS, 5)),
            DMA((SLOTS, 5)),
            DMA((2 * REDUCED,)),
            DMA((2 * REDUCED,)),
            DMA((2 * REDUCED if groups > 1 else 1, reduced_groups)),
            DMA((2 * REDUCED if groups > 1 else 1, reduced_groups)),
            DMA,
            DMA((SLOTS, 5)),
            DMA((SLOTS, 5)),
            DMA((OWNED,)),
            DMA((5,)),
            DMA((5,)),
            DMA((groups,)),
            DMA((groups,)),
            DMA((replicas,)),
            DMA((replicas,)),
            DMA((sections,)),
            DMA((sections,)),
            DMA((sections,)),
            DMA((sections,)),
            DMA((3,)),
            DMA((3, sections)),
            DMA((1, sections)),
            DMA((1,)),
            DMA((5,)),
            DMA((5,)),
            pltpu.SemaphoreType.REGULAR,
            pltpu.SemaphoreType.REGULAR((len(WAVES),)),
            pltpu.SemaphoreType.REGULAR((len(WAVES),)),
        ],
        compiler_params=pltpu.CompilerParams(
            collective_id=0, has_side_effects=True, vmem_limit_bytes=VMEM_BYTES
        ),
    )(
        tokens, cotangent, seg_doc, gain, bias,
        wide.reshape(2, 2, 2, PIECE, 4 * D), half.reshape(2, 2, 2, 2, PIECE, D), wide, half,
    )


VMEM_BYTES = 62 * 1024 * 1024


def close_kernel(
    total, packs, smalls, rows_in, grads_in,
    wide_out, half_out, gain_out, bias_out, rows_out, grads_out,
    blocks, packed, result, rows, grads, block_sem, result_sem, pack_sem, rows_sem, back_sem,
):
    me = lax.axis_index("section")
    near = me < 2
    groups = packs.shape[0]
    pack_copy = pltpu.make_async_copy(packs, packed, pack_sem)
    loads = [
        pltpu.make_async_copy(total.at[place], blocks.at[place], block_sem.at[place])
        for place in range(OWNED)
    ]
    passing = [
        (
            pltpu.make_async_copy(source, buffer, rows_sem.at[i]),
            pltpu.make_async_copy(buffer, target, back_sem.at[i]),
        )
        for i, (source, buffer, target) in enumerate(
            ((rows_in, rows, rows_out), (grads_in, grads, grads_out))
        )
    ]
    pack_copy.start()
    for load in loads:
        load.start()
    for arrive, _ in passing:
        arrive.start()

    every = jnp.sum(smalls[...], axis=0)
    mine = smalls[me]
    for row, out in ((0, gain_out), (1, bias_out)):
        value = jnp.where(me == 0, every[row : row + 1], every[2 + row : 3 + row])
        out[...] = jnp.where(near, value, 0.0) + mine[4 + row : 5 + row]

    pack_copy.wait()
    factors = packed[...].reshape(groups * CUBE // 2 * SLAB, PACK)
    stores = []
    for place in range(OWNED):
        if place < 4:
            left = factors[:, 0:D] if place < 3 else factors[:, LEFT_OUT:RIGHT]
            right = factors[:, RIGHT + place * D : RIGHT + (place + 1) * D]
            target = wide_out.at[0, :, pl.ds(place * D, D)]
        else:
            left = factors[:, LEFT_HALF + (place - 4) * D : LEFT_HALF + (place - 3) * D]
            right = factors[:, RIGHT_HALF:]
            target = half_out.at[0, pl.ds((place - 4) * D, D)]
        loads[place].wait()
        for strip in range(2):
            rows_of = pl.ds(strip * WIDTH, WIDTH)
            summed = blocks[place, strip].reshape(WIDTH, D).astype(F32)
            result[place, rows_of] = jnp.where(near, summed, 0.0) + outer(
                left[:, strip * WIDTH : (strip + 1) * WIDTH], right
            )
        store = pltpu.make_async_copy(result.at[place], target, result_sem.at[place])
        store.start()
        stores.append(store)
    for arrive, leave in passing:
        arrive.wait()
        leave.start()
    for store in stores:
        store.wait()
    for _, leave in passing:
        leave.wait()


def close(total, packs, smalls, rows, grads):
    in_vmem = pl.BlockSpec(memory_space=pltpu.VMEM)
    anywhere = pl.BlockSpec(memory_space=pl.ANY)
    return pl.pallas_call(
        close_kernel,
        out_shape=(
            jax.ShapeDtypeStruct((1, D, 4 * D), F32),
            jax.ShapeDtypeStruct((1, 2 * D, D), F32),
            jax.ShapeDtypeStruct((1, D), F32),
            jax.ShapeDtypeStruct((1, D), F32),
            jax.ShapeDtypeStruct(rows.shape, LOW),
            jax.ShapeDtypeStruct(rows.shape, LOW),
        ),
        in_specs=[anywhere, anywhere, in_vmem, anywhere, anywhere],
        out_specs=[anywhere, anywhere, in_vmem, in_vmem, anywhere, anywhere],
        scratch_shapes=[
            pltpu.VMEM(total.shape, LOW),
            pltpu.VMEM(packs.shape, LOW),
            pltpu.VMEM((OWNED, D, D), F32),
            pltpu.VMEM(rows.shape, LOW),
            pltpu.VMEM(rows.shape, LOW),
            DMA((OWNED,)),
            DMA((OWNED,)),
            DMA,
            DMA((2,)),
            DMA((2,)),
        ],
        compiler_params=pltpu.CompilerParams(vmem_limit_bytes=VMEM_BYTES),
    )(total, packs, smalls, rows, grads)


def on_device(tokens, cotangent, seg_doc, wide_in, half_out, norm_gain, norm_bias):
    sections = lax.axis_size("section")
    replicas = lax.axis_size("dp")
    rows, grads, total, packs, smalls, _ = run_layers(
        sections, replicas, tokens, cotangent, seg_doc, norm_gain, norm_bias, wide_in[0], half_out[0]
    )
    wide_grad, half_grad, gain_grad, bias_grad, layer_out, tokens_grad = close(
        total, packs, smalls, rows, grads
    )
    return layer_out, tokens_grad, wide_grad, half_grad, gain_grad, bias_grad


def solution(mesh):
    placed = (
        P(("dp", "section"), None),
        P(("dp", "section"), None),
        P("dp", None),
        P("section", None, None),
        P("section", None, None),
        P("section", None),
        P("section", None),
    )
    return jax.shard_map(
        on_device,
        mesh=mesh,
        in_specs=placed,
        out_specs=(
            P(("dp", "section"), None),
            P(("dp", "section"), None),
            P("section", None, None),
            P("section", None, None),
            P("section", None),
            P("section", None),
        ),
        check_vma=False,
    )
```
